32 devices in a mesh: dp: 8 (over z, x), seq: 4 (over y, core).
Axes of the slice: x: 2, y: 2, z: 4, core: 2. Of those that a mesh axis runs over, the one named last changes fastest.
Arguments:
- tokens: bfloat16 [8, 4096, 768], P('dp', 'seq'), may hold values from -6 to 6
- cotangent: bfloat16 [8, 4096, 768], P('dp', 'seq'), may hold values from -6 to 6
- in_weight: float32 [768, 3352], P('dp'), may hold values from -0.21875 to 0.21875
- in_moment: float32 [768, 3352], P('dp'), may hold values from -32 to 32
- in_second: float32 [768, 3352], P('dp'), may hold values from 2.94912 to 11.79648
- out_weight: float32 [1536, 768], P('dp'), may hold values from -0.15625 to 0.15625
- out_moment: float32 [1536, 768], P('dp'), may hold values from -128 to 128
- out_second: float32 [1536, 768], P('dp'), may hold values from 32.768 to 131.072
- channels: float32 [11336], replicated, as said below
- channel_moment: float32 [11336], replicated, as said below
- channel_second: float32 [11336], replicated, as said below
Outputs:
- block_out: float32 [8, 4096, 768], P('dp', 'seq')
- token_grad: float32 [8, 4096, 768], P('dp', 'seq')
- in_weight_new: float32 [768, 3352], P('dp')
- in_moment_new: float32 [768, 3352], P('dp')
- in_second_new: float32 [768, 3352], P('dp')
- out_weight_new: float32 [1536, 768], P('dp')
- out_moment_new: float32 [1536, 768], P('dp')
- out_second_new: float32 [1536, 768], P('dp')
- channels_new: float32 [11336], replicated
- channel_moment_new: float32 [11336], replicated
- channel_second_new: float32 [11336], replicated
The draws below stay inside these ranges and needn't reach their ends.
Inputs may be any that keep to these rules, and one draw needn't show every extreme that they name: channels holds in order pre_gain (768), norm_gain (1536), conv_weight (1792 x 4, row by row), conv_bias (1792), step_bias, rate_log, skip_gain (24 each). `channel_moment`: laid out like channels. `channel_second`: laid out like channels, every entry positive.
All inputs are finite; a program needn't handle non-finite values.
Results may differ from the reference program's by a relative error of at most 0.012.
The reference program's roundings to bfloat16 on the way count: a program that leaves them out, or rounds other values in their place, can miss the bound.
Values may be sent and summed in bfloat16 or wider, within the bound.
No kernel may reach another device: no remote copies, remote signals or barrier semaphores. Data moves between devices by JAX's collectives and lax.ppermute only.
A program may use at most 192 MiB of HBM per device.

```python
import math
import jax
import jax.numpy as jnp
from jax import lax

D = 768
HEADS = 24
HEADDIM = 64
STATE = 128
CONV = 4
STRETCH = 256
STEP = 10
INNER = 1536
XBC = 1792
PROJ = 3352
NCH = 11336
LEN = 4096
SEQUENCES = 8
TOKENS = 32768


def segment_scales(pre_scale, norm_scale, conv_scale, head_scale):
    return jnp.concatenate([jnp.full((D,), pre_scale, jnp.float32), jnp.full((INNER,), norm_scale, jnp.float32), jnp.full((XBC * CONV + XBC,), conv_scale, jnp.float32), jnp.full((3 * HEADS,), head_scale, jnp.float32)])


def draw_channels(key, part):
    key = jax.random.fold_in(key, 11)
    subkeys = jax.random.split(key, 7)
    gain_low, gain_high, rate_high = (0.8, 1.2, 16.0)
    pre_gain = jax.random.uniform(subkeys[0], (D,), jnp.float32, gain_low, gain_high)
    norm_gain = jax.random.uniform(subkeys[1], (INNER,), jnp.float32, gain_low, gain_high)
    conv_weight = jax.random.uniform(subkeys[2], (XBC * CONV,), jnp.float32, -0.85, 0.85)
    conv_bias = jax.random.uniform(subkeys[3], (XBC,), jnp.float32, -0.5, 0.5)
    floor_step = jnp.exp(jax.random.uniform(subkeys[4], (HEADS,), jnp.float32, jnp.log(0.001), jnp.log(0.1)))
    step_bias = floor_step + jnp.log(-jnp.expm1(-floor_step))
    rate_log = jnp.log(jax.random.uniform(subkeys[5], (HEADS,), jnp.float32, 1.0, rate_high))
    skip_gain = jax.random.uniform(subkeys[6], (HEADS,), jnp.float32, 0.5, 1.5)
    return jnp.concatenate([pre_gain, norm_gain, conv_weight, conv_bias, step_bias, rate_log, skip_gain])


def draw_channel_moment(key, part):
    key = jax.random.fold_in(key, 12)
    scales = segment_scales(0.6, 0.7, 0.3, 3.0) * (0.111 * jnp.sqrt(jnp.float32(TOKENS)))
    values = jnp.clip(jax.random.normal(key, (NCH,), jnp.float32), -4.0, 4.0)
    return scales * values


def draw_channel_second(key, part):
    key = jax.random.fold_in(key, 13)
    scales = segment_scales(0.6, 0.7, 0.3, 3.0)
    factor = jnp.exp(jax.random.uniform(key, (NCH,), jnp.float32, 0.0, jnp.log(4.0)))
    return 0.001 * jnp.float32(TOKENS) * scales * scales * factor


def shard_levels(own_key, dims, cuts, smallest, top_value):
    level, own = 1.0, jax.random.fold_in(own_key, 6)
    for position, blocks in cuts:
        steps = jnp.exp(jax.random.uniform(jax.random.fold_in(own, position), (blocks,), jnp.float32, smallest / len(cuts), top_value / len(cuts)))
        level = level * jnp.repeat(steps, dims[position] // blocks).reshape([-1 if axis == position else 1 for axis in range(len(dims))])
    return level


def bell_draw(stream_key, shape, width, reach, shards=(), kind=jnp.bfloat16):
    factor_of = shard_levels(stream_key, shape, shards, -0.22, 0.18) if shards else 1.0
    array = jax.random.normal(stream_key, shape, jnp.float32) * width * factor_of
    return jnp.minimum(jnp.maximum(array, -reach), reach).astype(kind)


def setup_inputs(seed: int = 0) -> dict:
    arg_keys = jax.random.split(jax.random.key(seed), 12)
    tokens = bell_draw(arg_keys[0], (SEQUENCES, LEN, D), 1.0, 6.0, ((0, 8), (1, 4)))
    cotangent = bell_draw(arg_keys[1], (SEQUENCES, LEN, D), 1.0, 6.0, ((0, 8), (1, 4)))
    in_weight = bell_draw(arg_keys[2], (D, PROJ), D ** -0.5, 0.21875, ((0, 8),), jnp.float32)
    in_moment = bell_draw(arg_keys[3], (D, PROJ), (0.0333 * TOKENS ** 0.5), 32.0, ((0, 8),), jnp.float32)
    in_second = jnp.clip(jnp.exp(math.log(11.79648) - 1.3862944 * jax.random.uniform(arg_keys[4], (D, PROJ), jnp.float32) ** shard_levels(arg_keys[4], (D, PROJ), ((0, 8),), -0.2, 0.2)), 2.94912, 11.79648)
    out_weight = bell_draw(arg_keys[5], (INNER, D), INNER ** -0.5, 0.15625, ((0, 8),), jnp.float32)
    out_moment = bell_draw(arg_keys[6], (INNER, D), (0.111 * TOKENS ** 0.5), 128.0, ((0, 8),), jnp.float32)
    out_second = jnp.clip(jnp.exp(math.log(131.072) - 1.3862944 * jax.random.uniform(arg_keys[7], (INNER, D), jnp.float32) ** shard_levels(arg_keys[7], (INNER, D), ((0, 8),), -0.2, 0.2)), 32.768, 131.072)
    channels = draw_channels(jax.random.fold_in(arg_keys[11], 71), 0)
    channel_moment = draw_channel_moment(jax.random.fold_in(arg_keys[11], 71), 0)
    channel_second = draw_channel_second(jax.random.fold_in(arg_keys[11], 71), 0)
    return dict(tokens=tokens, cotangent=cotangent, in_weight=in_weight, in_moment=in_moment, in_second=in_second, out_weight=out_weight, out_moment=out_moment, out_second=out_second, channels=channels, channel_moment=channel_moment, channel_second=channel_second)


highest = lax.Precision.HIGHEST
norm_eps = 1e-05
beta_one = 0.9
beta_two = 0.999
adam_eps = 1e-08
rate_matrix = 0.1
rate_channel = 0.5
decay_matrix = 0.1

@jax.custom_vjp
def low(v):
    return lax.optimization_barrier(v.astype(jnp.bfloat16)).astype(jnp.float32)

@jax.custom_vjp
def low_back(v):
    return v

def low_keep(v):
    return (low(v), None)

def low_pass(kept, grad):
    return (grad,)

def back_keep(v):
    return (v, None)

def back_low(kept, grad):
    return (low(grad),)
low.defvjp(low_keep, low_pass)
low_back.defvjp(back_keep, back_low)

def unpack_channels(channels):
    pieces = []
    offset = 0
    for piece_len in (D, INNER, XBC * CONV, XBC, HEADS, HEADS, HEADS):
        pieces.append(channels[offset:offset + piece_len])
        offset = offset + piece_len
    pre_gain, norm_gain, conv_flat, conv_bias, step_bias, rate_log, skip_gain = pieces
    return (pre_gain, norm_gain, conv_flat.reshape(XBC, CONV), conv_bias, step_bias, rate_log, skip_gain)

def pre_norm(tok_vals, pre_gain):
    return tok_vals * lax.rsqrt(lax.optimization_barrier(jnp.mean(tok_vals * tok_vals, -1, keepdims=True)) + norm_eps) * pre_gain

def causal_conv(values, weights, bias_row):
    length = values.shape[0]
    padded = jnp.concatenate([jnp.zeros((CONV - 1, values.shape[1]), jnp.float32), values], axis=0)
    summed = jnp.zeros_like(values) + bias_row[None, :]
    for offset in range(CONV):
        summed = summed + padded[offset:offset + length] * weights[:, offset][None, :]
    return jax.nn.silu(summed)

def state_space(inputs, steps, rates, write_keys, read_keys):
    seq_len = inputs.shape[0]
    head_count = inputs.shape[1]
    blocks = seq_len // STRETCH
    lower_mask = jnp.arange(STRETCH)[:, None] >= jnp.arange(STRETCH)[None, :]

    def block_step(carry_state, block_data):
        block_inputs, block_steps, block_write, block_read = block_data
        log_decay = -block_steps * rates[None, :]
        cumul = jnp.cumsum(log_decay, axis=0)
        cumul_heads = cumul.T
        gaps_log = cumul_heads[:, :, None] - cumul_heads[:, None, :]
        decays = jnp.exp(jnp.where(lower_mask[None, :, :], gaps_log, -1e+30))
        scores = jnp.dot(block_read, block_write.T, precision=highest)
        scaled = block_inputs * block_steps[:, :, None]
        within = jnp.einsum('hij,jhp->ihp', decays * scores[None, :, :], scaled, precision=highest)
        carried = jnp.einsum('in,hpn->ihp', block_read, carry_state, precision=highest) * jnp.exp(cumul)[:, :, None]
        tail_decay = jnp.exp(cumul[-1][None, :] - cumul)
        state_next = carry_state * jnp.exp(cumul[-1])[:, None, None] + jnp.einsum('jhp,jn->hpn', scaled * tail_decay[:, :, None], block_write, precision=highest)
        return (state_next, within + carried)
    state_zero = jnp.zeros((head_count, HEADDIM, STATE), jnp.float32)
    packed = (inputs.reshape(blocks, STRETCH, head_count, HEADDIM), steps.reshape(blocks, STRETCH, head_count), write_keys.reshape(blocks, STRETCH, STATE), read_keys.reshape(blocks, STRETCH, STATE))
    last_state, outputs = lax.scan(jax.checkpoint(block_step), state_zero, packed)
    return outputs.reshape(seq_len, head_count, HEADDIM)

def mixer_heads(conv_vals, step_raw, step_bias, rate_log, skip_gain):
    head_count = step_raw.shape[1]
    head_width = head_count * HEADDIM
    inputs = conv_vals[:, :head_width].reshape(-1, head_count, HEADDIM)
    write_keys = conv_vals[:, head_width:head_width + STATE]
    read_keys = conv_vals[:, head_width + STATE:]
    steps = jax.nn.softplus(step_raw + step_bias[None, :])
    mixed = state_space(inputs, steps, jnp.exp(rate_log), write_keys, read_keys) + skip_gain[None, :, None] * inputs
    return mixed.reshape(-1, head_width)

def gate_norm(mixed, gate_vals, norm_gain):
    gated = mixed * jax.nn.silu(gate_vals)
    return gated * lax.rsqrt(lax.optimization_barrier(jnp.mean(gated * gated, -1, keepdims=True)) + norm_eps) * norm_gain

def adamw_step(weight, moment, second, gradient, step_rate, decay_rate):
    moment_next = beta_one * moment + (1.0 - beta_one) * gradient
    second_next = beta_two * second + (1.0 - beta_two) * gradient * gradient
    first_fix = 1.0 - beta_one ** STEP
    second_fix = 1.0 - beta_two ** STEP
    update = moment_next / first_fix / (jnp.sqrt(second_next / second_fix) + adam_eps)
    return (weight - step_rate * (update + decay_rate * weight), moment_next, second_next)

def layer(tok_vals, in_weight, out_weight, channels):
    pre_gain, norm_gain, conv_weight, conv_bias, step_bias, rate_log, skip_gain = unpack_channels(channels)
    normed = low(pre_norm(tok_vals, pre_gain))
    projected = low_back(low(jnp.dot(normed, low(in_weight), precision=highest)))
    gate_vals = projected[:, :INNER]
    conv_src = projected[:, INNER:INNER + XBC]
    step_raw = projected[:, INNER + XBC:]
    conv_vals = low(causal_conv(conv_src, conv_weight, conv_bias))
    mixed = low(mixer_heads(conv_vals, step_raw, step_bias, rate_log, skip_gain))
    hidden = low(gate_norm(mixed, gate_vals, norm_gain))
    return tok_vals + jnp.dot(hidden, low(out_weight), precision=highest)

def reference(tokens, cotangent, in_weight, in_moment, in_second, out_weight, out_moment, out_second, channels, channel_moment, channel_second):

    def one_sequence(totals, seq_pair):
        seq_tokens, seq_cot = seq_pair
        result, pullback = jax.vjp(layer, seq_tokens.astype(jnp.float32), in_weight, out_weight, channels)
        tok_grad, in_grad, out_grad, chan_grad = pullback(seq_cot.astype(jnp.float32))
        return ((totals[0] + in_grad, totals[1] + out_grad, totals[2] + chan_grad), (result, tok_grad))
    grad_zero = (jnp.zeros_like(in_weight), jnp.zeros_like(out_weight), jnp.zeros_like(channels))
    sums, outputs = lax.scan(one_sequence, grad_zero, (tokens, cotangent))
    in_grad, out_grad, chan_grad = sums
    block_out, token_grad = outputs
    in_new, in_mom, in_sec = adamw_step(in_weight, in_moment, in_second, in_grad, rate_matrix, decay_matrix)
    out_new, out_mom, out_sec = adamw_step(out_weight, out_moment, out_second, out_grad, rate_matrix, decay_matrix)
    chan_new, chan_mom, chan_sec = adamw_step(channels, channel_moment, channel_second, chan_grad, rate_channel, 0.0)
    return (block_out, token_grad, in_new, in_mom, in_sec, out_new, out_mom, out_sec, chan_new, chan_mom, chan_sec)
```

```python
import math

import jax
import jax.numpy as jnp
from jax import lax
from jax.experimental import pallas as pl
from jax.experimental.pallas import tpu as pltpu
from jax.sharding import PartitionSpec as P

D = 768
HEADS = 24
HEADDIM = 64
STATE = 128
CONV = 4
STEP = 10
INNER = 1536
XBC = 1792
PROJ = 3352
SIDE = 1920
LANES = 128
CHUNK = 128
PAIRS = HEADS // 2
TILES = XBC // LANES
EXTRA = 16

norm_eps = 1e-05
beta_one = 0.9
beta_two = 0.999
adam_eps = 1e-08
rate_matrix = 0.1
rate_channel = 0.5
decay_matrix = 0.1
LOG2E = 1.0 / math.log(2.0)
VMEM = 56 * 1024 * 1024

f32 = jnp.float32
bf16 = jnp.bfloat16
NT = (((1,), (1,)), ((), ()))
TN = (((0,), (0,)), ((), ()))


def dot(a, b):
    return jnp.dot(a, b, preferred_element_type=f32)


def dot_nt(a, b):
    return lax.dot_general(a, b, NT, preferred_element_type=f32)


def dot_tn(a, b):
    return lax.dot_general(a, b, TN, preferred_element_type=f32)


def dot_full(a, b):
    return jnp.dot(a, b, preferred_element_type=f32, precision=lax.Precision.HIGHEST)


def sigmoid(v):
    return 0.5 * jnp.tanh(0.5 * v) + 0.5


def halves(v):
    high = v.astype(bf16)
    return high, (v - high.astype(f32)).astype(bf16)


def expand(v, spread):
    high, rest = halves(v)
    return dot(jnp.concatenate([high, rest], axis=1), spread)


def fold(v):
    return jnp.sum(v.reshape(v.shape[0] // 8, 8, v.shape[1]), axis=0)


def lane(i):
    return slice(i * LANES, (i + 1) * LANES)


def iota(shape, dim):
    return lax.broadcasted_iota(jnp.int32, shape, dim)


def tri(lower):
    rows, cols = iota((CHUNK, CHUNK), 0), iota((CHUNK, CHUNK), 1)
    return (rows >= cols) if lower else (rows <= cols)


def conv_pre(ext, convp, tile):
    cols = lane(tile)
    taps = [ext[5 + k : 5 + k + CHUNK, cols] for k in range(CONV)]
    pre = taps[0] * convp[0:1, cols] + convp[4:5, cols]
    for k in range(1, CONV):
        pre = pre + taps[k] * convp[k : k + 1, cols]
    return pre, taps


def pair_stack(v):
    side = iota(v.shape, 1) < HEADDIM
    zero = jnp.zeros_like(v)
    return jnp.concatenate([jnp.where(side, v, zero), jnp.where(side, zero, v)], axis=0)


def conv_state_kernel(
    proj, halo, convp, headp, spread, x_out, bc_out, u_out, cum_out, cumt_out, dt_out, hst_out,
    pfx_out, send_out, ext, state, scaled, total,
):
    step = pl.program_id(0)

    @pl.when(step == 0)
    def _():
        ext[0:8, :] = halo[8:16, :].astype(f32)
        state[...] = jnp.zeros_like(state)
        total[...] = jnp.zeros_like(total)

    @pl.when(step > 0)
    def _():
        ext[0:8, :] = ext[CHUNK : CHUNK + 8, :]

    ext[8:, :] = proj[:, :XBC].astype(f32)
    raw = proj[:, XBC:].astype(f32) + headp[0:1, :]
    steps = jnp.maximum(raw, 0.0) + jnp.log1p(jnp.exp(-jnp.abs(raw)))
    log_decay = steps * (headp[1:2, :] * (-LOG2E))
    cum = dot_full(jnp.where(tri(True), 1.0, 0.0), log_decay)
    cum_out[...] = cum
    cumt_out[...] = jnp.transpose(cum)[0:32, :]
    dt_out[...] = steps
    last = cum[CHUNK - 1 : CHUNK, :]
    steps_wide = expand(steps, spread[...])
    tail_wide = expand(jnp.exp2(last - cum), spread[...])
    for tile in range(TILES):
        pre, _ = conv_pre(ext, convp, tile)
        value = (pre * sigmoid(pre)).astype(bf16)
        if tile < PAIRS:
            x_out[:, lane(tile)] = value
            u = (value.astype(f32) * steps_wide[:, lane(tile)]).astype(bf16)
            u_out[:, lane(tile)] = u
            scaled[:, lane(tile)] = (u.astype(f32) * tail_wide[:, lane(tile)]).astype(bf16)
        else:
            bc_out[:, lane(tile - PAIRS)] = value
    decay = expand(jnp.broadcast_to(jnp.exp2(last), (8, LANES)), spread[...])[0:1, :]
    new_state = state[...] * decay + dot_tn(bc_out[:, :STATE], scaled[...])
    state[...] = new_state
    hst_out[0] = new_state
    new_total = total[...] + jnp.broadcast_to(last, (8, LANES))
    total[...] = new_total
    pfx_out[0] = new_total

    @pl.when(step == pl.num_programs(0) - 1)
    def _():
        send_out[:STATE, :] = new_state.astype(bf16)
        row = iota((EXTRA, LANES), 0)
        wide = jnp.broadcast_to(new_total[0:1, :], (EXTRA, LANES))
        high, rest = halves(wide)
        left = (wide - high.astype(f32) - rest.astype(f32)).astype(bf16)
        parts = jnp.where(
            row == 0,
            high.astype(f32),
            jnp.where(row == 1, rest.astype(f32), jnp.where(row == 2, left.astype(f32), 0.0)),
        )
        send_out[STATE:, :] = dot(parts.astype(bf16), spread[:LANES, :]).astype(bf16)


def within_kernel(u, bc, cum, cumt, y_out):
    scores = jnp.where(tri(True), dot_nt(bc[:, STATE:], bc[:, :STATE]), 0.0)
    for pair in range(PAIRS):
        weights = []
        for head in (2 * pair, 2 * pair + 1):
            gap = cum[:, head : head + 1] - cumt[head : head + 1, :]
            weights.append((jnp.exp2(jnp.minimum(gap, 0.0)) * scores).astype(bf16))
        y_out[:, lane(pair)] = dot(jnp.concatenate(weights, axis=1), pair_stack(u[:, lane(pair)]))


def arrived(gathered, logs, rank, groups, later):
    sums = [
        jnp.sum(logs[g].astype(f32), axis=0, keepdims=True) for g in range(groups)
    ]
    entered = jnp.zeros((STATE, INNER), f32)
    for g in range(groups):
        between = jnp.zeros((1, INNER), f32)
        for s in range(groups):
            if (s < g) if later else (s > g):
                inside = (s > rank) if later else (s < rank)
                between = between + jnp.where(inside, sums[s], 0.0)
        counts = (g > rank) if later else (g < rank)
        weight = jnp.where(counts, jnp.exp2(between), 0.0)
        entered = entered + gathered[g].astype(f32) * weight
    return entered


def gate_kernel(
    groups, rank, y_in, x, bc, cum, hst, gathered, logs, gate, tok, cot, wout, spread, rows,
    block_out, hidden_out, y_out, dy_out, dgate_out, dcc_out, ust_out, glocal_out, ng_out, h0_out,
    prefix, h0, hg_all, gated_all, dy_scaled,
):
    step = pl.program_id(0)

    @pl.when(step == 0)
    def _():
        value = arrived(gathered, logs, rank[0], groups, False)
        h0[...] = value
        h0_out[...] = value
        prefix[...] = jnp.zeros_like(prefix)
        glocal_out[...] = jnp.zeros_like(glocal_out)
        ng_out[...] = jnp.zeros_like(ng_out)

    start = expand(jnp.exp2(prefix[...]), spread[...])[0:1, :]
    state = h0[...] * start + jnp.where(step > 0, hst[0], 0.0)
    state_low = state.astype(bf16)
    grown = expand(jnp.exp2(cum[...]), spread[...])
    carried = dot(bc[:, STATE:], state_low)
    hg_all[...] = dot_nt(cot[...], wout[...])
    squares = jnp.zeros((CHUNK, LANES), f32)
    cross = jnp.zeros((CHUNK, LANES), f32)
    for tile in range(PAIRS):
        cols = lane(tile)
        y = y_in[:, cols] + carried[:, cols] * grown[:, cols]
        y_out[:, cols] = y
        mixed = (y + rows[1:2, cols] * x[:, cols].astype(f32)).astype(bf16).astype(f32)
        gate_val = gate[:, cols].astype(f32)
        gated = mixed * (gate_val * sigmoid(gate_val))
        gated_all[:, cols] = gated
        squares = squares + gated * gated
        cross = cross + gated * (hg_all[:, cols] * rows[0:1, cols])
    mean = jnp.sum(squares, axis=1, keepdims=True) * (1.0 / INNER)
    scale = lax.rsqrt(mean + norm_eps)
    cross_mean = jnp.sum(cross, axis=1, keepdims=True) * (1.0 / INNER) * scale * scale * scale
    for tile in range(PAIRS):
        cols = lane(tile)
        gated = gated_all[:, cols]
        normal = gated * scale
        hidden_out[:, cols] = (normal * rows[0:1, cols]).astype(bf16)
        grad = hg_all[:, cols]
        ng_out[:, cols] += fold(grad * normal)
        dgated = grad * rows[0:1, cols] * scale - gated * cross_mean
        gate_val = gate[:, cols].astype(f32)
        sig = sigmoid(gate_val)
        silu = gate_val * sig
        mixed = (y_out[:, cols] + rows[1:2, cols] * x[:, cols].astype(f32)).astype(bf16).astype(f32)
        dgate_out[:, cols] = (dgated * mixed * (sig + silu * (1.0 - sig))).astype(bf16)
        dy = (dgated * silu).astype(bf16)
        dy_out[:, cols] = dy
        dy_scaled[:, cols] = (dy.astype(f32) * grown[:, cols]).astype(bf16)
    block_out[...] = tok[...].astype(f32) + dot(hidden_out[...], wout[...])
    update = dot_tn(bc[:, STATE:], dy_scaled[...])
    ust_out[0] = update
    glocal_out[...] += update * start
    dcc_out[...] = dot_nt(dy_scaled[...], state_low)
    prefix[...] += jnp.broadcast_to(cum[CHUNK - 1 : CHUNK, :], (8, LANES))


def within_back_kernel(u, dy, bc, cum, cumt, dxs_out, dbc_out):
    upper = tri(False)
    scores = jnp.where(upper, dot_nt(bc[:, :STATE], bc[:, STATE:]), 0.0)
    total = jnp.zeros((CHUNK, CHUNK), f32)
    for pair in range(PAIRS):
        stacked = pair_stack(dy[:, lane(pair)])
        products = dot_nt(u[:, lane(pair)], stacked)
        weights = []
        for half in range(2):
            head = 2 * pair + half
            gap = cumt[head : head + 1, :] - cum[:, head : head + 1]
            decay = jnp.exp2(jnp.minimum(gap, 0.0))
            weights.append((decay * scores).astype(bf16))
            total = total + decay * products[:, lane(half)]
        dxs_out[:, lane(pair)] = dot(jnp.concatenate(weights, axis=1), stacked)
    low = jnp.where(upper, total, 0.0).astype(bf16)
    dbc_out[:, :STATE] = dot(low, bc[:, STATE:])
    dbc_out[:, STATE:] = dot_tn(low, bc[:, :STATE])


def back_kernel(
    groups, rank, dxs, dy, x, u, y, bc, dbc, dcc, cum, dt, hst, pfx, h0, gathered, logs, ust, proj,
    before, halo, convp, headp, spread, collect, rows,
    pg_out, first_out, tail_out, wg_out, hg_out, skip_out,
    gstate, ext, dext, scaled, prod_q, prod_p,
):
    step = pl.program_id(0)
    chunk = pl.num_programs(0) - 1 - step

    @pl.when(step == 0)
    def _():
        gstate[...] = arrived(gathered, logs, rank[0], groups, True)
        dext[CHUNK:, :] = jnp.zeros((8, XBC), f32)
        wg_out[...] = jnp.zeros_like(wg_out)
        hg_out[...] = jnp.zeros_like(hg_out)
        skip_out[...] = jnp.zeros_like(skip_out)

    @pl.when(step > 0)
    def _():
        dext[CHUNK:, :] = dext[0:8, :]

    @pl.when(chunk == 0)
    def _():
        ext[0:8, :] = halo[8:16, :].astype(f32)

    @pl.when(chunk > 0)
    def _():
        ext[0:8, :] = before[8:16, :XBC].astype(f32)

    ext[8:, :] = proj[:, :XBC].astype(f32)
    grad_state = gstate[...]
    grad_low = grad_state.astype(bf16)
    last = cum[CHUNK - 1 : CHUNK, :]
    tail_wide = expand(jnp.exp2(last - cum[...]), spread[...])
    steps_wide = expand(dt[...], spread[...])
    reach = dot(bc[:, :STATE], grad_low)

    def conv_back(tile, grad):
        cols = lane(tile)
        pre, taps = conv_pre(ext, convp, tile)
        sig = sigmoid(pre)
        dpre = grad * (sig + pre * sig * (1.0 - sig))
        dext[0:CHUNK, cols] = dpre
        for k in range(CONV):
            wg_out[8 * k : 8 * k + 8, cols] += fold(dpre * taps[k])
        wg_out[32:40, cols] += fold(dpre)
        source = dpre * convp[3:4, cols]
        for k in range(CONV - 1):
            source = source + dext[3 - k : 3 - k + CHUNK, cols] * convp[k : k + 1, cols]
        pg_out[:, cols] = source.astype(bf16)

        @pl.when(step == 0)
        def _():
            tail_out[:, cols] = source[CHUNK - 8 :, :]

    for tile in range(PAIRS):
        cols = lane(tile)
        dxs_full = dxs[:, cols] + tail_wide[:, cols] * reach[:, cols]
        uf = u[:, cols].astype(f32)
        dyf = dy[:, cols].astype(f32)
        scaled[:, cols] = (uf * tail_wide[:, cols]).astype(bf16)
        q = uf * dxs_full
        high, rest = halves(q)
        prod_q[:, cols] = high
        prod_q[:, INNER + tile * LANES : INNER + (tile + 1) * LANES] = rest
        high, rest = halves(dyf * y[:, cols] - q)
        prod_p[:, cols] = high
        prod_p[:, INNER + tile * LANES : INNER + (tile + 1) * LANES] = rest
        skip_out[:, cols] += fold(dyf * x[:, cols].astype(f32))
        conv_back(tile, rows[1:2, cols] * dyf + steps_wide[:, cols] * dxs_full)
    conv_back(PAIRS, dbc[:, :STATE] + dot_nt(scaled[...], grad_low))
    conv_back(PAIRS + 1, dbc[:, STATE:] + dcc[...])
    first_out[...] = dext[0:8, :]

    q_heads = dot(prod_q[...], collect[...])
    gap_heads = dot(prod_p[...], collect[...])
    end = expand(jnp.exp2(pfx[0]), spread[...])[0:1, :]
    meet = fold(grad_state * (hst[0] + h0[...] * end))
    meet_high, meet_rest = halves(meet)
    meet_heads = jnp.sum(
        dot(jnp.concatenate([meet_high, meet_rest], axis=1), collect[...]), axis=0, keepdims=True
    )
    dlog = dot_full(jnp.where(tri(False), 1.0, 0.0), gap_heads) + meet_heads
    sig = sigmoid(proj[:, XBC:].astype(f32) + headp[0:1, :])
    steps = dt[...]
    ratio = jnp.where(steps > 1e-30, sig / jnp.maximum(steps, 1e-30), 1.0)
    raw_grad = q_heads * ratio - dlog * headp[1:2, :] * sig
    pg_out[:, XBC:] = raw_grad.astype(bf16)
    hg_out[0:8, :] += fold(raw_grad)
    hg_out[8:16, :] += fold(dlog * steps * headp[1:2, :]) * (-1.0)
    decay = expand(jnp.broadcast_to(jnp.exp2(last), (8, LANES)), spread[...])[0:1, :]
    gstate[...] = grad_state * decay + ust[0]


def full(shape):
    return pl.BlockSpec(shape, lambda c: (0,) * len(shape))


def by_chunk(width, rows=CHUNK):
    return pl.BlockSpec((rows, width), lambda c: (c, 0))


def shape(dims, dtype):
    return jax.ShapeDtypeStruct(dims, dtype)


def params():
    return pltpu.CompilerParams(dimension_semantics=("arbitrary",), vmem_limit_bytes=VMEM)


def cost(flops, moved):
    return pl.CostEstimate(flops=flops, bytes_accessed=moved, transcendentals=0)


def spread_map():
    heads = jnp.arange(LANES)[:, None]
    cols = jnp.arange(INNER)[None, :] // HEADDIM
    once = (heads == cols).astype(bf16)
    return jnp.concatenate([once, once], axis=0)


def unpack_channels(channels):
    pieces = []
    offset = 0
    for piece_len in (D, INNER, XBC * CONV, XBC, HEADS, HEADS, HEADS):
        pieces.append(channels[offset : offset + piece_len])
        offset = offset + piece_len
    pre_gain, norm_gain, conv_flat, conv_bias, step_bias, rate_log, skip_gain = pieces
    return (
        pre_gain,
        norm_gain,
        conv_flat.reshape(XBC, CONV),
        conv_bias,
        step_bias,
        rate_log,
        skip_gain,
    )


def pre_norm(tok_vals, pre_gain):
    return (
        tok_vals * lax.rsqrt(jnp.mean(tok_vals * tok_vals, -1, keepdims=True) + norm_eps) * pre_gain
    )


def adamw_step(weight, moment, second, gradient, step_rate, decay_rate):
    moment_next = beta_one * moment + (1.0 - beta_one) * gradient
    second_next = beta_two * second + (1.0 - beta_two) * gradient * gradient
    first_fix = 1.0 - beta_one**STEP
    second_fix = 1.0 - beta_two**STEP
    update = moment_next / first_fix / (jnp.sqrt(second_next / second_fix) + adam_eps)
    return (weight - step_rate * (update + decay_rate * weight), moment_next, second_next)


def local(
    tokens,
    cotangent,
    in_weight,
    in_moment,
    in_second,
    out_weight,
    out_moment,
    out_second,
    channels,
    channel_moment,
    channel_second,
):
    groups = lax.axis_size("seq")
    everyone = ("dp", "seq")
    seq_rank = lax.axis_index("seq")
    rank = seq_rank.astype(jnp.int32).reshape(1)
    pre_gain, norm_gain, conv_weight, conv_bias, step_bias, rate_log, skip_gain = unpack_channels(
        channels
    )
    tok_low = tokens[0]
    cot_low = cotangent[0]
    count = tok_low.shape[0]
    chunks = count // CHUNK

    def quarter(weight):
        size = weight.shape[0] // groups
        return lax.dynamic_slice_in_dim(weight, seq_rank * size, size, 0).astype(bf16)

    in_part = quarter(in_weight)
    side_part = jnp.pad(in_part[:, INNER:], ((0, 0), (0, SIDE + INNER - PROJ)))
    full_side = lax.all_gather(side_part, everyone, axis=0, tiled=True)
    full_gate = lax.all_gather(in_part[:, :INNER], everyone, axis=0, tiled=True)
    full_out = lax.all_gather(quarter(out_weight), everyone, axis=0, tiled=True)

    forward = [(s, s + 1) for s in range(groups - 1)]
    backward = [(s + 1, s) for s in range(groups - 1)]
    tok_halo = lax.ppermute(tok_low[count - 16 :], "seq", forward)
    halo_norm = pre_norm(tok_halo.astype(f32), pre_gain).astype(bf16)
    tok_vals = tok_low.astype(f32)
    normed_low = pre_norm(tok_vals, pre_gain).astype(bf16)

    convp = jnp.concatenate(
        [conv_weight.T, conv_bias[None, :], jnp.zeros((3, XBC), f32)], axis=0
    )
    pad_heads = lambda v: jnp.pad(v, (0, LANES - HEADS))[None, :]
    headp = jnp.concatenate(
        [pad_heads(step_bias), pad_heads(jnp.exp(rate_log)), jnp.zeros((6, LANES), f32)], axis=0
    )
    rows = jnp.concatenate(
        [norm_gain[None, :], jnp.repeat(skip_gain, HEADDIM)[None, :], jnp.zeros((6, INNER), f32)],
        axis=0,
    )
    spread = spread_map()
    collect = jnp.concatenate([spread[:LANES].T, spread[:LANES].T], axis=0)

    proj = dot(normed_low, full_side).astype(bf16)
    halo = dot(halo_norm, full_side[:, :XBC]).astype(bf16)

    x, bc, u, cum, cumt, dt, hst, pfx, send = pl.pallas_call(
        conv_state_kernel,
        grid=(chunks,),
        in_specs=[
            by_chunk(SIDE), full((16, XBC)), full((8, XBC)), full((8, LANES)),
            full((2 * LANES, INNER)),
        ],
        out_specs=[
            by_chunk(INNER), by_chunk(2 * STATE), by_chunk(INNER), by_chunk(LANES),
            pl.BlockSpec((32, CHUNK), lambda c: (0, c)), by_chunk(LANES),
            pl.BlockSpec((1, STATE, INNER), lambda c: (c, 0, 0)),
            pl.BlockSpec((1, 8, LANES), lambda c: (c, 0, 0)),
            full((STATE + EXTRA, INNER)),
        ],
        out_shape=[
            shape((count, INNER), bf16), shape((count, 2 * STATE), bf16),
            shape((count, INNER), bf16), shape((count, LANES), f32), shape((32, count), f32),
            shape((count, LANES), f32), shape((chunks, STATE, INNER), f32),
            shape((chunks, 8, LANES), f32), shape((STATE + EXTRA, INNER), bf16),
        ],
        scratch_shapes=[
            pltpu.VMEM((CHUNK + 8, XBC), f32), pltpu.VMEM((STATE, INNER), f32),
            pltpu.VMEM((CHUNK, INNER), bf16), pltpu.VMEM((8, LANES), f32),
        ],
        compiler_params=params(),
        cost_estimate=cost(10**9, 24 * 2**20),
        name="conv_state",
    )(proj, halo, convp, headp, spread)

    states = lax.all_gather(send, "seq", axis=0, tiled=False)

    y_within = pl.pallas_call(
        within_kernel,
        grid=(chunks,),
        in_specs=[
            by_chunk(INNER), by_chunk(2 * STATE), by_chunk(LANES),
            pl.BlockSpec((32, CHUNK), lambda c: (0, c)),
        ],
        out_specs=by_chunk(INNER),
        out_shape=shape((count, INNER), f32),
        compiler_params=params(),
        cost_estimate=cost(4 * 10**9, 16 * 2**20),
        name="within",
    )(u, bc, cum, cumt)
    gate = dot(normed_low, full_gate).astype(bf16)

    gathered_spec = full((groups, STATE, INNER))
    logs_spec = pl.BlockSpec((groups, EXTRA, INNER), lambda c: (0, STATE // EXTRA, 0))
    smem = pl.BlockSpec(memory_space=pltpu.SMEM)

    def gate_call(*refs):
        gate_kernel(groups, *refs)

    block, hidden, y, dy, dgate, dcc, ust, glocal, ng, h0 = pl.pallas_call(
        gate_call,
        grid=(chunks,),
        in_specs=[
            smem, by_chunk(INNER), by_chunk(INNER), by_chunk(2 * STATE), by_chunk(LANES),
            pl.BlockSpec((1, STATE, INNER), lambda c: (jnp.maximum(c - 1, 0), 0, 0)),
            gathered_spec, logs_spec, by_chunk(INNER), by_chunk(D), by_chunk(D),
            full((INNER, D)), full((2 * LANES, INNER)), full((8, INNER)),
        ],
        out_specs=[
            by_chunk(D), by_chunk(INNER), by_chunk(INNER), by_chunk(INNER), by_chunk(INNER),
            by_chunk(LANES), pl.BlockSpec((1, STATE, INNER), lambda c: (c, 0, 0)),
            full((STATE, INNER)), full((8, INNER)), full((STATE, INNER)),
        ],
        out_shape=[
            shape((count, D), f32), shape((count, INNER), bf16), shape((count, INNER), f32),
            shape((count, INNER), bf16), shape((count, INNER), bf16), shape((count, LANES), f32),
            shape((chunks, STATE, INNER), f32), shape((STATE, INNER), f32), shape((8, INNER), f32),
            shape((STATE, INNER), f32),
        ],
        scratch_shapes=[
            pltpu.VMEM((8, LANES), f32), pltpu.VMEM((STATE, INNER), f32),
            pltpu.VMEM((CHUNK, INNER), f32), pltpu.VMEM((CHUNK, INNER), f32),
            pltpu.VMEM((CHUNK, INNER), bf16),
        ],
        compiler_params=params(),
        cost_estimate=cost(8 * 10**9, 48 * 2**20),
        name="gate_norm",
    )(
        rank, y_within, x, bc, cum, hst, states, states, gate, tok_low, cot_low, full_out, spread,
        rows,
    )

    grads = lax.all_gather(glocal.astype(bf16), "seq", axis=0, tiled=False)

    dxs, dbc = pl.pallas_call(
        within_back_kernel,
        grid=(chunks,),
        in_specs=[
            by_chunk(INNER), by_chunk(INNER), by_chunk(2 * STATE), by_chunk(LANES),
            pl.BlockSpec((32, CHUNK), lambda c: (0, c)),
        ],
        out_specs=[by_chunk(INNER), by_chunk(2 * STATE)],
        out_shape=[shape((count, INNER), f32), shape((count, 2 * STATE), f32)],
        compiler_params=params(),
        cost_estimate=cost(8 * 10**9, 16 * 2**20),
        name="within_back",
    )(u, dy, bc, cum, cumt)

    def summed(left, right):
        product = lax.dot_general(left, right, TN, preferred_element_type=f32).astype(bf16)
        return lax.psum_scatter(product, everyone, scatter_dimension=0, tiled=True)

    out_scattered = summed(hidden, cot_low)
    gate_scattered = summed(normed_low, dgate)

    def back(width, height=CHUNK):
        return pl.BlockSpec((height, width), lambda c: (chunks - 1 - c, 0))

    def back_three(height):
        return pl.BlockSpec((1, height, INNER), lambda c: (chunks - 1 - c, 0, 0))

    def back_call(*refs):
        back_kernel(groups, *refs)

    per = CHUNK // 16
    pg, first, tail, wg, hgr, skip = pl.pallas_call(
        back_call,
        grid=(chunks,),
        in_specs=[
            smem, back(INNER), back(INNER), back(INNER), back(INNER), back(INNER), back(2 * STATE),
            back(2 * STATE), back(LANES), back(LANES), back(LANES), back_three(STATE),
            pl.BlockSpec((1, 8, LANES), lambda c: (chunks - 1 - c, 0, 0)),
            full((STATE, INNER)), gathered_spec, logs_spec, back_three(STATE), back(SIDE),
            pl.BlockSpec(
                (16, SIDE), lambda c: (jnp.maximum((chunks - 1 - c) * per - 1, 0), 0)
            ),
            full((16, XBC)), full((8, XBC)), full((8, LANES)), full((2 * LANES, INNER)),
            full((2 * INNER, LANES)), full((8, INNER)),
        ],
        out_specs=[
            back(SIDE), full((8, XBC)), full((8, XBC)), full((40, XBC)), full((16, LANES)),
            full((8, INNER)),
        ],
        out_shape=[
            shape((count, SIDE), bf16), shape((8, XBC), f32), shape((8, XBC), f32),
            shape((40, XBC), f32), shape((16, LANES), f32), shape((8, INNER), f32),
        ],
        scratch_shapes=[
            pltpu.VMEM((STATE, INNER), f32), pltpu.VMEM((CHUNK + 8, XBC), f32),
            pltpu.VMEM((CHUNK + 8, XBC), f32), pltpu.VMEM((CHUNK, INNER), bf16),
            pltpu.VMEM((CHUNK, 2 * INNER), bf16), pltpu.VMEM((CHUNK, 2 * INNER), bf16),
        ],
        compiler_params=params(),
        cost_estimate=cost(4 * 10**9, 48 * 2**20),
        name="mixer_back",
    )(
        rank, dxs, dy, x, u, y, bc, dbc, dcc, cum, dt, hst, pfx, h0, grads, states, ust, proj, proj,
        halo, convp, headp, spread, collect, rows,
    )

    after = lax.ppermute(first, "seq", backward)
    fixes = [jnp.zeros((5, XBC), f32)]
    for m in range(CONV - 1):
        fix = convp[0] * after[m]
        for k in range(1, m + 1):
            fix = fix + convp[k] * after[m - k]
        fixes.append(fix[None, :])
    tail_low = (tail + jnp.concatenate(fixes, axis=0)).astype(bf16)
    pg = lax.dynamic_update_slice(pg, tail_low, (count - 8, 0))

    side_scattered = summed(normed_low, pg)

    normed_grad = lax.dot_general(dgate, full_gate, NT, preferred_element_type=f32)
    normed_grad = normed_grad + lax.dot_general(pg, full_side, NT, preferred_element_type=f32)
    _, norm_pull = jax.vjp(pre_norm, tok_vals, pre_gain)
    tok_norm_grad, pre_gain_grad = norm_pull(normed_grad)
    token_grad = (cot_low.astype(f32) + tok_norm_grad)[None]

    wg_sum = jnp.sum(wg.reshape(5, 8, XBC), axis=1)
    chan_grad = jnp.concatenate(
        [
            pre_gain_grad,
            jnp.sum(ng, axis=0),
            wg_sum[:CONV].T.reshape(-1),
            wg_sum[CONV],
            jnp.sum(hgr[:8, :HEADS], axis=0),
            jnp.sum(hgr[8:, :HEADS], axis=0),
            jnp.sum(skip.reshape(8, HEADS, HEADDIM), axis=(0, 2)),
        ]
    )
    chan_grad = lax.psum(chan_grad, everyone)

    def owned(part):
        return lax.all_gather(part, "seq", axis=0, tiled=True).astype(f32)

    out_grad = owned(out_scattered)
    in_grad = jnp.concatenate(
        [owned(gate_scattered), owned(side_scattered)[:, : PROJ - INNER]], axis=1
    )
    in_new, in_mom, in_sec = adamw_step(
        in_weight, in_moment, in_second, in_grad, rate_matrix, decay_matrix
    )
    out_new, out_mom, out_sec = adamw_step(
        out_weight, out_moment, out_second, out_grad, rate_matrix, decay_matrix
    )
    chan_new, chan_mom, chan_sec = adamw_step(
        channels, channel_moment, channel_second, chan_grad, rate_channel, 0.0
    )
    return (
        block[None],
        token_grad,
        in_new,
        in_mom,
        in_sec,
        out_new,
        out_mom,
        out_sec,
        chan_new,
        chan_mom,
        chan_sec,
    )


def solution(mesh):
    acts = P("dp", "seq", None)
    rows = P("dp", None)
    specs = (acts, acts) + (rows,) * 6 + (P(),) * 3
    return jax.shard_map(local, mesh=mesh, in_specs=specs, out_specs=specs, check_vma=False)
```

```python
import math

import jax
import jax.numpy as jnp
from jax import lax
from jax.experimental import pallas as pl
from jax.experimental.pallas import tpu as pltpu
from jax.sharding import PartitionSpec as P

D = 768
HEADS = 24
HEADDIM = 64
STATE = 128
CONV = 4
STEP = 10
INNER = 1536
XBC = 1792
PROJ = 3352
SIDE = 1920
LANES = 128
CHUNK = 128
PAIRS = HEADS // 2
TILES = XBC // LANES
EXTRA = 16

norm_eps = 1e-05
beta_one = 0.9
beta_two = 0.999
adam_eps = 1e-08
rate_matrix = 0.1
rate_channel = 0.5
decay_matrix = 0.1
LOG2E = 1.0 / math.log(2.0)
VMEM = 56 * 1024 * 1024

f32 = jnp.float32
bf16 = jnp.bfloat16
NT = (((1,), (1,)), ((), ()))
TN = (((0,), (0,)), ((), ()))


def dot(a, b):
    return jnp.dot(a, b, preferred_element_type=f32)


def dot_nt(a, b):
    return lax.dot_general(a, b, NT, preferred_element_type=f32)


def dot_tn(a, b):
    return lax.dot_general(a, b, TN, preferred_element_type=f32)


def dot_full(a, b):
    return jnp.dot(a, b, preferred_element_type=f32, precision=lax.Precision.HIGHEST)


def sigmoid(v):
    return 0.5 * jnp.tanh(0.5 * v) + 0.5


def halves(v):
    high = v.astype(bf16)
    return high, (v - high.astype(f32)).astype(bf16)


def expand(v, spread):
    high, rest = halves(v)
    return dot(jnp.concatenate([high, rest], axis=1), spread)


def fold(v):
    return jnp.sum(v.reshape(v.shape[0] // 8, 8, v.shape[1]), axis=0)


def lane(i):
    return slice(i * LANES, (i + 1) * LANES)


def iota(shape, dim):
    return lax.broadcasted_iota(jnp.int32, shape, dim)


def tri(lower):
    rows, cols = iota((CHUNK, CHUNK), 0), iota((CHUNK, CHUNK), 1)
    return (rows >= cols) if lower else (rows <= cols)


def conv_pre(ext, convp, tile):
    cols = lane(tile)
    taps = [ext[5 + k : 5 + k + CHUNK, cols] for k in range(CONV)]
    pre = taps[0] * convp[0:1, cols] + convp[4:5, cols]
    for k in range(1, CONV):
        pre = pre + taps[k] * convp[k : k + 1, cols]
    return pre, taps


def pair_stack(v):
    side = iota(v.shape, 1) < HEADDIM
    zero = jnp.zeros_like(v)
    return jnp.concatenate([jnp.where(side, v, zero), jnp.where(side, zero, v)], axis=0)


def conv_state_kernel(
    proj, halo, convp, headp, spread, x_out, bc_out, u_out, cum_out, cumt_out, dt_out, hst_out,
    pfx_out, send_out, ext, state, scaled, total,
):
    step = pl.program_id(0)

    @pl.when(step == 0)
    def _():
        ext[0:8, :] = halo[8:16, :].astype(f32)
        state[...] = jnp.zeros_like(state)
        total[...] = jnp.zeros_like(total)

    @pl.when(step > 0)
    def _():
        ext[0:8, :] = ext[CHUNK : CHUNK + 8, :]

    ext[8:, :] = proj[:, :XBC].astype(f32)
    raw = proj[:, XBC:].astype(f32) + headp[0:1, :]
    steps = jnp.maximum(raw, 0.0) + jnp.log1p(jnp.exp(-jnp.abs(raw)))
    log_decay = steps * (headp[1:2, :] * (-LOG2E))
    cum = dot_full(jnp.where(tri(True), 1.0, 0.0), log_decay)
    cum_out[...] = cum
    cumt_out[...] = jnp.transpose(cum)[0:32, :]
    dt_out[...] = steps
    last = cum[CHUNK - 1 : CHUNK, :]
    steps_wide = expand(steps, spread[...])
    tail_wide = expand(jnp.exp2(last - cum), spread[...])
    for tile in range(TILES):
        pre, _ = conv_pre(ext, convp, tile)
        value = (pre * sigmoid(pre)).astype(bf16)
        if tile < PAIRS:
            x_out[:, lane(tile)] = value
            u = (value.astype(f32) * steps_wide[:, lane(tile)]).astype(bf16)
            u_out[:, lane(tile)] = u
            scaled[:, lane(tile)] = (u.astype(f32) * tail_wide[:, lane(tile)]).astype(bf16)
        else:
            bc_out[:, lane(tile - PAIRS)] = value
    decay = expand(jnp.broadcast_to(jnp.exp2(last), (8, LANES)), spread[...])[0:1, :]
    new_state = state[...] * decay + dot_tn(bc_out[:, :STATE], scaled[...])
    state[...] = new_state
    hst_out[0] = new_state
    new_total = total[...] + jnp.broadcast_to(last, (8, LANES))
    total[...] = new_total
    pfx_out[0] = new_total

    @pl.when(step == pl.num_programs(0) - 1)
    def _():
        send_out[:STATE, :] = new_state.astype(bf16)
        row = iota((EXTRA, LANES), 0)
        wide = jnp.broadcast_to(new_total[0:1, :], (EXTRA, LANES))
        high, rest = halves(wide)
        left = (wide - high.astype(f32) - rest.astype(f32)).astype(bf16)
        parts = jnp.where(
            row == 0,
            high.astype(f32),
            jnp.where(row == 1, rest.astype(f32), jnp.where(row == 2, left.astype(f32), 0.0)),
        )
        send_out[STATE:, :] = dot(parts.astype(bf16), spread[:LANES, :]).astype(bf16)


def within_kernel(u, bc, cum, cumt, y_out):
    scores = jnp.where(tri(True), dot_nt(bc[:, STATE:], bc[:, :STATE]), 0.0)
    for pair in range(PAIRS):
        weights = []
        for head in (2 * pair, 2 * pair + 1):
            gap = cum[:, head : head + 1] - cumt[head : head + 1, :]
            weights.append((jnp.exp2(jnp.minimum(gap, 0.0)) * scores).astype(bf16))
        y_out[:, lane(pair)] = dot(jnp.concatenate(weights, axis=1), pair_stack(u[:, lane(pair)]))


def arrived(gathered, logs, rank, groups, later):
    sums = [
        jnp.sum(logs[g].astype(f32), axis=0, keepdims=True) for g in range(groups)
    ]
    entered = jnp.zeros((STATE, INNER), f32)
    for g in range(groups):
        between = jnp.zeros((1, INNER), f32)
        for s in range(groups):
            if (s < g) if later else (s > g):
                inside = (s > rank) if later else (s < rank)
                between = between + jnp.where(inside, sums[s], 0.0)
        counts = (g > rank) if later else (g < rank)
        weight = jnp.where(counts, jnp.exp2(between), 0.0)
        entered = entered + gathered[g].astype(f32) * weight
    return entered


def gate_kernel(
    groups, rank, y_in, x, bc, cum, hst, gathered, logs, gate, tok, cot, wout, spread, rows,
    block_out, hidden_out, y_out, dy_out, dgate_out, dcc_out, ust_out, glocal_out, ng_out, h0_out,
    prefix, h0, hg_all, gated_all, dy_scaled,
):
    step = pl.program_id(0)

    @pl.when(step == 0)
    def _():
        value = arrived(gathered, logs, rank[0], groups, False)
        h0[...] = value
        h0_out[...] = value
        prefix[...] = jnp.zeros_like(prefix)
        glocal_out[...] = jnp.zeros_like(glocal_out)
        ng_out[...] = jnp.zeros_like(ng_out)

    start = expand(jnp.exp2(prefix[...]), spread[...])[0:1, :]
    state = h0[...] * start + jnp.where(step > 0, hst[0], 0.0)
    state_low = state.astype(bf16)
    grown = expand(jnp.exp2(cum[...]), spread[...])
    carried = dot(bc[:, STATE:], state_low)
    hg_all[...] = dot_nt(cot[...], wout[...])
    squares = jnp.zeros((CHUNK, LANES), f32)
    cross = jnp.zeros((CHUNK, LANES), f32)
    for tile in range(PAIRS):
        cols = lane(tile)
        y = y_in[:, cols] + carried[:, cols] * grown[:, cols]
        y_out[:, cols] = y
        mixed = (y + rows[1:2, cols] * x[:, cols].astype(f32)).astype(bf16).astype(f32)
        gate_val = gate[:, cols].astype(f32)
        gated = mixed * (gate_val * sigmoid(gate_val))
        gated_all[:, cols] = gated
        squares = squares + gated * gated
        cross = cross + gated * (hg_all[:, cols] * rows[0:1, cols])
    mean = jnp.sum(squares, axis=1, keepdims=True) * (1.0 / INNER)
    scale = lax.rsqrt(mean + norm_eps)
    cross_mean = jnp.sum(cross, axis=1, keepdims=True) * (1.0 / INNER) * scale * scale * scale
    for tile in range(PAIRS):
        cols = lane(tile)
        gated = gated_all[:, cols]
        normal = gated * scale
        hidden_out[:, cols] = (normal * rows[0:1, cols]).astype(bf16)
        grad = hg_all[:, cols]
        ng_out[:, cols] += fold(grad * normal)
        dgated = grad * rows[0:1, cols] * scale - gated * cross_mean
        gate_val = gate[:, cols].astype(f32)
        sig = sigmoid(gate_val)
        silu = gate_val * sig
        mixed = (y_out[:, cols] + rows[1:2, cols] * x[:, cols].astype(f32)).astype(bf16).astype(f32)
        dgate_out[:, cols] = (dgated * mixed * (sig + silu * (1.0 - sig))).astype(bf16)
        dy = (dgated * silu).astype(bf16)
        dy_out[:, cols] = dy
        dy_scaled[:, cols] = (dy.astype(f32) * grown[:, cols]).astype(bf16)
    block_out[...] = tok[...].astype(f32) + dot(hidden_out[...], wout[...])
    update = dot_tn(bc[:, STATE:], dy_scaled[...])
    ust_out[0] = update
    glocal_out[...] += update * start
    dcc_out[...] = dot_nt(dy_scaled[...], state_low)
    prefix[...] += jnp.broadcast_to(cum[CHUNK - 1 : CHUNK, :], (8, LANES))


def within_back_kernel(u, dy, bc, cum, cumt, dxs_out, dbc_out):
    upper = tri(False)
    scores = jnp.where(upper, dot_nt(bc[:, :STATE], bc[:, STATE:]), 0.0)
    total = jnp.zeros((CHUNK, CHUNK), f32)
    for pair in range(PAIRS):
        stacked = pair_stack(dy[:, lane(pair)])
        products = dot_nt(u[:, lane(pair)], stacked)
        weights = []
        for half in range(2):
            head = 2 * pair + half
            gap = cumt[head : head + 1, :] - cum[:, head : head + 1]
            decay = jnp.exp2(jnp.minimum(gap, 0.0))
            weights.append((decay * scores).astype(bf16))
            total = total + decay * products[:, lane(half)]
        dxs_out[:, lane(pair)] = dot(jnp.concatenate(weights, axis=1), stacked)
    low = jnp.where(upper, total, 0.0).astype(bf16)
    dbc_out[:, :STATE] = dot(low, bc[:, STATE:])
    dbc_out[:, STATE:] = dot_tn(low, bc[:, :STATE])


def back_kernel(
    groups, rank, dxs, dy, x, u, y, bc, dbc, dcc, cum, dt, hst, pfx, h0, gathered, logs, ust, proj,
    before, halo, convp, headp, spread, collect, rows,
    pg_out, first_out, tail_out, wg_out, hg_out, skip_out,
    gstate, ext, dext, scaled, prod_q, prod_p,
):
    step = pl.program_id(0)
    chunk = pl.num_programs(0) - 1 - step

    @pl.when(step == 0)
    def _():
        gstate[...] = arrived(gathered, logs, rank[0], groups, True)
        dext[CHUNK:, :] = jnp.zeros((8, XBC), f32)
        wg_out[...] = jnp.zeros_like(wg_out)
        hg_out[...] = jnp.zeros_like(hg_out)
        skip_out[...] = jnp.zeros_like(skip_out)

    @pl.when(step > 0)
    def _():
        dext[CHUNK:, :] = dext[0:8, :]

    @pl.when(chunk == 0)
    def _():
        ext[0:8, :] = halo[8:16, :].astype(f32)

    @pl.when(chunk > 0)
    def _():
        ext[0:8, :] = before[8:16, :XBC].astype(f32)

    ext[8:, :] = proj[:, :XBC].astype(f32)
    grad_state = gstate[...]
    grad_low = grad_state.astype(bf16)
    last = cum[CHUNK - 1 : CHUNK, :]
    tail_wide = expand(jnp.exp2(last - cum[...]), spread[...])
    steps_wide = expand(dt[...], spread[...])
    reach = dot(bc[:, :STATE], grad_low)

    def conv_back(tile, grad):
        cols = lane(tile)
        pre, taps = conv_pre(ext, convp, tile)
        sig = sigmoid(pre)
        dpre = grad * (sig + pre * sig * (1.0 - sig))
        dext[0:CHUNK, cols] = dpre
        for k in range(CONV):
            wg_out[8 * k : 8 * k + 8, cols] += fold(dpre * taps[k])
        wg_out[32:40, cols] += fold(dpre)
        source = dpre * convp[3:4, cols]
        for k in range(CONV - 1):
            source = source + dext[3 - k : 3 - k + CHUNK, cols] * convp[k : k + 1, cols]
        pg_out[:, cols] = source.astype(bf16)

        @pl.when(step == 0)
        def _():
            tail_out[:, cols] = source[CHUNK - 8 :, :]

    for tile in range(PAIRS):
        cols = lane(tile)
        dxs_full = dxs[:, cols] + tail_wide[:, cols] * reach[:, cols]
        uf = u[:, cols].astype(f32)
        dyf = dy[:, cols].astype(f32)
        scaled[:, cols] = (uf * tail_wide[:, cols]).astype(bf16)
        q = uf * dxs_full
        high, rest = halves(q)
        prod_q[:, cols] = high
        prod_q[:, INNER + tile * LANES : INNER + (tile + 1) * LANES] = rest
        high, rest = halves(dyf * y[:, cols] - q)
        prod_p[:, cols] = high
        prod_p[:, INNER + tile * LANES : INNER + (tile + 1) * LANES] = rest
        skip_out[:, cols] += fold(dyf * x[:, cols].astype(f32))
        conv_back(tile, rows[1:2, cols] * dyf + steps_wide[:, cols] * dxs_full)
    conv_back(PAIRS, dbc[:, :STATE] + dot_nt(scaled[...], grad_low))
    conv_back(PAIRS + 1, dbc[:, STATE:] + dcc[...])
    first_out[...] = dext[0:8, :]

    q_heads = dot(prod_q[...], collect[...])
    gap_heads = dot(prod_p[...], collect[...])
    end = expand(jnp.exp2(pfx[0]), spread[...])[0:1, :]
    meet = fold(grad_state * (hst[0] + h0[...] * end))
    meet_high, meet_rest = halves(meet)
    meet_heads = jnp.sum(
        dot(jnp.concatenate([meet_high, meet_rest], axis=1), collect[...]), axis=0, keepdims=True
    )
    dlog = dot_full(jnp.where(tri(False), 1.0, 0.0), gap_heads) + meet_heads
    sig = sigmoid(proj[:, XBC:].astype(f32) + headp[0:1, :])
    steps = dt[...]
    ratio = jnp.where(steps > 1e-30, sig / jnp.maximum(steps, 1e-30), 1.0)
    raw_grad = q_heads * ratio - dlog * headp[1:2, :] * sig
    pg_out[:, XBC:] = raw_grad.astype(bf16)
    hg_out[0:8, :] += fold(raw_grad)
    hg_out[8:16, :] += fold(dlog * steps * headp[1:2, :]) * (-1.0)
    decay = expand(jnp.broadcast_to(jnp.exp2(last), (8, LANES)), spread[...])[0:1, :]
    gstate[...] = grad_state * decay + ust[0]


def swap(v, axis, bit):
    size = lax.axis_size(axis)
    return lax.ppermute(v, axis, [(i, i ^ (1 << bit)) for i in range(size)])


def mesh_bits():
    found = []
    for axis in ("dp", "seq"):
        for bit in reversed(range(lax.axis_size(axis).bit_length() - 1)):
            found.append((axis, bit))
    return found


def mine(axis, bit):
    return (lax.axis_index(axis) >> bit) & 1


def gather_pairs(v, bits):
    dims = v.shape
    for place, (axis, bit) in enumerate(bits):
        other = swap(v, axis, bit)
        second = mine(axis, bit) == 1
        v = jnp.stack([jnp.where(second, other, v), jnp.where(second, v, other)], axis=place)
    return v.reshape((dims[0] << len(bits),) + dims[1:])


def scatter_pairs(v, bits):
    width = v.shape[1]
    v = v.reshape((2,) * len(bits) + (v.shape[0] >> len(bits), width))
    for place in reversed(range(len(bits))):
        axis, bit = bits[place]
        own = mine(axis, bit)
        keep = lax.dynamic_index_in_dim(v, own, place, keepdims=False)
        give = lax.dynamic_index_in_dim(v, 1 - own, place, keepdims=False)
        v = (keep.astype(f32) + swap(give, axis, bit).astype(f32)).astype(v.dtype)
    return v


def sum_pairs(v, bits):
    for axis, bit in bits:
        v = v + swap(v, axis, bit)
    return v


def full(shape):
    return pl.BlockSpec(shape, lambda c: (0,) * len(shape))


def by_chunk(width, rows=CHUNK):
    return pl.BlockSpec((rows, width), lambda c: (c, 0))


def shape(dims, dtype):
    return jax.ShapeDtypeStruct(dims, dtype)


def params():
    return pltpu.CompilerParams(dimension_semantics=("arbitrary",), vmem_limit_bytes=VMEM)


def cost(flops, moved):
    return pl.CostEstimate(flops=flops, bytes_accessed=moved, transcendentals=0)


def spread_map():
    heads = jnp.arange(LANES)[:, None]
    cols = jnp.arange(INNER)[None, :] // HEADDIM
    once = (heads == cols).astype(bf16)
    return jnp.concatenate([once, once], axis=0)


def unpack_channels(channels):
    pieces = []
    offset = 0
    for piece_len in (D, INNER, XBC * CONV, XBC, HEADS, HEADS, HEADS):
        pieces.append(channels[offset : offset + piece_len])
        offset = offset + piece_len
    pre_gain, norm_gain, conv_flat, conv_bias, step_bias, rate_log, skip_gain = pieces
    return (
        pre_gain,
        norm_gain,
        conv_flat.reshape(XBC, CONV),
        conv_bias,
        step_bias,
        rate_log,
        skip_gain,
    )


def pre_norm(tok_vals, pre_gain):
    return (
        tok_vals * lax.rsqrt(jnp.mean(tok_vals * tok_vals, -1, keepdims=True) + norm_eps) * pre_gain
    )


def adamw_step(weight, moment, second, gradient, step_rate, decay_rate):
    moment_next = beta_one * moment + (1.0 - beta_one) * gradient
    second_next = beta_two * second + (1.0 - beta_two) * gradient * gradient
    first_fix = 1.0 - beta_one**STEP
    second_fix = 1.0 - beta_two**STEP
    update = moment_next / first_fix / (jnp.sqrt(second_next / second_fix) + adam_eps)
    return (weight - step_rate * (update + decay_rate * weight), moment_next, second_next)


def local(
    tokens,
    cotangent,
    in_weight,
    in_moment,
    in_second,
    out_weight,
    out_moment,
    out_second,
    channels,
    channel_moment,
    channel_second,
):
    groups = lax.axis_size("seq")
    bits = mesh_bits()
    seq_bits = [(axis, bit) for axis, bit in bits if axis == "seq"]
    seq_rank = lax.axis_index("seq")
    rank = seq_rank.astype(jnp.int32).reshape(1)
    pre_gain, norm_gain, conv_weight, conv_bias, step_bias, rate_log, skip_gain = unpack_channels(
        channels
    )
    tok_low = tokens[0]
    cot_low = cotangent[0]
    count = tok_low.shape[0]
    chunks = count // CHUNK

    def quarter(weight):
        size = weight.shape[0] // groups
        return lax.dynamic_slice_in_dim(weight, seq_rank * size, size, 0).astype(bf16)

    in_part = quarter(in_weight)
    side_part = jnp.pad(in_part[:, INNER:], ((0, 0), (0, SIDE + INNER - PROJ)))
    full_side = gather_pairs(side_part, bits)
    full_gate = gather_pairs(in_part[:, :INNER], bits)
    full_out = gather_pairs(quarter(out_weight), bits)

    forward = [(s, s + 1) for s in range(groups - 1)]
    backward = [(s + 1, s) for s in range(groups - 1)]
    tok_halo = lax.ppermute(tok_low[count - 16 :], "seq", forward)
    halo_norm = pre_norm(tok_halo.astype(f32), pre_gain).astype(bf16)
    tok_vals = tok_low.astype(f32)
    normed_low = pre_norm(tok_vals, pre_gain).astype(bf16)

    convp = jnp.concatenate(
        [conv_weight.T, conv_bias[None, :], jnp.zeros((3, XBC), f32)], axis=0
    )
    pad_heads = lambda v: jnp.pad(v, (0, LANES - HEADS))[None, :]
    headp = jnp.concatenate(
        [pad_heads(step_bias), pad_heads(jnp.exp(rate_log)), jnp.zeros((6, LANES), f32)], axis=0
    )
    rows = jnp.concatenate(
        [norm_gain[None, :], jnp.repeat(skip_gain, HEADDIM)[None, :], jnp.zeros((6, INNER), f32)],
        axis=0,
    )
    spread = spread_map()
    collect = jnp.concatenate([spread[:LANES].T, spread[:LANES].T], axis=0)

    proj = dot(normed_low, full_side).astype(bf16)
    halo = dot(halo_norm, full_side[:, :XBC]).astype(bf16)

    x, bc, u, cum, cumt, dt, hst, pfx, send = pl.pallas_call(
        conv_state_kernel,
        grid=(chunks,),
        in_specs=[
            by_chunk(SIDE), full((16, XBC)), full((8, XBC)), full((8, LANES)),
            full((2 * LANES, INNER)),
        ],
        out_specs=[
            by_chunk(INNER), by_chunk(2 * STATE), by_chunk(INNER), by_chunk(LANES),
            pl.BlockSpec((32, CHUNK), lambda c: (0, c)), by_chunk(LANES),
            pl.BlockSpec((1, STATE, INNER), lambda c: (c, 0, 0)),
            pl.BlockSpec((1, 8, LANES), lambda c: (c, 0, 0)),
            full((STATE + EXTRA, INNER)),
        ],
        out_shape=[
            shape((count, INNER), bf16), shape((count, 2 * STATE), bf16),
            shape((count, INNER), bf16), shape((count, LANES), f32), shape((32, count), f32),
            shape((count, LANES), f32), shape((chunks, STATE, INNER), f32),
            shape((chunks, 8, LANES), f32), shape((STATE + EXTRA, INNER), bf16),
        ],
        scratch_shapes=[
            pltpu.VMEM((CHUNK + 8, XBC), f32), pltpu.VMEM((STATE, INNER), f32),
            pltpu.VMEM((CHUNK, INNER), bf16), pltpu.VMEM((8, LANES), f32),
        ],
        compiler_params=params(),
        cost_estimate=cost(10**9, 24 * 2**20),
        name="conv_state",
    )(proj, halo, convp, headp, spread)

    states = lax.all_gather(send, "seq", axis=0, tiled=False)

    y_within = pl.pallas_call(
        within_kernel,
        grid=(chunks,),
        in_specs=[
            by_chunk(INNER), by_chunk(2 * STATE), by_chunk(LANES),
            pl.BlockSpec((32, CHUNK), lambda c: (0, c)),
        ],
        out_specs=by_chunk(INNER),
        out_shape=shape((count, INNER), f32),
        compiler_params=params(),
        cost_estimate=cost(4 * 10**9, 16 * 2**20),
        name="within",
    )(u, bc, cum, cumt)
    gate = dot(normed_low, full_gate).astype(bf16)

    gathered_spec = full((groups, STATE, INNER))
    logs_spec = pl.BlockSpec((groups, EXTRA, INNER), lambda c: (0, STATE // EXTRA, 0))
    smem = pl.BlockSpec(memory_space=pltpu.SMEM)

    def gate_call(*refs):
        gate_kernel(groups, *refs)

    block, hidden, y, dy, dgate, dcc, ust, glocal, ng, h0 = pl.pallas_call(
        gate_call,
        grid=(chunks,),
        in_specs=[
            smem, by_chunk(INNER), by_chunk(INNER), by_chunk(2 * STATE), by_chunk(LANES),
            pl.BlockSpec((1, STATE, INNER), lambda c: (jnp.maximum(c - 1, 0), 0, 0)),
            gathered_spec, logs_spec, by_chunk(INNER), by_chunk(D), by_chunk(D),
            full((INNER, D)), full((2 * LANES, INNER)), full((8, INNER)),
        ],
        out_specs=[
            by_chunk(D), by_chunk(INNER), by_chunk(INNER), by_chunk(INNER), by_chunk(INNER),
            by_chunk(LANES), pl.BlockSpec((1, STATE, INNER), lambda c: (c, 0, 0)),
            full((STATE, INNER)), full((8, INNER)), full((STATE, INNER)),
        ],
        out_shape=[
            shape((count, D), f32), shape((count, INNER), bf16), shape((count, INNER), f32),
            shape((count, INNER), bf16), shape((count, INNER), bf16), shape((count, LANES), f32),
            shape((chunks, STATE, INNER), f32), shape((STATE, INNER), f32), shape((8, INNER), f32),
            shape((STATE, INNER), f32),
        ],
        scratch_shapes=[
            pltpu.VMEM((8, LANES), f32), pltpu.VMEM((STATE, INNER), f32),
            pltpu.VMEM((CHUNK, INNER), f32), pltpu.VMEM((CHUNK, INNER), f32),
            pltpu.VMEM((CHUNK, INNER), bf16),
        ],
        compiler_params=params(),
        cost_estimate=cost(8 * 10**9, 48 * 2**20),
        name="gate_norm",
    )(
        rank, y_within, x, bc, cum, hst, states, states, gate, tok_low, cot_low, full_out, spread,
        rows,
    )

    grads = lax.all_gather(glocal.astype(bf16), "seq", axis=0, tiled=False)

    dxs, dbc = pl.pallas_call(
        within_back_kernel,
        grid=(chunks,),
        in_specs=[
            by_chunk(INNER), by_chunk(INNER), by_chunk(2 * STATE), by_chunk(LANES),
            pl.BlockSpec((32, CHUNK), lambda c: (0, c)),
        ],
        out_specs=[by_chunk(INNER), by_chunk(2 * STATE)],
        out_shape=[shape((count, INNER), f32), shape((count, 2 * STATE), f32)],
        compiler_params=params(),
        cost_estimate=cost(8 * 10**9, 16 * 2**20),
        name="within_back",
    )(u, dy, bc, cum, cumt)

    def summed(left, right):
        product = lax.dot_general(left, right, TN, preferred_element_type=f32).astype(bf16)
        return scatter_pairs(product, bits)

    out_scattered = summed(hidden, cot_low)
    gate_scattered = summed(normed_low, dgate)

    def back(width, height=CHUNK):
        return pl.BlockSpec((height, width), lambda c: (chunks - 1 - c, 0))

    def back_three(height):
        return pl.BlockSpec((1, height, INNER), lambda c: (chunks - 1 - c, 0, 0))

    def back_call(*refs):
        back_kernel(groups, *refs)

    per = CHUNK // 16
    pg, first, tail, wg, hgr, skip = pl.pallas_call(
        back_call,
        grid=(chunks,),
        in_specs=[
            smem, back(INNER), back(INNER), back(INNER), back(INNER), back(INNER), back(2 * STATE),
            back(2 * STATE), back(LANES), back(LANES), back(LANES), back_three(STATE),
            pl.BlockSpec((1, 8, LANES), lambda c: (chunks - 1 - c, 0, 0)),
            full((STATE, INNER)), gathered_spec, logs_spec, back_three(STATE), back(SIDE),
            pl.BlockSpec(
                (16, SIDE), lambda c: (jnp.maximum((chunks - 1 - c) * per - 1, 0), 0)
            ),
            full((16, XBC)), full((8, XBC)), full((8, LANES)), full((2 * LANES, INNER)),
            full((2 * INNER, LANES)), full((8, INNER)),
        ],
        out_specs=[
            back(SIDE), full((8, XBC)), full((8, XBC)), full((40, XBC)), full((16, LANES)),
            full((8, INNER)),
        ],
        out_shape=[
            shape((count, SIDE), bf16), shape((8, XBC), f32), shape((8, XBC), f32),
            shape((40, XBC), f32), shape((16, LANES), f32), shape((8, INNER), f32),
        ],
        scratch_shapes=[
            pltpu.VMEM((STATE, INNER), f32), pltpu.VMEM((CHUNK + 8, XBC), f32),
            pltpu.VMEM((CHUNK + 8, XBC), f32), pltpu.VMEM((CHUNK, INNER), bf16),
            pltpu.VMEM((CHUNK, 2 * INNER), bf16), pltpu.VMEM((CHUNK, 2 * INNER), bf16),
        ],
        compiler_params=params(),
        cost_estimate=cost(4 * 10**9, 48 * 2**20),
        name="mixer_back",
    )(
        rank, dxs, dy, x, u, y, bc, dbc, dcc, cum, dt, hst, pfx, h0, grads, states, ust, proj, proj,
        halo, convp, headp, spread, collect, rows,
    )

    after = lax.ppermute(first, "seq", backward)
    fixes = [jnp.zeros((5, XBC), f32)]
    for m in range(CONV - 1):
        fix = convp[0] * after[m]
        for k in range(1, m + 1):
            fix = fix + convp[k] * after[m - k]
        fixes.append(fix[None, :])
    tail_low = (tail + jnp.concatenate(fixes, axis=0)).astype(bf16)
    pg = lax.dynamic_update_slice(pg, tail_low, (count - 8, 0))

    side_scattered = summed(normed_low, pg)

    normed_grad = lax.dot_general(dgate, full_gate, NT, preferred_element_type=f32)
    normed_grad = normed_grad + lax.dot_general(pg, full_side, NT, preferred_element_type=f32)
    _, norm_pull = jax.vjp(pre_norm, tok_vals, pre_gain)
    tok_norm_grad, pre_gain_grad = norm_pull(normed_grad)
    token_grad = (cot_low.astype(f32) + tok_norm_grad)[None]

    wg_sum = jnp.sum(wg.reshape(5, 8, XBC), axis=1)
    chan_grad = jnp.concatenate(
        [
            pre_gain_grad,
            jnp.sum(ng, axis=0),
            wg_sum[:CONV].T.reshape(-1),
            wg_sum[CONV],
            jnp.sum(hgr[:8, :HEADS], axis=0),
            jnp.sum(hgr[8:, :HEADS], axis=0),
            jnp.sum(skip.reshape(8, HEADS, HEADDIM), axis=(0, 2)),
        ]
    )
    chan_grad = sum_pairs(chan_grad, bits)

    def owned(part):
        return gather_pairs(part, seq_bits).astype(f32)

    out_grad = owned(out_scattered)
    in_grad = jnp.concatenate(
        [owned(gate_scattered), owned(side_scattered)[:, : PROJ - INNER]], axis=1
    )
    in_new, in_mom, in_sec = adamw_step(
        in_weight, in_moment, in_second, in_grad, rate_matrix, decay_matrix
    )
    out_new, out_mom, out_sec = adamw_step(
        out_weight, out_moment, out_second, out_grad, rate_matrix, decay_matrix
    )
    chan_new, chan_mom, chan_sec = adamw_step(
        channels, channel_moment, channel_second, chan_grad, rate_channel, 0.0
    )
    return (
        block[None],
        token_grad,
        in_new,
        in_mom,
        in_sec,
        out_new,
        out_mom,
        out_sec,
        chan_new,
        chan_mom,
        chan_sec,
    )


def solution(mesh):
    acts = P("dp", "seq", None)
    rows = P("dp", None)
    specs = (acts, acts) + (rows,) * 6 + (P(),) * 3
    return jax.shard_map(local, mesh=mesh, in_specs=specs, out_specs=specs, check_vma=False)
```

```python
import math

import jax
import jax.numpy as jnp
from jax import lax
from jax.experimental import pallas as pl
from jax.experimental.pallas import tpu as pltpu
from jax.sharding import PartitionSpec as P

D = 768
HEADS = 24
HEADDIM = 64
STATE = 128
CONV = 4
STEP = 10
INNER = 1536
XBC = 1792
PROJ = 3352
SIDE = 1920
LANES = 128
CHUNK = 128
PAIRS = HEADS // 2
TILES = XBC // LANES
EXTRA = 16

norm_eps = 1e-05
beta_one = 0.9
beta_two = 0.999
adam_eps = 1e-08
rate_matrix = 0.1
rate_channel = 0.5
decay_matrix = 0.1
LOG2E = 1.0 / math.log(2.0)
VMEM = 56 * 1024 * 1024

f32 = jnp.float32
bf16 = jnp.bfloat16
NT = (((1,), (1,)), ((), ()))
TN = (((0,), (0,)), ((), ()))


def dot(a, b):
    return jnp.dot(a, b, preferred_element_type=f32)


def dot_nt(a, b):
    return lax.dot_general(a, b, NT, preferred_element_type=f32)


def dot_tn(a, b):
    return lax.dot_general(a, b, TN, preferred_element_type=f32)


def dot_full(a, b):
    return jnp.dot(a, b, preferred_element_type=f32, precision=lax.Precision.HIGHEST)


def sigmoid(v):
    return 0.5 * jnp.tanh(0.5 * v) + 0.5


def halves(v):
    high = v.astype(bf16)
    return high, (v - high.astype(f32)).astype(bf16)


def expand(v, spread):
    high, rest = halves(v)
    return dot(jnp.concatenate([high, rest], axis=1), spread)


def fold(v):
    return jnp.sum(v.reshape(v.shape[0] // 8, 8, v.shape[1]), axis=0)


def lane(i):
    return slice(i * LANES, (i + 1) * LANES)


def iota(shape, dim):
    return lax.broadcasted_iota(jnp.int32, shape, dim)


def tri(lower):
    rows, cols = iota((CHUNK, CHUNK), 0), iota((CHUNK, CHUNK), 1)
    return (rows >= cols) if lower else (rows <= cols)


def conv_pre(ext, convp, tile):
    cols = lane(tile)
    taps = [ext[5 + k : 5 + k + CHUNK, cols] for k in range(CONV)]
    pre = taps[0] * convp[0:1, cols] + convp[4:5, cols]
    for k in range(1, CONV):
        pre = pre + taps[k] * convp[k : k + 1, cols]
    return pre, taps


def pair_stack(v):
    side = iota(v.shape, 1) < HEADDIM
    zero = jnp.zeros_like(v)
    return jnp.concatenate([jnp.where(side, v, zero), jnp.where(side, zero, v)], axis=0)


def conv_state_kernel(
    proj, halo, convp, headp, spread, x_out, bc_out, u_out, cum_out, cumt_out, dt_out, hst_out,
    pfx_out, send_out, ext, state, scaled, total,
):
    step = pl.program_id(0)

    @pl.when(step == 0)
    def _():
        ext[0:8, :] = halo[8:16, :].astype(f32)
        state[...] = jnp.zeros_like(state)
        total[...] = jnp.zeros_like(total)

    @pl.when(step > 0)
    def _():
        ext[0:8, :] = ext[CHUNK : CHUNK + 8, :]

    ext[8:, :] = proj[:, :XBC].astype(f32)
    raw = proj[:, XBC:].astype(f32) + headp[0:1, :]
    steps = jnp.maximum(raw, 0.0) + jnp.log1p(jnp.exp(-jnp.abs(raw)))
    log_decay = steps * (headp[1:2, :] * (-LOG2E))
    cum = dot_full(jnp.where(tri(True), 1.0, 0.0), log_decay)
    cum_out[...] = cum
    cumt_out[...] = jnp.transpose(cum)[0:32, :]
    dt_out[...] = steps
    last = cum[CHUNK - 1 : CHUNK, :]
    steps_wide = expand(steps, spread[...])
    tail_wide = expand(jnp.exp2(last - cum), spread[...])
    for tile in range(TILES):
        pre, _ = conv_pre(ext, convp, tile)
        value = (pre * sigmoid(pre)).astype(bf16)
        if tile < PAIRS:
            x_out[:, lane(tile)] = value
            u = (value.astype(f32) * steps_wide[:, lane(tile)]).astype(bf16)
            u_out[:, lane(tile)] = u
            scaled[:, lane(tile)] = (u.astype(f32) * tail_wide[:, lane(tile)]).astype(bf16)
        else:
            bc_out[:, lane(tile - PAIRS)] = value
    decay = expand(jnp.broadcast_to(jnp.exp2(last), (8, LANES)), spread[...])[0:1, :]
    new_state = state[...] * decay + dot_tn(bc_out[:, :STATE], scaled[...])
    state[...] = new_state
    hst_out[0] = new_state
    new_total = total[...] + jnp.broadcast_to(last, (8, LANES))
    total[...] = new_total
    pfx_out[0] = new_total

    @pl.when(step == pl.num_programs(0) - 1)
    def _():
        send_out[:STATE, :] = new_state.astype(bf16)
        row = iota((EXTRA, LANES), 0)
        wide = jnp.broadcast_to(new_total[0:1, :], (EXTRA, LANES))
        high, rest = halves(wide)
        left = (wide - high.astype(f32) - rest.astype(f32)).astype(bf16)
        parts = jnp.where(
            row == 0,
            high.astype(f32),
            jnp.where(row == 1, rest.astype(f32), jnp.where(row == 2, left.astype(f32), 0.0)),
        )
        send_out[STATE:, :] = dot(parts.astype(bf16), spread[:LANES, :]).astype(bf16)


def within_kernel(u, bc, cum, cumt, y_out):
    scores = jnp.where(tri(True), dot_nt(bc[:, STATE:], bc[:, :STATE]), 0.0)
    for pair in range(PAIRS):
        weights = []
        for head in (2 * pair, 2 * pair + 1):
            gap = cum[:, head : head + 1] - cumt[head : head + 1, :]
            weights.append((jnp.exp2(jnp.minimum(gap, 0.0)) * scores).astype(bf16))
        y_out[:, lane(pair)] = dot(jnp.concatenate(weights, axis=1), pair_stack(u[:, lane(pair)]))


def arrived(gathered, logs, rank, groups, later):
    sums = [
        jnp.sum(logs[g].astype(f32), axis=0, keepdims=True) for g in range(groups)
    ]
    entered = jnp.zeros((STATE, INNER), f32)
    for g in range(groups):
        between = jnp.zeros((1, INNER), f32)
        for s in range(groups):
            if (s < g) if later else (s > g):
                inside = (s > rank) if later else (s < rank)
                between = between + jnp.where(inside, sums[s], 0.0)
        counts = (g > rank) if later else (g < rank)
        weight = jnp.where(counts, jnp.exp2(between), 0.0)
        entered = entered + gathered[g].astype(f32) * weight
    return entered


def gate_kernel(
    groups, rank, y_in, x, bc, cum, hst, gathered, logs, gate, tok, cot, wout, spread, rows,
    block_out, hidden_out, y_out, dy_out, dgate_out, dcc_out, ust_out, glocal_out, ng_out, h0_out,
    prefix, h0, hg_all, gated_all, dy_scaled,
):
    step = pl.program_id(0)

    @pl.when(step == 0)
    def _():
        value = arrived(gathered, logs, rank[0], groups, False)
        h0[...] = value
        h0_out[...] = value
        prefix[...] = jnp.zeros_like(prefix)
        glocal_out[...] = jnp.zeros_like(glocal_out)
        ng_out[...] = jnp.zeros_like(ng_out)

    start = expand(jnp.exp2(prefix[...]), spread[...])[0:1, :]
    state = h0[...] * start + jnp.where(step > 0, hst[0], 0.0)
    state_low = state.astype(bf16)
    grown = expand(jnp.exp2(cum[...]), spread[...])
    carried = dot(bc[:, STATE:], state_low)
    hg_all[...] = dot_nt(cot[...], wout[...])
    squares = jnp.zeros((CHUNK, LANES), f32)
    cross = jnp.zeros((CHUNK, LANES), f32)
    for tile in range(PAIRS):
        cols = lane(tile)
        y = y_in[:, cols] + carried[:, cols] * grown[:, cols]
        y_out[:, cols] = y
        mixed = (y + rows[1:2, cols] * x[:, cols].astype(f32)).astype(bf16).astype(f32)
        gate_val = gate[:, cols].astype(f32)
        gated = mixed * (gate_val * sigmoid(gate_val))
        gated_all[:, cols] = gated
        squares = squares + gated * gated
        cross = cross + gated * (hg_all[:, cols] * rows[0:1, cols])
    mean = jnp.sum(squares, axis=1, keepdims=True) * (1.0 / INNER)
    scale = lax.rsqrt(mean + norm_eps)
    cross_mean = jnp.sum(cross, axis=1, keepdims=True) * (1.0 / INNER) * scale * scale * scale
    for tile in range(PAIRS):
        cols = lane(tile)
        gated = gated_all[:, cols]
        normal = gated * scale
        hidden_out[:, cols] = (normal * rows[0:1, cols]).astype(bf16)
        grad = hg_all[:, cols]
        ng_out[:, cols] += fold(grad * normal)
        dgated = grad * rows[0:1, cols] * scale - gated * cross_mean
        gate_val = gate[:, cols].astype(f32)
        sig = sigmoid(gate_val)
        silu = gate_val * sig
        mixed = (y_out[:, cols] + rows[1:2, cols] * x[:, cols].astype(f32)).astype(bf16).astype(f32)
        dgate_out[:, cols] = (dgated * mixed * (sig + silu * (1.0 - sig))).astype(bf16)
        dy = (dgated * silu).astype(bf16)
        dy_out[:, cols] = dy
        dy_scaled[:, cols] = (dy.astype(f32) * grown[:, cols]).astype(bf16)
    block_out[...] = tok[...].astype(f32) + dot(hidden_out[...], wout[...])
    update = dot_tn(bc[:, STATE:], dy_scaled[...])
    ust_out[0] = update
    glocal_out[...] += update * start
    dcc_out[...] = dot_nt(dy_scaled[...], state_low)
    prefix[...] += jnp.broadcast_to(cum[CHUNK - 1 : CHUNK, :], (8, LANES))


def within_back_kernel(u, dy, bc, cum, cumt, dxs_out, dbc_out):
    upper = tri(False)
    scores = jnp.where(upper, dot_nt(bc[:, :STATE], bc[:, STATE:]), 0.0)
    total = jnp.zeros((CHUNK, CHUNK), f32)
    for pair in range(PAIRS):
        stacked = pair_stack(dy[:, lane(pair)])
        products = dot_nt(u[:, lane(pair)], stacked)
        weights = []
        for half in range(2):
            head = 2 * pair + half
            gap = cumt[head : head + 1, :] - cum[:, head : head + 1]
            decay = jnp.exp2(jnp.minimum(gap, 0.0))
            weights.append((decay * scores).astype(bf16))
            total = total + decay * products[:, lane(half)]
        dxs_out[:, lane(pair)] = dot(jnp.concatenate(weights, axis=1), stacked)
    low = jnp.where(upper, total, 0.0).astype(bf16)
    dbc_out[:, :STATE] = dot(low, bc[:, STATE:])
    dbc_out[:, STATE:] = dot_tn(low, bc[:, :STATE])


def back_kernel(
    groups, rank, dxs, dy, x, u, y, bc, dbc, dcc, cum, dt, hst, pfx, h0, gathered, logs, ust, proj,
    before, halo, convp, headp, spread, collect, rows,
    pg_out, first_out, tail_out, wg_out, hg_out, skip_out,
    gstate, ext, dext, scaled, prod_q, prod_p,
):
    step = pl.program_id(0)
    chunk = pl.num_programs(0) - 1 - step

    @pl.when(step == 0)
    def _():
        gstate[...] = arrived(gathered, logs, rank[0], groups, True)
        dext[CHUNK:, :] = jnp.zeros((8, XBC), f32)
        wg_out[...] = jnp.zeros_like(wg_out)
        hg_out[...] = jnp.zeros_like(hg_out)
        skip_out[...] = jnp.zeros_like(skip_out)

    @pl.when(step > 0)
    def _():
        dext[CHUNK:, :] = dext[0:8, :]

    @pl.when(chunk == 0)
    def _():
        ext[0:8, :] = halo[8:16, :].astype(f32)

    @pl.when(chunk > 0)
    def _():
        ext[0:8, :] = before[8:16, :XBC].astype(f32)

    ext[8:, :] = proj[:, :XBC].astype(f32)
    grad_state = gstate[...]
    grad_low = grad_state.astype(bf16)
    last = cum[CHUNK - 1 : CHUNK, :]
    tail_wide = expand(jnp.exp2(last - cum[...]), spread[...])
    steps_wide = expand(dt[...], spread[...])
    reach = dot(bc[:, :STATE], grad_low)

    def conv_back(tile, grad):
        cols = lane(tile)
        pre, taps = conv_pre(ext, convp, tile)
        sig = sigmoid(pre)
        dpre = grad * (sig + pre * sig * (1.0 - sig))
        dext[0:CHUNK, cols] = dpre
        for k in range(CONV):
            wg_out[8 * k : 8 * k + 8, cols] += fold(dpre * taps[k])
        wg_out[32:40, cols] += fold(dpre)
        source = dpre * convp[3:4, cols]
        for k in range(CONV - 1):
            source = source + dext[3 - k : 3 - k + CHUNK, cols] * convp[k : k + 1, cols]
        pg_out[:, cols] = source.astype(bf16)

        @pl.when(step == 0)
        def _():
            tail_out[:, cols] = source[CHUNK - 8 :, :]

    for tile in range(PAIRS):
        cols = lane(tile)
        dxs_full = dxs[:, cols] + tail_wide[:, cols] * reach[:, cols]
        uf = u[:, cols].astype(f32)
        dyf = dy[:, cols].astype(f32)
        scaled[:, cols] = (uf * tail_wide[:, cols]).astype(bf16)
        q = uf * dxs_full
        high, rest = halves(q)
        prod_q[:, cols] = high
        prod_q[:, INNER + tile * LANES : INNER + (tile + 1) * LANES] = rest
        high, rest = halves(dyf * y[:, cols] - q)
        prod_p[:, cols] = high
        prod_p[:, INNER + tile * LANES : INNER + (tile + 1) * LANES] = rest
        skip_out[:, cols] += fold(dyf * x[:, cols].astype(f32))
        conv_back(tile, rows[1:2, cols] * dyf + steps_wide[:, cols] * dxs_full)
    conv_back(PAIRS, dbc[:, :STATE] + dot_nt(scaled[...], grad_low))
    conv_back(PAIRS + 1, dbc[:, STATE:] + dcc[...])
    first_out[...] = dext[0:8, :]

    q_heads = dot(prod_q[...], collect[...])
    gap_heads = dot(prod_p[...], collect[...])
    end = expand(jnp.exp2(pfx[0]), spread[...])[0:1, :]
    meet = fold(grad_state * (hst[0] + h0[...] * end))
    meet_high, meet_rest = halves(meet)
    meet_heads = jnp.sum(
        dot(jnp.concatenate([meet_high, meet_rest], axis=1), collect[...]), axis=0, keepdims=True
    )
    dlog = dot_full(jnp.where(tri(False), 1.0, 0.0), gap_heads) + meet_heads
    sig = sigmoid(proj[:, XBC:].astype(f32) + headp[0:1, :])
    steps = dt[...]
    ratio = jnp.where(steps > 1e-30, sig / jnp.maximum(steps, 1e-30), 1.0)
    raw_grad = q_heads * ratio - dlog * headp[1:2, :] * sig
    pg_out[:, XBC:] = raw_grad.astype(bf16)
    hg_out[0:8, :] += fold(raw_grad)
    hg_out[8:16, :] += fold(dlog * steps * headp[1:2, :]) * (-1.0)
    decay = expand(jnp.broadcast_to(jnp.exp2(last), (8, LANES)), spread[...])[0:1, :]
    gstate[...] = grad_state * decay + ust[0]


def swap(v, axis, bit):
    size = lax.axis_size(axis)
    return lax.ppermute(v, axis, [(i, i ^ (1 << bit)) for i in range(size)])


def mesh_bits():
    found = []
    for axis in ("dp", "seq"):
        for bit in reversed(range(lax.axis_size(axis).bit_length() - 1)):
            found.append((axis, bit))
    return found


def mine(axis, bit):
    return (lax.axis_index(axis) >> bit) & 1


def merge_pair(v, other, place, axis, bit):
    second = mine(axis, bit) == 1
    return jnp.stack([jnp.where(second, other, v), jnp.where(second, v, other)], axis=place)


def gather_step(v, place, axis, bit):
    return merge_pair(v, swap(v, axis, bit), place, axis, bit)


def gather_pairs(v, bits, lead=0):
    for place, (axis, bit) in enumerate(bits):
        v = gather_step(v, lead + place, axis, bit)
    return v


def flat(v):
    return v.reshape(-1, v.shape[-1])


def gather_crossed(v, bits):
    cross = len(bits) - 3
    v = gather_pairs(v, bits[:cross])
    half = v.shape[-1] // 256 * 128
    left, right = v[..., :half], v[..., half:]
    left = gather_step(left, cross, *bits[cross])
    right = gather_step(right, cross, *bits[cross + 1])
    left = gather_step(left, cross + 1, *bits[cross + 1])
    right = gather_step(right, cross, *bits[cross])
    left = gather_step(left, cross + 2, *bits[cross + 2])
    right = gather_step(right, cross + 2, *bits[cross + 2])
    return jnp.concatenate([flat(left), flat(right)], axis=1)


def split_pair(v, place, axis, bit):
    own = mine(axis, bit)
    keep = lax.dynamic_index_in_dim(v, own, place, keepdims=False)
    give = lax.dynamic_index_in_dim(v, 1 - own, place, keepdims=False)
    return keep, give


def add_low(keep, got):
    return (keep.astype(f32) + got.astype(f32)).astype(keep.dtype)


def scatter_step(v, place, axis, bit):
    keep, give = split_pair(v, place, axis, bit)
    return add_low(keep, swap(give, axis, bit))


def sum_pairs(v, bits):
    for axis, bit in bits:
        v = v + swap(v, axis, bit)
    return v


def full(shape):
    return pl.BlockSpec(shape, lambda c: (0,) * len(shape))


def by_chunk(width, rows=CHUNK):
    return pl.BlockSpec((rows, width), lambda c: (c, 0))


def shape(dims, dtype):
    return jax.ShapeDtypeStruct(dims, dtype)


def params():
    return pltpu.CompilerParams(dimension_semantics=("arbitrary",), vmem_limit_bytes=VMEM)


def cost(flops, moved):
    return pl.CostEstimate(flops=flops, bytes_accessed=moved, transcendentals=0)


def spread_map():
    heads = jnp.arange(LANES)[:, None]
    cols = jnp.arange(INNER)[None, :] // HEADDIM
    once = (heads == cols).astype(bf16)
    return jnp.concatenate([once, once], axis=0)


def unpack_channels(channels):
    pieces = []
    offset = 0
    for piece_len in (D, INNER, XBC * CONV, XBC, HEADS, HEADS, HEADS):
        pieces.append(channels[offset : offset + piece_len])
        offset = offset + piece_len
    pre_gain, norm_gain, conv_flat, conv_bias, step_bias, rate_log, skip_gain = pieces
    return (
        pre_gain,
        norm_gain,
        conv_flat.reshape(XBC, CONV),
        conv_bias,
        step_bias,
        rate_log,
        skip_gain,
    )


def pre_norm(tok_vals, pre_gain):
    return (
        tok_vals * lax.rsqrt(jnp.mean(tok_vals * tok_vals, -1, keepdims=True) + norm_eps) * pre_gain
    )


def adamw_step(weight, moment, second, gradient, step_rate, decay_rate):
    moment_next = beta_one * moment + (1.0 - beta_one) * gradient
    second_next = beta_two * second + (1.0 - beta_two) * gradient * gradient
    first_fix = 1.0 - beta_one**STEP
    second_fix = 1.0 - beta_two**STEP
    update = moment_next / first_fix / (jnp.sqrt(second_next / second_fix) + adam_eps)
    return (weight - step_rate * (update + decay_rate * weight), moment_next, second_next)


def local(
    tokens,
    cotangent,
    in_weight,
    in_moment,
    in_second,
    out_weight,
    out_moment,
    out_second,
    channels,
    channel_moment,
    channel_second,
):
    groups = lax.axis_size("seq")
    bits = mesh_bits()
    seq_bits = [(axis, bit) for axis, bit in bits if axis == "seq"]
    seq_rank = lax.axis_index("seq")
    rank = seq_rank.astype(jnp.int32).reshape(1)
    pre_gain, norm_gain, conv_weight, conv_bias, step_bias, rate_log, skip_gain = unpack_channels(
        channels
    )
    tok_low = tokens[0]
    cot_low = cotangent[0]
    count = tok_low.shape[0]
    chunks = count // CHUNK

    def quarter(weight):
        size = weight.shape[0] // groups
        return lax.dynamic_slice_in_dim(weight, seq_rank * size, size, 0).astype(bf16)

    in_part = quarter(in_weight)
    side_part = jnp.pad(in_part[:, INNER:], ((0, 0), (0, SIDE + INNER - PROJ)))
    full_side = gather_crossed(side_part, bits)

    beside = [
        lax.all_gather(part, "dp", axis=0, tiled=False)
        for part in (in_part[:, :INNER], quarter(out_weight))
    ]
    (y_axis, y_bit), (core_axis, core_bit) = seq_bits

    forward = [(s, s + 1) for s in range(groups - 1)]
    backward = [(s + 1, s) for s in range(groups - 1)]
    tok_halo = lax.ppermute(tok_low[count - 16 :], "seq", forward)
    halo_norm = pre_norm(tok_halo.astype(f32), pre_gain).astype(bf16)
    tok_vals = tok_low.astype(f32)
    normed_low = pre_norm(tok_vals, pre_gain).astype(bf16)

    convp = jnp.concatenate(
        [conv_weight.T, conv_bias[None, :], jnp.zeros((3, XBC), f32)], axis=0
    )
    pad_heads = lambda v: jnp.pad(v, (0, LANES - HEADS))[None, :]
    headp = jnp.concatenate(
        [pad_heads(step_bias), pad_heads(jnp.exp(rate_log)), jnp.zeros((6, LANES), f32)], axis=0
    )
    rows = jnp.concatenate(
        [norm_gain[None, :], jnp.repeat(skip_gain, HEADDIM)[None, :], jnp.zeros((6, INNER), f32)],
        axis=0,
    )
    spread = spread_map()
    collect = jnp.concatenate([spread[:LANES].T, spread[:LANES].T], axis=0)

    proj = dot(normed_low, full_side).astype(bf16)
    halo = dot(halo_norm, full_side[:, :XBC]).astype(bf16)
    proj, halo, beside = lax.optimization_barrier((proj, halo, beside))
    others = [swap(part, y_axis, y_bit) for part in beside]

    x, bc, u, cum, cumt, dt, hst, pfx, send = pl.pallas_call(
        conv_state_kernel,
        grid=(chunks,),
        in_specs=[
            by_chunk(SIDE), full((16, XBC)), full((8, XBC)), full((8, LANES)),
            full((2 * LANES, INNER)),
        ],
        out_specs=[
            by_chunk(INNER), by_chunk(2 * STATE), by_chunk(INNER), by_chunk(LANES),
            pl.BlockSpec((32, CHUNK), lambda c: (0, c)), by_chunk(LANES),
            pl.BlockSpec((1, STATE, INNER), lambda c: (c, 0, 0)),
            pl.BlockSpec((1, 8, LANES), lambda c: (c, 0, 0)),
            full((STATE + EXTRA, INNER)),
        ],
        out_shape=[
            shape((count, INNER), bf16), shape((count, 2 * STATE), bf16),
            shape((count, INNER), bf16), shape((count, LANES), f32), shape((32, count), f32),
            shape((count, LANES), f32), shape((chunks, STATE, INNER), f32),
            shape((chunks, 8, LANES), f32), shape((STATE + EXTRA, INNER), bf16),
        ],
        scratch_shapes=[
            pltpu.VMEM((CHUNK + 8, XBC), f32), pltpu.VMEM((STATE, INNER), f32),
            pltpu.VMEM((CHUNK, INNER), bf16), pltpu.VMEM((8, LANES), f32),
        ],
        compiler_params=params(),
        cost_estimate=cost(24 * 10**9, 24 * 2**20),
        name="conv_state",
    )(proj, halo, convp, headp, spread)

    states = lax.all_gather(send, "seq", axis=0, tiled=False)
    (x, bc, u, cum, cumt, dt, hst, pfx), others = lax.optimization_barrier(
        ((x, bc, u, cum, cumt, dt, hst, pfx), others)
    )
    beside = [merge_pair(part, other, 1, y_axis, y_bit) for part, other in zip(beside, others)]
    others = [swap(part, core_axis, core_bit) for part in beside]

    y_within = pl.pallas_call(
        within_kernel,
        grid=(chunks,),
        in_specs=[
            by_chunk(INNER), by_chunk(2 * STATE), by_chunk(LANES),
            pl.BlockSpec((32, CHUNK), lambda c: (0, c)),
        ],
        out_specs=by_chunk(INNER),
        out_shape=shape((count, INNER), f32),
        compiler_params=params(),
        cost_estimate=cost(11 * 10**9, 16 * 2**20),
        name="within",
    )(u, bc, cum, cumt)
    y_within, others = lax.optimization_barrier((y_within, others))
    full_gate, full_out = [
        flat(merge_pair(part, other, 2, core_axis, core_bit)) for part, other in zip(beside, others)
    ]
    gate = dot(normed_low, full_gate).astype(bf16)

    gathered_spec = full((groups, STATE, INNER))
    logs_spec = pl.BlockSpec((groups, EXTRA, INNER), lambda c: (0, STATE // EXTRA, 0))
    smem = pl.BlockSpec(memory_space=pltpu.SMEM)

    def gate_call(*refs):
        gate_kernel(groups, *refs)

    block, hidden, y, dy, dgate, dcc, ust, glocal, ng, h0 = pl.pallas_call(
        gate_call,
        grid=(chunks,),
        in_specs=[
            smem, by_chunk(INNER), by_chunk(INNER), by_chunk(2 * STATE), by_chunk(LANES),
            pl.BlockSpec((1, STATE, INNER), lambda c: (jnp.maximum(c - 1, 0), 0, 0)),
            gathered_spec, logs_spec, by_chunk(INNER), by_chunk(D), by_chunk(D),
            full((INNER, D)), full((2 * LANES, INNER)), full((8, INNER)),
        ],
        out_specs=[
            by_chunk(D), by_chunk(INNER), by_chunk(INNER), by_chunk(INNER), by_chunk(INNER),
            by_chunk(LANES), pl.BlockSpec((1, STATE, INNER), lambda c: (c, 0, 0)),
            full((STATE, INNER)), full((8, INNER)), full((STATE, INNER)),
        ],
        out_shape=[
            shape((count, D), f32), shape((count, INNER), bf16), shape((count, INNER), f32),
            shape((count, INNER), bf16), shape((count, INNER), bf16), shape((count, LANES), f32),
            shape((chunks, STATE, INNER), f32), shape((STATE, INNER), f32), shape((8, INNER), f32),
            shape((STATE, INNER), f32),
        ],
        scratch_shapes=[
            pltpu.VMEM((8, LANES), f32), pltpu.VMEM((STATE, INNER), f32),
            pltpu.VMEM((CHUNK, INNER), f32), pltpu.VMEM((CHUNK, INNER), f32),
            pltpu.VMEM((CHUNK, INNER), bf16),
        ],
        compiler_params=params(),
        cost_estimate=cost(30 * 10**9, 48 * 2**20),
        name="gate_norm",
    )(
        rank, y_within, x, bc, cum, hst, states, states, gate, tok_low, cot_low, full_out, spread,
        rows,
    )

    grads = lax.all_gather(glocal.astype(bf16), "seq", axis=0, tiled=False)

    def product(left, right):
        return lax.dot_general(left, right, TN, preferred_element_type=f32).astype(bf16)

    def blocks(v, cut):
        return v.reshape((2,) * len(cut) + (v.shape[0] >> len(cut), v.shape[1]))

    dp_size = lax.axis_size("dp")

    def by_owner(v):
        return v.reshape(dp_size, 2, 2, v.shape[0] // (4 * dp_size), v.shape[1])

    keeps, gives = zip(
        *[
            split_pair(by_owner(product(left, right)), 2, core_axis, core_bit)
            for left, right in ((hidden, cot_low), (normed_low, dgate))
        ]
    )
    first_got = [swap(give, core_axis, core_bit) for give in gives]
    anywhere = pl.BlockSpec(memory_space=pl.ANY)

    def within_back_call(u, dy, bc, cum, cumt, sent_a, sent_b, dxs_out, dbc_out):
        within_back_kernel(u, dy, bc, cum, cumt, dxs_out, dbc_out)

    dxs, dbc = pl.pallas_call(
        within_back_call,
        grid=(chunks,),
        in_specs=[
            by_chunk(INNER), by_chunk(INNER), by_chunk(2 * STATE), by_chunk(LANES),
            pl.BlockSpec((32, CHUNK), lambda c: (0, c)), anywhere, anywhere,
        ],
        out_specs=[by_chunk(INNER), by_chunk(2 * STATE)],
        out_shape=[shape((count, INNER), f32), shape((count, 2 * STATE), f32)],
        compiler_params=params(),
        cost_estimate=cost(12 * 10**9, 16 * 2**20),
        name="within_back",
    )(u, dy, bc, cum, cumt, *gives)

    halves_got, dxs, dbc = lax.optimization_barrier((first_got, dxs, dbc))
    keeps, gives = zip(
        *[
            split_pair(add_low(keep, got), 1, y_axis, y_bit)
            for keep, got in zip(keeps, halves_got)
        ]
    )
    second_got = [swap(give, y_axis, y_bit) for give in gives]

    def back(width, height=CHUNK):
        return pl.BlockSpec((height, width), lambda c: (chunks - 1 - c, 0))

    def back_three(height):
        return pl.BlockSpec((1, height, INNER), lambda c: (chunks - 1 - c, 0, 0))

    def back_call(sent_a, sent_b, *refs):
        back_kernel(groups, *refs)

    per = CHUNK // 16
    pg, first, tail, wg, hgr, skip = pl.pallas_call(
        back_call,
        grid=(chunks,),
        in_specs=[
            anywhere, anywhere, smem, back(INNER), back(INNER), back(INNER), back(INNER), back(INNER), back(2 * STATE),
            back(2 * STATE), back(LANES), back(LANES), back(LANES), back_three(STATE),
            pl.BlockSpec((1, 8, LANES), lambda c: (chunks - 1 - c, 0, 0)),
            full((STATE, INNER)), gathered_spec, logs_spec, back_three(STATE), back(SIDE),
            pl.BlockSpec(
                (16, SIDE), lambda c: (jnp.maximum((chunks - 1 - c) * per - 1, 0), 0)
            ),
            full((16, XBC)), full((8, XBC)), full((8, LANES)), full((2 * LANES, INNER)),
            full((2 * INNER, LANES)), full((8, INNER)),
        ],
        out_specs=[
            back(SIDE), full((8, XBC)), full((8, XBC)), full((40, XBC)), full((16, LANES)),
            full((8, INNER)),
        ],
        out_shape=[
            shape((count, SIDE), bf16), shape((8, XBC), f32), shape((8, XBC), f32),
            shape((40, XBC), f32), shape((16, LANES), f32), shape((8, INNER), f32),
        ],
        scratch_shapes=[
            pltpu.VMEM((STATE, INNER), f32), pltpu.VMEM((CHUNK + 8, XBC), f32),
            pltpu.VMEM((CHUNK + 8, XBC), f32), pltpu.VMEM((CHUNK, INNER), bf16),
            pltpu.VMEM((CHUNK, 2 * INNER), bf16), pltpu.VMEM((CHUNK, 2 * INNER), bf16),
        ],
        compiler_params=params(),
        cost_estimate=cost(47 * 10**9, 48 * 2**20),
        name="mixer_back",
    )(
        *gives, rank, dxs, dy, x, u, y, bc, dbc, dcc, cum, dt, hst, pfx, h0, grads, states, ust, proj, proj,
        halo, convp, headp, spread, collect, rows,
    )

    second_got, pg, first, tail, wg, hgr, skip = lax.optimization_barrier(
        (second_got, pg, first, tail, wg, hgr, skip)
    )
    after = lax.ppermute(first, "seq", backward)
    fixes = [jnp.zeros((5, XBC), f32)]
    for m in range(CONV - 1):
        fix = convp[0] * after[m]
        for k in range(1, m + 1):
            fix = fix + convp[k] * after[m - k]
        fixes.append(fix[None, :])
    tail_low = (tail + jnp.concatenate(fixes, axis=0)).astype(bf16)
    pg = lax.dynamic_update_slice(pg, tail_low, (count - 8, 0))

    out_scattered, gate_scattered = [
        lax.psum_scatter(flat(add_low(keep, got)), "dp", scatter_dimension=0, tiled=True)
        for keep, got in zip(keeps, second_got)
    ]

    cross = len(bits) - 3
    half = SIDE // 256 * 128
    left = blocks(product(normed_low, pg[:, :half]), bits)
    right = blocks(product(normed_low, pg[:, half:]), bits)
    barrier = lax.optimization_barrier
    keep_l, give_l = split_pair(left, cross + 2, core_axis, core_bit)
    keep_r, give_r = split_pair(right, cross + 2, core_axis, core_bit)
    got_l, got_r = swap(give_l, core_axis, core_bit), swap(give_r, core_axis, core_bit)
    pg, dgate, _, _ = barrier((pg, dgate, give_l, give_r))
    normed_grad = lax.dot_general(dgate, full_gate, NT, preferred_element_type=f32)
    normed_grad = normed_grad + lax.dot_general(pg, full_side, NT, preferred_element_type=f32)
    got_l, got_r, normed_grad = barrier((got_l, got_r, normed_grad))
    x_axis, x_bit = bits[cross]
    keep_l, give_l = split_pair(add_low(keep_l, got_l), cross + 1, y_axis, y_bit)
    keep_r, give_r = split_pair(add_low(keep_r, got_r), cross, x_axis, x_bit)
    got_l, got_r = swap(give_l, y_axis, y_bit), swap(give_r, x_axis, x_bit)
    normed_grad, _, _ = barrier((normed_grad, give_l, give_r))
    _, norm_pull = jax.vjp(pre_norm, tok_vals, pre_gain)
    tok_norm_grad, pre_gain_grad = norm_pull(normed_grad)
    token_grad = (cot_low.astype(f32) + tok_norm_grad)[None]
    got_l, got_r, token_grad, pre_gain_grad = barrier((got_l, got_r, token_grad, pre_gain_grad))
    left = scatter_step(add_low(keep_l, got_l), cross, x_axis, x_bit)
    right = scatter_step(add_low(keep_r, got_r), cross, y_axis, y_bit)
    side_scattered = jnp.concatenate([left, right], axis=-1)
    side_scattered, out_scattered, gate_scattered = barrier(
        (side_scattered, out_scattered, gate_scattered)
    )
    for place in reversed(range(cross)):
        side_scattered = scatter_step(side_scattered, place, *bits[place])

    wg_sum = jnp.sum(wg.reshape(5, 8, XBC), axis=1)
    chan_grad = jnp.concatenate(
        [
            pre_gain_grad,
            jnp.sum(ng, axis=0),
            wg_sum[:CONV].T.reshape(-1),
            wg_sum[CONV],
            jnp.sum(hgr[:8, :HEADS], axis=0),
            jnp.sum(hgr[8:, :HEADS], axis=0),
            jnp.sum(skip.reshape(8, HEADS, HEADDIM), axis=(0, 2)),
        ]
    )
    chan_grad = sum_pairs(chan_grad, bits)

    def owned(part):
        return flat(gather_pairs(part, seq_bits)).astype(f32)

    out_grad = owned(out_scattered)
    in_grad = jnp.concatenate(
        [owned(gate_scattered), owned(side_scattered)[:, : PROJ - INNER]], axis=1
    )
    in_new, in_mom, in_sec = adamw_step(
        in_weight, in_moment, in_second, in_grad, rate_matrix, decay_matrix
    )
    out_new, out_mom, out_sec = adamw_step(
        out_weight, out_moment, out_second, out_grad, rate_matrix, decay_matrix
    )
    chan_new, chan_mom, chan_sec = adamw_step(
        channels, channel_moment, channel_second, chan_grad, rate_channel, 0.0
    )
    return (
        block[None],
        token_grad,
        in_new,
        in_mom,
        in_sec,
        out_new,
        out_mom,
        out_sec,
        chan_new,
        chan_mom,
        chan_sec,
    )


def solution(mesh):
    acts = P("dp", "seq", None)
    rows = P("dp", None)
    specs = (acts, acts) + (rows,) * 6 + (P(),) * 3
    return jax.shard_map(local, mesh=mesh, in_specs=specs, out_specs=specs, check_vma=False)
```

```python
import math

import jax
import jax.numpy as jnp
from jax import lax
from jax.experimental import pallas as pl
from jax.experimental.pallas import tpu as pltpu
from jax.sharding import PartitionSpec as P

D = 768
HEADS = 24
HEADDIM = 64
STATE = 128
CONV = 4
STEP = 10
INNER = 1536
XBC = 1792
PROJ = 3352
SIDE = 1920
LANES = 128
CHUNK = 128
PAIRS = HEADS // 2
TILES = XBC // LANES
EXTRA = 16

norm_eps = 1e-05
beta_one = 0.9
beta_two = 0.999
adam_eps = 1e-08
rate_matrix = 0.1
rate_channel = 0.5
decay_matrix = 0.1
LOG2E = 1.0 / math.log(2.0)
VMEM = 56 * 1024 * 1024

f32 = jnp.float32
bf16 = jnp.bfloat16
NT = (((1,), (1,)), ((), ()))
TN = (((0,), (0,)), ((), ()))


def dot(a, b):
    return jnp.dot(a, b, preferred_element_type=f32)


def dot_nt(a, b):
    return lax.dot_general(a, b, NT, preferred_element_type=f32)


def dot_tn(a, b):
    return lax.dot_general(a, b, TN, preferred_element_type=f32)


def sigmoid(v):
    return 0.5 * jnp.tanh(0.5 * v) + 0.5


def halves(v):
    high = v.astype(bf16)
    return high, (v - high.astype(f32)).astype(bf16)


def running(mask, v):
    high, rest = halves(v)
    left = (v - high.astype(f32) - rest.astype(f32)).astype(bf16)
    parts = dot(jnp.where(mask, 1.0, 0.0).astype(bf16), jnp.concatenate([high, rest, left], axis=1))
    return parts[:, :LANES] + parts[:, LANES : 2 * LANES] + parts[:, 2 * LANES :]


def expand(v, spread):
    high, rest = halves(v)
    return dot(jnp.concatenate([high, rest], axis=1), spread)


def fold(v):
    return jnp.sum(v.reshape(v.shape[0] // 8, 8, v.shape[1]), axis=0)


def lane(i):
    return slice(i * LANES, (i + 1) * LANES)


def iota(shape, dim):
    return lax.broadcasted_iota(jnp.int32, shape, dim)


def tri(lower):
    rows, cols = iota((CHUNK, CHUNK), 0), iota((CHUNK, CHUNK), 1)
    return (rows >= cols) if lower else (rows <= cols)


def conv_pre(ext, convp, tile):
    cols = lane(tile)
    taps = [ext[5 + k : 5 + k + CHUNK, cols] for k in range(CONV)]
    pre = taps[0] * convp[0:1, cols] + convp[4:5, cols]
    for k in range(1, CONV):
        pre = pre + taps[k] * convp[k : k + 1, cols]
    return pre, taps


def pair_stack(v):
    side = iota(v.shape, 1) < HEADDIM
    zero = jnp.zeros_like(v)
    return jnp.concatenate([jnp.where(side, v, zero), jnp.where(side, zero, v)], axis=0)


def conv_state_kernel(
    proj, halo, convp, headp, spread, x_out, bc_out, u_out, cum_out, cumt_out, dt_out, hst_out,
    pfx_out, send_out, ext, state, scaled, total,
):
    step = pl.program_id(0)

    @pl.when(step == 0)
    def _():
        ext[0:8, :] = halo[8:16, :].astype(f32)
        state[...] = jnp.zeros_like(state)
        total[...] = jnp.zeros_like(total)

    @pl.when(step > 0)
    def _():
        ext[0:8, :] = ext[CHUNK : CHUNK + 8, :]

    ext[8:, :] = proj[:, :XBC].astype(f32)
    raw = proj[:, XBC:].astype(f32) + headp[0:1, :]
    steps = jnp.maximum(raw, 0.0) + jnp.log1p(jnp.exp(-jnp.abs(raw)))
    log_decay = steps * (headp[1:2, :] * (-LOG2E))
    cum = running(tri(True), log_decay)
    cum_out[...] = cum
    cumt_out[...] = jnp.transpose(cum)[0:32, :]
    dt_out[...] = steps
    last = cum[CHUNK - 1 : CHUNK, :]
    decayed = jnp.broadcast_to(jnp.exp2(last), (8, LANES))
    wide = expand(jnp.concatenate([steps, jnp.exp2(last - cum), decayed], axis=0), spread[...])
    steps_wide, tail_wide = wide[:CHUNK], wide[CHUNK : 2 * CHUNK]
    decay = wide[2 * CHUNK : 2 * CHUNK + 1]
    for tile in range(TILES):
        pre, _ = conv_pre(ext, convp, tile)
        value = (pre * sigmoid(pre)).astype(bf16)
        if tile < PAIRS:
            x_out[:, lane(tile)] = value
            u = (value.astype(f32) * steps_wide[:, lane(tile)]).astype(bf16)
            u_out[:, lane(tile)] = u
            scaled[:, lane(tile)] = (u.astype(f32) * tail_wide[:, lane(tile)]).astype(bf16)
        else:
            bc_out[:, lane(tile - PAIRS)] = value
    new_state = state[...] * decay + dot_tn(bc_out[:, :STATE], scaled[...])
    state[...] = new_state
    hst_out[0] = new_state
    new_total = total[...] + jnp.broadcast_to(last, (8, LANES))
    total[...] = new_total
    pfx_out[0] = new_total

    @pl.when(step == pl.num_programs(0) - 1)
    def _():
        send_out[:STATE, :] = new_state.astype(bf16)
        row = iota((EXTRA, LANES), 0)
        wide = jnp.broadcast_to(new_total[0:1, :], (EXTRA, LANES))
        high, rest = halves(wide)
        left = (wide - high.astype(f32) - rest.astype(f32)).astype(bf16)
        parts = jnp.where(
            row == 0,
            high.astype(f32),
            jnp.where(row == 1, rest.astype(f32), jnp.where(row == 2, left.astype(f32), 0.0)),
        )
        send_out[STATE:, :] = dot(parts.astype(bf16), spread[:LANES, :]).astype(bf16)


def within_kernel(u, bc, cum, cumt, y_out):
    scores = jnp.where(tri(True), dot_nt(bc[:, STATE:], bc[:, :STATE]), 0.0)
    for pair in range(PAIRS):
        weights = []
        for head in (2 * pair, 2 * pair + 1):
            gap = cum[:, head : head + 1] - cumt[head : head + 1, :]
            weights.append((jnp.exp2(jnp.minimum(gap, 0.0)) * scores).astype(bf16))
        y_out[:, lane(pair)] = dot(jnp.concatenate(weights, axis=1), pair_stack(u[:, lane(pair)]))


def arrived(gathered, logs, rank, groups, later):
    sums = [
        jnp.sum(logs[g].astype(f32), axis=0, keepdims=True) for g in range(groups)
    ]
    entered = jnp.zeros((STATE, INNER), f32)
    for g in range(groups):
        between = jnp.zeros((1, INNER), f32)
        for s in range(groups):
            if (s < g) if later else (s > g):
                inside = (s > rank) if later else (s < rank)
                between = between + jnp.where(inside, sums[s], 0.0)
        counts = (g > rank) if later else (g < rank)
        weight = jnp.where(counts, jnp.exp2(between), 0.0)
        entered = entered + gathered[g].astype(f32) * weight
    return entered


def gate_kernel(
    groups, rank, y_in, x, bc, cum, hst, gathered, logs, gate, tok, cot, wout, spread, rows,
    block_out, hidden_out, y_out, dy_out, dgate_out, dcc_out, ust_out, glocal_out, ng_out, h0_out,
    prefix, h0, hg_all, gated_all, dy_scaled,
):
    step = pl.program_id(0)

    @pl.when(step == 0)
    def _():
        value = arrived(gathered, logs, rank[0], groups, False)
        h0[...] = value
        h0_out[...] = value
        prefix[...] = jnp.zeros_like(prefix)
        glocal_out[...] = jnp.zeros_like(glocal_out)
        ng_out[...] = jnp.zeros_like(ng_out)

    wide = expand(jnp.exp2(jnp.concatenate([cum[...], prefix[...]], axis=0)), spread[...])
    grown, start = wide[:CHUNK], wide[CHUNK : CHUNK + 1]
    state = h0[...] * start + jnp.where(step > 0, hst[0], 0.0)
    state_low = state.astype(bf16)
    carried = dot(bc[:, STATE:], state_low)
    hg_all[...] = dot_nt(cot[...], wout[...])
    squares = jnp.zeros((CHUNK, LANES), f32)
    cross = jnp.zeros((CHUNK, LANES), f32)
    for tile in range(PAIRS):
        cols = lane(tile)
        y = y_in[:, cols] + carried[:, cols] * grown[:, cols]
        y_out[:, cols] = y
        mixed = (y + rows[1:2, cols] * x[:, cols].astype(f32)).astype(bf16).astype(f32)
        gate_val = gate[:, cols].astype(f32)
        gated = mixed * (gate_val * sigmoid(gate_val))
        gated_all[:, cols] = gated
        squares = squares + gated * gated
        cross = cross + gated * (hg_all[:, cols] * rows[0:1, cols])
    mean = jnp.sum(squares, axis=1, keepdims=True) * (1.0 / INNER)
    scale = lax.rsqrt(mean + norm_eps)
    cross_mean = jnp.sum(cross, axis=1, keepdims=True) * (1.0 / INNER) * scale * scale * scale
    for tile in range(PAIRS):
        cols = lane(tile)
        gated = gated_all[:, cols]
        normal = gated * scale
        hidden_out[:, cols] = (normal * rows[0:1, cols]).astype(bf16)
        grad = hg_all[:, cols]
        ng_out[:, cols] += fold(grad * normal)
        dgated = grad * rows[0:1, cols] * scale - gated * cross_mean
        gate_val = gate[:, cols].astype(f32)
        sig = sigmoid(gate_val)
        silu = gate_val * sig
        mixed = (y_out[:, cols] + rows[1:2, cols] * x[:, cols].astype(f32)).astype(bf16).astype(f32)
        dgate_out[:, cols] = (dgated * mixed * (sig + silu * (1.0 - sig))).astype(bf16)
        dy = (dgated * silu).astype(bf16)
        dy_out[:, cols] = dy
        dy_scaled[:, cols] = (dy.astype(f32) * grown[:, cols]).astype(bf16)
    block_out[...] = tok[...].astype(f32) + dot(hidden_out[...], wout[...])
    update = dot_tn(bc[:, STATE:], dy_scaled[...])
    ust_out[0] = update
    glocal_out[...] += update * start
    dcc_out[...] = dot_nt(dy_scaled[...], state_low)
    prefix[...] += jnp.broadcast_to(cum[CHUNK - 1 : CHUNK, :], (8, LANES))


def within_back_kernel(u, dy, bc, cum, cumt, dxs_out, dbc_out):
    upper = tri(False)
    scores = jnp.where(upper, dot_nt(bc[:, :STATE], bc[:, STATE:]), 0.0)
    total = jnp.zeros((CHUNK, CHUNK), f32)
    for pair in range(PAIRS):
        stacked = pair_stack(dy[:, lane(pair)])
        products = dot_nt(u[:, lane(pair)], stacked)
        weights = []
        for half in range(2):
            head = 2 * pair + half
            gap = cumt[head : head + 1, :] - cum[:, head : head + 1]
            decay = jnp.exp2(jnp.minimum(gap, 0.0))
            weights.append((decay * scores).astype(bf16))
            total = total + decay * products[:, lane(half)]
        dxs_out[:, lane(pair)] = dot(jnp.concatenate(weights, axis=1), stacked)
    low = jnp.where(upper, total, 0.0).astype(bf16)
    dbc_out[:, :STATE] = dot(low, bc[:, STATE:])
    dbc_out[:, STATE:] = dot_tn(low, bc[:, :STATE])


def back_kernel(
    groups, rank, dxs, dy, x, u, y, bc, dbc, dcc, cum, dt, hst, pfx, h0, gathered, logs, ust, proj,
    before, halo, convp, headp, spread, collect, rows,
    pg_out, first_out, tail_out, wg_out, hg_out, skip_out,
    gstate, ext, dext, scaled, prod,
):
    step = pl.program_id(0)
    chunk = pl.num_programs(0) - 1 - step

    @pl.when(step == 0)
    def _():
        gstate[...] = arrived(gathered, logs, rank[0], groups, True)
        dext[CHUNK:, :] = jnp.zeros((8, XBC), f32)
        wg_out[...] = jnp.zeros_like(wg_out)
        hg_out[...] = jnp.zeros_like(hg_out)
        skip_out[...] = jnp.zeros_like(skip_out)

    @pl.when(step > 0)
    def _():
        dext[CHUNK:, :] = dext[0:8, :]

    @pl.when(chunk == 0)
    def _():
        ext[0:8, :] = halo[8:16, :].astype(f32)

    @pl.when(chunk > 0)
    def _():
        ext[0:8, :] = before[8:16, :XBC].astype(f32)

    ext[8:, :] = proj[:, :XBC].astype(f32)
    grad_state = gstate[...]
    grad_low = grad_state.astype(bf16)
    last = cum[CHUNK - 1 : CHUNK, :]
    decayed = jnp.broadcast_to(jnp.exp2(last), (8, LANES))
    wide = expand(
        jnp.concatenate([jnp.exp2(last - cum[...]), dt[...], decayed, jnp.exp2(pfx[0])], axis=0),
        spread[...],
    )
    tail_wide, steps_wide = wide[:CHUNK], wide[CHUNK : 2 * CHUNK]
    decay = wide[2 * CHUNK : 2 * CHUNK + 1]
    end = wide[2 * CHUNK + 8 : 2 * CHUNK + 9]
    reach = dot(bc[:, :STATE], grad_low)

    def conv_back(tile, grad):
        cols = lane(tile)
        pre, taps = conv_pre(ext, convp, tile)
        sig = sigmoid(pre)
        dpre = grad * (sig + pre * sig * (1.0 - sig))
        dext[0:CHUNK, cols] = dpre
        for k in range(CONV):
            wg_out[8 * k : 8 * k + 8, cols] += fold(dpre * taps[k])
        wg_out[32:40, cols] += fold(dpre)
        source = dpre * convp[3:4, cols]
        for k in range(CONV - 1):
            source = source + dext[3 - k : 3 - k + CHUNK, cols] * convp[k : k + 1, cols]
        pg_out[:, cols] = source.astype(bf16)

        @pl.when(step == 0)
        def _():
            tail_out[:, cols] = source[CHUNK - 8 :, :]

    for tile in range(PAIRS):
        cols = lane(tile)
        dxs_full = dxs[:, cols] + tail_wide[:, cols] * reach[:, cols]
        uf = u[:, cols].astype(f32)
        dyf = dy[:, cols].astype(f32)
        scaled[:, cols] = (uf * tail_wide[:, cols]).astype(bf16)
        q = uf * dxs_full
        high, rest = halves(q)
        prod[:CHUNK, cols] = high
        prod[:CHUNK, INNER + tile * LANES : INNER + (tile + 1) * LANES] = rest
        high, rest = halves(dyf * y[:, cols] - q)
        prod[CHUNK : 2 * CHUNK, cols] = high
        prod[CHUNK : 2 * CHUNK, INNER + tile * LANES : INNER + (tile + 1) * LANES] = rest
        skip_out[:, cols] += fold(dyf * x[:, cols].astype(f32))
        conv_back(tile, rows[1:2, cols] * dyf + steps_wide[:, cols] * dxs_full)
    conv_back(PAIRS, dbc[:, :STATE] + dot_nt(scaled[...], grad_low))
    conv_back(PAIRS + 1, dbc[:, STATE:] + dcc[...])
    first_out[...] = dext[0:8, :]

    meet = fold(grad_state * (hst[0] + h0[...] * end))
    meet = jnp.concatenate([meet, jnp.zeros_like(meet)], axis=0)
    high, rest = halves(meet)
    prod[2 * CHUNK :, :INNER] = high
    prod[2 * CHUNK :, INNER:] = rest
    heads = dot(prod[...], collect[...])
    q_heads, gap_heads = heads[:CHUNK], heads[CHUNK : 2 * CHUNK]
    meet_heads = jnp.sum(heads[2 * CHUNK :], axis=0, keepdims=True)
    dlog = running(tri(False), gap_heads) + meet_heads
    sig = sigmoid(proj[:, XBC:].astype(f32) + headp[0:1, :])
    steps = dt[...]
    ratio = jnp.where(steps > 1e-30, sig / jnp.maximum(steps, 1e-30), 1.0)
    raw_grad = q_heads * ratio - dlog * headp[1:2, :] * sig
    pg_out[:, XBC:] = raw_grad.astype(bf16)
    hg_out[0:8, :] += fold(raw_grad)
    hg_out[8:16, :] += fold(dlog * steps * headp[1:2, :]) * (-1.0)
    gstate[...] = grad_state * decay + ust[0]


def swap(v, axis, bit):
    size = lax.axis_size(axis)
    return lax.ppermute(v, axis, [(i, i ^ (1 << bit)) for i in range(size)])


def mesh_bits():
    found = []
    for axis in ("dp", "seq"):
        for bit in reversed(range(lax.axis_size(axis).bit_length() - 1)):
            found.append((axis, bit))
    return found


def mine(axis, bit):
    return (lax.axis_index(axis) >> bit) & 1


def merge_pair(v, other, place, axis, bit):
    second = mine(axis, bit) == 1
    return jnp.stack([jnp.where(second, other, v), jnp.where(second, v, other)], axis=place)


def gather_step(v, place, axis, bit):
    return merge_pair(v, swap(v, axis, bit), place, axis, bit)


def gather_pairs(v, bits, lead=0):
    for place, (axis, bit) in enumerate(bits):
        v = gather_step(v, lead + place, axis, bit)
    return v


def flat(v):
    return v.reshape(-1, v.shape[-1])


def blocks(v, bits):
    return v.reshape((2,) * len(bits) + (v.shape[0] >> len(bits), v.shape[1]))


def split_pair(v, place, axis, bit):
    own = mine(axis, bit)
    keep = lax.dynamic_index_in_dim(v, own, place, keepdims=False)
    give = lax.dynamic_index_in_dim(v, 1 - own, place, keepdims=False)
    return keep, give


def add_low(keep, got):
    return (keep.astype(f32) + got.astype(f32)).astype(keep.dtype)


def scatter_step(v, place, axis, bit):
    keep, give = split_pair(v, place, axis, bit)
    return add_low(keep, swap(give, axis, bit))


def scatter_pairs(v, bits, lead=0):
    for place in reversed(range(len(bits))):
        v = scatter_step(v, lead + place, *bits[place])
    return v


def sum_pairs(v, bits):
    for axis, bit in bits:
        v = v + swap(v, axis, bit)
    return v


def full(shape):
    return pl.BlockSpec(shape, lambda c: (0,) * len(shape))


def by_chunk(width, rows=CHUNK):
    return pl.BlockSpec((rows, width), lambda c: (c, 0))


def shape(dims, dtype):
    return jax.ShapeDtypeStruct(dims, dtype)


def params():
    return pltpu.CompilerParams(dimension_semantics=("arbitrary",), vmem_limit_bytes=VMEM)


def cost(flops, moved):
    return pl.CostEstimate(flops=flops, bytes_accessed=moved, transcendentals=0)


def spread_map():
    heads = jnp.arange(LANES)[:, None]
    cols = jnp.arange(INNER)[None, :] // HEADDIM
    once = (heads == cols).astype(bf16)
    return jnp.concatenate([once, once], axis=0)


def unpack_channels(channels):
    pieces = []
    offset = 0
    for piece_len in (D, INNER, XBC * CONV, XBC, HEADS, HEADS, HEADS):
        pieces.append(channels[offset : offset + piece_len])
        offset = offset + piece_len
    pre_gain, norm_gain, conv_flat, conv_bias, step_bias, rate_log, skip_gain = pieces
    return (
        pre_gain,
        norm_gain,
        conv_flat.reshape(XBC, CONV),
        conv_bias,
        step_bias,
        rate_log,
        skip_gain,
    )


def pre_norm(tok_vals, pre_gain):
    return (
        tok_vals * lax.rsqrt(jnp.mean(tok_vals * tok_vals, -1, keepdims=True) + norm_eps) * pre_gain
    )


def adamw_step(weight, moment, second, gradient, step_rate, decay_rate):
    moment_next = beta_one * moment + (1.0 - beta_one) * gradient
    second_next = beta_two * second + (1.0 - beta_two) * gradient * gradient
    first_fix = 1.0 - beta_one**STEP
    second_fix = 1.0 - beta_two**STEP
    update = moment_next / first_fix / (jnp.sqrt(second_next / second_fix) + adam_eps)
    return (weight - step_rate * (update + decay_rate * weight), moment_next, second_next)


def local(
    tokens,
    cotangent,
    in_weight,
    in_moment,
    in_second,
    out_weight,
    out_moment,
    out_second,
    channels,
    channel_moment,
    channel_second,
):
    groups = lax.axis_size("seq")
    bits = mesh_bits()
    seq_bits = [(axis, bit) for axis, bit in bits if axis == "seq"]
    seq_rank = lax.axis_index("seq")
    rank = seq_rank.astype(jnp.int32).reshape(1)
    pre_gain, norm_gain, conv_weight, conv_bias, step_bias, rate_log, skip_gain = unpack_channels(
        channels
    )
    tok_low = tokens[0]
    cot_low = cotangent[0]
    count = tok_low.shape[0]
    chunks = count // CHUNK

    def quarter(weight):
        size = weight.shape[0] // groups
        return lax.dynamic_slice_in_dim(weight, seq_rank * size, size, 0).astype(bf16)

    in_part = quarter(in_weight)
    side_part = jnp.pad(in_part[:, INNER:], ((0, 0), (0, SIDE + INNER - PROJ)))
    out_rows = out_weight.shape[0] // groups
    in_rows = in_weight.shape[0] // groups
    beside = jnp.concatenate(
        [quarter(out_weight), in_part[:, :D], in_part[:, D:INNER]], axis=0
    )
    barrier = lax.optimization_barrier
    cross = len(bits) - 3
    (x_axis, x_bit), (y_axis, y_bit), (core_axis, core_bit) = bits[cross:]
    side = gather_pairs(side_part, bits[:cross])
    side, beside = barrier((side, beside))
    half = SIDE // 256 * 128
    left, right = side[..., :half], side[..., half:]
    got_l, got_r = swap(left, x_axis, x_bit), swap(right, y_axis, y_bit)
    early = cross // 2
    beside = gather_pairs(beside, bits[:early])
    got_l, got_r, beside = barrier((got_l, got_r, beside))
    left = merge_pair(left, got_l, cross, x_axis, x_bit)
    right = merge_pair(right, got_r, cross, y_axis, y_bit)
    got_l, got_r = swap(left, y_axis, y_bit), swap(right, x_axis, x_bit)
    beside = gather_pairs(beside, bits[early:cross], early)
    got_l, got_r, beside = barrier((got_l, got_r, beside))
    left = merge_pair(left, got_l, cross + 1, y_axis, y_bit)
    right = merge_pair(right, got_r, cross, x_axis, x_bit)
    got_l, got_r = swap(left, core_axis, core_bit), swap(right, core_axis, core_bit)
    got_b = swap(beside, x_axis, x_bit)
    left = merge_pair(left, got_l, cross + 2, core_axis, core_bit)
    right = merge_pair(right, got_r, cross + 2, core_axis, core_bit)
    full_side = jnp.concatenate([flat(left), flat(right)], axis=1)

    forward = [(s, s + 1) for s in range(groups - 1)]
    backward = [(s + 1, s) for s in range(groups - 1)]
    tok_halo = lax.ppermute(tok_low[count - 16 :], "seq", forward)
    halo_norm = pre_norm(tok_halo.astype(f32), pre_gain).astype(bf16)
    tok_vals = tok_low.astype(f32)
    normed_low = pre_norm(tok_vals, pre_gain).astype(bf16)

    convp = jnp.concatenate(
        [conv_weight.T, conv_bias[None, :], jnp.zeros((3, XBC), f32)], axis=0
    )
    pad_heads = lambda v: jnp.pad(v, (0, LANES - HEADS))[None, :]
    headp = jnp.concatenate(
        [pad_heads(step_bias), pad_heads(jnp.exp(rate_log)), jnp.zeros((6, LANES), f32)], axis=0
    )
    rows = jnp.concatenate(
        [norm_gain[None, :], jnp.repeat(skip_gain, HEADDIM)[None, :], jnp.zeros((6, INNER), f32)],
        axis=0,
    )
    spread = spread_map()
    collect = jnp.concatenate([spread[:LANES].T, spread[:LANES].T], axis=0)

    proj = dot(normed_low, full_side).astype(bf16)
    halo = dot(halo_norm, full_side[:, :XBC]).astype(bf16)
    proj, halo, got_b = barrier((proj, halo, got_b))
    beside = merge_pair(beside, got_b, cross, x_axis, x_bit)
    got_b = swap(beside, y_axis, y_bit)

    x, bc, u, cum, cumt, dt, hst, pfx, send = pl.pallas_call(
        conv_state_kernel,
        grid=(chunks,),
        in_specs=[
            by_chunk(SIDE), full((16, XBC)), full((8, XBC)), full((8, LANES)),
            full((2 * LANES, INNER)),
        ],
        out_specs=[
            by_chunk(INNER), by_chunk(2 * STATE), by_chunk(INNER), by_chunk(LANES),
            pl.BlockSpec((32, CHUNK), lambda c: (0, c)), by_chunk(LANES),
            pl.BlockSpec((1, STATE, INNER), lambda c: (c, 0, 0)),
            pl.BlockSpec((1, 8, LANES), lambda c: (c, 0, 0)),
            full((STATE + EXTRA, INNER)),
        ],
        out_shape=[
            shape((count, INNER), bf16), shape((count, 2 * STATE), bf16),
            shape((count, INNER), bf16), shape((count, LANES), f32), shape((32, count), f32),
            shape((count, LANES), f32), shape((chunks, STATE, INNER), f32),
            shape((chunks, 8, LANES), f32), shape((STATE + EXTRA, INNER), bf16),
        ],
        scratch_shapes=[
            pltpu.VMEM((CHUNK + 8, XBC), f32), pltpu.VMEM((STATE, INNER), f32),
            pltpu.VMEM((CHUNK, INNER), bf16), pltpu.VMEM((8, LANES), f32),
        ],
        compiler_params=params(),
        cost_estimate=cost(24 * 10**9, 24 * 2**20),
        name="conv_state",
    )(proj, halo, convp, headp, spread)

    states = lax.all_gather(send, "seq", axis=0, tiled=False)
    x, bc, u, cum, cumt, dt, hst, pfx, got_b = barrier(
        (x, bc, u, cum, cumt, dt, hst, pfx, got_b)
    )
    beside = merge_pair(beside, got_b, cross + 1, y_axis, y_bit)
    got_b = swap(beside, core_axis, core_bit)

    y_within = pl.pallas_call(
        within_kernel,
        grid=(chunks,),
        in_specs=[
            by_chunk(INNER), by_chunk(2 * STATE), by_chunk(LANES),
            pl.BlockSpec((32, CHUNK), lambda c: (0, c)),
        ],
        out_specs=by_chunk(INNER),
        out_shape=shape((count, INNER), f32),
        compiler_params=params(),
        cost_estimate=cost(11 * 10**9, 16 * 2**20),
        name="within",
    )(u, bc, cum, cumt)
    y_within, got_b = barrier((y_within, got_b))
    beside = merge_pair(beside, got_b, cross + 2, core_axis, core_bit)
    full_out = flat(beside[..., :out_rows, :])
    full_gate = jnp.concatenate(
        [
            flat(beside[..., out_rows : out_rows + in_rows, :]),
            flat(beside[..., out_rows + in_rows :, :]),
        ],
        axis=1,
    )
    gate = dot(normed_low, full_gate).astype(bf16)

    gathered_spec = full((groups, STATE, INNER))
    logs_spec = pl.BlockSpec((groups, EXTRA, INNER), lambda c: (0, STATE // EXTRA, 0))
    smem = pl.BlockSpec(memory_space=pltpu.SMEM)

    def gate_call(*refs):
        gate_kernel(groups, *refs)

    block, hidden, y, dy, dgate, dcc, ust, glocal, ng, h0 = pl.pallas_call(
        gate_call,
        grid=(chunks,),
        in_specs=[
            smem, by_chunk(INNER), by_chunk(INNER), by_chunk(2 * STATE), by_chunk(LANES),
            pl.BlockSpec((1, STATE, INNER), lambda c: (jnp.maximum(c - 1, 0), 0, 0)),
            gathered_spec, logs_spec, by_chunk(INNER), by_chunk(D), by_chunk(D),
            full((INNER, D)), full((2 * LANES, INNER)), full((8, INNER)),
        ],
        out_specs=[
            by_chunk(D), by_chunk(INNER), by_chunk(INNER), by_chunk(INNER), by_chunk(INNER),
            by_chunk(LANES), pl.BlockSpec((1, STATE, INNER), lambda c: (c, 0, 0)),
            full((STATE, INNER)), full((8, INNER)), full((STATE, INNER)),
        ],
        out_shape=[
            shape((count, D), f32), shape((count, INNER), bf16), shape((count, INNER), f32),
            shape((count, INNER), bf16), shape((count, INNER), bf16), shape((count, LANES), f32),
            shape((chunks, STATE, INNER), f32), shape((STATE, INNER), f32), shape((8, INNER), f32),
            shape((STATE, INNER), f32),
        ],
        scratch_shapes=[
            pltpu.VMEM((8, LANES), f32), pltpu.VMEM((STATE, INNER), f32),
            pltpu.VMEM((CHUNK, INNER), f32), pltpu.VMEM((CHUNK, INNER), f32),
            pltpu.VMEM((CHUNK, INNER), bf16),
        ],
        compiler_params=params(),
        cost_estimate=cost(30 * 10**9, 48 * 2**20),
        name="gate_norm",
    )(
        rank, y_within, x, bc, cum, hst, states, states, gate, tok_low, cot_low, full_out, spread,
        rows,
    )

    grads = lax.all_gather(glocal.astype(bf16), "seq", axis=0, tiled=False)

    def product(left, right):
        return lax.dot_general(left, right, TN, preferred_element_type=f32).astype(bf16)

    beside = jnp.concatenate(
        [
            blocks(product(hidden, cot_low), bits),
            blocks(product(normed_low, dgate[:, :D]), bits),
            blocks(product(normed_low, dgate[:, D:]), bits),
        ],
        axis=-2,
    )
    keep_b, give_b = split_pair(beside, cross + 2, core_axis, core_bit)
    got_b = swap(give_b, core_axis, core_bit)
    anywhere = pl.BlockSpec(memory_space=pl.ANY)

    def within_back_call(u, dy, bc, cum, cumt, sent, dxs_out, dbc_out):
        within_back_kernel(u, dy, bc, cum, cumt, dxs_out, dbc_out)

    dxs, dbc = pl.pallas_call(
        within_back_call,
        grid=(chunks,),
        in_specs=[
            by_chunk(INNER), by_chunk(INNER), by_chunk(2 * STATE), by_chunk(LANES),
            pl.BlockSpec((32, CHUNK), lambda c: (0, c)), anywhere,
        ],
        out_specs=[by_chunk(INNER), by_chunk(2 * STATE)],
        out_shape=[shape((count, INNER), f32), shape((count, 2 * STATE), f32)],
        compiler_params=params(),
        cost_estimate=cost(12 * 10**9, 16 * 2**20),
        name="within_back",
    )(u, dy, bc, cum, cumt, give_b)

    got_b, dxs, dbc = barrier((got_b, dxs, dbc))
    keep_b, give_b = split_pair(add_low(keep_b, got_b), cross + 1, y_axis, y_bit)
    got_b = swap(give_b, y_axis, y_bit)

    def back(width, height=CHUNK):
        return pl.BlockSpec((height, width), lambda c: (chunks - 1 - c, 0))

    def back_three(height):
        return pl.BlockSpec((1, height, INNER), lambda c: (chunks - 1 - c, 0, 0))

    def back_call(sent, *refs):
        back_kernel(groups, *refs)

    per = CHUNK // 16
    pg, first, tail, wg, hgr, skip = pl.pallas_call(
        back_call,
        grid=(chunks,),
        in_specs=[
            anywhere, smem, back(INNER), back(INNER), back(INNER), back(INNER), back(INNER), back(2 * STATE),
            back(2 * STATE), back(LANES), back(LANES), back(LANES), back_three(STATE),
            pl.BlockSpec((1, 8, LANES), lambda c: (chunks - 1 - c, 0, 0)),
            full((STATE, INNER)), gathered_spec, logs_spec, back_three(STATE), back(SIDE),
            pl.BlockSpec(
                (16, SIDE), lambda c: (jnp.maximum((chunks - 1 - c) * per - 1, 0), 0)
            ),
            full((16, XBC)), full((8, XBC)), full((8, LANES)), full((2 * LANES, INNER)),
            full((2 * INNER, LANES)), full((8, INNER)),
        ],
        out_specs=[
            back(SIDE), full((8, XBC)), full((8, XBC)), full((40, XBC)), full((16, LANES)),
            full((8, INNER)),
        ],
        out_shape=[
            shape((count, SIDE), bf16), shape((8, XBC), f32), shape((8, XBC), f32),
            shape((40, XBC), f32), shape((16, LANES), f32), shape((8, INNER), f32),
        ],
        scratch_shapes=[
            pltpu.VMEM((STATE, INNER), f32), pltpu.VMEM((CHUNK + 8, XBC), f32),
            pltpu.VMEM((CHUNK + 8, XBC), f32), pltpu.VMEM((CHUNK, INNER), bf16),
            pltpu.VMEM((2 * CHUNK + 16, 2 * INNER), bf16),
        ],
        compiler_params=params(),
        cost_estimate=cost(47 * 10**9, 48 * 2**20),
        name="mixer_back",
    )(
        give_b, rank, dxs, dy, x, u, y, bc, dbc, dcc, cum, dt, hst, pfx, h0, grads, states, ust, proj, proj,
        halo, convp, headp, spread, collect, rows,
    )

    got_b, pg, first, tail, wg, hgr, skip = barrier((got_b, pg, first, tail, wg, hgr, skip))
    keep_b, give_b = split_pair(add_low(keep_b, got_b), cross, x_axis, x_bit)
    got_b = swap(give_b, x_axis, x_bit)
    after = lax.ppermute(first, "seq", backward)
    fixes = [jnp.zeros((5, XBC), f32)]
    for m in range(CONV - 1):
        fix = convp[0] * after[m]
        for k in range(1, m + 1):
            fix = fix + convp[k] * after[m - k]
        fixes.append(fix[None, :])
    tail_low = (tail + jnp.concatenate(fixes, axis=0)).astype(bf16)
    pg = lax.dynamic_update_slice(pg, tail_low, (count - 8, 0))

    left = blocks(product(normed_low, pg[:, :half]), bits)
    right = blocks(product(normed_low, pg[:, half:]), bits)
    keep_l, give_l = split_pair(left, cross + 2, core_axis, core_bit)
    keep_r, give_r = split_pair(right, cross + 2, core_axis, core_bit)
    got_l, got_r = swap(give_l, core_axis, core_bit), swap(give_r, core_axis, core_bit)
    pg, dgate, _, _ = barrier((pg, dgate, give_l, give_r))
    normed_grad = lax.dot_general(dgate, full_gate, NT, preferred_element_type=f32)
    normed_grad = normed_grad + lax.dot_general(pg, full_side, NT, preferred_element_type=f32)
    got_l, got_r, got_b, normed_grad = barrier((got_l, got_r, got_b, normed_grad))
    keep_l, give_l = split_pair(add_low(keep_l, got_l), cross + 1, y_axis, y_bit)
    keep_r, give_r = split_pair(add_low(keep_r, got_r), cross, x_axis, x_bit)
    got_l, got_r = swap(give_l, y_axis, y_bit), swap(give_r, x_axis, x_bit)
    beside = scatter_pairs(add_low(keep_b, got_b), bits[early:cross], early)
    normed_grad, _, _ = barrier((normed_grad, give_l, give_r))
    _, norm_pull = jax.vjp(pre_norm, tok_vals, pre_gain)
    tok_norm_grad, pre_gain_grad = norm_pull(normed_grad)
    token_grad = (cot_low.astype(f32) + tok_norm_grad)[None]
    got_l, got_r, beside, token_grad, pre_gain_grad = barrier(
        (got_l, got_r, beside, token_grad, pre_gain_grad)
    )
    wg_sum = jnp.sum(wg.reshape(5, 8, XBC), axis=1)
    chan_grad = jnp.concatenate(
        [
            pre_gain_grad,
            jnp.sum(ng, axis=0),
            wg_sum[:CONV].T.reshape(-1),
            wg_sum[CONV],
            jnp.sum(hgr[:8, :HEADS], axis=0),
            jnp.sum(hgr[8:, :HEADS], axis=0),
            jnp.sum(skip.reshape(8, HEADS, HEADDIM), axis=(0, 2)),
        ]
    )

    def together(side_got, beside, chan):
        return barrier((side_got, beside, chan))

    keep_l, give_l = split_pair(add_low(keep_l, got_l), cross, x_axis, x_bit)
    keep_r, give_r = split_pair(add_low(keep_r, got_r), cross, y_axis, y_bit)
    got_l, got_r = swap(give_l, x_axis, x_bit), swap(give_r, y_axis, y_bit)
    beside = scatter_pairs(beside, bits[:early])
    chan_grad = sum_pairs(chan_grad, bits[cross + 2 :])
    (got_l, got_r), beside, chan_grad = together((got_l, got_r), beside, chan_grad)
    side = jnp.concatenate([add_low(keep_l, got_l), add_low(keep_r, got_r)], axis=-1)
    sums = [bits[:early], bits[early:cross], bits[cross : cross + 1], bits[cross + 1 : cross + 2]]
    side = scatter_pairs(side, bits[early:cross], early)
    beside = gather_step(beside, 0, y_axis, y_bit)
    chan_grad = sum_pairs(chan_grad, sums[0])
    side, beside, chan_grad = together(side, beside, chan_grad)
    side = scatter_pairs(side, bits[:early])
    beside = gather_step(beside, 1, core_axis, core_bit)
    chan_grad = sum_pairs(chan_grad, sums[1])
    side, beside, chan_grad = together(side, beside, chan_grad)
    got = swap(side, y_axis, y_bit)
    chan_grad = sum_pairs(chan_grad, sums[2])
    got, chan_grad = barrier((got, chan_grad))
    side = merge_pair(side, got, 0, y_axis, y_bit)
    got = swap(side, core_axis, core_bit)
    chan_grad = sum_pairs(chan_grad, sums[3])
    side = flat(merge_pair(side, got, 1, core_axis, core_bit))

    beside = beside.astype(f32)
    out_grad = flat(beside[..., :out_rows, :])
    in_grad = jnp.concatenate(
        [
            flat(beside[..., out_rows : out_rows + in_rows, :]),
            flat(beside[..., out_rows + in_rows :, :]),
            side[:, : PROJ - INNER].astype(f32),
        ],
        axis=1,
    )
    in_new, in_mom, in_sec = adamw_step(
        in_weight, in_moment, in_second, in_grad, rate_matrix, decay_matrix
    )
    out_new, out_mom, out_sec = adamw_step(
        out_weight, out_moment, out_second, out_grad, rate_matrix, decay_matrix
    )
    chan_new, chan_mom, chan_sec = adamw_step(
        channels, channel_moment, channel_second, chan_grad, rate_channel, 0.0
    )
    return (
        block[None],
        token_grad,
        in_new,
        in_mom,
        in_sec,
        out_new,
        out_mom,
        out_sec,
        chan_new,
        chan_mom,
        chan_sec,
    )


def solution(mesh):
    acts = P("dp", "seq", None)
    rows = P("dp", None)
    specs = (acts, acts) + (rows,) * 6 + (P(),) * 3
    return jax.shard_map(local, mesh=mesh, in_specs=specs, out_specs=specs, check_vma=False)
```

```python
import math

import jax
import jax.numpy as jnp
from jax import lax
from jax.experimental import pallas as pl
from jax.experimental.pallas import tpu as pltpu
from jax.sharding import PartitionSpec as P

D = 768
HEADS = 24
HEADDIM = 64
STATE = 128
CONV = 4
STEP = 10
INNER = 1536
XBC = 1792
PROJ = 3352
SIDE = 1920
LANES = 128
CHUNK = 128
ROWS = 32
PAIRS = HEADS // 2
TILES = XBC // LANES
EXTRA = 16

norm_eps = 1e-05
beta_one = 0.9
beta_two = 0.999
adam_eps = 1e-08
rate_matrix = 0.1
rate_channel = 0.5
decay_matrix = 0.1
LOG2E = 1.0 / math.log(2.0)
VMEM = 56 * 1024 * 1024

f32 = jnp.float32
bf16 = jnp.bfloat16
NT = (((1,), (1,)), ((), ()))
TN = (((0,), (0,)), ((), ()))


def dot(a, b):
    return jnp.dot(a, b, preferred_element_type=f32)


def dot_nt(a, b):
    return lax.dot_general(a, b, NT, preferred_element_type=f32)


def dot_tn(a, b):
    return lax.dot_general(a, b, TN, preferred_element_type=f32)


def sigmoid(v):
    return 0.5 * jnp.tanh(0.5 * v) + 0.5


def halves(v):
    high = v.astype(bf16)
    return high, (v - high.astype(f32)).astype(bf16)


def running(mask, v):
    high, rest = halves(v)
    left = (v - high.astype(f32) - rest.astype(f32)).astype(bf16)
    parts = dot(jnp.where(mask, 1.0, 0.0).astype(bf16), jnp.concatenate([high, rest, left], axis=1))
    return parts[:, :LANES] + parts[:, LANES : 2 * LANES] + parts[:, 2 * LANES :]


def expand(v, spread):
    high, rest = halves(v)
    return dot(jnp.concatenate([high, rest], axis=1), spread)


def fold(v):
    return jnp.sum(v.reshape(v.shape[0] // 8, 8, v.shape[1]), axis=0)


def lane(i):
    return slice(i * LANES, (i + 1) * LANES)


def iota(shape, dim):
    return lax.broadcasted_iota(jnp.int32, shape, dim)


def tri(lower):
    rows, cols = iota((CHUNK, CHUNK), 0), iota((CHUNK, CHUNK), 1)
    return (rows >= cols) if lower else (rows <= cols)


def conv_rows(convp, tile):
    return [jnp.broadcast_to(convp[k : k + 1, lane(tile)], (ROWS, LANES)) for k in range(CONV + 1)]


def conv_pre(ext, weights, tile, start):
    cols = lane(tile)
    taps = [ext[5 + k + start : 5 + k + start + ROWS, cols] for k in range(CONV)]
    pre = taps[0] * weights[0] + weights[CONV]
    for k in range(1, CONV):
        pre = pre + taps[k] * weights[k]
    return pre, taps


def pieces():
    return [(start, slice(start, start + ROWS)) for start in range(0, CHUNK, ROWS)]


def pair_stack(v):
    side = iota(v.shape, 1) < HEADDIM
    zero = jnp.zeros_like(v)
    return jnp.concatenate([jnp.where(side, v, zero), jnp.where(side, zero, v)], axis=0)


def conv_state_kernel(
    proj, halo, convp, headp, spread, x_out, bc_out, u_out, cum_out, cumt_out, dt_out, hst_out,
    pfx_out, send_out, ext, state, scaled, total,
):
    step = pl.program_id(0)

    @pl.when(step == 0)
    def _():
        ext[0:8, :] = halo[8:16, :].astype(f32)
        state[...] = jnp.zeros_like(state)
        total[...] = jnp.zeros_like(total)

    @pl.when(step > 0)
    def _():
        ext[0:8, :] = ext[CHUNK : CHUNK + 8, :]

    ext[8:, :] = proj[:, :XBC].astype(f32)
    raw = proj[:, XBC:].astype(f32) + headp[0:1, :]
    steps = jnp.maximum(raw, 0.0) + jnp.log1p(jnp.exp(-jnp.abs(raw)))
    log_decay = steps * (headp[1:2, :] * (-LOG2E))
    cum = running(tri(True), log_decay)
    cum_out[...] = cum
    cumt_out[...] = jnp.transpose(cum)[0:32, :]
    dt_out[...] = steps
    last = cum[CHUNK - 1 : CHUNK, :]
    decayed = jnp.broadcast_to(jnp.exp2(last), (8, LANES))
    wide = expand(jnp.concatenate([steps, jnp.exp2(last - cum), decayed], axis=0), spread[...])
    steps_wide, tail_wide = wide[:CHUNK], wide[CHUNK : 2 * CHUNK]
    decay = wide[2 * CHUNK : 2 * CHUNK + 1]
    for tile in range(TILES):
        cols = lane(tile)
        weights = conv_rows(convp, tile)
        for start, part in pieces():
            pre, _ = conv_pre(ext, weights, tile, start)
            value = (pre * sigmoid(pre)).astype(bf16)
            if tile < PAIRS:
                x_out[part, cols] = value
                u = (value.astype(f32) * steps_wide[part, cols]).astype(bf16)
                u_out[part, cols] = u
                scaled[part, cols] = (u.astype(f32) * tail_wide[part, cols]).astype(bf16)
            else:
                bc_out[part, lane(tile - PAIRS)] = value
    new_state = state[...] * decay + dot_tn(bc_out[:, :STATE], scaled[...])
    state[...] = new_state
    hst_out[0] = new_state
    new_total = total[...] + jnp.broadcast_to(last, (8, LANES))
    total[...] = new_total
    pfx_out[0] = new_total

    @pl.when(step == pl.num_programs(0) - 1)
    def _():
        send_out[:STATE, :] = new_state.astype(bf16)
        row = iota((EXTRA, LANES), 0)
        wide = jnp.broadcast_to(new_total[0:1, :], (EXTRA, LANES))
        high, rest = halves(wide)
        left = (wide - high.astype(f32) - rest.astype(f32)).astype(bf16)
        parts = jnp.where(
            row == 0,
            high.astype(f32),
            jnp.where(row == 1, rest.astype(f32), jnp.where(row == 2, left.astype(f32), 0.0)),
        )
        send_out[STATE:, :] = dot(parts.astype(bf16), spread[:LANES, :]).astype(bf16)


def within_kernel(u, bc, cum, cumt, y_out, weights):
    scores = jnp.where(tri(True), dot_nt(bc[:, STATE:], bc[:, :STATE]), 0.0)
    for _, part in pieces():
        rows_cum = cum[part, :]
        rows_scores = scores[part]
        for head in range(HEADS):
            gap = rows_cum[:, head : head + 1] - cumt[head : head + 1, :]
            weights[part, lane(head)] = (jnp.exp2(jnp.minimum(gap, 0.0)) * rows_scores).astype(bf16)
    for pair in range(PAIRS):
        both = slice(2 * pair * LANES, 2 * (pair + 1) * LANES)
        y_out[:, lane(pair)] = dot(weights[:, both], pair_stack(u[:, lane(pair)]))


def arrived(gathered, logs, rank, groups, later):
    sums = [
        jnp.sum(logs[g].astype(f32), axis=0, keepdims=True) for g in range(groups)
    ]
    entered = jnp.zeros((STATE, INNER), f32)
    for g in range(groups):
        between = jnp.zeros((1, INNER), f32)
        for s in range(groups):
            if (s < g) if later else (s > g):
                inside = (s > rank) if later else (s < rank)
                between = between + jnp.where(inside, sums[s], 0.0)
        counts = (g > rank) if later else (g < rank)
        weight = jnp.where(counts, jnp.exp2(between), 0.0)
        entered = entered + gathered[g].astype(f32) * weight
    return entered


def gate_kernel(
    groups, rank, y_in, x, bc, cum, hst, gathered, logs, gate, tok, cot, wout, spread, rows,
    block_out, hidden_out, y_out, dy_out, dgate_out, dcc_out, ust_out, glocal_out, ng_out, h0_out,
    prefix, h0, hg_all, mixed_all, dy_scaled,
):
    step = pl.program_id(0)

    @pl.when(step == 0)
    def _():
        value = arrived(gathered, logs, rank[0], groups, False)
        h0[...] = value
        h0_out[...] = value
        prefix[...] = jnp.zeros_like(prefix)
        glocal_out[...] = jnp.zeros_like(glocal_out)
        ng_out[...] = jnp.zeros_like(ng_out)

    wide = expand(jnp.exp2(jnp.concatenate([cum[...], prefix[...]], axis=0)), spread[...])
    grown, start = wide[:CHUNK], wide[CHUNK : CHUNK + 1]
    state = h0[...] * start + jnp.where(step > 0, hst[0], 0.0)
    state_low = state.astype(bf16)
    carried = dot(bc[:, STATE:], state_low)
    hg_all[...] = dot_nt(cot[...], wout[...])
    gain, skip = rows[0:1, :], rows[1:2, :]
    for _, part in pieces():
        squares = jnp.zeros((ROWS, LANES), f32)
        cross = jnp.zeros((ROWS, LANES), f32)
        for tile in range(PAIRS):
            cols = lane(tile)
            y = y_in[part, cols] + carried[part, cols] * grown[part, cols]
            y_out[part, cols] = y
            mixed = (y + skip[:, cols] * x[part, cols].astype(f32)).astype(bf16)
            mixed_all[part, cols] = mixed
            gate_val = gate[part, cols].astype(f32)
            gated = mixed.astype(f32) * (gate_val * sigmoid(gate_val))
            squares = squares + gated * gated
            cross = cross + gated * (hg_all[part, cols] * gain[:, cols])
        mean = jnp.sum(squares, axis=1, keepdims=True) * (1.0 / INNER)
        scale = lax.rsqrt(mean + norm_eps)
        cross_mean = jnp.sum(cross, axis=1, keepdims=True) * (1.0 / INNER) * scale * scale * scale
        scale = jnp.broadcast_to(scale, (ROWS, LANES))
        cross_mean = jnp.broadcast_to(cross_mean, (ROWS, LANES))
        for tile in range(PAIRS):
            cols = lane(tile)
            gate_val = gate[part, cols].astype(f32)
            sig = sigmoid(gate_val)
            silu = gate_val * sig
            mixed = mixed_all[part, cols].astype(f32)
            gated = mixed * silu
            normal = gated * scale
            hidden_out[part, cols] = (normal * gain[:, cols]).astype(bf16)
            grad = hg_all[part, cols]
            ng_out[:, cols] += fold(grad * normal)
            dgated = grad * gain[:, cols] * scale - gated * cross_mean
            dgate_out[part, cols] = (dgated * mixed * (sig + silu * (1.0 - sig))).astype(bf16)
            dy = (dgated * silu).astype(bf16)
            dy_out[part, cols] = dy
            dy_scaled[part, cols] = (dy.astype(f32) * grown[part, cols]).astype(bf16)
    block_out[...] = tok[...].astype(f32) + dot(hidden_out[...], wout[...])
    update = dot_tn(bc[:, STATE:], dy_scaled[...])
    ust_out[0] = update
    glocal_out[...] += update * start
    dcc_out[...] = dot_nt(dy_scaled[...], state_low)
    prefix[...] += jnp.broadcast_to(cum[CHUNK - 1 : CHUNK, :], (8, LANES))


def within_back_kernel(u, dy, bc, cum, cumt, dxs_out, dbc_out, weights, products, low):
    upper = tri(False)
    scores = jnp.where(upper, dot_nt(bc[:, :STATE], bc[:, STATE:]), 0.0)
    for pair in range(PAIRS):
        both = slice(2 * pair * LANES, 2 * (pair + 1) * LANES)
        products[:, both] = dot_nt(u[:, lane(pair)], pair_stack(dy[:, lane(pair)]))
    for _, part in pieces():
        rows_cum = cum[part, :]
        rows_scores = scores[part]
        total = jnp.zeros((ROWS, LANES), f32)
        for head in range(HEADS):
            gap = cumt[head : head + 1, :] - rows_cum[:, head : head + 1]
            decay = jnp.exp2(jnp.minimum(gap, 0.0))
            weights[part, lane(head)] = (decay * rows_scores).astype(bf16)
            total = total + decay * products[part, lane(head)]
        low[part, :] = jnp.where(upper[part], total, 0.0).astype(bf16)
    for pair in range(PAIRS):
        both = slice(2 * pair * LANES, 2 * (pair + 1) * LANES)
        dxs_out[:, lane(pair)] = dot(weights[:, both], pair_stack(dy[:, lane(pair)]))
    dbc_out[:, :STATE] = dot(low[...], bc[:, STATE:])
    dbc_out[:, STATE:] = dot_tn(low[...], bc[:, :STATE])


def back_kernel(
    groups, rank, dxs, dy, x, u, y, bc, dbc, dcc, cum, dt, hst, pfx, h0, gathered, logs, ust, proj,
    before, halo, convp, headp, spread, collect, rows,
    pg_out, first_out, tail_out, wg_out, hg_out, skip_out,
    gstate, ext, dext, scaled, prod,
):
    step = pl.program_id(0)
    chunk = pl.num_programs(0) - 1 - step

    @pl.when(step == 0)
    def _():
        gstate[...] = arrived(gathered, logs, rank[0], groups, True)
        dext[CHUNK:, :] = jnp.zeros((8, XBC), f32)
        wg_out[...] = jnp.zeros_like(wg_out)
        hg_out[...] = jnp.zeros_like(hg_out)
        skip_out[...] = jnp.zeros_like(skip_out)

    @pl.when(step > 0)
    def _():
        dext[CHUNK:, :] = dext[0:8, :]

    @pl.when(chunk == 0)
    def _():
        ext[0:8, :] = halo[8:16, :].astype(f32)

    @pl.when(chunk > 0)
    def _():
        ext[0:8, :] = before[8:16, :XBC].astype(f32)

    ext[8:, :] = proj[:, :XBC].astype(f32)
    grad_state = gstate[...]
    grad_low = grad_state.astype(bf16)
    last = cum[CHUNK - 1 : CHUNK, :]
    decayed = jnp.broadcast_to(jnp.exp2(last), (8, LANES))
    wide = expand(
        jnp.concatenate([jnp.exp2(last - cum[...]), dt[...], decayed, jnp.exp2(pfx[0])], axis=0),
        spread[...],
    )
    tail_wide, steps_wide = wide[:CHUNK], wide[CHUNK : 2 * CHUNK]
    decay = wide[2 * CHUNK : 2 * CHUNK + 1]
    end = wide[2 * CHUNK + 8 : 2 * CHUNK + 9]
    reach = dot(bc[:, :STATE], grad_low)

    def conv_back(tile, grad_of):
        cols = lane(tile)
        weights = conv_rows(convp, tile)
        sums = [jnp.zeros((8, LANES), f32) for _ in range(CONV + 1)]
        for start, part in reversed(pieces()):
            grad = grad_of(part)
            pre, taps = conv_pre(ext, weights, tile, start)
            sig = sigmoid(pre)
            dpre = grad * (sig + pre * sig * (1.0 - sig))
            dext[part, cols] = dpre
            sums = [total + fold(dpre * tap) for total, tap in zip(sums, taps)] + [
                sums[CONV] + fold(dpre)
            ]
            source = dpre * weights[3]
            for k in range(CONV - 1):
                source = source + dext[start + 3 - k : start + 3 - k + ROWS, cols] * weights[k]
            pg_out[part, cols] = source.astype(bf16)
            if start + ROWS == CHUNK:

                @pl.when(step == 0)
                def _():
                    tail_out[:, cols] = source[ROWS - 8 :, :]

        for k in range(CONV + 1):
            wg_out[8 * k : 8 * k + 8, cols] += sums[k]

    for tile in range(PAIRS):
        cols = lane(tile)
        rest_cols = slice(INNER + tile * LANES, INNER + (tile + 1) * LANES)
        skip_row = jnp.broadcast_to(rows[1:2, cols], (ROWS, LANES))
        skips = []

        def grad_of(part, cols=cols, rest_cols=rest_cols, skip_row=skip_row, skips=skips):
            below = slice(CHUNK + part.start, CHUNK + part.stop)
            dxs_full = dxs[part, cols] + tail_wide[part, cols] * reach[part, cols]
            uf = u[part, cols].astype(f32)
            dyf = dy[part, cols].astype(f32)
            scaled[part, cols] = (uf * tail_wide[part, cols]).astype(bf16)
            q = uf * dxs_full
            prod[part, cols], prod[part, rest_cols] = halves(q)
            prod[below, cols], prod[below, rest_cols] = halves(dyf * y[part, cols] - q)
            skips.append(fold(dyf * x[part, cols].astype(f32)))
            return skip_row * dyf + steps_wide[part, cols] * dxs_full

        conv_back(tile, grad_of)
        skip_out[:, cols] += sum(skips[1:], skips[0])
    dwrite = dot_nt(scaled[...], grad_low)
    conv_back(PAIRS, lambda part: dbc[part, :STATE] + dwrite[part])
    conv_back(PAIRS + 1, lambda part: dbc[part, STATE:] + dcc[part, :])
    first_out[...] = dext[0:8, :]

    meet = fold(grad_state * (hst[0] + h0[...] * end))
    meet = jnp.concatenate([meet, jnp.zeros_like(meet)], axis=0)
    high, rest = halves(meet)
    prod[2 * CHUNK :, :INNER] = high
    prod[2 * CHUNK :, INNER:] = rest
    heads = dot(prod[...], collect[...])
    q_heads, gap_heads = heads[:CHUNK], heads[CHUNK : 2 * CHUNK]
    meet_heads = jnp.sum(heads[2 * CHUNK :], axis=0, keepdims=True)
    dlog = running(tri(False), gap_heads) + meet_heads
    sig = sigmoid(proj[:, XBC:].astype(f32) + headp[0:1, :])
    steps = dt[...]
    ratio = jnp.where(steps > 1e-30, sig / jnp.maximum(steps, 1e-30), 1.0)
    raw_grad = q_heads * ratio - dlog * headp[1:2, :] * sig
    pg_out[:, XBC:] = raw_grad.astype(bf16)
    hg_out[0:8, :] += fold(raw_grad)
    hg_out[8:16, :] += fold(dlog * steps * headp[1:2, :]) * (-1.0)
    gstate[...] = grad_state * decay + ust[0]


def swap(v, axis, bit):
    size = lax.axis_size(axis)
    return lax.ppermute(v, axis, [(i, i ^ (1 << bit)) for i in range(size)])


def mesh_bits():
    found = []
    for axis in ("dp", "seq"):
        for bit in reversed(range(lax.axis_size(axis).bit_length() - 1)):
            found.append((axis, bit))
    return found


def mine(axis, bit):
    return (lax.axis_index(axis) >> bit) & 1


def merge_pair(v, other, place, axis, bit):
    second = mine(axis, bit) == 1
    return jnp.stack([jnp.where(second, other, v), jnp.where(second, v, other)], axis=place)


def gather_step(v, place, axis, bit):
    return merge_pair(v, swap(v, axis, bit), place, axis, bit)


def gather_pairs(v, bits, lead=0):
    for place, (axis, bit) in enumerate(bits):
        v = gather_step(v, lead + place, axis, bit)
    return v


def flat(v):
    return v.reshape(-1, v.shape[-1])


def blocks(v, bits):
    return v.reshape((2,) * len(bits) + (v.shape[0] >> len(bits), v.shape[1]))


def split_pair(v, place, axis, bit):
    own = mine(axis, bit)
    keep = lax.dynamic_index_in_dim(v, own, place, keepdims=False)
    give = lax.dynamic_index_in_dim(v, 1 - own, place, keepdims=False)
    return keep, give


def add_low(keep, got):
    return (keep.astype(f32) + got.astype(f32)).astype(keep.dtype)


def scatter_step(v, place, axis, bit):
    keep, give = split_pair(v, place, axis, bit)
    return add_low(keep, swap(give, axis, bit))


def scatter_pairs(v, bits, lead=0):
    for place in reversed(range(len(bits))):
        v = scatter_step(v, lead + place, *bits[place])
    return v


def sum_pairs(v, bits):
    for axis, bit in bits:
        v = v + swap(v, axis, bit)
    return v


def full(shape):
    return pl.BlockSpec(shape, lambda c: (0,) * len(shape))


def by_chunk(width, rows=CHUNK):
    return pl.BlockSpec((rows, width), lambda c: (c, 0))


def shape(dims, dtype):
    return jax.ShapeDtypeStruct(dims, dtype)


def params():
    return pltpu.CompilerParams(dimension_semantics=("arbitrary",), vmem_limit_bytes=VMEM)


def cost(flops, moved):
    return pl.CostEstimate(flops=flops, bytes_accessed=moved, transcendentals=0)


def spread_map():
    heads = jnp.arange(LANES)[:, None]
    cols = jnp.arange(INNER)[None, :] // HEADDIM
    once = (heads == cols).astype(bf16)
    return jnp.concatenate([once, once], axis=0)


def unpack_channels(channels):
    pieces = []
    offset = 0
    for piece_len in (D, INNER, XBC * CONV, XBC, HEADS, HEADS, HEADS):
        pieces.append(channels[offset : offset + piece_len])
        offset = offset + piece_len
    pre_gain, norm_gain, conv_flat, conv_bias, step_bias, rate_log, skip_gain = pieces
    return (
        pre_gain,
        norm_gain,
        conv_flat.reshape(XBC, CONV),
        conv_bias,
        step_bias,
        rate_log,
        skip_gain,
    )


def pre_norm(tok_vals, pre_gain):
    return (
        tok_vals * lax.rsqrt(jnp.mean(tok_vals * tok_vals, -1, keepdims=True) + norm_eps) * pre_gain
    )


def adamw_step(weight, moment, second, gradient, step_rate, decay_rate):
    moment_next = beta_one * moment + (1.0 - beta_one) * gradient
    second_next = beta_two * second + (1.0 - beta_two) * gradient * gradient
    first_fix = 1.0 - beta_one**STEP
    second_fix = 1.0 - beta_two**STEP
    update = moment_next / first_fix / (jnp.sqrt(second_next / second_fix) + adam_eps)
    return (weight - step_rate * (update + decay_rate * weight), moment_next, second_next)


def local(
    tokens,
    cotangent,
    in_weight,
    in_moment,
    in_second,
    out_weight,
    out_moment,
    out_second,
    channels,
    channel_moment,
    channel_second,
):
    groups = lax.axis_size("seq")
    bits = mesh_bits()
    seq_bits = [(axis, bit) for axis, bit in bits if axis == "seq"]
    seq_rank = lax.axis_index("seq")
    rank = seq_rank.astype(jnp.int32).reshape(1)
    pre_gain, norm_gain, conv_weight, conv_bias, step_bias, rate_log, skip_gain = unpack_channels(
        channels
    )
    tok_low = tokens[0]
    cot_low = cotangent[0]
    count = tok_low.shape[0]
    chunks = count // CHUNK

    def quarter(weight):
        size = weight.shape[0] // groups
        return lax.dynamic_slice_in_dim(weight, seq_rank * size, size, 0).astype(bf16)

    in_part = quarter(in_weight)
    side_part = jnp.pad(in_part[:, INNER:], ((0, 0), (0, SIDE + INNER - PROJ)))
    out_rows = out_weight.shape[0] // groups
    in_rows = in_weight.shape[0] // groups
    beside = jnp.concatenate(
        [quarter(out_weight), in_part[:, :D], in_part[:, D:INNER]], axis=0
    )
    barrier = lax.optimization_barrier
    cross = len(bits) - 3
    (x_axis, x_bit), (y_axis, y_bit), (core_axis, core_bit) = bits[cross:]
    side = gather_pairs(side_part, bits[:cross])
    side, beside = barrier((side, beside))
    half = SIDE // 256 * 128
    left, right = side[..., :half], side[..., half:]
    got_l, got_r = swap(left, x_axis, x_bit), swap(right, y_axis, y_bit)
    early = cross // 2
    beside = gather_pairs(beside, bits[:early])
    left = merge_pair(left, got_l, cross, x_axis, x_bit)
    right = merge_pair(right, got_r, cross, y_axis, y_bit)
    got_l, got_r = swap(left, y_axis, y_bit), swap(right, x_axis, x_bit)
    beside, left, right = barrier((beside, left, right))
    beside = gather_pairs(beside, bits[early:cross], early)
    left = merge_pair(left, got_l, cross + 1, y_axis, y_bit)
    right = merge_pair(right, got_r, cross, x_axis, x_bit)
    got_l, got_r = swap(left, core_axis, core_bit), swap(right, core_axis, core_bit)
    beside, left, right = barrier((beside, left, right))
    got_b = swap(beside, x_axis, x_bit)
    left = merge_pair(left, got_l, cross + 2, core_axis, core_bit)
    right = merge_pair(right, got_r, cross + 2, core_axis, core_bit)
    full_side = jnp.concatenate([flat(left), flat(right)], axis=1)

    forward = [(s, s + 1) for s in range(groups - 1)]
    backward = [(s + 1, s) for s in range(groups - 1)]
    tok_halo = lax.ppermute(tok_low[count - 16 :], "seq", forward)
    halo_norm = pre_norm(tok_halo.astype(f32), pre_gain).astype(bf16)
    tok_vals = tok_low.astype(f32)
    normed_low = pre_norm(tok_vals, pre_gain).astype(bf16)

    convp = jnp.concatenate(
        [conv_weight.T, conv_bias[None, :], jnp.zeros((3, XBC), f32)], axis=0
    )
    pad_heads = lambda v: jnp.pad(v, (0, LANES - HEADS))[None, :]
    headp = jnp.concatenate(
        [pad_heads(step_bias), pad_heads(jnp.exp(rate_log)), jnp.zeros((6, LANES), f32)], axis=0
    )
    rows = jnp.concatenate(
        [norm_gain[None, :], jnp.repeat(skip_gain, HEADDIM)[None, :], jnp.zeros((6, INNER), f32)],
        axis=0,
    )
    spread = spread_map()
    collect = jnp.concatenate([spread[:LANES].T, spread[:LANES].T], axis=0)

    proj = dot(normed_low, full_side).astype(bf16)
    halo = dot(halo_norm, full_side[:, :XBC]).astype(bf16)
    proj, halo, got_b = barrier((proj, halo, got_b))
    beside = merge_pair(beside, got_b, cross, x_axis, x_bit)
    got_b = swap(beside, y_axis, y_bit)

    x, bc, u, cum, cumt, dt, hst, pfx, send = pl.pallas_call(
        conv_state_kernel,
        grid=(chunks,),
        in_specs=[
            by_chunk(SIDE), full((16, XBC)), full((8, XBC)), full((8, LANES)),
            full((2 * LANES, INNER)),
        ],
        out_specs=[
            by_chunk(INNER), by_chunk(2 * STATE), by_chunk(INNER), by_chunk(LANES),
            pl.BlockSpec((32, CHUNK), lambda c: (0, c)), by_chunk(LANES),
            pl.BlockSpec((1, STATE, INNER), lambda c: (c, 0, 0)),
            pl.BlockSpec((1, 8, LANES), lambda c: (c, 0, 0)),
            full((STATE + EXTRA, INNER)),
        ],
        out_shape=[
            shape((count, INNER), bf16), shape((count, 2 * STATE), bf16),
            shape((count, INNER), bf16), shape((count, LANES), f32), shape((32, count), f32),
            shape((count, LANES), f32), shape((chunks, STATE, INNER), f32),
            shape((chunks, 8, LANES), f32), shape((STATE + EXTRA, INNER), bf16),
        ],
        scratch_shapes=[
            pltpu.VMEM((CHUNK + 8, XBC), f32), pltpu.VMEM((STATE, INNER), f32),
            pltpu.VMEM((CHUNK, INNER), bf16), pltpu.VMEM((8, LANES), f32),
        ],
        compiler_params=params(),
        cost_estimate=cost(24 * 10**9, 24 * 2**20),
        name="conv_state",
    )(proj, halo, convp, headp, spread)

    states = lax.all_gather(send, "seq", axis=0, tiled=False)
    x, bc, u, cum, cumt, dt, hst, pfx, got_b = barrier(
        (x, bc, u, cum, cumt, dt, hst, pfx, got_b)
    )
    beside = merge_pair(beside, got_b, cross + 1, y_axis, y_bit)
    got_b = swap(beside, core_axis, core_bit)

    y_within = pl.pallas_call(
        within_kernel,
        grid=(chunks,),
        in_specs=[
            by_chunk(INNER), by_chunk(2 * STATE), by_chunk(LANES),
            pl.BlockSpec((32, CHUNK), lambda c: (0, c)),
        ],
        out_specs=by_chunk(INNER),
        out_shape=shape((count, INNER), f32),
        scratch_shapes=[pltpu.VMEM((CHUNK, HEADS * LANES), bf16)],
        compiler_params=params(),
        cost_estimate=cost(11 * 10**9, 16 * 2**20),
        name="within",
    )(u, bc, cum, cumt)
    y_within, got_b = barrier((y_within, got_b))
    beside = merge_pair(beside, got_b, cross + 2, core_axis, core_bit)
    full_out = flat(beside[..., :out_rows, :])
    full_gate = jnp.concatenate(
        [
            flat(beside[..., out_rows : out_rows + in_rows, :]),
            flat(beside[..., out_rows + in_rows :, :]),
        ],
        axis=1,
    )
    gate = dot(normed_low, full_gate).astype(bf16)

    gathered_spec = full((groups, STATE, INNER))
    logs_spec = pl.BlockSpec((groups, EXTRA, INNER), lambda c: (0, STATE // EXTRA, 0))
    smem = pl.BlockSpec(memory_space=pltpu.SMEM)

    def gate_call(*refs):
        gate_kernel(groups, *refs)

    block, hidden, y, dy, dgate, dcc, ust, glocal, ng, h0 = pl.pallas_call(
        gate_call,
        grid=(chunks,),
        in_specs=[
            smem, by_chunk(INNER), by_chunk(INNER), by_chunk(2 * STATE), by_chunk(LANES),
            pl.BlockSpec((1, STATE, INNER), lambda c: (jnp.maximum(c - 1, 0), 0, 0)),
            gathered_spec, logs_spec, by_chunk(INNER), by_chunk(D), by_chunk(D),
            full((INNER, D)), full((2 * LANES, INNER)), full((8, INNER)),
        ],
        out_specs=[
            by_chunk(D), by_chunk(INNER), by_chunk(INNER), by_chunk(INNER), by_chunk(INNER),
            by_chunk(LANES), pl.BlockSpec((1, STATE, INNER), lambda c: (c, 0, 0)),
            full((STATE, INNER)), full((8, INNER)), full((STATE, INNER)),
        ],
        out_shape=[
            shape((count, D), f32), shape((count, INNER), bf16), shape((count, INNER), f32),
            shape((count, INNER), bf16), shape((count, INNER), bf16), shape((count, LANES), f32),
            shape((chunks, STATE, INNER), f32), shape((STATE, INNER), f32), shape((8, INNER), f32),
            shape((STATE, INNER), f32),
        ],
        scratch_shapes=[
            pltpu.VMEM((8, LANES), f32), pltpu.VMEM((STATE, INNER), f32),
            pltpu.VMEM((CHUNK, INNER), f32), pltpu.VMEM((CHUNK, INNER), bf16),
            pltpu.VMEM((CHUNK, INNER), bf16),
        ],
        compiler_params=params(),
        cost_estimate=cost(30 * 10**9, 48 * 2**20),
        name="gate_norm",
    )(
        rank, y_within, x, bc, cum, hst, states, states, gate, tok_low, cot_low, full_out, spread,
        rows,
    )

    grads = lax.all_gather(glocal.astype(bf16), "seq", axis=0, tiled=False)

    def product(left, right):
        return lax.dot_general(left, right, TN, preferred_element_type=f32).astype(bf16)

    beside = jnp.concatenate(
        [
            blocks(product(hidden, cot_low), bits),
            blocks(product(normed_low, dgate[:, :D]), bits),
            blocks(product(normed_low, dgate[:, D:]), bits),
        ],
        axis=-2,
    )
    keep_b, give_b = split_pair(beside, cross + 2, core_axis, core_bit)
    got_b = swap(give_b, core_axis, core_bit)
    anywhere = pl.BlockSpec(memory_space=pl.ANY)

    def within_back_call(u, dy, bc, cum, cumt, sent, *rest):
        within_back_kernel(u, dy, bc, cum, cumt, *rest)

    dxs, dbc = pl.pallas_call(
        within_back_call,
        grid=(chunks,),
        in_specs=[
            by_chunk(INNER), by_chunk(INNER), by_chunk(2 * STATE), by_chunk(LANES),
            pl.BlockSpec((32, CHUNK), lambda c: (0, c)), anywhere,
        ],
        out_specs=[by_chunk(INNER), by_chunk(2 * STATE)],
        out_shape=[shape((count, INNER), f32), shape((count, 2 * STATE), f32)],
        scratch_shapes=[
            pltpu.VMEM((CHUNK, HEADS * LANES), bf16), pltpu.VMEM((CHUNK, HEADS * LANES), f32),
            pltpu.VMEM((CHUNK, LANES), bf16),
        ],
        compiler_params=params(),
        cost_estimate=cost(12 * 10**9, 16 * 2**20),
        name="within_back",
    )(u, dy, bc, cum, cumt, give_b)

    got_b, dxs, dbc = barrier((got_b, dxs, dbc))
    keep_b, give_b = split_pair(add_low(keep_b, got_b), cross + 1, y_axis, y_bit)
    got_b = swap(give_b, y_axis, y_bit)

    def back(width, height=CHUNK):
        return pl.BlockSpec((height, width), lambda c: (chunks - 1 - c, 0))

    def back_three(height):
        return pl.BlockSpec((1, height, INNER), lambda c: (chunks - 1 - c, 0, 0))

    def back_call(sent, *refs):
        back_kernel(groups, *refs)

    per = CHUNK // 16
    pg, first, tail, wg, hgr, skip = pl.pallas_call(
        back_call,
        grid=(chunks,),
        in_specs=[
            anywhere, smem, back(INNER), back(INNER), back(INNER), back(INNER), back(INNER), back(2 * STATE),
            back(2 * STATE), back(LANES), back(LANES), back(LANES), back_three(STATE),
            pl.BlockSpec((1, 8, LANES), lambda c: (chunks - 1 - c, 0, 0)),
            full((STATE, INNER)), gathered_spec, logs_spec, back_three(STATE), back(SIDE),
            pl.BlockSpec(
                (16, SIDE), lambda c: (jnp.maximum((chunks - 1 - c) * per - 1, 0), 0)
            ),
            full((16, XBC)), full((8, XBC)), full((8, LANES)), full((2 * LANES, INNER)),
            full((2 * INNER, LANES)), full((8, INNER)),
        ],
        out_specs=[
            back(SIDE), full((8, XBC)), full((8, XBC)), full((40, XBC)), full((16, LANES)),
            full((8, INNER)),
        ],
        out_shape=[
            shape((count, SIDE), bf16), shape((8, XBC), f32), shape((8, XBC), f32),
            shape((40, XBC), f32), shape((16, LANES), f32), shape((8, INNER), f32),
        ],
        scratch_shapes=[
            pltpu.VMEM((STATE, INNER), f32), pltpu.VMEM((CHUNK + 8, XBC), f32),
            pltpu.VMEM((CHUNK + 8, XBC), f32), pltpu.VMEM((CHUNK, INNER), bf16),
            pltpu.VMEM((2 * CHUNK + 16, 2 * INNER), bf16),
        ],
        compiler_params=params(),
        cost_estimate=cost(47 * 10**9, 48 * 2**20),
        name="mixer_back",
    )(
        give_b, rank, dxs, dy, x, u, y, bc, dbc, dcc, cum, dt, hst, pfx, h0, grads, states, ust, proj, proj,
        halo, convp, headp, spread, collect, rows,
    )

    got_b, pg, first, tail, wg, hgr, skip = barrier((got_b, pg, first, tail, wg, hgr, skip))
    keep_b, give_b = split_pair(add_low(keep_b, got_b), cross, x_axis, x_bit)
    got_b = swap(give_b, x_axis, x_bit)
    after = lax.ppermute(first, "seq", backward)
    fixes = [jnp.zeros((5, XBC), f32)]
    for m in range(CONV - 1):
        fix = convp[0] * after[m]
        for k in range(1, m + 1):
            fix = fix + convp[k] * after[m - k]
        fixes.append(fix[None, :])
    tail_low = (tail + jnp.concatenate(fixes, axis=0)).astype(bf16)
    pg = lax.dynamic_update_slice(pg, tail_low, (count - 8, 0))

    left = blocks(product(normed_low, pg[:, :half]), bits)
    right = blocks(product(normed_low, pg[:, half:]), bits)
    keep_l, give_l = split_pair(left, cross + 2, core_axis, core_bit)
    keep_r, give_r = split_pair(right, cross + 2, core_axis, core_bit)
    got_l, got_r = swap(give_l, core_axis, core_bit), swap(give_r, core_axis, core_bit)
    pg, dgate, _, _ = barrier((pg, dgate, give_l, give_r))
    normed_grad = lax.dot_general(dgate, full_gate, NT, preferred_element_type=f32)
    normed_grad = normed_grad + lax.dot_general(pg, full_side, NT, preferred_element_type=f32)
    got_l, got_r, got_b, normed_grad, wg, hgr, skip, ng = barrier(
        (got_l, got_r, got_b, normed_grad, wg, hgr, skip, ng)
    )
    keep_l, give_l = split_pair(add_low(keep_l, got_l), cross + 1, y_axis, y_bit)
    keep_r, give_r = split_pair(add_low(keep_r, got_r), cross, x_axis, x_bit)
    got_l, got_r = swap(give_l, y_axis, y_bit), swap(give_r, x_axis, x_bit)
    beside = scatter_pairs(add_low(keep_b, got_b), bits[early:cross], early)
    normed_grad, _, _ = barrier((normed_grad, give_l, give_r))
    _, norm_pull = jax.vjp(pre_norm, tok_vals, pre_gain)
    tok_norm_grad, pre_gain_grad = norm_pull(normed_grad)
    token_grad = (cot_low.astype(f32) + tok_norm_grad)[None]
    got_l, got_r, beside, token_grad, pre_gain_grad = barrier(
        (got_l, got_r, beside, token_grad, pre_gain_grad)
    )
    wg_sum = jnp.sum(wg.reshape(5, 8, XBC), axis=1)
    chan_grad = jnp.concatenate(
        [
            pre_gain_grad,
            jnp.sum(ng, axis=0),
            wg_sum[:CONV].T.reshape(-1),
            wg_sum[CONV],
            jnp.sum(hgr[:8, :HEADS], axis=0),
            jnp.sum(hgr[8:, :HEADS], axis=0),
            jnp.sum(skip.reshape(8, HEADS, HEADDIM), axis=(0, 2)),
        ]
    )

    def together(side_got, beside, chan):
        return barrier((side_got, beside, chan))

    keep_l, give_l = split_pair(add_low(keep_l, got_l), cross, x_axis, x_bit)
    keep_r, give_r = split_pair(add_low(keep_r, got_r), cross, y_axis, y_bit)
    got_l, got_r = swap(give_l, x_axis, x_bit), swap(give_r, y_axis, y_bit)
    beside = scatter_pairs(beside, bits[:early])
    chan_grad = sum_pairs(chan_grad, bits[cross + 2 :])
    (got_l, got_r), beside, chan_grad = together((got_l, got_r), beside, chan_grad)
    side = jnp.concatenate([add_low(keep_l, got_l), add_low(keep_r, got_r)], axis=-1)
    sums = [bits[:early], bits[early:cross], bits[cross : cross + 1], bits[cross + 1 : cross + 2]]
    side = scatter_pairs(side, bits[early:cross], early)
    beside = gather_step(beside, 0, y_axis, y_bit)
    chan_grad = sum_pairs(chan_grad, sums[0])
    side, beside, chan_grad = together(side, beside, chan_grad)
    side = scatter_pairs(side, bits[:early])
    beside = gather_step(beside, 1, core_axis, core_bit)
    chan_grad = sum_pairs(chan_grad, sums[1])
    side, beside, chan_grad = together(side, beside, chan_grad)
    got = swap(side, y_axis, y_bit)
    chan_grad = sum_pairs(chan_grad, sums[2])
    got, chan_grad = barrier((got, chan_grad))
    side = merge_pair(side, got, 0, y_axis, y_bit)
    got = swap(side, core_axis, core_bit)
    chan_grad = sum_pairs(chan_grad, sums[3])
    side = flat(merge_pair(side, got, 1, core_axis, core_bit))

    beside = beside.astype(f32)
    out_grad = flat(beside[..., :out_rows, :])
    in_grad = jnp.concatenate(
        [
            flat(beside[..., out_rows : out_rows + in_rows, :]),
            flat(beside[..., out_rows + in_rows :, :]),
            side[:, : PROJ - INNER].astype(f32),
        ],
        axis=1,
    )
    in_new, in_mom, in_sec = adamw_step(
        in_weight, in_moment, in_second, in_grad, rate_matrix, decay_matrix
    )
    out_new, out_mom, out_sec = adamw_step(
        out_weight, out_moment, out_second, out_grad, rate_matrix, decay_matrix
    )
    chan_new, chan_mom, chan_sec = adamw_step(
        channels, channel_moment, channel_second, chan_grad, rate_channel, 0.0
    )
    return (
        block[None],
        token_grad,
        in_new,
        in_mom,
        in_sec,
        out_new,
        out_mom,
        out_sec,
        chan_new,
        chan_mom,
        chan_sec,
    )


def solution(mesh):
    acts = P("dp", "seq", None)
    rows = P("dp", None)
    specs = (acts, acts) + (rows,) * 6 + (P(),) * 3
    return jax.shard_map(local, mesh=mesh, in_specs=specs, out_specs=specs, check_vma=False)
```

```python
import math

import jax
import jax.numpy as jnp
from jax import lax
from jax.experimental import pallas as pl
from jax.experimental.pallas import tpu as pltpu
from jax.sharding import PartitionSpec as P

D = 768
HEADS = 24
HEADDIM = 64
STATE = 128
CONV = 4
STEP = 10
INNER = 1536
XBC = 1792
PROJ = 3352
SIDE = 1920
LANES = 128
CHUNK = 128
ROWS = 32
PAIRS = HEADS // 2
TILES = XBC // LANES
EXTRA = 16

norm_eps = 1e-05
beta_one = 0.9
beta_two = 0.999
adam_eps = 1e-08
rate_matrix = 0.1
rate_channel = 0.5
decay_matrix = 0.1
LOG2E = 1.0 / math.log(2.0)
VMEM = 20 * 1024 * 1024

f32 = jnp.float32
bf16 = jnp.bfloat16
NT = (((1,), (1,)), ((), ()))
TN = (((0,), (0,)), ((), ()))


def dot(a, b):
    return jnp.dot(a, b, preferred_element_type=f32)


def dot_nt(a, b):
    return lax.dot_general(a, b, NT, preferred_element_type=f32)


def dot_tn(a, b):
    return lax.dot_general(a, b, TN, preferred_element_type=f32)


def sigmoid(v):
    return 0.5 * jnp.tanh(0.5 * v) + 0.5


def halves(v):
    high = v.astype(bf16)
    return high, (v - high.astype(f32)).astype(bf16)


def running(mask, v):
    high, rest = halves(v)
    left = (v - high.astype(f32) - rest.astype(f32)).astype(bf16)
    parts = dot(jnp.where(mask, 1.0, 0.0).astype(bf16), jnp.concatenate([high, rest, left], axis=1))
    return parts[:, :LANES] + parts[:, LANES : 2 * LANES] + parts[:, 2 * LANES :]


def expand(v, spread):
    high, rest = halves(v)
    return dot(jnp.concatenate([high, rest], axis=1), spread)


def fold(v):
    return jnp.sum(v.reshape(v.shape[0] // 8, 8, v.shape[1]), axis=0)


def lane(i):
    return slice(i * LANES, (i + 1) * LANES)


def iota(shape, dim):
    return lax.broadcasted_iota(jnp.int32, shape, dim)


def tri(lower):
    rows, cols = iota((CHUNK, CHUNK), 0), iota((CHUNK, CHUNK), 1)
    return (rows >= cols) if lower else (rows <= cols)


def conv_rows(convp, tile):
    return [jnp.broadcast_to(convp[k : k + 1, lane(tile)], (ROWS, LANES)) for k in range(CONV + 1)]


def conv_pre(ext, weights, tile, start):
    cols = lane(tile)
    taps = [ext[5 + k + start : 5 + k + start + ROWS, cols] for k in range(CONV)]
    pre = taps[0] * weights[0] + weights[CONV]
    for k in range(1, CONV):
        pre = pre + taps[k] * weights[k]
    return pre, taps


def pieces():
    return [(start, slice(start, start + ROWS)) for start in range(0, CHUNK, ROWS)]


def pair_stack(v):
    side = iota(v.shape, 1) < HEADDIM
    zero = jnp.zeros_like(v)
    return jnp.concatenate([jnp.where(side, v, zero), jnp.where(side, zero, v)], axis=0)


def conv_state_kernel(
    proj, halo, convp, headp, spread, x_out, bc_out, u_out, cum_out, cumt_out, dt_out, hst_out,
    pfx_out, send_out, ext, state, scaled, total,
):
    step = pl.program_id(0)

    @pl.when(step == 0)
    def _():
        ext[0:8, :] = halo[8:16, :].astype(f32)
        state[...] = jnp.zeros_like(state)
        total[...] = jnp.zeros_like(total)

    @pl.when(step > 0)
    def _():
        ext[0:8, :] = ext[CHUNK : CHUNK + 8, :]

    ext[8:, :] = proj[:, :XBC].astype(f32)
    raw = proj[:, XBC:].astype(f32) + headp[0:1, :]
    steps = jnp.maximum(raw, 0.0) + jnp.log1p(jnp.exp(-jnp.abs(raw)))
    log_decay = steps * (headp[1:2, :] * (-LOG2E))
    cum = running(tri(True), log_decay)
    cum_out[...] = cum
    cumt_out[...] = jnp.transpose(cum)[0:32, :]
    dt_out[...] = steps
    last = cum[CHUNK - 1 : CHUNK, :]
    decayed = jnp.broadcast_to(jnp.exp2(last), (8, LANES))
    wide = expand(jnp.concatenate([steps, jnp.exp2(last - cum), decayed], axis=0), spread[...])
    steps_wide, tail_wide = wide[:CHUNK], wide[CHUNK : 2 * CHUNK]
    decay = wide[2 * CHUNK : 2 * CHUNK + 1]
    for tile in range(TILES):
        cols = lane(tile)
        weights = conv_rows(convp, tile)
        for start, part in pieces():
            pre, _ = conv_pre(ext, weights, tile, start)
            value = (pre * sigmoid(pre)).astype(bf16)
            if tile < PAIRS:
                x_out[part, cols] = value
                u = (value.astype(f32) * steps_wide[part, cols]).astype(bf16)
                u_out[part, cols] = u
                scaled[part, cols] = (u.astype(f32) * tail_wide[part, cols]).astype(bf16)
            else:
                bc_out[part, lane(tile - PAIRS)] = value
    new_state = state[...] * decay + dot_tn(bc_out[:, :STATE], scaled[...])
    state[...] = new_state
    hst_out[0] = new_state
    new_total = total[...] + jnp.broadcast_to(last, (8, LANES))
    total[...] = new_total
    pfx_out[0] = new_total

    @pl.when(step == pl.num_programs(0) - 1)
    def _():
        send_out[:STATE, :] = new_state.astype(bf16)
        row = iota((EXTRA, LANES), 0)
        wide = jnp.broadcast_to(new_total[0:1, :], (EXTRA, LANES))
        high, rest = halves(wide)
        left = (wide - high.astype(f32) - rest.astype(f32)).astype(bf16)
        parts = jnp.where(
            row == 0,
            high.astype(f32),
            jnp.where(row == 1, rest.astype(f32), jnp.where(row == 2, left.astype(f32), 0.0)),
        )
        send_out[STATE:, :] = dot(parts.astype(bf16), spread[:LANES, :]).astype(bf16)


def within_kernel(u, bc, cum, cumt, y_out, weights):
    scores = jnp.where(tri(True), dot_nt(bc[:, STATE:], bc[:, :STATE]), 0.0)
    for _, part in pieces():
        rows_cum = cum[part, :]
        rows_scores = scores[part]
        for head in range(HEADS):
            gap = rows_cum[:, head : head + 1] - cumt[head : head + 1, :]
            weights[part, lane(head)] = (jnp.exp2(jnp.minimum(gap, 0.0)) * rows_scores).astype(bf16)
    for pair in range(PAIRS):
        both = slice(2 * pair * LANES, 2 * (pair + 1) * LANES)
        y_out[:, lane(pair)] = dot(weights[:, both], pair_stack(u[:, lane(pair)]))


def arrived(gathered, logs, rank, groups, later):
    sums = [
        jnp.sum(logs[g].astype(f32), axis=0, keepdims=True) for g in range(groups)
    ]
    entered = jnp.zeros((STATE, INNER), f32)
    for g in range(groups):
        between = jnp.zeros((1, INNER), f32)
        for s in range(groups):
            if (s < g) if later else (s > g):
                inside = (s > rank) if later else (s < rank)
                between = between + jnp.where(inside, sums[s], 0.0)
        counts = (g > rank) if later else (g < rank)
        weight = jnp.where(counts, jnp.exp2(between), 0.0)
        entered = entered + gathered[g].astype(f32) * weight
    return entered


def gate_kernel(
    groups, rank, y_in, x, bc, cum, hst, gathered, logs, gate, tok, cot, wout, spread, rows,
    block_out, hidden_out, y_out, dy_out, dgate_out, dcc_out, ust_out, glocal_out, ng_out, h0_out,
    prefix, h0, hg_all, mixed_all, dy_scaled,
):
    step = pl.program_id(0)

    @pl.when(step == 0)
    def _():
        value = arrived(gathered, logs, rank[0], groups, False)
        h0[...] = value
        h0_out[...] = value
        prefix[...] = jnp.zeros_like(prefix)
        glocal_out[...] = jnp.zeros_like(glocal_out)
        ng_out[...] = jnp.zeros_like(ng_out)

    wide = expand(jnp.exp2(jnp.concatenate([cum[...], prefix[...]], axis=0)), spread[...])
    grown, start = wide[:CHUNK], wide[CHUNK : CHUNK + 1]
    state = h0[...] * start + jnp.where(step > 0, hst[0], 0.0)
    state_low = state.astype(bf16)
    carried = dot(bc[:, STATE:], state_low)
    hg_all[...] = dot_nt(cot[...], wout[...])
    gain, skip = rows[0:1, :], rows[1:2, :]
    for _, part in pieces():
        squares = jnp.zeros((ROWS, LANES), f32)
        cross = jnp.zeros((ROWS, LANES), f32)
        for tile in range(PAIRS):
            cols = lane(tile)
            y = y_in[part, cols] + carried[part, cols] * grown[part, cols]
            y_out[part, cols] = y
            mixed = (y + skip[:, cols] * x[part, cols].astype(f32)).astype(bf16)
            mixed_all[part, cols] = mixed
            gate_val = gate[part, cols].astype(f32)
            gated = mixed.astype(f32) * (gate_val * sigmoid(gate_val))
            squares = squares + gated * gated
            cross = cross + gated * (hg_all[part, cols] * gain[:, cols])
        mean = jnp.sum(squares, axis=1, keepdims=True) * (1.0 / INNER)
        scale = lax.rsqrt(mean + norm_eps)
        cross_mean = jnp.sum(cross, axis=1, keepdims=True) * (1.0 / INNER) * scale * scale * scale
        scale = jnp.broadcast_to(scale, (ROWS, LANES))
        cross_mean = jnp.broadcast_to(cross_mean, (ROWS, LANES))
        for tile in range(PAIRS):
            cols = lane(tile)
            gate_val = gate[part, cols].astype(f32)
            sig = sigmoid(gate_val)
            silu = gate_val * sig
            mixed = mixed_all[part, cols].astype(f32)
            gated = mixed * silu
            normal = gated * scale
            hidden_out[part, cols] = (normal * gain[:, cols]).astype(bf16)
            grad = hg_all[part, cols]
            ng_out[:, cols] += fold(grad * normal)
            dgated = grad * gain[:, cols] * scale - gated * cross_mean
            dgate_out[part, cols] = (dgated * mixed * (sig + silu * (1.0 - sig))).astype(bf16)
            dy = (dgated * silu).astype(bf16)
            dy_out[part, cols] = dy
            dy_scaled[part, cols] = (dy.astype(f32) * grown[part, cols]).astype(bf16)
    block_out[...] = tok[...].astype(f32) + dot(hidden_out[...], wout[...])
    update = dot_tn(bc[:, STATE:], dy_scaled[...])
    ust_out[0] = update
    glocal_out[...] += update * start
    dcc_out[...] = dot_nt(dy_scaled[...], state_low)
    prefix[...] += jnp.broadcast_to(cum[CHUNK - 1 : CHUNK, :], (8, LANES))


def within_back_kernel(u, dy, bc, cum, cumt, dxs_out, dbc_out, weights, products, low):
    upper = tri(False)
    scores = jnp.where(upper, dot_nt(bc[:, :STATE], bc[:, STATE:]), 0.0)
    for pair in range(PAIRS):
        both = slice(2 * pair * LANES, 2 * (pair + 1) * LANES)
        products[:, both] = dot_nt(u[:, lane(pair)], pair_stack(dy[:, lane(pair)]))
    for _, part in pieces():
        rows_cum = cum[part, :]
        rows_scores = scores[part]
        total = jnp.zeros((ROWS, LANES), f32)
        for head in range(HEADS):
            gap = cumt[head : head + 1, :] - rows_cum[:, head : head + 1]
            decay = jnp.exp2(jnp.minimum(gap, 0.0))
            weights[part, lane(head)] = (decay * rows_scores).astype(bf16)
            total = total + decay * products[part, lane(head)]
        low[part, :] = jnp.where(upper[part], total, 0.0).astype(bf16)
    for pair in range(PAIRS):
        both = slice(2 * pair * LANES, 2 * (pair + 1) * LANES)
        dxs_out[:, lane(pair)] = dot(weights[:, both], pair_stack(dy[:, lane(pair)]))
    dbc_out[:, :STATE] = dot(low[...], bc[:, STATE:])
    dbc_out[:, STATE:] = dot_tn(low[...], bc[:, :STATE])


def back_kernel(
    groups, rank, dxs, dy, x, u, y, bc, dbc, dcc, cum, dt, hst, pfx, h0, gathered, logs, ust, proj,
    before, halo, convp, headp, spread, collect, rows,
    pg_out, first_out, tail_out, wg_out, hg_out, skip_out,
    gstate, ext, dext, scaled, prod,
):
    step = pl.program_id(0)
    chunk = pl.num_programs(0) - 1 - step

    @pl.when(step == 0)
    def _():
        gstate[...] = arrived(gathered, logs, rank[0], groups, True)
        dext[CHUNK:, :] = jnp.zeros((8, XBC), f32)
        wg_out[...] = jnp.zeros_like(wg_out)
        hg_out[...] = jnp.zeros_like(hg_out)
        skip_out[...] = jnp.zeros_like(skip_out)

    @pl.when(step > 0)
    def _():
        dext[CHUNK:, :] = dext[0:8, :]

    @pl.when(chunk == 0)
    def _():
        ext[0:8, :] = halo[8:16, :].astype(f32)

    @pl.when(chunk > 0)
    def _():
        ext[0:8, :] = before[8:16, :XBC].astype(f32)

    ext[8:, :] = proj[:, :XBC].astype(f32)
    grad_state = gstate[...]
    grad_low = grad_state.astype(bf16)
    last = cum[CHUNK - 1 : CHUNK, :]
    decayed = jnp.broadcast_to(jnp.exp2(last), (8, LANES))
    wide = expand(
        jnp.concatenate([jnp.exp2(last - cum[...]), dt[...], decayed, jnp.exp2(pfx[0])], axis=0),
        spread[...],
    )
    tail_wide, steps_wide = wide[:CHUNK], wide[CHUNK : 2 * CHUNK]
    decay = wide[2 * CHUNK : 2 * CHUNK + 1]
    end = wide[2 * CHUNK + 8 : 2 * CHUNK + 9]
    reach = dot(bc[:, :STATE], grad_low)

    def conv_back(tile, grad_of):
        cols = lane(tile)
        weights = conv_rows(convp, tile)
        sums = [jnp.zeros((8, LANES), f32) for _ in range(CONV + 1)]
        for start, part in reversed(pieces()):
            grad = grad_of(part)
            pre, taps = conv_pre(ext, weights, tile, start)
            sig = sigmoid(pre)
            dpre = grad * (sig + pre * sig * (1.0 - sig))
            dext[part, cols] = dpre
            sums = [total + fold(dpre * tap) for total, tap in zip(sums, taps)] + [
                sums[CONV] + fold(dpre)
            ]
            source = dpre * weights[3]
            for k in range(CONV - 1):
                source = source + dext[start + 3 - k : start + 3 - k + ROWS, cols] * weights[k]
            pg_out[part, cols] = source.astype(bf16)
            if start + ROWS == CHUNK:

                @pl.when(step == 0)
                def _():
                    tail_out[:, cols] = source[ROWS - 8 :, :]

        for k in range(CONV + 1):
            wg_out[8 * k : 8 * k + 8, cols] += sums[k]

    for tile in range(PAIRS):
        cols = lane(tile)
        rest_cols = slice(INNER + tile * LANES, INNER + (tile + 1) * LANES)
        skip_row = jnp.broadcast_to(rows[1:2, cols], (ROWS, LANES))
        skips = []

        def grad_of(part, cols=cols, rest_cols=rest_cols, skip_row=skip_row, skips=skips):
            below = slice(CHUNK + part.start, CHUNK + part.stop)
            dxs_full = dxs[part, cols] + tail_wide[part, cols] * reach[part, cols]
            uf = u[part, cols].astype(f32)
            dyf = dy[part, cols].astype(f32)
            scaled[part, cols] = (uf * tail_wide[part, cols]).astype(bf16)
            q = uf * dxs_full
            prod[part, cols], prod[part, rest_cols] = halves(q)
            prod[below, cols], prod[below, rest_cols] = halves(dyf * y[part, cols] - q)
            skips.append(fold(dyf * x[part, cols].astype(f32)))
            return skip_row * dyf + steps_wide[part, cols] * dxs_full

        conv_back(tile, grad_of)
        skip_out[:, cols] += sum(skips[1:], skips[0])
    dwrite = dot_nt(scaled[...], grad_low)
    conv_back(PAIRS, lambda part: dbc[part, :STATE] + dwrite[part])
    conv_back(PAIRS + 1, lambda part: dbc[part, STATE:] + dcc[part, :])
    first_out[...] = dext[0:8, :]

    meet = fold(grad_state * (hst[0] + h0[...] * end))
    meet = jnp.concatenate([meet, jnp.zeros_like(meet)], axis=0)
    high, rest = halves(meet)
    prod[2 * CHUNK :, :INNER] = high
    prod[2 * CHUNK :, INNER:] = rest
    heads = dot(prod[...], collect[...])
    q_heads, gap_heads = heads[:CHUNK], heads[CHUNK : 2 * CHUNK]
    meet_heads = jnp.sum(heads[2 * CHUNK :], axis=0, keepdims=True)
    dlog = running(tri(False), gap_heads) + meet_heads
    sig = sigmoid(proj[:, XBC:].astype(f32) + headp[0:1, :])
    steps = dt[...]
    ratio = jnp.where(steps > 1e-30, sig / jnp.maximum(steps, 1e-30), 1.0)
    raw_grad = q_heads * ratio - dlog * headp[1:2, :] * sig
    pg_out[:, XBC:] = raw_grad.astype(bf16)
    hg_out[0:8, :] += fold(raw_grad)
    hg_out[8:16, :] += fold(dlog * steps * headp[1:2, :]) * (-1.0)
    gstate[...] = grad_state * decay + ust[0]


def swap(v, axis, bit):
    size = lax.axis_size(axis)
    return lax.ppermute(v, axis, [(i, i ^ (1 << bit)) for i in range(size)])


def mesh_bits():
    found = []
    for axis in ("dp", "seq"):
        for bit in reversed(range(lax.axis_size(axis).bit_length() - 1)):
            found.append((axis, bit))
    return found


def mine(axis, bit):
    return (lax.axis_index(axis) >> bit) & 1


def merge_pair(v, other, place, axis, bit):
    second = mine(axis, bit) == 1
    return jnp.stack([jnp.where(second, other, v), jnp.where(second, v, other)], axis=place)


def gather_step(v, place, axis, bit):
    return merge_pair(v, swap(v, axis, bit), place, axis, bit)


def gather_pairs(v, bits, lead=0):
    for place, (axis, bit) in enumerate(bits):
        v = gather_step(v, lead + place, axis, bit)
    return v


def flat(v):
    return v.reshape(-1, v.shape[-1])


def blocks(v, bits):
    return v.reshape((2,) * len(bits) + (v.shape[0] >> len(bits), v.shape[1]))


def split_pair(v, place, axis, bit):
    own = mine(axis, bit)
    keep = lax.dynamic_index_in_dim(v, own, place, keepdims=False)
    give = lax.dynamic_index_in_dim(v, 1 - own, place, keepdims=False)
    return keep, give


def add_low(keep, got):
    return (keep.astype(f32) + got.astype(f32)).astype(keep.dtype)


def scatter_step(v, place, axis, bit):
    keep, give = split_pair(v, place, axis, bit)
    return add_low(keep, swap(give, axis, bit))


def scatter_pairs(v, bits, lead=0):
    for place in reversed(range(len(bits))):
        v = scatter_step(v, lead + place, *bits[place])
    return v


def sum_pairs(v, bits):
    for axis, bit in bits:
        v = v + swap(v, axis, bit)
    return v


def full(shape):
    return pl.BlockSpec(shape, lambda c: (0,) * len(shape))


def by_chunk(width, rows=CHUNK):
    return pl.BlockSpec((rows, width), lambda c: (c, 0))


def shape(dims, dtype):
    return jax.ShapeDtypeStruct(dims, dtype)


def params():
    return pltpu.CompilerParams(dimension_semantics=("arbitrary",), vmem_limit_bytes=VMEM)


def cost(flops, moved):
    return pl.CostEstimate(flops=flops, bytes_accessed=moved, transcendentals=0)


def spread_map():
    heads = jnp.arange(LANES)[:, None]
    cols = jnp.arange(INNER)[None, :] // HEADDIM
    once = (heads == cols).astype(bf16)
    return jnp.concatenate([once, once], axis=0)


def unpack_channels(channels):
    pieces = []
    offset = 0
    for piece_len in (D, INNER, XBC * CONV, XBC, HEADS, HEADS, HEADS):
        pieces.append(channels[offset : offset + piece_len])
        offset = offset + piece_len
    pre_gain, norm_gain, conv_flat, conv_bias, step_bias, rate_log, skip_gain = pieces
    return (
        pre_gain,
        norm_gain,
        conv_flat.reshape(XBC, CONV),
        conv_bias,
        step_bias,
        rate_log,
        skip_gain,
    )


def pre_norm(tok_vals, pre_gain):
    return (
        tok_vals * lax.rsqrt(jnp.mean(tok_vals * tok_vals, -1, keepdims=True) + norm_eps) * pre_gain
    )


def adamw_step(weight, moment, second, gradient, step_rate, decay_rate):
    moment_next = beta_one * moment + (1.0 - beta_one) * gradient
    second_next = beta_two * second + (1.0 - beta_two) * gradient * gradient
    first_fix = 1.0 - beta_one**STEP
    second_fix = 1.0 - beta_two**STEP
    update = moment_next / first_fix / (jnp.sqrt(second_next / second_fix) + adam_eps)
    return (weight - step_rate * (update + decay_rate * weight), moment_next, second_next)


def local(
    tokens,
    cotangent,
    in_weight,
    in_moment,
    in_second,
    out_weight,
    out_moment,
    out_second,
    channels,
    channel_moment,
    channel_second,
):
    groups = lax.axis_size("seq")
    bits = mesh_bits()
    seq_bits = [(axis, bit) for axis, bit in bits if axis == "seq"]
    seq_rank = lax.axis_index("seq")
    rank = seq_rank.astype(jnp.int32).reshape(1)
    pre_gain, norm_gain, conv_weight, conv_bias, step_bias, rate_log, skip_gain = unpack_channels(
        channels
    )
    tok_low = tokens[0]
    cot_low = cotangent[0]
    count = tok_low.shape[0]
    chunks = count // CHUNK

    def quarter(weight):
        size = weight.shape[0] // groups
        return lax.dynamic_slice_in_dim(weight, seq_rank * size, size, 0).astype(bf16)

    in_part = quarter(in_weight)
    side_part = jnp.pad(in_part[:, INNER:], ((0, 0), (0, SIDE + INNER - PROJ)))
    out_rows = out_weight.shape[0] // groups
    in_rows = in_weight.shape[0] // groups
    beside = jnp.concatenate(
        [quarter(out_weight), in_part[:, :D], in_part[:, D:INNER]], axis=0
    )
    barrier = lax.optimization_barrier
    cross = len(bits) - 3
    (x_axis, x_bit), (y_axis, y_bit), (core_axis, core_bit) = bits[cross:]
    side = gather_pairs(side_part, bits[:cross])
    side, beside = barrier((side, beside))
    half = SIDE // 256 * 128
    left, right = side[..., :half], side[..., half:]
    got_l, got_r = swap(left, x_axis, x_bit), swap(right, y_axis, y_bit)
    early = cross // 2
    beside = gather_pairs(beside, bits[:early])
    left = merge_pair(left, got_l, cross, x_axis, x_bit)
    right = merge_pair(right, got_r, cross, y_axis, y_bit)
    got_l, got_r = swap(left, y_axis, y_bit), swap(right, x_axis, x_bit)
    beside, left, right = barrier((beside, left, right))
    beside = gather_pairs(beside, bits[early:cross], early)
    left = merge_pair(left, got_l, cross + 1, y_axis, y_bit)
    right = merge_pair(right, got_r, cross, x_axis, x_bit)
    got_l, got_r = swap(left, core_axis, core_bit), swap(right, core_axis, core_bit)
    beside, left, right = barrier((beside, left, right))
    got_b = swap(beside, x_axis, x_bit)
    left = merge_pair(left, got_l, cross + 2, core_axis, core_bit)
    right = merge_pair(right, got_r, cross + 2, core_axis, core_bit)
    full_side = jnp.concatenate([flat(left), flat(right)], axis=1)

    forward = [(s, s + 1) for s in range(groups - 1)]
    backward = [(s + 1, s) for s in range(groups - 1)]
    tok_halo = lax.ppermute(tok_low[count - 16 :], "seq", forward)
    halo_norm = pre_norm(tok_halo.astype(f32), pre_gain).astype(bf16)
    tok_vals = tok_low.astype(f32)
    normed_low = pre_norm(tok_vals, pre_gain).astype(bf16)

    convp = jnp.concatenate(
        [conv_weight.T, conv_bias[None, :], jnp.zeros((3, XBC), f32)], axis=0
    )
    pad_heads = lambda v: jnp.pad(v, (0, LANES - HEADS))[None, :]
    headp = jnp.concatenate(
        [pad_heads(step_bias), pad_heads(jnp.exp(rate_log)), jnp.zeros((6, LANES), f32)], axis=0
    )
    rows = jnp.concatenate(
        [norm_gain[None, :], jnp.repeat(skip_gain, HEADDIM)[None, :], jnp.zeros((6, INNER), f32)],
        axis=0,
    )
    spread = spread_map()
    collect = jnp.concatenate([spread[:LANES].T, spread[:LANES].T], axis=0)

    proj = dot(normed_low, full_side).astype(bf16)
    halo = dot(halo_norm, full_side[:, :XBC]).astype(bf16)
    proj, halo, got_b = barrier((proj, halo, got_b))
    beside = merge_pair(beside, got_b, cross, x_axis, x_bit)
    got_b = swap(beside, y_axis, y_bit)

    x, bc, u, cum, cumt, dt, hst, pfx, send = pl.pallas_call(
        conv_state_kernel,
        grid=(chunks,),
        in_specs=[
            by_chunk(SIDE), full((16, XBC)), full((8, XBC)), full((8, LANES)),
            full((2 * LANES, INNER)),
        ],
        out_specs=[
            by_chunk(INNER), by_chunk(2 * STATE), by_chunk(INNER), by_chunk(LANES),
            pl.BlockSpec((32, CHUNK), lambda c: (0, c)), by_chunk(LANES),
            pl.BlockSpec((1, STATE, INNER), lambda c: (c, 0, 0)),
            pl.BlockSpec((1, 8, LANES), lambda c: (c, 0, 0)),
            full((STATE + EXTRA, INNER)),
        ],
        out_shape=[
            shape((count, INNER), bf16), shape((count, 2 * STATE), bf16),
            shape((count, INNER), bf16), shape((count, LANES), f32), shape((32, count), f32),
            shape((count, LANES), f32), shape((chunks, STATE, INNER), f32),
            shape((chunks, 8, LANES), f32), shape((STATE + EXTRA, INNER), bf16),
        ],
        scratch_shapes=[
            pltpu.VMEM((CHUNK + 8, XBC), f32), pltpu.VMEM((STATE, INNER), f32),
            pltpu.VMEM((CHUNK, INNER), bf16), pltpu.VMEM((8, LANES), f32),
        ],
        compiler_params=params(),
        cost_estimate=cost(24 * 10**9, 24 * 2**20),
        name="conv_state",
    )(proj, halo, convp, headp, spread)

    states = lax.all_gather(send, "seq", axis=0, tiled=False)
    x, bc, u, cum, cumt, dt, hst, pfx, got_b = barrier(
        (x, bc, u, cum, cumt, dt, hst, pfx, got_b)
    )
    beside = merge_pair(beside, got_b, cross + 1, y_axis, y_bit)
    got_b = swap(beside, core_axis, core_bit)

    y_within = pl.pallas_call(
        within_kernel,
        grid=(chunks,),
        in_specs=[
            by_chunk(INNER), by_chunk(2 * STATE), by_chunk(LANES),
            pl.BlockSpec((32, CHUNK), lambda c: (0, c)),
        ],
        out_specs=by_chunk(INNER),
        out_shape=shape((count, INNER), f32),
        scratch_shapes=[pltpu.VMEM((CHUNK, HEADS * LANES), bf16)],
        compiler_params=params(),
        cost_estimate=cost(11 * 10**9, 16 * 2**20),
        name="within",
    )(u, bc, cum, cumt)
    y_within, got_b = barrier((y_within, got_b))
    beside = merge_pair(beside, got_b, cross + 2, core_axis, core_bit)
    full_out = flat(beside[..., :out_rows, :])
    full_gate = jnp.concatenate(
        [
            flat(beside[..., out_rows : out_rows + in_rows, :]),
            flat(beside[..., out_rows + in_rows :, :]),
        ],
        axis=1,
    )
    gate = dot(normed_low, full_gate).astype(bf16)

    gathered_spec = full((groups, STATE, INNER))
    logs_spec = pl.BlockSpec((groups, EXTRA, INNER), lambda c: (0, STATE // EXTRA, 0))
    smem = pl.BlockSpec(memory_space=pltpu.SMEM)

    def gate_call(*refs):
        gate_kernel(groups, *refs)

    block, hidden, y, dy, dgate, dcc, ust, glocal, ng, h0 = pl.pallas_call(
        gate_call,
        grid=(chunks,),
        in_specs=[
            smem, by_chunk(INNER), by_chunk(INNER), by_chunk(2 * STATE), by_chunk(LANES),
            pl.BlockSpec((1, STATE, INNER), lambda c: (jnp.maximum(c - 1, 0), 0, 0)),
            gathered_spec, logs_spec, by_chunk(INNER), by_chunk(D), by_chunk(D),
            full((INNER, D)), full((2 * LANES, INNER)), full((8, INNER)),
        ],
        out_specs=[
            by_chunk(D), by_chunk(INNER), by_chunk(INNER), by_chunk(INNER), by_chunk(INNER),
            by_chunk(LANES), pl.BlockSpec((1, STATE, INNER), lambda c: (c, 0, 0)),
            full((STATE, INNER)), full((8, INNER)), full((STATE, INNER)),
        ],
        out_shape=[
            shape((count, D), f32), shape((count, INNER), bf16), shape((count, INNER), f32),
            shape((count, INNER), bf16), shape((count, INNER), bf16), shape((count, LANES), f32),
            shape((chunks, STATE, INNER), f32), shape((STATE, INNER), f32), shape((8, INNER), f32),
            shape((STATE, INNER), f32),
        ],
        scratch_shapes=[
            pltpu.VMEM((8, LANES), f32), pltpu.VMEM((STATE, INNER), f32),
            pltpu.VMEM((CHUNK, INNER), f32), pltpu.VMEM((CHUNK, INNER), bf16),
            pltpu.VMEM((CHUNK, INNER), bf16),
        ],
        compiler_params=params(),
        cost_estimate=cost(30 * 10**9, 48 * 2**20),
        name="gate_norm",
    )(
        rank, y_within, x, bc, cum, hst, states, states, gate, tok_low, cot_low, full_out, spread,
        rows,
    )

    grads = lax.all_gather(glocal.astype(bf16), "seq", axis=0, tiled=False)

    def product(left, right):
        return lax.dot_general(left, right, TN, preferred_element_type=f32).astype(bf16)

    beside = jnp.concatenate(
        [
            blocks(product(hidden, cot_low), bits),
            blocks(product(normed_low, dgate[:, :D]), bits),
            blocks(product(normed_low, dgate[:, D:]), bits),
        ],
        axis=-2,
    )
    keep_b, give_b = split_pair(beside, cross + 2, core_axis, core_bit)
    got_b = swap(give_b, core_axis, core_bit)
    anywhere = pl.BlockSpec(memory_space=pl.ANY)

    def within_back_call(u, dy, bc, cum, cumt, sent, *rest):
        within_back_kernel(u, dy, bc, cum, cumt, *rest)

    dxs, dbc = pl.pallas_call(
        within_back_call,
        grid=(chunks,),
        in_specs=[
            by_chunk(INNER), by_chunk(INNER), by_chunk(2 * STATE), by_chunk(LANES),
            pl.BlockSpec((32, CHUNK), lambda c: (0, c)), anywhere,
        ],
        out_specs=[by_chunk(INNER), by_chunk(2 * STATE)],
        out_shape=[shape((count, INNER), f32), shape((count, 2 * STATE), f32)],
        scratch_shapes=[
            pltpu.VMEM((CHUNK, HEADS * LANES), bf16), pltpu.VMEM((CHUNK, HEADS * LANES), f32),
            pltpu.VMEM((CHUNK, LANES), bf16),
        ],
        compiler_params=params(),
        cost_estimate=cost(12 * 10**9, 16 * 2**20),
        name="within_back",
    )(u, dy, bc, cum, cumt, give_b)

    got_b, dxs, dbc = barrier((got_b, dxs, dbc))
    keep_b, give_b = split_pair(add_low(keep_b, got_b), cross + 1, y_axis, y_bit)
    got_b = swap(give_b, y_axis, y_bit)

    def back(width, height=CHUNK):
        return pl.BlockSpec((height, width), lambda c: (chunks - 1 - c, 0))

    def back_three(height):
        return pl.BlockSpec((1, height, INNER), lambda c: (chunks - 1 - c, 0, 0))

    def back_call(sent, *refs):
        back_kernel(groups, *refs)

    per = CHUNK // 16
    pg, first, tail, wg, hgr, skip = pl.pallas_call(
        back_call,
        grid=(chunks,),
        in_specs=[
            anywhere, smem, back(INNER), back(INNER), back(INNER), back(INNER), back(INNER), back(2 * STATE),
            back(2 * STATE), back(LANES), back(LANES), back(LANES), back_three(STATE),
            pl.BlockSpec((1, 8, LANES), lambda c: (chunks - 1 - c, 0, 0)),
            full((STATE, INNER)), gathered_spec, logs_spec, back_three(STATE), back(SIDE),
            pl.BlockSpec(
                (16, SIDE), lambda c: (jnp.maximum((chunks - 1 - c) * per - 1, 0), 0)
            ),
            full((16, XBC)), full((8, XBC)), full((8, LANES)), full((2 * LANES, INNER)),
            full((2 * INNER, LANES)), full((8, INNER)),
        ],
        out_specs=[
            back(SIDE), full((8, XBC)), full((8, XBC)), full((40, XBC)), full((16, LANES)),
            full((8, INNER)),
        ],
        out_shape=[
            shape((count, SIDE), bf16), shape((8, XBC), f32), shape((8, XBC), f32),
            shape((40, XBC), f32), shape((16, LANES), f32), shape((8, INNER), f32),
        ],
        scratch_shapes=[
            pltpu.VMEM((STATE, INNER), f32), pltpu.VMEM((CHUNK + 8, XBC), f32),
            pltpu.VMEM((CHUNK + 8, XBC), f32), pltpu.VMEM((CHUNK, INNER), bf16),
            pltpu.VMEM((2 * CHUNK + 16, 2 * INNER), bf16),
        ],
        compiler_params=params(),
        cost_estimate=cost(47 * 10**9, 48 * 2**20),
        name="mixer_back",
    )(
        give_b, rank, dxs, dy, x, u, y, bc, dbc, dcc, cum, dt, hst, pfx, h0, grads, states, ust, proj, proj,
        halo, convp, headp, spread, collect, rows,
    )

    got_b, pg, first, tail, wg, hgr, skip = barrier((got_b, pg, first, tail, wg, hgr, skip))
    keep_b, give_b = split_pair(add_low(keep_b, got_b), cross, x_axis, x_bit)
    got_b = swap(give_b, x_axis, x_bit)
    after = lax.ppermute(first, "seq", backward)
    fixes = [jnp.zeros((5, XBC), f32)]
    for m in range(CONV - 1):
        fix = convp[0] * after[m]
        for k in range(1, m + 1):
            fix = fix + convp[k] * after[m - k]
        fixes.append(fix[None, :])
    tail_low = (tail + jnp.concatenate(fixes, axis=0)).astype(bf16)
    pg = lax.dynamic_update_slice(pg, tail_low, (count - 8, 0))

    left = blocks(product(normed_low, pg[:, :half]), bits)
    right = blocks(product(normed_low, pg[:, half:]), bits)
    keep_l, give_l = split_pair(left, cross + 2, core_axis, core_bit)
    keep_r, give_r = split_pair(right, cross + 2, core_axis, core_bit)
    got_l, got_r = swap(give_l, core_axis, core_bit), swap(give_r, core_axis, core_bit)
    pg, dgate, _, _ = barrier((pg, dgate, give_l, give_r))
    normed_grad = lax.dot_general(dgate, full_gate, NT, preferred_element_type=f32)
    normed_grad = normed_grad + lax.dot_general(pg, full_side, NT, preferred_element_type=f32)
    got_l, got_r, got_b, normed_grad, wg, hgr, skip, ng = barrier(
        (got_l, got_r, got_b, normed_grad, wg, hgr, skip, ng)
    )
    keep_l, give_l = split_pair(add_low(keep_l, got_l), cross + 1, y_axis, y_bit)
    keep_r, give_r = split_pair(add_low(keep_r, got_r), cross, x_axis, x_bit)
    got_l, got_r = swap(give_l, y_axis, y_bit), swap(give_r, x_axis, x_bit)
    beside = scatter_pairs(add_low(keep_b, got_b), bits[early:cross], early)
    normed_grad, _, _ = barrier((normed_grad, give_l, give_r))
    _, norm_pull = jax.vjp(pre_norm, tok_vals, pre_gain)
    tok_norm_grad, pre_gain_grad = norm_pull(normed_grad)
    token_grad = (cot_low.astype(f32) + tok_norm_grad)[None]
    got_l, got_r, beside, token_grad, pre_gain_grad = barrier(
        (got_l, got_r, beside, token_grad, pre_gain_grad)
    )
    wg_sum = jnp.sum(wg.reshape(5, 8, XBC), axis=1)
    chan_grad = jnp.concatenate(
        [
            pre_gain_grad,
            jnp.sum(ng, axis=0),
            wg_sum[:CONV].T.reshape(-1),
            wg_sum[CONV],
            jnp.sum(hgr[:8, :HEADS], axis=0),
            jnp.sum(hgr[8:, :HEADS], axis=0),
            jnp.sum(skip.reshape(8, HEADS, HEADDIM), axis=(0, 2)),
        ]
    )

    def together(side_got, beside, chan):
        return barrier((side_got, beside, chan))

    keep_l, give_l = split_pair(add_low(keep_l, got_l), cross, x_axis, x_bit)
    keep_r, give_r = split_pair(add_low(keep_r, got_r), cross, y_axis, y_bit)
    got_l, got_r = swap(give_l, x_axis, x_bit), swap(give_r, y_axis, y_bit)
    beside = scatter_pairs(beside, bits[:early])
    chan_grad = sum_pairs(chan_grad, bits[cross + 2 :])
    (got_l, got_r), beside, chan_grad = together((got_l, got_r), beside, chan_grad)
    side = jnp.concatenate([add_low(keep_l, got_l), add_low(keep_r, got_r)], axis=-1)
    sums = [bits[:early], bits[early:cross], bits[cross : cross + 1], bits[cross + 1 : cross + 2]]
    side = scatter_pairs(side, bits[early:cross], early)
    beside = gather_step(beside, 0, y_axis, y_bit)
    chan_grad = sum_pairs(chan_grad, sums[0])
    side, beside, chan_grad = together(side, beside, chan_grad)
    side = scatter_pairs(side, bits[:early])
    beside = gather_step(beside, 1, core_axis, core_bit)
    chan_grad = sum_pairs(chan_grad, sums[1])
    side, beside, chan_grad = together(side, beside, chan_grad)
    got = swap(side, y_axis, y_bit)
    chan_grad = sum_pairs(chan_grad, sums[2])
    got, chan_grad = barrier((got, chan_grad))
    side = merge_pair(side, got, 0, y_axis, y_bit)
    got = swap(side, core_axis, core_bit)
    chan_grad = sum_pairs(chan_grad, sums[3])
    side = flat(merge_pair(side, got, 1, core_axis, core_bit))

    beside = beside.astype(f32)
    out_grad = flat(beside[..., :out_rows, :])
    in_grad = jnp.concatenate(
        [
            flat(beside[..., out_rows : out_rows + in_rows, :]),
            flat(beside[..., out_rows + in_rows :, :]),
            side[:, : PROJ - INNER].astype(f32),
        ],
        axis=1,
    )
    in_new, in_mom, in_sec = adamw_step(
        in_weight, in_moment, in_second, in_grad, rate_matrix, decay_matrix
    )
    out_new, out_mom, out_sec = adamw_step(
        out_weight, out_moment, out_second, out_grad, rate_matrix, decay_matrix
    )
    chan_new, chan_mom, chan_sec = adamw_step(
        channels, channel_moment, channel_second, chan_grad, rate_channel, 0.0
    )
    return (
        block[None],
        token_grad,
        in_new,
        in_mom,
        in_sec,
        out_new,
        out_mom,
        out_sec,
        chan_new,
        chan_mom,
        chan_sec,
    )


def solution(mesh):
    acts = P("dp", "seq", None)
    rows = P("dp", None)
    specs = (acts, acts) + (rows,) * 6 + (P(),) * 3
    return jax.shard_map(local, mesh=mesh, in_specs=specs, out_specs=specs, check_vma=False)
```

```python
import math

import jax
import jax.numpy as jnp
from jax import lax
from jax.experimental import pallas as pl
from jax.experimental.pallas import tpu as pltpu
from jax.sharding import PartitionSpec as P

D = 768
HEADS = 24
HEADDIM = 64
STATE = 128
CONV = 4
STEP = 10
INNER = 1536
XBC = 1792
PROJ = 3352
SIDE = 1920
LANES = 128
CHUNK = 128
ROWS = 32
PAIRS = HEADS // 2
TILES = XBC // LANES
EXTRA = 16

norm_eps = 1e-05
beta_one = 0.9
beta_two = 0.999
adam_eps = 1e-08
rate_matrix = 0.1
rate_channel = 0.5
decay_matrix = 0.1
LOG2E = 1.0 / math.log(2.0)
VMEM = 56 * 1024 * 1024

f32 = jnp.float32
bf16 = jnp.bfloat16
NT = (((1,), (1,)), ((), ()))
TN = (((0,), (0,)), ((), ()))


def dot(a, b):
    return jnp.dot(a, b, preferred_element_type=f32)


def dot_nt(a, b):
    return lax.dot_general(a, b, NT, preferred_element_type=f32)


def dot_tn(a, b):
    return lax.dot_general(a, b, TN, preferred_element_type=f32)


def sigmoid(v):
    return 0.5 * jnp.tanh(0.5 * v) + 0.5


def halves(v):
    high = v.astype(bf16)
    return high, (v - high.astype(f32)).astype(bf16)


def running(mask, v):
    high, rest = halves(v)
    left = (v - high.astype(f32) - rest.astype(f32)).astype(bf16)
    parts = dot(jnp.where(mask, 1.0, 0.0).astype(bf16), jnp.concatenate([high, rest, left], axis=1))
    return parts[:, :LANES] + parts[:, LANES : 2 * LANES] + parts[:, 2 * LANES :]


def expand(v, spread):
    high, rest = halves(v)
    return dot(jnp.concatenate([high, rest], axis=1), spread)


def fold(v):
    return jnp.sum(v.reshape(v.shape[0] // 8, 8, v.shape[1]), axis=0)


def lane(i):
    return slice(i * LANES, (i + 1) * LANES)


def iota(shape, dim):
    return lax.broadcasted_iota(jnp.int32, shape, dim)


def tri(lower):
    rows, cols = iota((CHUNK, CHUNK), 0), iota((CHUNK, CHUNK), 1)
    return (rows >= cols) if lower else (rows <= cols)


def conv_rows(convp, tile):
    return [jnp.broadcast_to(convp[k : k + 1, lane(tile)], (ROWS, LANES)) for k in range(CONV + 1)]


def conv_pre(shifted, proj, weights, tile, part):
    cols = lane(tile)
    taps = [
        shifted[k * CHUNK + part.start : k * CHUNK + part.stop, cols] for k in range(CONV - 1)
    ] + [proj[part, cols].astype(f32)]
    pre = taps[0] * weights[0] + weights[CONV]
    for k in range(1, CONV):
        pre = pre + taps[k] * weights[k]
    return pre, taps


def pieces():
    return [(start, slice(start, start + ROWS)) for start in range(0, CHUNK, ROWS)]


def pair_stack(v):
    side = iota(v.shape, 1) < HEADDIM
    zero = jnp.zeros_like(v)
    return jnp.concatenate([jnp.where(side, v, zero), jnp.where(side, zero, v)], axis=0)


def conv_state_kernel(
    proj, halo, convp, headp, spread, shifts, x_out, bc_out, u_out, cum_out, cumt_out, dt_out, hst_out,
    pfx_out, send_out, ext, shifted, state, scaled, total,
):
    step = pl.program_id(0)

    @pl.when(step == 0)
    def _():
        ext[0:16, :] = halo[...]
        state[...] = jnp.zeros_like(state)
        total[...] = jnp.zeros_like(total)

    @pl.when(step > 0)
    def _():
        ext[0:16, :] = ext[CHUNK : CHUNK + 16, :]

    ext[16:, :] = proj[:, :XBC]
    shifted[...] = dot(shifts[...], ext[...])
    raw = proj[:, XBC:].astype(f32) + headp[0:1, :]
    steps = jnp.maximum(raw, 0.0) + jnp.log1p(jnp.exp(-jnp.abs(raw)))
    log_decay = steps * (headp[1:2, :] * (-LOG2E))
    cum = running(tri(True), log_decay)
    cum_out[...] = cum
    cumt_out[...] = jnp.transpose(cum)[0:32, :]
    dt_out[...] = steps
    last = cum[CHUNK - 1 : CHUNK, :]
    decayed = jnp.broadcast_to(jnp.exp2(last), (8, LANES))
    wide = expand(jnp.concatenate([steps, jnp.exp2(last - cum), decayed], axis=0), spread[...])
    steps_wide, tail_wide = wide[:CHUNK], wide[CHUNK : 2 * CHUNK]
    decay = wide[2 * CHUNK : 2 * CHUNK + 1]
    for tile in range(TILES):
        cols = lane(tile)
        weights = conv_rows(convp, tile)
        for _, part in pieces():
            pre, _ = conv_pre(shifted, proj, weights, tile, part)
            value = (pre * sigmoid(pre)).astype(bf16)
            if tile < PAIRS:
                x_out[part, cols] = value
                u = (value.astype(f32) * steps_wide[part, cols]).astype(bf16)
                u_out[part, cols] = u
                scaled[part, cols] = (u.astype(f32) * tail_wide[part, cols]).astype(bf16)
            else:
                bc_out[part, lane(tile - PAIRS)] = value
    new_state = state[...] * decay + dot_tn(bc_out[:, :STATE], scaled[...])
    state[...] = new_state
    hst_out[0] = new_state
    new_total = total[...] + jnp.broadcast_to(last, (8, LANES))
    total[...] = new_total
    pfx_out[0] = new_total

    @pl.when(step == pl.num_programs(0) - 1)
    def _():
        send_out[:STATE, :] = new_state.astype(bf16)
        row = iota((EXTRA, LANES), 0)
        wide = jnp.broadcast_to(new_total[0:1, :], (EXTRA, LANES))
        high, rest = halves(wide)
        left = (wide - high.astype(f32) - rest.astype(f32)).astype(bf16)
        parts = jnp.where(
            row == 0,
            high.astype(f32),
            jnp.where(row == 1, rest.astype(f32), jnp.where(row == 2, left.astype(f32), 0.0)),
        )
        send_out[STATE:, :] = dot(parts.astype(bf16), spread[:LANES, :]).astype(bf16)


def within_kernel(u, bc, cum, cumt, y_out, weights):
    scores = jnp.where(tri(True), dot_nt(bc[:, STATE:], bc[:, :STATE]), 0.0)
    for _, part in pieces():
        rows_cum = cum[part, :]
        rows_scores = scores[part]
        for head in range(HEADS):
            gap = rows_cum[:, head : head + 1] - cumt[head : head + 1, :]
            weights[part, lane(head)] = (jnp.exp2(jnp.minimum(gap, 0.0)) * rows_scores).astype(bf16)
    for pair in range(PAIRS):
        both = slice(2 * pair * LANES, 2 * (pair + 1) * LANES)
        y_out[:, lane(pair)] = dot(weights[:, both], pair_stack(u[:, lane(pair)]))


def arrived(gathered, logs, rank, groups, later):
    sums = [
        jnp.sum(logs[g].astype(f32), axis=0, keepdims=True) for g in range(groups)
    ]
    entered = jnp.zeros((STATE, INNER), f32)
    for g in range(groups):
        between = jnp.zeros((1, INNER), f32)
        for s in range(groups):
            if (s < g) if later else (s > g):
                inside = (s > rank) if later else (s < rank)
                between = between + jnp.where(inside, sums[s], 0.0)
        counts = (g > rank) if later else (g < rank)
        weight = jnp.where(counts, jnp.exp2(between), 0.0)
        entered = entered + gathered[g].astype(f32) * weight
    return entered


def gate_kernel(
    groups, rank, y_in, x, bc, cum, hst, gathered, logs, gate, tok, cot, wout, spread, rows,
    block_out, hidden_out, y_out, dy_out, dgate_out, dcc_out, ust_out, glocal_out, ng_out, h0_out,
    prefix, h0, hg_all, mixed_all, dy_scaled,
):
    step = pl.program_id(0)

    @pl.when(step == 0)
    def _():
        value = arrived(gathered, logs, rank[0], groups, False)
        h0[...] = value
        h0_out[...] = value
        prefix[...] = jnp.zeros_like(prefix)
        glocal_out[...] = jnp.zeros_like(glocal_out)
        ng_out[...] = jnp.zeros_like(ng_out)

    wide = expand(jnp.exp2(jnp.concatenate([cum[...], prefix[...]], axis=0)), spread[...])
    grown, start = wide[:CHUNK], wide[CHUNK : CHUNK + 1]
    state = h0[...] * start + jnp.where(step > 0, hst[0], 0.0)
    state_low = state.astype(bf16)
    carried = dot(bc[:, STATE:], state_low)
    hg_all[...] = dot_nt(cot[...], wout[...])
    gain, skip = rows[0:1, :], rows[1:2, :]
    for _, part in pieces():
        squares = jnp.zeros((ROWS, LANES), f32)
        cross = jnp.zeros((ROWS, LANES), f32)
        for tile in range(PAIRS):
            cols = lane(tile)
            y = y_in[part, cols] + carried[part, cols] * grown[part, cols]
            y_out[part, cols] = y
            mixed = (y + skip[:, cols] * x[part, cols].astype(f32)).astype(bf16)
            mixed_all[part, cols] = mixed
            gate_val = gate[part, cols].astype(f32)
            gated = mixed.astype(f32) * (gate_val * sigmoid(gate_val))
            squares = squares + gated * gated
            cross = cross + gated * (hg_all[part, cols] * gain[:, cols])
        mean = jnp.sum(squares, axis=1, keepdims=True) * (1.0 / INNER)
        scale = lax.rsqrt(mean + norm_eps)
        cross_mean = jnp.sum(cross, axis=1, keepdims=True) * (1.0 / INNER) * scale * scale * scale
        scale = jnp.broadcast_to(scale, (ROWS, LANES))
        cross_mean = jnp.broadcast_to(cross_mean, (ROWS, LANES))
        for tile in range(PAIRS):
            cols = lane(tile)
            gate_val = gate[part, cols].astype(f32)
            sig = sigmoid(gate_val)
            silu = gate_val * sig
            mixed = mixed_all[part, cols].astype(f32)
            gated = mixed * silu
            normal = gated * scale
            hidden_out[part, cols] = (normal * gain[:, cols]).astype(bf16)
            grad = hg_all[part, cols]
            ng_out[:, cols] += fold(grad * normal)
            dgated = grad * gain[:, cols] * scale - gated * cross_mean
            dgate_out[part, cols] = (dgated * mixed * (sig + silu * (1.0 - sig))).astype(bf16)
            dy = (dgated * silu).astype(bf16)
            dy_out[part, cols] = dy
            dy_scaled[part, cols] = (dy.astype(f32) * grown[part, cols]).astype(bf16)
    block_out[...] = tok[...].astype(f32) + dot(hidden_out[...], wout[...])
    update = dot_tn(bc[:, STATE:], dy_scaled[...])
    ust_out[0] = update
    glocal_out[...] += update * start
    dcc_out[...] = dot_nt(dy_scaled[...], state_low)
    prefix[...] += jnp.broadcast_to(cum[CHUNK - 1 : CHUNK, :], (8, LANES))


def within_back_kernel(u, dy, bc, cum, cumt, dxs_out, dbc_out, weights, products, low):
    upper = tri(False)
    scores = jnp.where(upper, dot_nt(bc[:, :STATE], bc[:, STATE:]), 0.0)
    for pair in range(PAIRS):
        both = slice(2 * pair * LANES, 2 * (pair + 1) * LANES)
        products[:, both] = dot_nt(u[:, lane(pair)], pair_stack(dy[:, lane(pair)]))
    for _, part in pieces():
        rows_cum = cum[part, :]
        rows_scores = scores[part]
        total = jnp.zeros((ROWS, LANES), f32)
        for head in range(HEADS):
            gap = cumt[head : head + 1, :] - rows_cum[:, head : head + 1]
            decay = jnp.exp2(jnp.minimum(gap, 0.0))
            weights[part, lane(head)] = (decay * rows_scores).astype(bf16)
            total = total + decay * products[part, lane(head)]
        low[part, :] = jnp.where(upper[part], total, 0.0).astype(bf16)
    for pair in range(PAIRS):
        both = slice(2 * pair * LANES, 2 * (pair + 1) * LANES)
        dxs_out[:, lane(pair)] = dot(weights[:, both], pair_stack(dy[:, lane(pair)]))
    dbc_out[:, :STATE] = dot(low[...], bc[:, STATE:])
    dbc_out[:, STATE:] = dot_tn(low[...], bc[:, :STATE])


def back_kernel(
    groups, rank, dxs, dy, x, u, y, bc, dbc, dcc, cum, dt, hst, pfx, h0, gathered, logs, ust, proj,
    before, halo, convp, headp, spread, collect, rows, shifts, ahead,
    pg_out, first_out, tail_out, wg_out, hg_out, skip_out,
    gstate, ext, shifted, dpres, dlow, scaled, prod,
):
    step = pl.program_id(0)
    chunk = pl.num_programs(0) - 1 - step

    @pl.when(step == 0)
    def _():
        gstate[...] = arrived(gathered, logs, rank[0], groups, True)
        dlow[CHUNK:, :] = jnp.zeros((16, XBC), bf16)
        wg_out[...] = jnp.zeros_like(wg_out)
        hg_out[...] = jnp.zeros_like(hg_out)
        skip_out[...] = jnp.zeros_like(skip_out)

    @pl.when(step > 0)
    def _():
        dlow[CHUNK:, :] = dlow[0:16, :]

    @pl.when(chunk == 0)
    def _():
        ext[0:16, :] = halo[...]

    @pl.when(chunk > 0)
    def _():
        ext[0:16, :] = before[:, :XBC]

    ext[16:, :] = proj[:, :XBC]
    shifted[...] = dot(shifts[...], ext[...])
    grad_state = gstate[...]
    grad_low = grad_state.astype(bf16)
    last = cum[CHUNK - 1 : CHUNK, :]
    decayed = jnp.broadcast_to(jnp.exp2(last), (8, LANES))
    wide = expand(
        jnp.concatenate([jnp.exp2(last - cum[...]), dt[...], decayed, jnp.exp2(pfx[0])], axis=0),
        spread[...],
    )
    tail_wide, steps_wide = wide[:CHUNK], wide[CHUNK : 2 * CHUNK]
    decay = wide[2 * CHUNK : 2 * CHUNK + 1]
    end = wide[2 * CHUNK + 8 : 2 * CHUNK + 9]
    reach = dot(bc[:, :STATE], grad_low)

    def conv_back(tile, grad_of):
        cols = lane(tile)
        weights = conv_rows(convp, tile)
        sums = [jnp.zeros((8, LANES), f32) for _ in range(CONV + 1)]
        for _, part in pieces():
            grad = grad_of(part)
            pre, taps = conv_pre(shifted, proj, weights, tile, part)
            sig = sigmoid(pre)
            dpre = grad * (sig + pre * sig * (1.0 - sig))
            dpres[part, cols] = dpre
            dlow[part, cols] = dpre.astype(bf16)
            sums = [total + fold(dpre * tap) for total, tap in zip(sums, taps)] + [
                sums[CONV] + fold(dpre)
            ]

        for k in range(CONV + 1):
            wg_out[8 * k : 8 * k + 8, cols] += sums[k]

    for tile in range(PAIRS):
        cols = lane(tile)
        rest_cols = slice(INNER + tile * LANES, INNER + (tile + 1) * LANES)
        skip_row = jnp.broadcast_to(rows[1:2, cols], (ROWS, LANES))
        skips = []

        def grad_of(part, cols=cols, rest_cols=rest_cols, skip_row=skip_row, skips=skips):
            below = slice(CHUNK + part.start, CHUNK + part.stop)
            dxs_full = dxs[part, cols] + tail_wide[part, cols] * reach[part, cols]
            uf = u[part, cols].astype(f32)
            dyf = dy[part, cols].astype(f32)
            scaled[part, cols] = (uf * tail_wide[part, cols]).astype(bf16)
            q = uf * dxs_full
            prod[part, cols], prod[part, rest_cols] = halves(q)
            prod[below, cols], prod[below, rest_cols] = halves(dyf * y[part, cols] - q)
            skips.append(fold(dyf * x[part, cols].astype(f32)))
            return skip_row * dyf + steps_wide[part, cols] * dxs_full

        conv_back(tile, grad_of)
        skip_out[:, cols] += sum(skips[1:], skips[0])
    dwrite = dot_nt(scaled[...], grad_low)
    conv_back(PAIRS, lambda part: dbc[part, :STATE] + dwrite[part])
    conv_back(PAIRS + 1, lambda part: dbc[part, STATE:] + dcc[part, :])
    first_out[...] = dpres[0:8, :]
    shifted[...] = dot(ahead[...], dlow[...])
    for tile in range(TILES):
        cols = lane(tile)
        weights = conv_rows(convp, tile)
        for _, part in pieces():
            source = dpres[part, cols] * weights[CONV - 1]
            for k in range(CONV - 1):
                block = (CONV - 2 - k) * CHUNK
                source = source + shifted[block + part.start : block + part.stop, cols] * weights[k]
            pg_out[part, cols] = source.astype(bf16)
            dpres[part, cols] = source

    @pl.when(step == 0)
    def _():
        tail_out[...] = dpres[CHUNK - 8 :, :]


    meet = fold(grad_state * (hst[0] + h0[...] * end))
    meet = jnp.concatenate([meet, jnp.zeros_like(meet)], axis=0)
    high, rest = halves(meet)
    prod[2 * CHUNK :, :INNER] = high
    prod[2 * CHUNK :, INNER:] = rest
    heads = dot(prod[...], collect[...])
    q_heads, gap_heads = heads[:CHUNK], heads[CHUNK : 2 * CHUNK]
    meet_heads = jnp.sum(heads[2 * CHUNK :], axis=0, keepdims=True)
    dlog = running(tri(False), gap_heads) + meet_heads
    sig = sigmoid(proj[:, XBC:].astype(f32) + headp[0:1, :])
    steps = dt[...]
    ratio = jnp.where(steps > 1e-30, sig / jnp.maximum(steps, 1e-30), 1.0)
    raw_grad = q_heads * ratio - dlog * headp[1:2, :] * sig
    pg_out[:, XBC:] = raw_grad.astype(bf16)
    hg_out[0:8, :] += fold(raw_grad)
    hg_out[8:16, :] += fold(dlog * steps * headp[1:2, :]) * (-1.0)
    gstate[...] = grad_state * decay + ust[0]


def swap(v, axis, bit):
    size = lax.axis_size(axis)
    return lax.ppermute(v, axis, [(i, i ^ (1 << bit)) for i in range(size)])


def mesh_bits():
    found = []
    for axis in ("dp", "seq"):
        for bit in reversed(range(lax.axis_size(axis).bit_length() - 1)):
            found.append((axis, bit))
    return found


def mine(axis, bit):
    return (lax.axis_index(axis) >> bit) & 1


def merge_pair(v, other, place, axis, bit):
    second = mine(axis, bit) == 1
    return jnp.stack([jnp.where(second, other, v), jnp.where(second, v, other)], axis=place)


def gather_step(v, place, axis, bit):
    return merge_pair(v, swap(v, axis, bit), place, axis, bit)


def gather_pairs(v, bits, lead=0):
    for place, (axis, bit) in enumerate(bits):
        v = gather_step(v, lead + place, axis, bit)
    return v


def flat(v):
    return v.reshape(-1, v.shape[-1])


def blocks(v, bits):
    return v.reshape((2,) * len(bits) + (v.shape[0] >> len(bits), v.shape[1]))


def split_pair(v, place, axis, bit):
    own = mine(axis, bit)
    keep = lax.dynamic_index_in_dim(v, own, place, keepdims=False)
    give = lax.dynamic_index_in_dim(v, 1 - own, place, keepdims=False)
    return keep, give


def add_low(keep, got):
    return (keep.astype(f32) + got.astype(f32)).astype(keep.dtype)


def scatter_step(v, place, axis, bit):
    keep, give = split_pair(v, place, axis, bit)
    return add_low(keep, swap(give, axis, bit))


def scatter_pairs(v, bits, lead=0):
    for place in reversed(range(len(bits))):
        v = scatter_step(v, lead + place, *bits[place])
    return v


def sum_pairs(v, bits):
    for axis, bit in bits:
        v = v + swap(v, axis, bit)
    return v


def full(shape):
    return pl.BlockSpec(shape, lambda c: (0,) * len(shape))


def by_chunk(width, rows=CHUNK):
    return pl.BlockSpec((rows, width), lambda c: (c, 0))


def shape(dims, dtype):
    return jax.ShapeDtypeStruct(dims, dtype)


def params():
    return pltpu.CompilerParams(dimension_semantics=("arbitrary",), vmem_limit_bytes=VMEM)


def cost(flops, moved):
    return pl.CostEstimate(flops=flops, bytes_accessed=moved, transcendentals=0)


def spread_map():
    heads = jnp.arange(LANES)[:, None]
    cols = jnp.arange(INNER)[None, :] // HEADDIM
    once = (heads == cols).astype(bf16)
    return jnp.concatenate([once, once], axis=0)


def shift_map(first):
    rows = jnp.arange((CONV - 1) * CHUNK)
    picked = rows % CHUNK + rows // CHUNK + first
    return (picked[:, None] == jnp.arange(CHUNK + 16)[None, :]).astype(bf16)


def unpack_channels(channels):
    pieces = []
    offset = 0
    for piece_len in (D, INNER, XBC * CONV, XBC, HEADS, HEADS, HEADS):
        pieces.append(channels[offset : offset + piece_len])
        offset = offset + piece_len
    pre_gain, norm_gain, conv_flat, conv_bias, step_bias, rate_log, skip_gain = pieces
    return (
        pre_gain,
        norm_gain,
        conv_flat.reshape(XBC, CONV),
        conv_bias,
        step_bias,
        rate_log,
        skip_gain,
    )


def pre_norm(tok_vals, pre_gain):
    return (
        tok_vals * lax.rsqrt(jnp.mean(tok_vals * tok_vals, -1, keepdims=True) + norm_eps) * pre_gain
    )


def adamw_step(weight, moment, second, gradient, step_rate, decay_rate):
    moment_next = beta_one * moment + (1.0 - beta_one) * gradient
    second_next = beta_two * second + (1.0 - beta_two) * gradient * gradient
    first_fix = 1.0 - beta_one**STEP
    second_fix = 1.0 - beta_two**STEP
    update = moment_next / first_fix / (jnp.sqrt(second_next / second_fix) + adam_eps)
    return (weight - step_rate * (update + decay_rate * weight), moment_next, second_next)


def local(
    tokens,
    cotangent,
    in_weight,
    in_moment,
    in_second,
    out_weight,
    out_moment,
    out_second,
    channels,
    channel_moment,
    channel_second,
):
    groups = lax.axis_size("seq")
    bits = mesh_bits()
    seq_bits = [(axis, bit) for axis, bit in bits if axis == "seq"]
    seq_rank = lax.axis_index("seq")
    rank = seq_rank.astype(jnp.int32).reshape(1)
    pre_gain, norm_gain, conv_weight, conv_bias, step_bias, rate_log, skip_gain = unpack_channels(
        channels
    )
    tok_low = tokens[0]
    cot_low = cotangent[0]
    count = tok_low.shape[0]
    chunks = count // CHUNK

    def quarter(weight):
        size = weight.shape[0] // groups
        return lax.dynamic_slice_in_dim(weight, seq_rank * size, size, 0).astype(bf16)

    in_part = quarter(in_weight)
    side_part = jnp.pad(in_part[:, INNER:], ((0, 0), (0, SIDE + INNER - PROJ)))
    out_rows = out_weight.shape[0] // groups
    in_rows = in_weight.shape[0] // groups
    beside = jnp.concatenate(
        [quarter(out_weight), in_part[:, :D], in_part[:, D:INNER]], axis=0
    )
    barrier = lax.optimization_barrier
    cross = len(bits) - 3
    (x_axis, x_bit), (y_axis, y_bit), (core_axis, core_bit) = bits[cross:]
    side = gather_pairs(side_part, bits[:cross])
    side, beside = barrier((side, beside))
    half = SIDE // 256 * 128
    left, right = side[..., :half], side[..., half:]
    got_l, got_r = swap(left, x_axis, x_bit), swap(right, y_axis, y_bit)
    early = cross // 2
    beside = gather_pairs(beside, bits[:early])
    left = merge_pair(left, got_l, cross, x_axis, x_bit)
    right = merge_pair(right, got_r, cross, y_axis, y_bit)
    got_l, got_r = swap(left, y_axis, y_bit), swap(right, x_axis, x_bit)
    beside, left, right = barrier((beside, left, right))
    beside = gather_pairs(beside, bits[early:cross], early)
    left = merge_pair(left, got_l, cross + 1, y_axis, y_bit)
    right = merge_pair(right, got_r, cross, x_axis, x_bit)
    got_l, got_r = swap(left, core_axis, core_bit), swap(right, core_axis, core_bit)
    beside, left, right = barrier((beside, left, right))
    got_b = swap(beside, x_axis, x_bit)
    left = merge_pair(left, got_l, cross + 2, core_axis, core_bit)
    right = merge_pair(right, got_r, cross + 2, core_axis, core_bit)
    full_side = jnp.concatenate([flat(left), flat(right)], axis=1)

    forward = [(s, s + 1) for s in range(groups - 1)]
    backward = [(s + 1, s) for s in range(groups - 1)]
    tok_halo = lax.ppermute(tok_low[count - 16 :], "seq", forward)
    halo_norm = pre_norm(tok_halo.astype(f32), pre_gain).astype(bf16)
    tok_vals = tok_low.astype(f32)
    normed_low = pre_norm(tok_vals, pre_gain).astype(bf16)

    convp = jnp.concatenate(
        [conv_weight.T, conv_bias[None, :], jnp.zeros((3, XBC), f32)], axis=0
    )
    pad_heads = lambda v: jnp.pad(v, (0, LANES - HEADS))[None, :]
    headp = jnp.concatenate(
        [pad_heads(step_bias), pad_heads(jnp.exp(rate_log)), jnp.zeros((6, LANES), f32)], axis=0
    )
    rows = jnp.concatenate(
        [norm_gain[None, :], jnp.repeat(skip_gain, HEADDIM)[None, :], jnp.zeros((6, INNER), f32)],
        axis=0,
    )
    spread = spread_map()
    collect = jnp.concatenate([spread[:LANES].T, spread[:LANES].T], axis=0)

    proj = dot(normed_low, full_side).astype(bf16)
    halo = dot(halo_norm, full_side[:, :XBC]).astype(bf16)
    proj, halo, got_b = barrier((proj, halo, got_b))
    beside = merge_pair(beside, got_b, cross, x_axis, x_bit)
    got_b = swap(beside, y_axis, y_bit)

    x, bc, u, cum, cumt, dt, hst, pfx, send = pl.pallas_call(
        conv_state_kernel,
        grid=(chunks,),
        in_specs=[
            by_chunk(SIDE), full((16, XBC)), full((8, XBC)), full((8, LANES)),
            full((2 * LANES, INNER)), full(((CONV - 1) * CHUNK, CHUNK + 16)),
        ],
        out_specs=[
            by_chunk(INNER), by_chunk(2 * STATE), by_chunk(INNER), by_chunk(LANES),
            pl.BlockSpec((32, CHUNK), lambda c: (0, c)), by_chunk(LANES),
            pl.BlockSpec((1, STATE, INNER), lambda c: (c, 0, 0)),
            pl.BlockSpec((1, 8, LANES), lambda c: (c, 0, 0)),
            full((STATE + EXTRA, INNER)),
        ],
        out_shape=[
            shape((count, INNER), bf16), shape((count, 2 * STATE), bf16),
            shape((count, INNER), bf16), shape((count, LANES), f32), shape((32, count), f32),
            shape((count, LANES), f32), shape((chunks, STATE, INNER), f32),
            shape((chunks, 8, LANES), f32), shape((STATE + EXTRA, INNER), bf16),
        ],
        scratch_shapes=[
            pltpu.VMEM((CHUNK + 16, XBC), bf16), pltpu.VMEM(((CONV - 1) * CHUNK, XBC), f32),
            pltpu.VMEM((STATE, INNER), f32), pltpu.VMEM((CHUNK, INNER), bf16),
            pltpu.VMEM((8, LANES), f32),
        ],
        compiler_params=params(),
        cost_estimate=cost(24 * 10**9, 24 * 2**20),
        name="conv_state",
    )(proj, halo, convp, headp, spread, shift_map(13))

    states = lax.all_gather(send, "seq", axis=0, tiled=False)
    x, bc, u, cum, cumt, dt, hst, pfx, got_b = barrier(
        (x, bc, u, cum, cumt, dt, hst, pfx, got_b)
    )
    beside = merge_pair(beside, got_b, cross + 1, y_axis, y_bit)
    got_b = swap(beside, core_axis, core_bit)

    y_within = pl.pallas_call(
        within_kernel,
        grid=(chunks,),
        in_specs=[
            by_chunk(INNER), by_chunk(2 * STATE), by_chunk(LANES),
            pl.BlockSpec((32, CHUNK), lambda c: (0, c)),
        ],
        out_specs=by_chunk(INNER),
        out_shape=shape((count, INNER), f32),
        scratch_shapes=[pltpu.VMEM((CHUNK, HEADS * LANES), bf16)],
        compiler_params=params(),
        cost_estimate=cost(11 * 10**9, 16 * 2**20),
        name="within",
    )(u, bc, cum, cumt)
    y_within, got_b = barrier((y_within, got_b))
    beside = merge_pair(beside, got_b, cross + 2, core_axis, core_bit)
    full_out = flat(beside[..., :out_rows, :])
    full_gate = jnp.concatenate(
        [
            flat(beside[..., out_rows : out_rows + in_rows, :]),
            flat(beside[..., out_rows + in_rows :, :]),
        ],
        axis=1,
    )
    gate = dot(normed_low, full_gate).astype(bf16)

    gathered_spec = full((groups, STATE, INNER))
    logs_spec = pl.BlockSpec((groups, EXTRA, INNER), lambda c: (0, STATE // EXTRA, 0))
    smem = pl.BlockSpec(memory_space=pltpu.SMEM)

    def gate_call(*refs):
        gate_kernel(groups, *refs)

    block, hidden, y, dy, dgate, dcc, ust, glocal, ng, h0 = pl.pallas_call(
        gate_call,
        grid=(chunks,),
        in_specs=[
            smem, by_chunk(INNER), by_chunk(INNER), by_chunk(2 * STATE), by_chunk(LANES),
            pl.BlockSpec((1, STATE, INNER), lambda c: (jnp.maximum(c - 1, 0), 0, 0)),
            gathered_spec, logs_spec, by_chunk(INNER), by_chunk(D), by_chunk(D),
            full((INNER, D)), full((2 * LANES, INNER)), full((8, INNER)),
        ],
        out_specs=[
            by_chunk(D), by_chunk(INNER), by_chunk(INNER), by_chunk(INNER), by_chunk(INNER),
            by_chunk(LANES), pl.BlockSpec((1, STATE, INNER), lambda c: (c, 0, 0)),
            full((STATE, INNER)), full((8, INNER)), full((STATE, INNER)),
        ],
        out_shape=[
            shape((count, D), f32), shape((count, INNER), bf16), shape((count, INNER), f32),
            shape((count, INNER), bf16), shape((count, INNER), bf16), shape((count, LANES), f32),
            shape((chunks, STATE, INNER), f32), shape((STATE, INNER), f32), shape((8, INNER), f32),
            shape((STATE, INNER), f32),
        ],
        scratch_shapes=[
            pltpu.VMEM((8, LANES), f32), pltpu.VMEM((STATE, INNER), f32),
            pltpu.VMEM((CHUNK, INNER), f32), pltpu.VMEM((CHUNK, INNER), bf16),
            pltpu.VMEM((CHUNK, INNER), bf16),
        ],
        compiler_params=params(),
        cost_estimate=cost(30 * 10**9, 48 * 2**20),
        name="gate_norm",
    )(
        rank, y_within, x, bc, cum, hst, states, states, gate, tok_low, cot_low, full_out, spread,
        rows,
    )

    grads = lax.all_gather(glocal.astype(bf16), "seq", axis=0, tiled=False)

    def product(left, right):
        return lax.dot_general(left, right, TN, preferred_element_type=f32).astype(bf16)

    beside = jnp.concatenate(
        [
            blocks(product(hidden, cot_low), bits),
            blocks(product(normed_low, dgate[:, :D]), bits),
            blocks(product(normed_low, dgate[:, D:]), bits),
        ],
        axis=-2,
    )
    keep_b, give_b = split_pair(beside, cross + 2, core_axis, core_bit)
    got_b = swap(give_b, core_axis, core_bit)
    anywhere = pl.BlockSpec(memory_space=pl.ANY)

    def within_back_call(u, dy, bc, cum, cumt, sent, *rest):
        within_back_kernel(u, dy, bc, cum, cumt, *rest)

    dxs, dbc = pl.pallas_call(
        within_back_call,
        grid=(chunks,),
        in_specs=[
            by_chunk(INNER), by_chunk(INNER), by_chunk(2 * STATE), by_chunk(LANES),
            pl.BlockSpec((32, CHUNK), lambda c: (0, c)), anywhere,
        ],
        out_specs=[by_chunk(INNER), by_chunk(2 * STATE)],
        out_shape=[shape((count, INNER), f32), shape((count, 2 * STATE), f32)],
        scratch_shapes=[
            pltpu.VMEM((CHUNK, HEADS * LANES), bf16), pltpu.VMEM((CHUNK, HEADS * LANES), f32),
            pltpu.VMEM((CHUNK, LANES), bf16),
        ],
        compiler_params=params(),
        cost_estimate=cost(12 * 10**9, 16 * 2**20),
        name="within_back",
    )(u, dy, bc, cum, cumt, give_b)

    got_b, dxs, dbc = barrier((got_b, dxs, dbc))
    keep_b, give_b = split_pair(add_low(keep_b, got_b), cross + 1, y_axis, y_bit)
    got_b = swap(give_b, y_axis, y_bit)

    def back(width, height=CHUNK):
        return pl.BlockSpec((height, width), lambda c: (chunks - 1 - c, 0))

    def back_three(height):
        return pl.BlockSpec((1, height, INNER), lambda c: (chunks - 1 - c, 0, 0))

    def back_call(sent, *refs):
        back_kernel(groups, *refs)

    per = CHUNK // 16
    pg, first, tail, wg, hgr, skip = pl.pallas_call(
        back_call,
        grid=(chunks,),
        in_specs=[
            anywhere, smem, back(INNER), back(INNER), back(INNER), back(INNER), back(INNER), back(2 * STATE),
            back(2 * STATE), back(LANES), back(LANES), back(LANES), back_three(STATE),
            pl.BlockSpec((1, 8, LANES), lambda c: (chunks - 1 - c, 0, 0)),
            full((STATE, INNER)), gathered_spec, logs_spec, back_three(STATE), back(SIDE),
            pl.BlockSpec(
                (16, SIDE), lambda c: (jnp.maximum((chunks - 1 - c) * per - 1, 0), 0)
            ),
            full((16, XBC)), full((8, XBC)), full((8, LANES)), full((2 * LANES, INNER)),
            full((2 * INNER, LANES)), full((8, INNER)),
            full(((CONV - 1) * CHUNK, CHUNK + 16)), full(((CONV - 1) * CHUNK, CHUNK + 16)),
        ],
        out_specs=[
            back(SIDE), full((8, XBC)), full((8, XBC)), full((40, XBC)), full((16, LANES)),
            full((8, INNER)),
        ],
        out_shape=[
            shape((count, SIDE), bf16), shape((8, XBC), f32), shape((8, XBC), f32),
            shape((40, XBC), f32), shape((16, LANES), f32), shape((8, INNER), f32),
        ],
        scratch_shapes=[
            pltpu.VMEM((STATE, INNER), f32), pltpu.VMEM((CHUNK + 16, XBC), bf16),
            pltpu.VMEM(((CONV - 1) * CHUNK, XBC), f32), pltpu.VMEM((CHUNK, XBC), f32),
            pltpu.VMEM((CHUNK + 16, XBC), bf16), pltpu.VMEM((CHUNK, INNER), bf16),
            pltpu.VMEM((2 * CHUNK + 16, 2 * INNER), bf16),
        ],
        compiler_params=params(),
        cost_estimate=cost(47 * 10**9, 48 * 2**20),
        name="mixer_back",
    )(
        give_b, rank, dxs, dy, x, u, y, bc, dbc, dcc, cum, dt, hst, pfx, h0, grads, states, ust, proj, proj,
        halo, convp, headp, spread, collect, rows, shift_map(13), shift_map(1),
    )

    got_b, pg, first, tail, wg, hgr, skip = barrier((got_b, pg, first, tail, wg, hgr, skip))
    keep_b, give_b = split_pair(add_low(keep_b, got_b), cross, x_axis, x_bit)
    got_b = swap(give_b, x_axis, x_bit)
    after = lax.ppermute(first, "seq", backward)
    fixes = [jnp.zeros((5, XBC), f32)]
    for m in range(CONV - 1):
        fix = convp[0] * after[m]
        for k in range(1, m + 1):
            fix = fix + convp[k] * after[m - k]
        fixes.append(fix[None, :])
    tail_low = (tail + jnp.concatenate(fixes, axis=0)).astype(bf16)
    pg = lax.dynamic_update_slice(pg, tail_low, (count - 8, 0))

    left = blocks(product(normed_low, pg[:, :half]), bits)
    right = blocks(product(normed_low, pg[:, half:]), bits)
    keep_l, give_l = split_pair(left, cross + 2, core_axis, core_bit)
    keep_r, give_r = split_pair(right, cross + 2, core_axis, core_bit)
    got_l, got_r = swap(give_l, core_axis, core_bit), swap(give_r, core_axis, core_bit)
    pg, dgate, _, _ = barrier((pg, dgate, give_l, give_r))
    normed_grad = lax.dot_general(dgate, full_gate, NT, preferred_element_type=f32)
    normed_grad = normed_grad + lax.dot_general(pg, full_side, NT, preferred_element_type=f32)
    got_l, got_r, got_b, normed_grad = barrier((got_l, got_r, got_b, normed_grad))
    keep_l, give_l = split_pair(add_low(keep_l, got_l), cross + 1, y_axis, y_bit)
    keep_r, give_r = split_pair(add_low(keep_r, got_r), cross, x_axis, x_bit)
    got_l, got_r = swap(give_l, y_axis, y_bit), swap(give_r, x_axis, x_bit)
    beside = add_low(keep_b, got_b)
    keep_b, give_b = split_pair(beside, cross - 1, *bits[cross - 1])
    got_b = swap(give_b, *bits[cross - 1])
    normed_grad, wg, hgr, skip, ng, _, _ = barrier(
        (normed_grad, wg, hgr, skip, ng, give_l, give_r)
    )
    _, norm_pull = jax.vjp(pre_norm, tok_vals, pre_gain)
    tok_norm_grad, pre_gain_grad = norm_pull(normed_grad)
    token_grad = (cot_low.astype(f32) + tok_norm_grad)[None]
    got_l, got_r, token_grad, pre_gain_grad = barrier((got_l, got_r, token_grad, pre_gain_grad))
    wg_sum = jnp.sum(wg.reshape(5, 8, XBC), axis=1)
    chan_grad = jnp.concatenate(
        [
            pre_gain_grad,
            jnp.sum(ng, axis=0),
            wg_sum[:CONV].T.reshape(-1),
            wg_sum[CONV],
            jnp.sum(hgr[:8, :HEADS], axis=0),
            jnp.sum(hgr[8:, :HEADS], axis=0),
            jnp.sum(skip.reshape(8, HEADS, HEADDIM), axis=(0, 2)),
        ]
    )

    keep_l, give_l = split_pair(add_low(keep_l, got_l), cross, x_axis, x_bit)
    keep_r, give_r = split_pair(add_low(keep_r, got_r), cross, y_axis, y_bit)
    got_l, got_r = swap(give_l, x_axis, x_bit), swap(give_r, y_axis, y_bit)
    sums = [bits[:early], bits[early:cross], bits[cross : cross + 1], bits[cross + 1 : cross + 2]]
    chan_grad = sum_pairs(chan_grad, bits[cross + 2 :])
    got_l, got_r, got_b, chan_grad = barrier((got_l, got_r, got_b, chan_grad))
    side = jnp.concatenate([add_low(keep_l, got_l), add_low(keep_r, got_r)], axis=-1)
    side = scatter_step(side, cross - 1, *bits[cross - 1])
    beside = scatter_pairs(add_low(keep_b, got_b), bits[: cross - 1])
    chan_grad = sum_pairs(chan_grad, sums[0])
    side, beside, chan_grad = barrier((side, beside, chan_grad))
    side = scatter_pairs(side, bits[: cross - 1])
    beside = gather_step(beside, 0, y_axis, y_bit)
    chan_grad = sum_pairs(chan_grad, sums[1])
    side, beside, chan_grad = barrier((side, beside, chan_grad))
    got = swap(side, y_axis, y_bit)
    beside = gather_step(beside, 1, core_axis, core_bit)
    chan_grad = sum_pairs(chan_grad, sums[2])
    got, beside, chan_grad = barrier((got, beside, chan_grad))
    side = merge_pair(side, got, 0, y_axis, y_bit)
    got = swap(side, core_axis, core_bit)
    chan_grad = sum_pairs(chan_grad, sums[3])
    side = flat(merge_pair(side, got, 1, core_axis, core_bit))

    beside = beside.astype(f32)
    out_grad = flat(beside[..., :out_rows, :])
    in_grad = jnp.concatenate(
        [
            flat(beside[..., out_rows : out_rows + in_rows, :]),
            flat(beside[..., out_rows + in_rows :, :]),
            side[:, : PROJ - INNER].astype(f32),
        ],
        axis=1,
    )
    in_new, in_mom, in_sec = adamw_step(
        in_weight, in_moment, in_second, in_grad, rate_matrix, decay_matrix
    )
    out_new, out_mom, out_sec = adamw_step(
        out_weight, out_moment, out_second, out_grad, rate_matrix, decay_matrix
    )
    chan_new, chan_mom, chan_sec = adamw_step(
        channels, channel_moment, channel_second, chan_grad, rate_channel, 0.0
    )
    return (
        block[None],
        token_grad,
        in_new,
        in_mom,
        in_sec,
        out_new,
        out_mom,
        out_sec,
        chan_new,
        chan_mom,
        chan_sec,
    )


def solution(mesh):
    acts = P("dp", "seq", None)
    rows = P("dp", None)
    specs = (acts, acts) + (rows,) * 6 + (P(),) * 3
    return jax.shard_map(local, mesh=mesh, in_specs=specs, out_specs=specs, check_vma=False)
```

```python
import math

import jax
import jax.numpy as jnp
from jax import lax
from jax.experimental import pallas as pl
from jax.experimental.pallas import tpu as pltpu
from jax.sharding import PartitionSpec as P

D = 768
HEADS = 24
HEADDIM = 64
STATE = 128
CONV = 4
STEP = 10
INNER = 1536
XBC = 1792
PROJ = 3352
SIDE = 1920
LANES = 128
CHUNK = 128
ROWS = 32
PAIRS = HEADS // 2
TILES = XBC // LANES
EXTRA = 16

norm_eps = 1e-05
beta_one = 0.9
beta_two = 0.999
adam_eps = 1e-08
rate_matrix = 0.1
rate_channel = 0.5
decay_matrix = 0.1
LOG2E = 1.0 / math.log(2.0)
VMEM = 56 * 1024 * 1024

f32 = jnp.float32
bf16 = jnp.bfloat16
NT = (((1,), (1,)), ((), ()))
TN = (((0,), (0,)), ((), ()))


def dot(a, b):
    return jnp.dot(a, b, preferred_element_type=f32)


def dot_nt(a, b):
    return lax.dot_general(a, b, NT, preferred_element_type=f32)


def dot_tn(a, b):
    return lax.dot_general(a, b, TN, preferred_element_type=f32)


def sigmoid(v):
    return 0.5 * jnp.tanh(0.5 * v) + 0.5


def halves(v):
    high = v.astype(bf16)
    return high, (v - high.astype(f32)).astype(bf16)


def running(mask, v):
    high, rest = halves(v)
    left = (v - high.astype(f32) - rest.astype(f32)).astype(bf16)
    parts = dot(jnp.where(mask, 1.0, 0.0).astype(bf16), jnp.concatenate([high, rest, left], axis=1))
    return parts[:, :LANES] + parts[:, LANES : 2 * LANES] + parts[:, 2 * LANES :]


def expand(v, spread):
    high, rest = halves(v)
    return dot(jnp.concatenate([high, rest], axis=1), spread)


def fold(v):
    return jnp.sum(v.reshape(v.shape[0] // 8, 8, v.shape[1]), axis=0)


def lane(i):
    return slice(i * LANES, (i + 1) * LANES)


def iota(shape, dim):
    return lax.broadcasted_iota(jnp.int32, shape, dim)


def tri(lower):
    rows, cols = iota((CHUNK, CHUNK), 0), iota((CHUNK, CHUNK), 1)
    return (rows >= cols) if lower else (rows <= cols)


def conv_rows(convp, tile):
    return [jnp.broadcast_to(convp[k : k + 1, lane(tile)], (ROWS, LANES)) for k in range(CONV + 1)]


def conv_pre(shifted, proj, weights, tile, part):
    cols = lane(tile)
    taps = [
        shifted[k * CHUNK + part.start : k * CHUNK + part.stop, cols] for k in range(CONV - 1)
    ] + [proj[part, cols].astype(f32)]
    pre = taps[0] * weights[0] + weights[CONV]
    for k in range(1, CONV):
        pre = pre + taps[k] * weights[k]
    return pre, taps


def pieces():
    return [(start, slice(start, start + ROWS)) for start in range(0, CHUNK, ROWS)]


def pair_stack(v):
    side = iota(v.shape, 1) < HEADDIM
    zero = jnp.zeros_like(v)
    return jnp.concatenate([jnp.where(side, v, zero), jnp.where(side, zero, v)], axis=0)


def conv_state_kernel(
    proj, halo, convp, headp, spread, shifts, x_out, bc_out, u_out, cum_out, cumt_out, dt_out, hst_out,
    pfx_out, send_out, ext, shifted, state, scaled, total,
):
    step = pl.program_id(0)

    @pl.when(step == 0)
    def _():
        ext[0:16, :] = halo[...]
        state[...] = jnp.zeros_like(state)
        total[...] = jnp.zeros_like(total)

    @pl.when(step > 0)
    def _():
        ext[0:16, :] = ext[CHUNK : CHUNK + 16, :]

    ext[16:, :] = proj[:, :XBC]
    shifted[...] = dot(shifts[...], ext[...])
    raw = proj[:, XBC:].astype(f32) + headp[0:1, :]
    steps = jnp.maximum(raw, 0.0) + jnp.log1p(jnp.exp(-jnp.abs(raw)))
    log_decay = steps * (headp[1:2, :] * (-LOG2E))
    cum = running(tri(True), log_decay)
    cum_out[...] = cum
    cumt_out[...] = jnp.transpose(cum)[0:32, :]
    dt_out[...] = steps
    last = cum[CHUNK - 1 : CHUNK, :]
    decayed = jnp.broadcast_to(jnp.exp2(last), (8, LANES))
    wide = expand(jnp.concatenate([steps, jnp.exp2(last - cum), decayed], axis=0), spread[...])
    steps_wide, tail_wide = wide[:CHUNK], wide[CHUNK : 2 * CHUNK]
    decay = wide[2 * CHUNK : 2 * CHUNK + 1]
    for tile in range(TILES):
        cols = lane(tile)
        weights = conv_rows(convp, tile)
        for _, part in pieces():
            pre, _ = conv_pre(shifted, proj, weights, tile, part)
            value = (pre * sigmoid(pre)).astype(bf16)
            if tile < PAIRS:
                x_out[part, cols] = value
                u = (value.astype(f32) * steps_wide[part, cols]).astype(bf16)
                u_out[part, cols] = u
                scaled[part, cols] = (u.astype(f32) * tail_wide[part, cols]).astype(bf16)
            else:
                bc_out[part, lane(tile - PAIRS)] = value
    new_state = state[...] * decay + dot_tn(bc_out[:, :STATE], scaled[...])
    state[...] = new_state
    hst_out[0] = new_state
    new_total = total[...] + jnp.broadcast_to(last, (8, LANES))
    total[...] = new_total
    pfx_out[0] = new_total

    @pl.when(step == pl.num_programs(0) - 1)
    def _():
        send_out[:STATE, :] = new_state.astype(bf16)
        row = iota((EXTRA, LANES), 0)
        wide = jnp.broadcast_to(new_total[0:1, :], (EXTRA, LANES))
        high, rest = halves(wide)
        left = (wide - high.astype(f32) - rest.astype(f32)).astype(bf16)
        parts = jnp.where(
            row == 0,
            high.astype(f32),
            jnp.where(row == 1, rest.astype(f32), jnp.where(row == 2, left.astype(f32), 0.0)),
        )
        send_out[STATE:, :] = dot(parts.astype(bf16), spread[:LANES, :]).astype(bf16)


def within_kernel(u, bc, cum, cumt, y_out, weights):
    scores = jnp.where(tri(True), dot_nt(bc[:, STATE:], bc[:, :STATE]), 0.0)
    for _, part in pieces():
        rows_cum = cum[part, :]
        rows_scores = scores[part]
        for head in range(HEADS):
            gap = rows_cum[:, head : head + 1] - cumt[head : head + 1, :]
            weights[part, lane(head)] = (jnp.exp2(jnp.minimum(gap, 0.0)) * rows_scores).astype(bf16)
    for pair in range(PAIRS):
        both = slice(2 * pair * LANES, 2 * (pair + 1) * LANES)
        y_out[:, lane(pair)] = dot(weights[:, both], pair_stack(u[:, lane(pair)]))


def arrived(gathered, logs, rank, groups, later):
    sums = [
        jnp.sum(logs[g].astype(f32), axis=0, keepdims=True) for g in range(groups)
    ]
    entered = jnp.zeros((STATE, INNER), f32)
    for g in range(groups):
        between = jnp.zeros((1, INNER), f32)
        for s in range(groups):
            if (s < g) if later else (s > g):
                inside = (s > rank) if later else (s < rank)
                between = between + jnp.where(inside, sums[s], 0.0)
        counts = (g > rank) if later else (g < rank)
        weight = jnp.where(counts, jnp.exp2(between), 0.0)
        entered = entered + gathered[g].astype(f32) * weight
    return entered


def gate_kernel(
    groups, rank, y_in, x, bc, cum, hst_a, hst_b, gathered, logs, gate, cot, wout, spread, rows,
    hidden_out, y_out, dy_out, dgate_out, dcc_out, ust_out, glocal_out, ng_out, h0_out,
    prefix, h0, hg_all, mixed_all, dy_scaled,
):
    step = pl.program_id(0)

    @pl.when(step == 0)
    def _():
        value = arrived(gathered, logs, rank[0], groups, False)
        h0[...] = value
        h0_out[...] = value
        prefix[...] = jnp.zeros_like(prefix)
        glocal_out[...] = jnp.zeros_like(glocal_out)
        ng_out[...] = jnp.zeros_like(ng_out)

    hg_all[...] = dot_nt(cot[...], wout[...])
    gain, skip = rows[0:1, :], rows[1:2, :]
    for sub in range(2):
        whole = slice(sub * CHUNK, (sub + 1) * CHUNK)
        cum_sub = cum[whole, :]
        wide = expand(jnp.exp2(jnp.concatenate([cum_sub, prefix[...]], axis=0)), spread[...])
        grown, start = wide[:CHUNK], wide[CHUNK : CHUNK + 1]
        before = jnp.where(step > 0, hst_a[0], 0.0) if sub == 0 else hst_b[0]
        state_low = (h0[...] * start + before).astype(bf16)
        read = bc[whole, STATE:]
        carried = dot(read, state_low)
        for first, piece in pieces():
            part = slice(sub * CHUNK + first, sub * CHUNK + first + ROWS)
            squares = jnp.zeros((ROWS, LANES), f32)
            cross = jnp.zeros((ROWS, LANES), f32)
            for tile in range(PAIRS):
                cols = lane(tile)
                y = y_in[part, cols] + carried[piece, cols] * grown[piece, cols]
                y_out[part, cols] = y
                mixed = (y + skip[:, cols] * x[part, cols].astype(f32)).astype(bf16)
                mixed_all[piece, cols] = mixed
                gate_val = gate[part, cols].astype(f32)
                gated = mixed.astype(f32) * (gate_val * sigmoid(gate_val))
                squares = squares + gated * gated
                cross = cross + gated * (hg_all[part, cols] * gain[:, cols])
            mean = jnp.sum(squares, axis=1, keepdims=True) * (1.0 / INNER)
            scale = lax.rsqrt(mean + norm_eps)
            cross_mean = jnp.sum(cross, axis=1, keepdims=True) * (1.0 / INNER)
            cross_mean = cross_mean * scale * scale * scale
            scale = jnp.broadcast_to(scale, (ROWS, LANES))
            cross_mean = jnp.broadcast_to(cross_mean, (ROWS, LANES))
            for tile in range(PAIRS):
                cols = lane(tile)
                gate_val = gate[part, cols].astype(f32)
                sig = sigmoid(gate_val)
                silu = gate_val * sig
                mixed = mixed_all[piece, cols].astype(f32)
                gated = mixed * silu
                normal = gated * scale
                hidden_out[part, cols] = (normal * gain[:, cols]).astype(bf16)
                grad = hg_all[part, cols]
                ng_out[:, cols] += fold(grad * normal)
                dgated = grad * gain[:, cols] * scale - gated * cross_mean
                dgate_out[part, cols] = (dgated * mixed * (sig + silu * (1.0 - sig))).astype(bf16)
                dy = (dgated * silu).astype(bf16)
                dy_out[part, cols] = dy
                dy_scaled[piece, cols] = (dy.astype(f32) * grown[piece, cols]).astype(bf16)
        update = dot_tn(read, dy_scaled[...])
        ust_out[sub] = update
        glocal_out[...] += update * start
        dcc_out[whole, :] = dot_nt(dy_scaled[...], state_low)
        prefix[...] += jnp.broadcast_to(cum_sub[CHUNK - 1 :, :], (8, LANES))


def within_back_kernel(u, dy, bc, cum, cumt, dxs_out, dbc_out, weights, products, low):
    upper = tri(False)
    scores = jnp.where(upper, dot_nt(bc[:, :STATE], bc[:, STATE:]), 0.0)
    for pair in range(PAIRS):
        both = slice(2 * pair * LANES, 2 * (pair + 1) * LANES)
        products[:, both] = dot_nt(u[:, lane(pair)], pair_stack(dy[:, lane(pair)]))
    for _, part in pieces():
        rows_cum = cum[part, :]
        rows_scores = scores[part]
        total = jnp.zeros((ROWS, LANES), f32)
        for head in range(HEADS):
            gap = cumt[head : head + 1, :] - rows_cum[:, head : head + 1]
            decay = jnp.exp2(jnp.minimum(gap, 0.0))
            weights[part, lane(head)] = (decay * rows_scores).astype(bf16)
            total = total + decay * products[part, lane(head)]
        low[part, :] = jnp.where(upper[part], total, 0.0).astype(bf16)
    for pair in range(PAIRS):
        both = slice(2 * pair * LANES, 2 * (pair + 1) * LANES)
        dxs_out[:, lane(pair)] = dot(weights[:, both], pair_stack(dy[:, lane(pair)]))
    dbc_out[:, :STATE] = dot(low[...], bc[:, STATE:])
    dbc_out[:, STATE:] = dot_tn(low[...], bc[:, :STATE])


def back_kernel(
    groups, rank, dxs, dy, x, u, y, bc, dbc, dcc, cum, dt, hst, pfx, h0, gathered, logs, ust, proj,
    before, halo, convp, headp, spread, collect, rows, shifts, ahead,
    pg_out, first_out, tail_out, wg_out, hg_out, skip_out,
    gstate, ext, shifted, dpres, dlow, scaled, prod,
):
    step = pl.program_id(0)
    chunk = pl.num_programs(0) - 1 - step

    @pl.when(step == 0)
    def _():
        gstate[...] = arrived(gathered, logs, rank[0], groups, True)
        dlow[CHUNK:, :] = jnp.zeros((16, XBC), bf16)
        wg_out[...] = jnp.zeros_like(wg_out)
        hg_out[...] = jnp.zeros_like(hg_out)
        skip_out[...] = jnp.zeros_like(skip_out)

    @pl.when(step > 0)
    def _():
        dlow[CHUNK:, :] = dlow[0:16, :]

    @pl.when(chunk == 0)
    def _():
        ext[0:16, :] = halo[...]

    @pl.when(chunk > 0)
    def _():
        ext[0:16, :] = before[:, :XBC]

    ext[16:, :] = proj[:, :XBC]
    shifted[...] = dot(shifts[...], ext[...])
    grad_state = gstate[...]
    grad_low = grad_state.astype(bf16)
    last = cum[CHUNK - 1 : CHUNK, :]
    decayed = jnp.broadcast_to(jnp.exp2(last), (8, LANES))
    wide = expand(
        jnp.concatenate([jnp.exp2(last - cum[...]), dt[...], decayed, jnp.exp2(pfx[0])], axis=0),
        spread[...],
    )
    tail_wide, steps_wide = wide[:CHUNK], wide[CHUNK : 2 * CHUNK]
    decay = wide[2 * CHUNK : 2 * CHUNK + 1]
    end = wide[2 * CHUNK + 8 : 2 * CHUNK + 9]
    reach = dot(bc[:, :STATE], grad_low)

    def conv_back(tile, grad_of):
        cols = lane(tile)
        weights = conv_rows(convp, tile)
        sums = [jnp.zeros((8, LANES), f32) for _ in range(CONV + 1)]
        for _, part in pieces():
            grad = grad_of(part)
            pre, taps = conv_pre(shifted, proj, weights, tile, part)
            sig = sigmoid(pre)
            dpre = grad * (sig + pre * sig * (1.0 - sig))
            dpres[part, cols] = dpre
            dlow[part, cols] = dpre.astype(bf16)
            sums = [total + fold(dpre * tap) for total, tap in zip(sums, taps)] + [
                sums[CONV] + fold(dpre)
            ]

        for k in range(CONV + 1):
            wg_out[8 * k : 8 * k + 8, cols] += sums[k]

    for tile in range(PAIRS):
        cols = lane(tile)
        rest_cols = slice(INNER + tile * LANES, INNER + (tile + 1) * LANES)
        skip_row = jnp.broadcast_to(rows[1:2, cols], (ROWS, LANES))
        skips = []

        def grad_of(part, cols=cols, rest_cols=rest_cols, skip_row=skip_row, skips=skips):
            below = slice(CHUNK + part.start, CHUNK + part.stop)
            dxs_full = dxs[part, cols] + tail_wide[part, cols] * reach[part, cols]
            uf = u[part, cols].astype(f32)
            dyf = dy[part, cols].astype(f32)
            scaled[part, cols] = (uf * tail_wide[part, cols]).astype(bf16)
            q = uf * dxs_full
            prod[part, cols], prod[part, rest_cols] = halves(q)
            prod[below, cols], prod[below, rest_cols] = halves(dyf * y[part, cols] - q)
            skips.append(fold(dyf * x[part, cols].astype(f32)))
            return skip_row * dyf + steps_wide[part, cols] * dxs_full

        conv_back(tile, grad_of)
        skip_out[:, cols] += sum(skips[1:], skips[0])
    dwrite = dot_nt(scaled[...], grad_low)
    conv_back(PAIRS, lambda part: dbc[part, :STATE] + dwrite[part])
    conv_back(PAIRS + 1, lambda part: dbc[part, STATE:] + dcc[part, :])
    first_out[...] = dpres[0:8, :]
    shifted[...] = dot(ahead[...], dlow[...])
    for tile in range(TILES):
        cols = lane(tile)
        weights = conv_rows(convp, tile)
        for _, part in pieces():
            source = dpres[part, cols] * weights[CONV - 1]
            for k in range(CONV - 1):
                block = (CONV - 2 - k) * CHUNK
                source = source + shifted[block + part.start : block + part.stop, cols] * weights[k]
            pg_out[part, cols] = source.astype(bf16)
            dpres[part, cols] = source

    @pl.when(step == 0)
    def _():
        tail_out[...] = dpres[CHUNK - 8 :, :]


    meet = fold(grad_state * (hst[0] + h0[...] * end))
    meet = jnp.concatenate([meet, jnp.zeros_like(meet)], axis=0)
    high, rest = halves(meet)
    prod[2 * CHUNK :, :INNER] = high
    prod[2 * CHUNK :, INNER:] = rest
    heads = dot(prod[...], collect[...])
    q_heads, gap_heads = heads[:CHUNK], heads[CHUNK : 2 * CHUNK]
    meet_heads = jnp.sum(heads[2 * CHUNK :], axis=0, keepdims=True)
    dlog = running(tri(False), gap_heads) + meet_heads
    sig = sigmoid(proj[:, XBC:].astype(f32) + headp[0:1, :])
    steps = dt[...]
    ratio = jnp.where(steps > 1e-30, sig / jnp.maximum(steps, 1e-30), 1.0)
    raw_grad = q_heads * ratio - dlog * headp[1:2, :] * sig
    pg_out[:, XBC:] = raw_grad.astype(bf16)
    hg_out[0:8, :] += fold(raw_grad)
    hg_out[8:16, :] += fold(dlog * steps * headp[1:2, :]) * (-1.0)
    gstate[...] = grad_state * decay + ust[0]


def swap(v, axis, bit):
    size = lax.axis_size(axis)
    return lax.ppermute(v, axis, [(i, i ^ (1 << bit)) for i in range(size)])


def mesh_bits():
    found = []
    for axis in ("dp", "seq"):
        for bit in reversed(range(lax.axis_size(axis).bit_length() - 1)):
            found.append((axis, bit))
    return found


def mine(axis, bit):
    return (lax.axis_index(axis) >> bit) & 1


def merge_pair(v, other, place, axis, bit):
    second = mine(axis, bit) == 1
    return jnp.stack([jnp.where(second, other, v), jnp.where(second, v, other)], axis=place)


def gather_step(v, place, axis, bit):
    return merge_pair(v, swap(v, axis, bit), place, axis, bit)


def gather_pairs(v, bits, lead=0):
    for place, (axis, bit) in enumerate(bits):
        v = gather_step(v, lead + place, axis, bit)
    return v


def flat(v):
    return v.reshape(-1, v.shape[-1])


def blocks(v, bits):
    return v.reshape((2,) * len(bits) + (v.shape[0] >> len(bits), v.shape[1]))


def split_pair(v, place, axis, bit):
    own = mine(axis, bit)
    keep = lax.dynamic_index_in_dim(v, own, place, keepdims=False)
    give = lax.dynamic_index_in_dim(v, 1 - own, place, keepdims=False)
    return keep, give


def add_low(keep, got):
    return (keep.astype(f32) + got.astype(f32)).astype(keep.dtype)


def scatter_step(v, place, axis, bit):
    keep, give = split_pair(v, place, axis, bit)
    return add_low(keep, swap(give, axis, bit))


def scatter_pairs(v, bits, lead=0):
    for place in reversed(range(len(bits))):
        v = scatter_step(v, lead + place, *bits[place])
    return v


def sum_pairs(v, bits):
    for axis, bit in bits:
        v = v + swap(v, axis, bit)
    return v


def full(shape):
    return pl.BlockSpec(shape, lambda c: (0,) * len(shape))


def by_chunk(width, rows=CHUNK):
    return pl.BlockSpec((rows, width), lambda c: (c, 0))


def shape(dims, dtype):
    return jax.ShapeDtypeStruct(dims, dtype)


def params():
    return pltpu.CompilerParams(dimension_semantics=("arbitrary",), vmem_limit_bytes=VMEM)


def cost(flops, moved):
    return pl.CostEstimate(flops=flops, bytes_accessed=moved, transcendentals=0)


def spread_map():
    heads = jnp.arange(LANES)[:, None]
    cols = jnp.arange(INNER)[None, :] // HEADDIM
    once = (heads == cols).astype(bf16)
    return jnp.concatenate([once, once], axis=0)


def shift_map(first):
    rows = jnp.arange((CONV - 1) * CHUNK)
    picked = rows % CHUNK + rows // CHUNK + first
    return (picked[:, None] == jnp.arange(CHUNK + 16)[None, :]).astype(bf16)


def unpack_channels(channels):
    pieces = []
    offset = 0
    for piece_len in (D, INNER, XBC * CONV, XBC, HEADS, HEADS, HEADS):
        pieces.append(channels[offset : offset + piece_len])
        offset = offset + piece_len
    pre_gain, norm_gain, conv_flat, conv_bias, step_bias, rate_log, skip_gain = pieces
    return (
        pre_gain,
        norm_gain,
        conv_flat.reshape(XBC, CONV),
        conv_bias,
        step_bias,
        rate_log,
        skip_gain,
    )


def pre_norm(tok_vals, pre_gain):
    return (
        tok_vals * lax.rsqrt(jnp.mean(tok_vals * tok_vals, -1, keepdims=True) + norm_eps) * pre_gain
    )


def adamw_step(weight, moment, second, gradient, step_rate, decay_rate):
    moment_next = beta_one * moment + (1.0 - beta_one) * gradient
    second_next = beta_two * second + (1.0 - beta_two) * gradient * gradient
    first_fix = 1.0 - beta_one**STEP
    second_fix = 1.0 - beta_two**STEP
    update = moment_next / first_fix / (jnp.sqrt(second_next / second_fix) + adam_eps)
    return (weight - step_rate * (update + decay_rate * weight), moment_next, second_next)


def local(
    tokens,
    cotangent,
    in_weight,
    in_moment,
    in_second,
    out_weight,
    out_moment,
    out_second,
    channels,
    channel_moment,
    channel_second,
):
    groups = lax.axis_size("seq")
    bits = mesh_bits()
    seq_bits = [(axis, bit) for axis, bit in bits if axis == "seq"]
    seq_rank = lax.axis_index("seq")
    rank = seq_rank.astype(jnp.int32).reshape(1)
    tok_low = tokens[0]
    cot_low = cotangent[0]
    count = tok_low.shape[0]
    chunks = count // CHUNK

    def quarter(weight):
        size = weight.shape[0] // groups
        return lax.dynamic_slice_in_dim(weight, seq_rank * size, size, 0).astype(bf16)

    in_part = quarter(in_weight)
    side_part = jnp.pad(in_part[:, INNER:], ((0, 0), (0, SIDE + INNER - PROJ)))
    out_rows = out_weight.shape[0] // groups
    in_rows = in_weight.shape[0] // groups
    beside = jnp.concatenate(
        [quarter(out_weight), in_part[:, :D], in_part[:, D:INNER]], axis=0
    )
    barrier = lax.optimization_barrier
    cross = len(bits) - 3
    (x_axis, x_bit), (y_axis, y_bit), (core_axis, core_bit) = bits[cross:]
    early = cross // 2
    side = gather_pairs(side_part, bits[:early])
    beside = gather_pairs(beside, bits[:early])
    side = gather_pairs(side, bits[early:cross], early)
    side, beside, channels, tok_low = barrier((side, beside, channels, tok_low))
    half = SIDE // 256 * 128
    left, right = side[..., :half], side[..., half:]
    got_l, got_r = swap(left, x_axis, x_bit), swap(right, y_axis, y_bit)
    beside = gather_pairs(beside, bits[early:cross], early)
    left = merge_pair(left, got_l, cross, x_axis, x_bit)
    right = merge_pair(right, got_r, cross, y_axis, y_bit)
    got_l, got_r = swap(left, y_axis, y_bit), swap(right, x_axis, x_bit)
    got_l, got_r, beside = barrier((got_l, got_r, beside))
    left = merge_pair(left, got_l, cross + 1, y_axis, y_bit)
    right = merge_pair(right, got_r, cross, x_axis, x_bit)
    got_l, got_r = swap(left, core_axis, core_bit), swap(right, core_axis, core_bit)
    beside_l, beside_r = beside[..., : D // 2], beside[..., D // 2 :]
    got_b = swap(beside_l, x_axis, x_bit), swap(beside_r, y_axis, y_bit)
    left = merge_pair(left, got_l, cross + 2, core_axis, core_bit)
    right = merge_pair(right, got_r, cross + 2, core_axis, core_bit)
    full_side = jnp.concatenate([flat(left), flat(right)], axis=1)

    pre_gain, norm_gain, conv_weight, conv_bias, step_bias, rate_log, skip_gain = unpack_channels(
        channels
    )
    forward = [(s, s + 1) for s in range(groups - 1)]
    backward = [(s + 1, s) for s in range(groups - 1)]
    tok_halo = lax.ppermute(tok_low[count - 16 :], "seq", forward)
    halo_norm = pre_norm(tok_halo.astype(f32), pre_gain).astype(bf16)
    tok_vals = tok_low.astype(f32)
    normed_low = pre_norm(tok_vals, pre_gain).astype(bf16)

    convp = jnp.concatenate(
        [conv_weight.T, conv_bias[None, :], jnp.zeros((3, XBC), f32)], axis=0
    )
    pad_heads = lambda v: jnp.pad(v, (0, LANES - HEADS))[None, :]
    headp = jnp.concatenate(
        [pad_heads(step_bias), pad_heads(jnp.exp(rate_log)), jnp.zeros((6, LANES), f32)], axis=0
    )
    rows = jnp.concatenate(
        [norm_gain[None, :], jnp.repeat(skip_gain, HEADDIM)[None, :], jnp.zeros((6, INNER), f32)],
        axis=0,
    )
    spread = spread_map()
    collect = jnp.concatenate([spread[:LANES].T, spread[:LANES].T], axis=0)

    proj = dot(normed_low, full_side).astype(bf16)
    halo = dot(halo_norm, full_side[:, :XBC]).astype(bf16)
    proj, halo, got_b = barrier((proj, halo, got_b))
    beside_l = merge_pair(beside_l, got_b[0], cross, x_axis, x_bit)
    beside_r = merge_pair(beside_r, got_b[1], cross, y_axis, y_bit)
    got_b = swap(beside_l, y_axis, y_bit), swap(beside_r, x_axis, x_bit)

    x, bc, u, cum, cumt, dt, hst, pfx, send = pl.pallas_call(
        conv_state_kernel,
        grid=(chunks,),
        in_specs=[
            by_chunk(SIDE), full((16, XBC)), full((8, XBC)), full((8, LANES)),
            full((2 * LANES, INNER)), full(((CONV - 1) * CHUNK, CHUNK + 16)),
        ],
        out_specs=[
            by_chunk(INNER), by_chunk(2 * STATE), by_chunk(INNER), by_chunk(LANES),
            pl.BlockSpec((32, CHUNK), lambda c: (0, c)), by_chunk(LANES),
            pl.BlockSpec((1, STATE, INNER), lambda c: (c, 0, 0)),
            pl.BlockSpec((1, 8, LANES), lambda c: (c, 0, 0)),
            full((STATE + EXTRA, INNER)),
        ],
        out_shape=[
            shape((count, INNER), bf16), shape((count, 2 * STATE), bf16),
            shape((count, INNER), bf16), shape((count, LANES), f32), shape((32, count), f32),
            shape((count, LANES), f32), shape((chunks, STATE, INNER), f32),
            shape((chunks, 8, LANES), f32), shape((STATE + EXTRA, INNER), bf16),
        ],
        scratch_shapes=[
            pltpu.VMEM((CHUNK + 16, XBC), bf16), pltpu.VMEM(((CONV - 1) * CHUNK, XBC), f32),
            pltpu.VMEM((STATE, INNER), f32), pltpu.VMEM((CHUNK, INNER), bf16),
            pltpu.VMEM((8, LANES), f32),
        ],
        compiler_params=params(),
        cost_estimate=cost(24 * 10**9, 24 * 2**20),
        name="conv_state",
    )(proj, halo, convp, headp, spread, shift_map(13))

    states = lax.all_gather(send, "seq", axis=0, tiled=False)
    x, bc, u, cum, cumt, dt, hst, pfx, got_b = barrier(
        (x, bc, u, cum, cumt, dt, hst, pfx, got_b)
    )
    beside_l = merge_pair(beside_l, got_b[0], cross + 1, y_axis, y_bit)
    beside_r = merge_pair(beside_r, got_b[1], cross, x_axis, x_bit)
    beside = jnp.concatenate([beside_l, beside_r], axis=-1)
    got_b = swap(beside, core_axis, core_bit)

    y_within = pl.pallas_call(
        within_kernel,
        grid=(chunks,),
        in_specs=[
            by_chunk(INNER), by_chunk(2 * STATE), by_chunk(LANES),
            pl.BlockSpec((32, CHUNK), lambda c: (0, c)),
        ],
        out_specs=by_chunk(INNER),
        out_shape=shape((count, INNER), f32),
        scratch_shapes=[pltpu.VMEM((CHUNK, HEADS * LANES), bf16)],
        compiler_params=params(),
        cost_estimate=cost(11 * 10**9, 16 * 2**20),
        name="within",
    )(u, bc, cum, cumt)
    y_within, got_b = barrier((y_within, got_b))
    beside = merge_pair(beside, got_b, cross + 2, core_axis, core_bit)
    full_out = flat(beside[..., :out_rows, :])
    full_gate = jnp.concatenate(
        [
            flat(beside[..., out_rows : out_rows + in_rows, :]),
            flat(beside[..., out_rows + in_rows :, :]),
        ],
        axis=1,
    )
    gate = dot(normed_low, full_gate).astype(bf16)

    gathered_spec = full((groups, STATE, INNER))
    logs_spec = pl.BlockSpec((groups, EXTRA, INNER), lambda c: (0, STATE // EXTRA, 0))
    smem = pl.BlockSpec(memory_space=pltpu.SMEM)

    def gate_call(*refs):
        gate_kernel(groups, *refs)

    def by_two(width):
        return by_chunk(width, 2 * CHUNK)

    hidden, y, dy, dgate, dcc, ust, glocal, ng, h0 = pl.pallas_call(
        gate_call,
        grid=(chunks // 2,),
        in_specs=[
            smem, by_two(INNER), by_two(INNER), by_two(2 * STATE), by_two(LANES),
            pl.BlockSpec((1, STATE, INNER), lambda c: (jnp.maximum(2 * c - 1, 0), 0, 0)),
            pl.BlockSpec((1, STATE, INNER), lambda c: (2 * c, 0, 0)),
            gathered_spec, logs_spec, by_two(INNER), by_two(D),
            full((INNER, D)), full((2 * LANES, INNER)), full((8, INNER)),
        ],
        out_specs=[
            by_two(INNER), by_two(INNER), by_two(INNER), by_two(INNER),
            by_two(LANES), pl.BlockSpec((2, STATE, INNER), lambda c: (c, 0, 0)),
            full((STATE, INNER)), full((8, INNER)), full((STATE, INNER)),
        ],
        out_shape=[
            shape((count, INNER), bf16), shape((count, INNER), f32),
            shape((count, INNER), bf16), shape((count, INNER), bf16), shape((count, LANES), f32),
            shape((chunks, STATE, INNER), f32), shape((STATE, INNER), f32), shape((8, INNER), f32),
            shape((STATE, INNER), f32),
        ],
        scratch_shapes=[
            pltpu.VMEM((8, LANES), f32), pltpu.VMEM((STATE, INNER), f32),
            pltpu.VMEM((2 * CHUNK, INNER), f32), pltpu.VMEM((CHUNK, INNER), bf16),
            pltpu.VMEM((CHUNK, INNER), bf16),
        ],
        compiler_params=params(),
        cost_estimate=cost(24 * 10**9, 48 * 2**20),
        name="gate_norm",
    )(
        rank, y_within, x, bc, cum, hst, hst, states, states, gate, cot_low, full_out, spread, rows,
    )

    grads = lax.all_gather(glocal.astype(bf16), "seq", axis=0, tiled=False)

    def product(left, right):
        return lax.dot_general(left, right, TN, preferred_element_type=f32).astype(bf16)

    beside = jnp.concatenate(
        [
            blocks(product(hidden, cot_low), bits),
            blocks(product(normed_low, dgate[:, :D]), bits),
            blocks(product(normed_low, dgate[:, D:]), bits),
        ],
        axis=-2,
    )
    keep_b, give_b = split_pair(beside, cross + 2, core_axis, core_bit)
    got_b = swap(give_b, core_axis, core_bit)
    anywhere = pl.BlockSpec(memory_space=pl.ANY)

    def within_back_call(u, dy, bc, cum, cumt, sent, *rest):
        within_back_kernel(u, dy, bc, cum, cumt, *rest)

    dxs, dbc = pl.pallas_call(
        within_back_call,
        grid=(chunks,),
        in_specs=[
            by_chunk(INNER), by_chunk(INNER), by_chunk(2 * STATE), by_chunk(LANES),
            pl.BlockSpec((32, CHUNK), lambda c: (0, c)), anywhere,
        ],
        out_specs=[by_chunk(INNER), by_chunk(2 * STATE)],
        out_shape=[shape((count, INNER), f32), shape((count, 2 * STATE), f32)],
        scratch_shapes=[
            pltpu.VMEM((CHUNK, HEADS * LANES), bf16), pltpu.VMEM((CHUNK, HEADS * LANES), f32),
            pltpu.VMEM((CHUNK, LANES), bf16),
        ],
        compiler_params=params(),
        cost_estimate=cost(12 * 10**9, 16 * 2**20),
        name="within_back",
    )(u, dy, bc, cum, cumt, give_b)

    got_b, dxs, dbc = barrier((got_b, dxs, dbc))
    keep_b, give_b = split_pair(add_low(keep_b, got_b), cross + 1, y_axis, y_bit)
    got_b = swap(give_b, y_axis, y_bit)

    def back(width, height=CHUNK):
        return pl.BlockSpec((height, width), lambda c: (chunks - 1 - c, 0))

    def back_three(height):
        return pl.BlockSpec((1, height, INNER), lambda c: (chunks - 1 - c, 0, 0))

    def back_call(sent, *refs):
        back_kernel(groups, *refs)

    per = CHUNK // 16
    pg, first, tail, wg, hgr, skip = pl.pallas_call(
        back_call,
        grid=(chunks,),
        in_specs=[
            anywhere, smem, back(INNER), back(INNER), back(INNER), back(INNER), back(INNER), back(2 * STATE),
            back(2 * STATE), back(LANES), back(LANES), back(LANES), back_three(STATE),
            pl.BlockSpec((1, 8, LANES), lambda c: (chunks - 1 - c, 0, 0)),
            full((STATE, INNER)), gathered_spec, logs_spec, back_three(STATE), back(SIDE),
            pl.BlockSpec(
                (16, SIDE), lambda c: (jnp.maximum((chunks - 1 - c) * per - 1, 0), 0)
            ),
            full((16, XBC)), full((8, XBC)), full((8, LANES)), full((2 * LANES, INNER)),
            full((2 * INNER, LANES)), full((8, INNER)),
            full(((CONV - 1) * CHUNK, CHUNK + 16)), full(((CONV - 1) * CHUNK, CHUNK + 16)),
        ],
        out_specs=[
            back(SIDE), full((8, XBC)), full((8, XBC)), full((40, XBC)), full((16, LANES)),
            full((8, INNER)),
        ],
        out_shape=[
            shape((count, SIDE), bf16), shape((8, XBC), f32), shape((8, XBC), f32),
            shape((40, XBC), f32), shape((16, LANES), f32), shape((8, INNER), f32),
        ],
        scratch_shapes=[
            pltpu.VMEM((STATE, INNER), f32), pltpu.VMEM((CHUNK + 16, XBC), bf16),
            pltpu.VMEM(((CONV - 1) * CHUNK, XBC), f32), pltpu.VMEM((CHUNK, XBC), f32),
            pltpu.VMEM((CHUNK + 16, XBC), bf16), pltpu.VMEM((CHUNK, INNER), bf16),
            pltpu.VMEM((2 * CHUNK + 16, 2 * INNER), bf16),
        ],
        compiler_params=params(),
        cost_estimate=cost(47 * 10**9, 48 * 2**20),
        name="mixer_back",
    )(
        give_b, rank, dxs, dy, x, u, y, bc, dbc, dcc, cum, dt, hst, pfx, h0, grads, states, ust, proj, proj,
        halo, convp, headp, spread, collect, rows, shift_map(13), shift_map(1),
    )

    got_b, pg, first, tail, wg, hgr, skip = barrier((got_b, pg, first, tail, wg, hgr, skip))
    keep_b, give_b = split_pair(add_low(keep_b, got_b), cross, x_axis, x_bit)
    got_b = swap(give_b, x_axis, x_bit)
    after = lax.ppermute(first, "seq", backward)
    fixes = [jnp.zeros((5, XBC), f32)]
    for m in range(CONV - 1):
        fix = convp[0] * after[m]
        for k in range(1, m + 1):
            fix = fix + convp[k] * after[m - k]
        fixes.append(fix[None, :])
    tail_low = (tail + jnp.concatenate(fixes, axis=0)).astype(bf16)
    pg = lax.dynamic_update_slice(pg, tail_low, (count - 8, 0))

    left = blocks(product(normed_low, pg[:, :half]), bits)
    right = blocks(product(normed_low, pg[:, half:]), bits)
    keep_l, give_l = split_pair(left, cross + 2, core_axis, core_bit)
    keep_r, give_r = split_pair(right, cross + 2, core_axis, core_bit)
    got_l, got_r = swap(give_l, core_axis, core_bit), swap(give_r, core_axis, core_bit)
    pg, dgate, _, _ = barrier((pg, dgate, give_l, give_r))
    normed_grad = lax.dot_general(dgate, full_gate, NT, preferred_element_type=f32)
    normed_grad = normed_grad + lax.dot_general(pg, full_side, NT, preferred_element_type=f32)
    got_l, got_r, got_b, normed_grad = barrier((got_l, got_r, got_b, normed_grad))
    keep_l, give_l = split_pair(add_low(keep_l, got_l), cross + 1, y_axis, y_bit)
    keep_r, give_r = split_pair(add_low(keep_r, got_r), cross, x_axis, x_bit)
    got_l, got_r = swap(give_l, y_axis, y_bit), swap(give_r, x_axis, x_bit)
    beside = add_low(keep_b, got_b)
    keep_b, give_b = split_pair(beside, cross - 1, *bits[cross - 1])
    got_b = swap(give_b, *bits[cross - 1])
    normed_grad, wg, hgr, skip, ng, _, _ = barrier(
        (normed_grad, wg, hgr, skip, ng, give_l, give_r)
    )
    _, norm_pull = jax.vjp(pre_norm, tok_vals, pre_gain)
    tok_norm_grad, pre_gain_grad = norm_pull(normed_grad)
    token_grad = (cot_low.astype(f32) + tok_norm_grad)[None]
    got_l, got_r, token_grad, pre_gain_grad = barrier((got_l, got_r, token_grad, pre_gain_grad))
    wg_sum = jnp.sum(wg.reshape(5, 8, XBC), axis=1)
    chan_grad = jnp.concatenate(
        [
            pre_gain_grad,
            jnp.sum(ng, axis=0),
            wg_sum[:CONV].T.reshape(-1),
            wg_sum[CONV],
            jnp.sum(hgr[:8, :HEADS], axis=0),
            jnp.sum(hgr[8:, :HEADS], axis=0),
            jnp.sum(skip.reshape(8, HEADS, HEADDIM), axis=(0, 2)),
        ]
    )

    keep_l, give_l = split_pair(add_low(keep_l, got_l), cross, x_axis, x_bit)
    keep_r, give_r = split_pair(add_low(keep_r, got_r), cross, y_axis, y_bit)
    got_l, got_r = swap(give_l, x_axis, x_bit), swap(give_r, y_axis, y_bit)
    sums = [bits[:early], bits[early:cross], bits[cross : cross + 1], bits[cross + 1 : cross + 2]]
    chan_grad = sum_pairs(chan_grad, bits[cross + 2 :])
    got_l, got_r, got_b, chan_grad = barrier((got_l, got_r, got_b, chan_grad))
    side = jnp.concatenate([add_low(keep_l, got_l), add_low(keep_r, got_r)], axis=-1)
    hidden, side = barrier((hidden, side))
    block = tok_vals + dot(hidden, full_out)
    side = scatter_step(side, cross - 1, *bits[cross - 1])
    beside = scatter_pairs(add_low(keep_b, got_b), bits[: cross - 1])
    chan_grad = sum_pairs(chan_grad, sums[0])
    side, beside, chan_grad = barrier((side, beside, chan_grad))
    side = scatter_pairs(side, bits[: cross - 1])
    beside = gather_step(beside, 0, y_axis, y_bit)
    chan_grad = sum_pairs(chan_grad, sums[1])
    side, beside, chan_grad, block = barrier((side, beside, chan_grad, block))
    got = swap(side, y_axis, y_bit)
    beside = gather_step(beside, 1, core_axis, core_bit)
    chan_grad = sum_pairs(chan_grad, sums[2])
    got, beside, chan_grad = barrier((got, beside, chan_grad))
    side = merge_pair(side, got, 0, y_axis, y_bit)
    got = swap(side, core_axis, core_bit)
    chan_grad = sum_pairs(chan_grad, sums[3])
    side = flat(merge_pair(side, got, 1, core_axis, core_bit))

    beside = beside.astype(f32)
    out_grad = flat(beside[..., :out_rows, :])
    in_grad = jnp.concatenate(
        [
            flat(beside[..., out_rows : out_rows + in_rows, :]),
            flat(beside[..., out_rows + in_rows :, :]),
            side[:, : PROJ - INNER].astype(f32),
        ],
        axis=1,
    )
    in_new, in_mom, in_sec = adamw_step(
        in_weight, in_moment, in_second, in_grad, rate_matrix, decay_matrix
    )
    out_new, out_mom, out_sec = adamw_step(
        out_weight, out_moment, out_second, out_grad, rate_matrix, decay_matrix
    )
    chan_new, chan_mom, chan_sec = adamw_step(
        channels, channel_moment, channel_second, chan_grad, rate_channel, 0.0
    )
    return (
        block[None],
        token_grad,
        in_new,
        in_mom,
        in_sec,
        out_new,
        out_mom,
        out_sec,
        chan_new,
        chan_mom,
        chan_sec,
    )


def solution(mesh):
    acts = P("dp", "seq", None)
    rows = P("dp", None)
    specs = (acts, acts) + (rows,) * 6 + (P(),) * 3
    return jax.shard_map(local, mesh=mesh, in_specs=specs, out_specs=specs, check_vma=False)
```

```python
import math

import jax
import jax.numpy as jnp
import ml_dtypes
import numpy as np
from jax import lax
from jax.experimental import pallas as pl
from jax.experimental.pallas import tpu as pltpu
from jax.sharding import PartitionSpec as P

D = 768
HEADS = 24
HEADDIM = 64
STATE = 128
CONV = 4
STEP = 10
INNER = 1536
XBC = 1792
PROJ = 3352
SIDE = 1920
LANES = 128
CHUNK = 128
ROWS = 32
PAIRS = HEADS // 2
TILES = XBC // LANES
EXTRA = 16

norm_eps = 1e-05
beta_one = 0.9
beta_two = 0.999
adam_eps = 1e-08
rate_matrix = 0.1
rate_channel = 0.5
decay_matrix = 0.1
LOG2E = 1.0 / math.log(2.0)
VMEM = 56 * 1024 * 1024

f32 = jnp.float32
bf16 = jnp.bfloat16
NT = (((1,), (1,)), ((), ()))
TN = (((0,), (0,)), ((), ()))


def dot(a, b):
    return jnp.dot(a, b, preferred_element_type=f32)


def dot_nt(a, b):
    return lax.dot_general(a, b, NT, preferred_element_type=f32)


def dot_tn(a, b):
    return lax.dot_general(a, b, TN, preferred_element_type=f32)


def sigmoid(v):
    return 0.5 * jnp.tanh(0.5 * v) + 0.5


def halves(v):
    high = v.astype(bf16)
    return high, (v - high.astype(f32)).astype(bf16)


def running(mask, v):
    high, rest = halves(v)
    left = (v - high.astype(f32) - rest.astype(f32)).astype(bf16)
    parts = dot(jnp.where(mask, 1.0, 0.0).astype(bf16), jnp.concatenate([high, rest, left], axis=1))
    return parts[:, :LANES] + parts[:, LANES : 2 * LANES] + parts[:, 2 * LANES :]


def expand(v, spread):
    high, rest = halves(v)
    return dot(jnp.concatenate([high, rest], axis=1), spread)


def fold(v):
    return jnp.sum(v.reshape(v.shape[0] // 8, 8, v.shape[1]), axis=0)


def lane(i):
    return slice(i * LANES, (i + 1) * LANES)


def iota(shape, dim):
    return lax.broadcasted_iota(jnp.int32, shape, dim)


def tri(lower):
    rows, cols = iota((CHUNK, CHUNK), 0), iota((CHUNK, CHUNK), 1)
    return (rows >= cols) if lower else (rows <= cols)


def conv_rows(convp, tile):
    return [jnp.broadcast_to(convp[k : k + 1, lane(tile)], (ROWS, LANES)) for k in range(CONV + 1)]


def conv_pre(shifted, proj, weights, tile, part):
    cols = lane(tile)
    taps = [
        shifted[k * CHUNK + part.start : k * CHUNK + part.stop, cols] for k in range(CONV - 1)
    ] + [proj[part, cols].astype(f32)]
    pre = taps[0] * weights[0] + weights[CONV]
    for k in range(1, CONV):
        pre = pre + taps[k] * weights[k]
    return pre, taps


def pieces():
    return [(start, slice(start, start + ROWS)) for start in range(0, CHUNK, ROWS)]


def pair_stack(v):
    side = iota(v.shape, 1) < HEADDIM
    zero = jnp.zeros_like(v)
    return jnp.concatenate([jnp.where(side, v, zero), jnp.where(side, zero, v)], axis=0)


def conv_state_kernel(
    proj, halo, convp, headp, spread, shifts, x_out, bc_out, u_out, cum_out, cumt_out, dt_out, hst_out,
    pfx_out, send_out, ext, shifted, state, scaled, total,
):
    step = pl.program_id(0)

    @pl.when(step == 0)
    def _():
        ext[0:16, :] = halo[...]
        state[...] = jnp.zeros_like(state)
        total[...] = jnp.zeros_like(total)

    @pl.when(step > 0)
    def _():
        ext[0:16, :] = ext[CHUNK : CHUNK + 16, :]

    ext[16:, :] = proj[:, :XBC]
    shifted[...] = dot(shifts[...], ext[...])
    raw = proj[:, XBC:].astype(f32) + headp[0:1, :]
    steps = jnp.maximum(raw, 0.0) + jnp.log1p(jnp.exp(-jnp.abs(raw)))
    log_decay = steps * (headp[1:2, :] * (-LOG2E))
    cum = running(tri(True), log_decay)
    cum_out[...] = cum
    cumt_out[...] = jnp.transpose(cum)[0:32, :]
    dt_out[...] = steps
    last = cum[CHUNK - 1 : CHUNK, :]
    decayed = jnp.broadcast_to(jnp.exp2(last), (8, LANES))
    wide = expand(jnp.concatenate([steps, jnp.exp2(last - cum), decayed], axis=0), spread[...])
    steps_wide, tail_wide = wide[:CHUNK], wide[CHUNK : 2 * CHUNK]
    decay = wide[2 * CHUNK : 2 * CHUNK + 1]
    for tile in range(TILES):
        cols = lane(tile)
        weights = conv_rows(convp, tile)
        for _, part in pieces():
            pre, _ = conv_pre(shifted, proj, weights, tile, part)
            value = (pre * sigmoid(pre)).astype(bf16)
            if tile < PAIRS:
                x_out[part, cols] = value
                u = (value.astype(f32) * steps_wide[part, cols]).astype(bf16)
                u_out[part, cols] = u
                scaled[part, cols] = (u.astype(f32) * tail_wide[part, cols]).astype(bf16)
            else:
                bc_out[part, lane(tile - PAIRS)] = value
    new_state = state[...] * decay + dot_tn(bc_out[:, :STATE], scaled[...])
    state[...] = new_state
    hst_out[0] = new_state
    new_total = total[...] + jnp.broadcast_to(last, (8, LANES))
    total[...] = new_total
    pfx_out[0] = new_total

    @pl.when(step == pl.num_programs(0) - 1)
    def _():
        send_out[:STATE, :] = new_state.astype(bf16)
        row = iota((EXTRA, LANES), 0)
        wide = jnp.broadcast_to(new_total[0:1, :], (EXTRA, LANES))
        high, rest = halves(wide)
        left = (wide - high.astype(f32) - rest.astype(f32)).astype(bf16)
        parts = jnp.where(
            row == 0,
            high.astype(f32),
            jnp.where(row == 1, rest.astype(f32), jnp.where(row == 2, left.astype(f32), 0.0)),
        )
        send_out[STATE:, :] = dot(parts.astype(bf16), spread[:LANES, :]).astype(bf16)


def within_kernel(u, bc, cum, cumt, y_out, weights):
    scores = jnp.where(tri(True), dot_nt(bc[:, STATE:], bc[:, :STATE]), 0.0)
    for _, part in pieces():
        rows_cum = cum[part, :]
        rows_scores = scores[part]
        for head in range(HEADS):
            gap = rows_cum[:, head : head + 1] - cumt[head : head + 1, :]
            weights[part, lane(head)] = (jnp.exp2(jnp.minimum(gap, 0.0)) * rows_scores).astype(bf16)
    for pair in range(PAIRS):
        both = slice(2 * pair * LANES, 2 * (pair + 1) * LANES)
        y_out[:, lane(pair)] = dot(weights[:, both], pair_stack(u[:, lane(pair)]))


def arrived(gathered, logs, rank, groups, later):
    sums = [
        jnp.sum(logs[g].astype(f32), axis=0, keepdims=True) for g in range(groups)
    ]
    entered = jnp.zeros((STATE, INNER), f32)
    for g in range(groups):
        between = jnp.zeros((1, INNER), f32)
        for s in range(groups):
            if (s < g) if later else (s > g):
                inside = (s > rank) if later else (s < rank)
                between = between + jnp.where(inside, sums[s], 0.0)
        counts = (g > rank) if later else (g < rank)
        weight = jnp.where(counts, jnp.exp2(between), 0.0)
        entered = entered + gathered[g].astype(f32) * weight
    return entered


def gate_kernel(
    groups, rank, y_in, x, bc, cum, hst_a, hst_b, gathered, logs, gate, tok, cot, wout, spread, rows,
    block_out, hidden_out, y_out, dy_out, dgate_out, dcc_out, ust_out, glocal_out, ng_out, h0_out,
    prefix, h0, gsum, hg_all, mixed_all, dy_scaled,
):
    step = pl.program_id(0)

    @pl.when(step == 0)
    def _():
        value = arrived(gathered, logs, rank[0], groups, False)
        h0[...] = value
        h0_out[...] = value
        prefix[...] = jnp.zeros_like(prefix)
        gsum[...] = jnp.zeros_like(gsum)
        ng_out[...] = jnp.zeros_like(ng_out)

    hg_all[...] = dot_nt(cot[...], wout[...])
    gain, skip = rows[0:1, :], rows[1:2, :]
    for sub in range(2):
        whole = slice(sub * CHUNK, (sub + 1) * CHUNK)
        cum_sub = cum[whole, :]
        wide = expand(jnp.exp2(jnp.concatenate([cum_sub, prefix[...]], axis=0)), spread[...])
        grown, start = wide[:CHUNK], wide[CHUNK : CHUNK + 1]
        before = jnp.where(step > 0, hst_a[0], 0.0) if sub == 0 else hst_b[0]
        state_low = (h0[...] * start + before).astype(bf16)
        read = bc[whole, STATE:]
        carried = dot(read, state_low)
        for first, piece in pieces():
            part = slice(sub * CHUNK + first, sub * CHUNK + first + ROWS)
            squares = jnp.zeros((ROWS, LANES), f32)
            cross = jnp.zeros((ROWS, LANES), f32)
            for tile in range(PAIRS):
                cols = lane(tile)
                y = y_in[part, cols] + carried[piece, cols] * grown[piece, cols]
                y_out[part, cols] = y
                mixed = (y + skip[:, cols] * x[part, cols].astype(f32)).astype(bf16)
                mixed_all[piece, cols] = mixed
                gate_val = gate[part, cols].astype(f32)
                gated = mixed.astype(f32) * (gate_val * sigmoid(gate_val))
                squares = squares + gated * gated
                cross = cross + gated * (hg_all[part, cols] * gain[:, cols])
            mean = jnp.sum(squares, axis=1, keepdims=True) * (1.0 / INNER)
            scale = lax.rsqrt(mean + norm_eps)
            cross_mean = jnp.sum(cross, axis=1, keepdims=True) * (1.0 / INNER)
            cross_mean = cross_mean * scale * scale * scale
            scale = jnp.broadcast_to(scale, (ROWS, LANES))
            cross_mean = jnp.broadcast_to(cross_mean, (ROWS, LANES))
            for tile in range(PAIRS):
                cols = lane(tile)
                gate_val = gate[part, cols].astype(f32)
                sig = sigmoid(gate_val)
                silu = gate_val * sig
                mixed = mixed_all[piece, cols].astype(f32)
                gated = mixed * silu
                normal = gated * scale
                hidden_out[part, cols] = (normal * gain[:, cols]).astype(bf16)
                grad = hg_all[part, cols]
                ng_out[:, cols] += fold(grad * normal)
                dgated = grad * gain[:, cols] * scale - gated * cross_mean
                dgate_out[part, cols] = (dgated * mixed * (sig + silu * (1.0 - sig))).astype(bf16)
                dy = (dgated * silu).astype(bf16)
                dy_out[part, cols] = dy
                dy_scaled[piece, cols] = (dy.astype(f32) * grown[piece, cols]).astype(bf16)
        update = dot_tn(read, dy_scaled[...])
        ust_out[sub] = update
        gsum[...] += update * start
        dcc_out[whole, :] = dot_nt(dy_scaled[...], state_low)
        prefix[...] += jnp.broadcast_to(cum_sub[CHUNK - 1 :, :], (8, LANES))
    block_out[...] = tok[...].astype(f32) + dot(hidden_out[...], wout[...])
    glocal_out[...] = gsum[...].astype(bf16)


def within_back_kernel(u, dy, bc, cum, cumt, dxs_out, dbc_out, weights, products, low):
    upper = tri(False)
    scores = jnp.where(upper, dot_nt(bc[:, :STATE], bc[:, STATE:]), 0.0)
    for pair in range(PAIRS):
        both = slice(2 * pair * LANES, 2 * (pair + 1) * LANES)
        products[:, both] = dot_nt(u[:, lane(pair)], pair_stack(dy[:, lane(pair)]))
    for _, part in pieces():
        rows_cum = cum[part, :]
        rows_scores = scores[part]
        total = jnp.zeros((ROWS, LANES), f32)
        for head in range(HEADS):
            gap = cumt[head : head + 1, :] - rows_cum[:, head : head + 1]
            decay = jnp.exp2(jnp.minimum(gap, 0.0))
            weights[part, lane(head)] = (decay * rows_scores).astype(bf16)
            total = total + decay * products[part, lane(head)]
        low[part, :] = jnp.where(upper[part], total, 0.0).astype(bf16)
    for pair in range(PAIRS):
        both = slice(2 * pair * LANES, 2 * (pair + 1) * LANES)
        dxs_out[:, lane(pair)] = dot(weights[:, both], pair_stack(dy[:, lane(pair)]))
    dbc_out[:, :STATE] = dot(low[...], bc[:, STATE:])
    dbc_out[:, STATE:] = dot_tn(low[...], bc[:, :STATE])


def back_kernel(
    groups, rank, dxs, dy, x, u, y, bc, dbc, dcc, cum, dt, hst, pfx, h0, gathered, logs, ust, proj,
    before, halo, convp, headp, spread, collect, rows, shifts, ahead,
    pg_out, first_out, tail_out, wg_out, hg_out, skip_out,
    gstate, ext, shifted, dpres, dlow, scaled, prod,
):
    step = pl.program_id(0)
    chunk = pl.num_programs(0) - 1 - step

    @pl.when(step == 0)
    def _():
        gstate[...] = arrived(gathered, logs, rank[0], groups, True)
        dlow[CHUNK:, :] = jnp.zeros((16, XBC), bf16)
        wg_out[...] = jnp.zeros_like(wg_out)
        hg_out[...] = jnp.zeros_like(hg_out)
        skip_out[...] = jnp.zeros_like(skip_out)

    @pl.when(step > 0)
    def _():
        dlow[CHUNK:, :] = dlow[0:16, :]

    @pl.when(chunk == 0)
    def _():
        ext[0:16, :] = halo[...]

    @pl.when(chunk > 0)
    def _():
        ext[0:16, :] = before[:, :XBC]

    ext[16:, :] = proj[:, :XBC]
    shifted[...] = dot(shifts[...], ext[...])
    grad_state = gstate[...]
    grad_low = grad_state.astype(bf16)
    last = cum[CHUNK - 1 : CHUNK, :]
    decayed = jnp.broadcast_to(jnp.exp2(last), (8, LANES))
    wide = expand(
        jnp.concatenate([jnp.exp2(last - cum[...]), dt[...], decayed, jnp.exp2(pfx[0])], axis=0),
        spread[...],
    )
    tail_wide, steps_wide = wide[:CHUNK], wide[CHUNK : 2 * CHUNK]
    decay = wide[2 * CHUNK : 2 * CHUNK + 1]
    end = wide[2 * CHUNK + 8 : 2 * CHUNK + 9]
    reach = dot(bc[:, :STATE], grad_low)

    def conv_back(tile, grad_of):
        cols = lane(tile)
        weights = conv_rows(convp, tile)
        sums = [jnp.zeros((8, LANES), f32) for _ in range(CONV + 1)]
        for _, part in pieces():
            grad = grad_of(part)
            pre, taps = conv_pre(shifted, proj, weights, tile, part)
            sig = sigmoid(pre)
            dpre = grad * (sig + pre * sig * (1.0 - sig))
            dpres[part, cols] = dpre
            dlow[part, cols] = dpre.astype(bf16)
            sums = [total + fold(dpre * tap) for total, tap in zip(sums, taps)] + [
                sums[CONV] + fold(dpre)
            ]

        for k in range(CONV + 1):
            wg_out[8 * k : 8 * k + 8, cols] += sums[k]

    for tile in range(PAIRS):
        cols = lane(tile)
        rest_cols = slice(INNER + tile * LANES, INNER + (tile + 1) * LANES)
        skip_row = jnp.broadcast_to(rows[1:2, cols], (ROWS, LANES))
        skips = []

        def grad_of(part, cols=cols, rest_cols=rest_cols, skip_row=skip_row, skips=skips):
            below = slice(CHUNK + part.start, CHUNK + part.stop)
            dxs_full = dxs[part, cols] + tail_wide[part, cols] * reach[part, cols]
            uf = u[part, cols].astype(f32)
            dyf = dy[part, cols].astype(f32)
            scaled[part, cols] = (uf * tail_wide[part, cols]).astype(bf16)
            q = uf * dxs_full
            prod[part, cols], prod[part, rest_cols] = halves(q)
            prod[below, cols], prod[below, rest_cols] = halves(dyf * y[part, cols] - q)
            skips.append(fold(dyf * x[part, cols].astype(f32)))
            return skip_row * dyf + steps_wide[part, cols] * dxs_full

        conv_back(tile, grad_of)
        skip_out[:, cols] += sum(skips[1:], skips[0])
    dwrite = dot_nt(scaled[...], grad_low)
    conv_back(PAIRS, lambda part: dbc[part, :STATE] + dwrite[part])
    conv_back(PAIRS + 1, lambda part: dbc[part, STATE:] + dcc[part, :])
    first_out[...] = dpres[0:8, :]
    shifted[...] = dot(ahead[...], dlow[...])
    for tile in range(TILES):
        cols = lane(tile)
        weights = conv_rows(convp, tile)
        for _, part in pieces():
            source = dpres[part, cols] * weights[CONV - 1]
            for k in range(CONV - 1):
                block = (CONV - 2 - k) * CHUNK
                source = source + shifted[block + part.start : block + part.stop, cols] * weights[k]
            pg_out[part, cols] = source.astype(bf16)
            dpres[part, cols] = source

    @pl.when(step == 0)
    def _():
        tail_out[...] = dpres[CHUNK - 8 :, :]


    meet = fold(grad_state * (hst[0] + h0[...] * end))
    meet = jnp.concatenate([meet, jnp.zeros_like(meet)], axis=0)
    high, rest = halves(meet)
    prod[2 * CHUNK :, :INNER] = high
    prod[2 * CHUNK :, INNER:] = rest
    heads = dot(prod[...], collect[...])
    q_heads, gap_heads = heads[:CHUNK], heads[CHUNK : 2 * CHUNK]
    meet_heads = jnp.sum(heads[2 * CHUNK :], axis=0, keepdims=True)
    dlog = running(tri(False), gap_heads) + meet_heads
    sig = sigmoid(proj[:, XBC:].astype(f32) + headp[0:1, :])
    steps = dt[...]
    ratio = jnp.where(steps > 1e-30, sig / jnp.maximum(steps, 1e-30), 1.0)
    raw_grad = q_heads * ratio - dlog * headp[1:2, :] * sig
    pg_out[:, XBC:] = raw_grad.astype(bf16)
    hg_out[0:8, :] += fold(raw_grad)
    hg_out[8:16, :] += fold(dlog * steps * headp[1:2, :]) * (-1.0)
    gstate[...] = grad_state * decay + ust[0]


def swap(v, axis, bit):
    size = lax.axis_size(axis)
    return lax.ppermute(v, axis, [(i, i ^ (1 << bit)) for i in range(size)])


def mesh_bits():
    found = []
    for axis in ("dp", "seq"):
        for bit in reversed(range(lax.axis_size(axis).bit_length() - 1)):
            found.append((axis, bit))
    return found


def mine(axis, bit):
    return (lax.axis_index(axis) >> bit) & 1


def merge_pair(v, other, place, axis, bit):
    second = mine(axis, bit) == 1
    return jnp.stack([jnp.where(second, other, v), jnp.where(second, v, other)], axis=place)


def gather_step(v, place, axis, bit):
    return merge_pair(v, swap(v, axis, bit), place, axis, bit)


def gather_pairs(v, bits, lead=0):
    for place, (axis, bit) in enumerate(bits):
        v = gather_step(v, lead + place, axis, bit)
    return v


def flat(v):
    return v.reshape(-1, v.shape[-1])


def blocks(v, bits):
    return v.reshape((2,) * len(bits) + (v.shape[0] >> len(bits), v.shape[1]))


def split_pair(v, place, axis, bit):
    own = mine(axis, bit)
    keep = lax.dynamic_index_in_dim(v, own, place, keepdims=False)
    give = lax.dynamic_index_in_dim(v, 1 - own, place, keepdims=False)
    return keep, give


def add_low(keep, got):
    return (keep.astype(f32) + got.astype(f32)).astype(keep.dtype)


def scatter_step(v, place, axis, bit):
    keep, give = split_pair(v, place, axis, bit)
    return add_low(keep, swap(give, axis, bit))


def scatter_pairs(v, bits, lead=0):
    for place in reversed(range(len(bits))):
        v = scatter_step(v, lead + place, *bits[place])
    return v


def sum_pairs(v, bits):
    for axis, bit in bits:
        v = v + swap(v, axis, bit)
    return v


def full(shape):
    return pl.BlockSpec(shape, lambda c: (0,) * len(shape))


def by_chunk(width, rows=CHUNK):
    return pl.BlockSpec((rows, width), lambda c: (c, 0))


def shape(dims, dtype):
    return jax.ShapeDtypeStruct(dims, dtype)


def params():
    return pltpu.CompilerParams(dimension_semantics=("arbitrary",), vmem_limit_bytes=VMEM)


def cost(flops, moved):
    return pl.CostEstimate(flops=flops, bytes_accessed=moved, transcendentals=0)


def spread_map():
    heads = np.arange(LANES)[:, None]
    cols = np.arange(INNER)[None, :] // HEADDIM
    once = (heads == cols).astype(ml_dtypes.bfloat16)
    return np.concatenate([once, once], axis=0)


def shift_map(first):
    rows = np.arange((CONV - 1) * CHUNK)
    picked = rows % CHUNK + rows // CHUNK + first
    return (picked[:, None] == np.arange(CHUNK + 16)[None, :]).astype(ml_dtypes.bfloat16)


def unpack_channels(channels):
    pieces = []
    offset = 0
    for piece_len in (D, INNER, XBC * CONV, XBC, HEADS, HEADS, HEADS):
        pieces.append(channels[offset : offset + piece_len])
        offset = offset + piece_len
    pre_gain, norm_gain, conv_flat, conv_bias, step_bias, rate_log, skip_gain = pieces
    return (
        pre_gain,
        norm_gain,
        conv_flat.reshape(XBC, CONV),
        conv_bias,
        step_bias,
        rate_log,
        skip_gain,
    )


def pre_norm(tok_vals, pre_gain):
    return (
        tok_vals * lax.rsqrt(jnp.mean(tok_vals * tok_vals, -1, keepdims=True) + norm_eps) * pre_gain
    )


def adamw_step(weight, moment, second, gradient, step_rate, decay_rate):
    moment_next = beta_one * moment + (1.0 - beta_one) * gradient
    second_next = beta_two * second + (1.0 - beta_two) * gradient * gradient
    first_fix = 1.0 - beta_one**STEP
    second_fix = 1.0 - beta_two**STEP
    update = moment_next / first_fix / (jnp.sqrt(second_next / second_fix) + adam_eps)
    return (weight - step_rate * (update + decay_rate * weight), moment_next, second_next)


def local(
    tokens,
    cotangent,
    in_weight,
    in_moment,
    in_second,
    out_weight,
    out_moment,
    out_second,
    channels,
    channel_moment,
    channel_second,
):
    groups = lax.axis_size("seq")
    bits = mesh_bits()
    seq_bits = [(axis, bit) for axis, bit in bits if axis == "seq"]
    seq_rank = lax.axis_index("seq")
    rank = seq_rank.astype(jnp.int32).reshape(1)
    tok_low = tokens[0]
    cot_low = cotangent[0]
    count = tok_low.shape[0]
    chunks = count // CHUNK

    def quarter(weight):
        size = weight.shape[0] // groups
        return lax.dynamic_slice_in_dim(weight, seq_rank * size, size, 0).astype(bf16)

    in_part = quarter(in_weight)
    side_part = jnp.pad(in_part[:, INNER:], ((0, 0), (0, SIDE + INNER - PROJ)))
    out_rows = out_weight.shape[0] // groups
    in_rows = in_weight.shape[0] // groups
    beside = jnp.concatenate(
        [quarter(out_weight), in_part[:, :D], in_part[:, D:INNER]], axis=0
    )
    barrier = lax.optimization_barrier
    cross = len(bits) - 3
    (x_axis, x_bit), (y_axis, y_bit), (core_axis, core_bit) = bits[cross:]
    early = cross // 2
    side = gather_pairs(side_part, bits[:early])
    beside = gather_pairs(beside, bits[:early])
    side = gather_pairs(side, bits[early:cross], early)
    side, beside, channels, tok_low = barrier((side, beside, channels, tok_low))
    half = SIDE // 256 * 128
    left, right = side[..., :half], side[..., half:]
    got_l, got_r = swap(left, x_axis, x_bit), swap(right, y_axis, y_bit)
    beside = gather_pairs(beside, bits[early:cross], early)
    left = merge_pair(left, got_l, cross, x_axis, x_bit)
    right = merge_pair(right, got_r, cross, y_axis, y_bit)
    got_l, got_r = swap(left, y_axis, y_bit), swap(right, x_axis, x_bit)
    got_l, got_r, beside = barrier((got_l, got_r, beside))
    left = merge_pair(left, got_l, cross + 1, y_axis, y_bit)
    right = merge_pair(right, got_r, cross, x_axis, x_bit)
    got_l, got_r = swap(left, core_axis, core_bit), swap(right, core_axis, core_bit)
    beside_l, beside_r = beside[..., : D // 2], beside[..., D // 2 :]
    got_b = swap(beside_l, x_axis, x_bit), swap(beside_r, y_axis, y_bit)
    left = merge_pair(left, got_l, cross + 2, core_axis, core_bit)
    right = merge_pair(right, got_r, cross + 2, core_axis, core_bit)
    full_side = jnp.concatenate([flat(left), flat(right)], axis=1)

    pre_gain, norm_gain, conv_weight, conv_bias, step_bias, rate_log, skip_gain = unpack_channels(
        channels
    )
    forward = [(s, s + 1) for s in range(groups - 1)]
    backward = [(s + 1, s) for s in range(groups - 1)]
    tok_halo = lax.ppermute(tok_low[count - 16 :], "seq", forward)
    halo_norm = pre_norm(tok_halo.astype(f32), pre_gain).astype(bf16)
    tok_vals = tok_low.astype(f32)
    normed_low = pre_norm(tok_vals, pre_gain).astype(bf16)

    convp = jnp.concatenate(
        [conv_weight.T, conv_bias[None, :], jnp.zeros((3, XBC), f32)], axis=0
    )
    pad_heads = lambda v: jnp.pad(v, (0, LANES - HEADS))[None, :]
    headp = jnp.concatenate(
        [pad_heads(step_bias), pad_heads(jnp.exp(rate_log)), jnp.zeros((6, LANES), f32)], axis=0
    )
    rows = jnp.concatenate(
        [norm_gain[None, :], jnp.repeat(skip_gain, HEADDIM)[None, :], jnp.zeros((6, INNER), f32)],
        axis=0,
    )
    spread = spread_map()
    collect = np.concatenate([spread[:LANES].T, spread[:LANES].T], axis=0)

    proj = dot(normed_low, full_side).astype(bf16)
    halo = dot(halo_norm, full_side[:, :XBC]).astype(bf16)
    proj, halo, got_b = barrier((proj, halo, got_b))
    beside_l = merge_pair(beside_l, got_b[0], cross, x_axis, x_bit)
    beside_r = merge_pair(beside_r, got_b[1], cross, y_axis, y_bit)
    got_b = swap(beside_l, y_axis, y_bit), swap(beside_r, x_axis, x_bit)

    x, bc, u, cum, cumt, dt, hst, pfx, send = pl.pallas_call(
        conv_state_kernel,
        grid=(chunks,),
        in_specs=[
            by_chunk(SIDE), full((16, XBC)), full((8, XBC)), full((8, LANES)),
            full((2 * LANES, INNER)), full(((CONV - 1) * CHUNK, CHUNK + 16)),
        ],
        out_specs=[
            by_chunk(INNER), by_chunk(2 * STATE), by_chunk(INNER), by_chunk(LANES),
            pl.BlockSpec((32, CHUNK), lambda c: (0, c)), by_chunk(LANES),
            pl.BlockSpec((1, STATE, INNER), lambda c: (c, 0, 0)),
            pl.BlockSpec((1, 8, LANES), lambda c: (c, 0, 0)),
            full((STATE + EXTRA, INNER)),
        ],
        out_shape=[
            shape((count, INNER), bf16), shape((count, 2 * STATE), bf16),
            shape((count, INNER), bf16), shape((count, LANES), f32), shape((32, count), f32),
            shape((count, LANES), f32), shape((chunks, STATE, INNER), f32),
            shape((chunks, 8, LANES), f32), shape((STATE + EXTRA, INNER), bf16),
        ],
        scratch_shapes=[
            pltpu.VMEM((CHUNK + 16, XBC), bf16), pltpu.VMEM(((CONV - 1) * CHUNK, XBC), f32),
            pltpu.VMEM((STATE, INNER), f32), pltpu.VMEM((CHUNK, INNER), bf16),
            pltpu.VMEM((8, LANES), f32),
        ],
        compiler_params=params(),
        cost_estimate=cost(24 * 10**9, 24 * 2**20),
        name="conv_state",
    )(proj, halo, convp, headp, spread, shift_map(13))

    states = lax.all_gather(send, "seq", axis=0, tiled=False)
    x, bc, u, cum, cumt, dt, hst, pfx, got_b = barrier(
        (x, bc, u, cum, cumt, dt, hst, pfx, got_b)
    )
    beside_l = merge_pair(beside_l, got_b[0], cross + 1, y_axis, y_bit)
    beside_r = merge_pair(beside_r, got_b[1], cross, x_axis, x_bit)
    beside = jnp.concatenate([beside_l, beside_r], axis=-1)
    got_b = swap(beside, core_axis, core_bit)

    y_within = pl.pallas_call(
        within_kernel,
        grid=(chunks,),
        in_specs=[
            by_chunk(INNER), by_chunk(2 * STATE), by_chunk(LANES),
            pl.BlockSpec((32, CHUNK), lambda c: (0, c)),
        ],
        out_specs=by_chunk(INNER),
        out_shape=shape((count, INNER), f32),
        scratch_shapes=[pltpu.VMEM((CHUNK, HEADS * LANES), bf16)],
        compiler_params=params(),
        cost_estimate=cost(11 * 10**9, 16 * 2**20),
        name="within",
    )(u, bc, cum, cumt)
    y_within, got_b = barrier((y_within, got_b))
    beside = merge_pair(beside, got_b, cross + 2, core_axis, core_bit)
    full_out = flat(beside[..., :out_rows, :])
    full_gate = jnp.concatenate(
        [
            flat(beside[..., out_rows : out_rows + in_rows, :]),
            flat(beside[..., out_rows + in_rows :, :]),
        ],
        axis=1,
    )
    gate = dot(normed_low, full_gate).astype(bf16)

    gathered_spec = full((groups, STATE, INNER))
    logs_spec = pl.BlockSpec((groups, EXTRA, INNER), lambda c: (0, STATE // EXTRA, 0))
    smem = pl.BlockSpec(memory_space=pltpu.SMEM)

    def gate_call(*refs):
        gate_kernel(groups, *refs)

    def by_two(width):
        return by_chunk(width, 2 * CHUNK)

    block, hidden, y, dy, dgate, dcc, ust, glocal, ng, h0 = pl.pallas_call(
        gate_call,
        grid=(chunks // 2,),
        in_specs=[
            smem, by_two(INNER), by_two(INNER), by_two(2 * STATE), by_two(LANES),
            pl.BlockSpec((1, STATE, INNER), lambda c: (jnp.maximum(2 * c - 1, 0), 0, 0)),
            pl.BlockSpec((1, STATE, INNER), lambda c: (2 * c, 0, 0)),
            gathered_spec, logs_spec, by_two(INNER), by_two(D), by_two(D),
            full((INNER, D)), full((2 * LANES, INNER)), full((8, INNER)),
        ],
        out_specs=[
            by_two(D), by_two(INNER), by_two(INNER), by_two(INNER), by_two(INNER),
            by_two(LANES), pl.BlockSpec((2, STATE, INNER), lambda c: (c, 0, 0)),
            full((STATE, INNER)), full((8, INNER)), full((STATE, INNER)),
        ],
        out_shape=[
            shape((count, D), f32), shape((count, INNER), bf16), shape((count, INNER), f32),
            shape((count, INNER), bf16), shape((count, INNER), bf16), shape((count, LANES), f32),
            shape((chunks, STATE, INNER), f32), shape((STATE, INNER), bf16), shape((8, INNER), f32),
            shape((STATE, INNER), f32),
        ],
        scratch_shapes=[
            pltpu.VMEM((8, LANES), f32), pltpu.VMEM((STATE, INNER), f32),
            pltpu.VMEM((STATE, INNER), f32), pltpu.VMEM((2 * CHUNK, INNER), f32), pltpu.VMEM((CHUNK, INNER), bf16),
            pltpu.VMEM((CHUNK, INNER), bf16),
        ],
        compiler_params=params(),
        cost_estimate=cost(24 * 10**9, 48 * 2**20),
        name="gate_norm",
    )(
        rank, y_within, x, bc, cum, hst, hst, states, states, gate, tok_low, cot_low, full_out, spread, rows,
    )

    grads = lax.all_gather(glocal, "seq", axis=0, tiled=False)

    def product(left, right):
        return lax.dot_general(left, right, TN, preferred_element_type=f32).astype(bf16)

    beside = jnp.concatenate(
        [
            blocks(product(hidden, cot_low), bits),
            blocks(product(normed_low, dgate[:, :D]), bits),
            blocks(product(normed_low, dgate[:, D:]), bits),
        ],
        axis=-2,
    )
    keep_b, give_b = split_pair(beside, cross + 2, core_axis, core_bit)
    got_b = swap(give_b, core_axis, core_bit)
    anywhere = pl.BlockSpec(memory_space=pl.ANY)

    def within_back_call(u, dy, bc, cum, cumt, sent, *rest):
        within_back_kernel(u, dy, bc, cum, cumt, *rest)

    dxs, dbc = pl.pallas_call(
        within_back_call,
        grid=(chunks,),
        in_specs=[
            by_chunk(INNER), by_chunk(INNER), by_chunk(2 * STATE), by_chunk(LANES),
            pl.BlockSpec((32, CHUNK), lambda c: (0, c)), anywhere,
        ],
        out_specs=[by_chunk(INNER), by_chunk(2 * STATE)],
        out_shape=[shape((count, INNER), f32), shape((count, 2 * STATE), f32)],
        scratch_shapes=[
            pltpu.VMEM((CHUNK, HEADS * LANES), bf16), pltpu.VMEM((CHUNK, HEADS * LANES), f32),
            pltpu.VMEM((CHUNK, LANES), bf16),
        ],
        compiler_params=params(),
        cost_estimate=cost(12 * 10**9, 16 * 2**20),
        name="within_back",
    )(u, dy, bc, cum, cumt, give_b)

    got_b, dxs, dbc = barrier((got_b, dxs, dbc))
    keep_b, give_b = split_pair(add_low(keep_b, got_b), cross + 1, y_axis, y_bit)
    got_b = swap(give_b, y_axis, y_bit)

    def back(width, height=CHUNK):
        return pl.BlockSpec((height, width), lambda c: (chunks - 1 - c, 0))

    def back_three(height):
        return pl.BlockSpec((1, height, INNER), lambda c: (chunks - 1 - c, 0, 0))

    def back_call(sent, *refs):
        back_kernel(groups, *refs)

    per = CHUNK // 16
    pg, first, tail, wg, hgr, skip = pl.pallas_call(
        back_call,
        grid=(chunks,),
        in_specs=[
            anywhere, smem, back(INNER), back(INNER), back(INNER), back(INNER), back(INNER), back(2 * STATE),
            back(2 * STATE), back(LANES), back(LANES), back(LANES), back_three(STATE),
            pl.BlockSpec((1, 8, LANES), lambda c: (chunks - 1 - c, 0, 0)),
            full((STATE, INNER)), gathered_spec, logs_spec, back_three(STATE), back(SIDE),
            pl.BlockSpec(
                (16, SIDE), lambda c: (jnp.maximum((chunks - 1 - c) * per - 1, 0), 0)
            ),
            full((16, XBC)), full((8, XBC)), full((8, LANES)), full((2 * LANES, INNER)),
            full((2 * INNER, LANES)), full((8, INNER)),
            full(((CONV - 1) * CHUNK, CHUNK + 16)), full(((CONV - 1) * CHUNK, CHUNK + 16)),
        ],
        out_specs=[
            back(SIDE), full((8, XBC)), full((8, XBC)), full((40, XBC)), full((16, LANES)),
            full((8, INNER)),
        ],
        out_shape=[
            shape((count, SIDE), bf16), shape((8, XBC), f32), shape((8, XBC), f32),
            shape((40, XBC), f32), shape((16, LANES), f32), shape((8, INNER), f32),
        ],
        scratch_shapes=[
            pltpu.VMEM((STATE, INNER), f32), pltpu.VMEM((CHUNK + 16, XBC), bf16),
            pltpu.VMEM(((CONV - 1) * CHUNK, XBC), f32), pltpu.VMEM((CHUNK, XBC), f32),
            pltpu.VMEM((CHUNK + 16, XBC), bf16), pltpu.VMEM((CHUNK, INNER), bf16),
            pltpu.VMEM((2 * CHUNK + 16, 2 * INNER), bf16),
        ],
        compiler_params=params(),
        cost_estimate=cost(47 * 10**9, 48 * 2**20),
        name="mixer_back",
    )(
        give_b, rank, dxs, dy, x, u, y, bc, dbc, dcc, cum, dt, hst, pfx, h0, grads, states, ust, proj, proj,
        halo, convp, headp, spread, collect, rows, shift_map(13), shift_map(1),
    )

    got_b, pg, first, tail, wg, hgr, skip = barrier((got_b, pg, first, tail, wg, hgr, skip))
    keep_b, give_b = split_pair(add_low(keep_b, got_b), cross, x_axis, x_bit)
    got_b = swap(give_b, x_axis, x_bit)
    after = lax.ppermute(first, "seq", backward)
    fixes = [jnp.zeros((5, XBC), f32)]
    for m in range(CONV - 1):
        fix = convp[0] * after[m]
        for k in range(1, m + 1):
            fix = fix + convp[k] * after[m - k]
        fixes.append(fix[None, :])
    tail_low = (tail + jnp.concatenate(fixes, axis=0)).astype(bf16)
    pg = lax.dynamic_update_slice(pg, tail_low, (count - 8, 0))

    left = blocks(product(normed_low, pg[:, :half]), bits)
    right = blocks(product(normed_low, pg[:, half:]), bits)
    keep_l, give_l = split_pair(left, cross + 2, core_axis, core_bit)
    keep_r, give_r = split_pair(right, cross + 2, core_axis, core_bit)
    got_l, got_r = swap(give_l, core_axis, core_bit), swap(give_r, core_axis, core_bit)
    pg, dgate, _, _ = barrier((pg, dgate, give_l, give_r))
    normed_grad = lax.dot_general(dgate, full_gate, NT, preferred_element_type=f32)
    normed_grad = normed_grad + lax.dot_general(pg, full_side, NT, preferred_element_type=f32)
    got_l, got_r, got_b, normed_grad = barrier((got_l, got_r, got_b, normed_grad))
    keep_l, give_l = split_pair(add_low(keep_l, got_l), cross + 1, y_axis, y_bit)
    keep_r, give_r = split_pair(add_low(keep_r, got_r), cross, x_axis, x_bit)
    got_l, got_r = swap(give_l, y_axis, y_bit), swap(give_r, x_axis, x_bit)
    beside = add_low(keep_b, got_b)
    keep_b, give_b = split_pair(beside, cross - 1, *bits[cross - 1])
    got_b = swap(give_b, *bits[cross - 1])
    normed_grad, wg, hgr, skip, ng, _, _, _ = barrier(
        (normed_grad, wg, hgr, skip, ng, give_l, give_r, give_b)
    )
    _, norm_pull = jax.vjp(pre_norm, tok_vals, pre_gain)
    tok_norm_grad, pre_gain_grad = norm_pull(normed_grad)
    token_grad = (cot_low.astype(f32) + tok_norm_grad)[None]
    got_l, got_r, got_b, token_grad, pre_gain_grad = barrier(
        (got_l, got_r, got_b, token_grad, pre_gain_grad)
    )
    wg_sum = jnp.sum(wg.reshape(5, 8, XBC), axis=1)
    chan_grad = jnp.concatenate(
        [
            pre_gain_grad,
            jnp.sum(ng, axis=0),
            wg_sum[:CONV].T.reshape(-1),
            wg_sum[CONV],
            jnp.sum(hgr[:8, :HEADS], axis=0),
            jnp.sum(hgr[8:, :HEADS], axis=0),
            jnp.sum(skip.reshape(8, HEADS, HEADDIM), axis=(0, 2)),
        ]
    )

    keep_l, give_l = split_pair(add_low(keep_l, got_l), cross, x_axis, x_bit)
    keep_r, give_r = split_pair(add_low(keep_r, got_r), cross, y_axis, y_bit)
    got_l, got_r = swap(give_l, x_axis, x_bit), swap(give_r, y_axis, y_bit)
    beside = scatter_pairs(add_low(keep_b, got_b), bits[: cross - 1])
    chan_grad = sum_pairs(chan_grad, bits[cross : cross + 1])
    got_l, got_r, beside, chan_grad = barrier((got_l, got_r, beside, chan_grad))
    side = jnp.concatenate([add_low(keep_l, got_l), add_low(keep_r, got_r)], axis=-1)
    for index, place in enumerate(reversed(range(cross))):
        keep, give = split_pair(side, place, *bits[place])
        got = swap(give, *bits[place])
        if index < 2:
            beside = gather_step(beside, index, *seq_bits[index])
        chan_grad = sum_pairs(chan_grad, [bits[place]])
        got, beside, chan_grad = barrier((got, beside, chan_grad))
        side = add_low(keep, got)
    got = swap(side, y_axis, y_bit)
    chan_grad = sum_pairs(chan_grad, seq_bits[:1])
    got, chan_grad = barrier((got, chan_grad))
    side = merge_pair(side, got, 0, y_axis, y_bit)
    got = swap(side, core_axis, core_bit)
    chan_grad = sum_pairs(chan_grad, seq_bits[1:])
    side = flat(merge_pair(side, got, 1, core_axis, core_bit))

    beside = beside.astype(f32)
    out_grad = flat(beside[..., :out_rows, :])
    in_grad = jnp.concatenate(
        [
            flat(beside[..., out_rows : out_rows + in_rows, :]),
            flat(beside[..., out_rows + in_rows :, :]),
            side[:, : PROJ - INNER].astype(f32),
        ],
        axis=1,
    )
    in_new, in_mom, in_sec = adamw_step(
        in_weight, in_moment, in_second, in_grad, rate_matrix, decay_matrix
    )
    out_new, out_mom, out_sec = adamw_step(
        out_weight, out_moment, out_second, out_grad, rate_matrix, decay_matrix
    )
    chan_new, chan_mom, chan_sec = adamw_step(
        channels, channel_moment, channel_second, chan_grad, rate_channel, 0.0
    )
    return (
        block[None],
        token_grad,
        in_new,
        in_mom,
        in_sec,
        out_new,
        out_mom,
        out_sec,
        chan_new,
        chan_mom,
        chan_sec,
    )


def solution(mesh):
    acts = P("dp", "seq", None)
    rows = P("dp", None)
    specs = (acts, acts) + (rows,) * 6 + (P(),) * 3
    return jax.shard_map(local, mesh=mesh, in_specs=specs, out_specs=specs, check_vma=False)
```

```python
import math

import jax
import jax.numpy as jnp
import ml_dtypes
import numpy as np
from jax import lax
from jax.experimental import pallas as pl
from jax.experimental.pallas import tpu as pltpu
from jax.sharding import PartitionSpec as P

D = 768
HEADS = 24
HEADDIM = 64
STATE = 128
CONV = 4
STEP = 10
INNER = 1536
XBC = 1792
PROJ = 3352
SIDE = 1920
LANES = 128
CHUNK = 128
ROWS = 32
PAIRS = HEADS // 2
TILES = XBC // LANES
EXTRA = 16

norm_eps = 1e-05
beta_one = 0.9
beta_two = 0.999
adam_eps = 1e-08
rate_matrix = 0.1
rate_channel = 0.5
decay_matrix = 0.1
LOG2E = 1.0 / math.log(2.0)
VMEM = 56 * 1024 * 1024

f32 = jnp.float32
bf16 = jnp.bfloat16
NT = (((1,), (1,)), ((), ()))
TN = (((0,), (0,)), ((), ()))


def dot(a, b):
    return jnp.dot(a, b, preferred_element_type=f32)


def dot_nt(a, b):
    return lax.dot_general(a, b, NT, preferred_element_type=f32)


def dot_tn(a, b):
    return lax.dot_general(a, b, TN, preferred_element_type=f32)


def sigmoid(v):
    return 0.5 * jnp.tanh(0.5 * v) + 0.5


def halves(v):
    high = v.astype(bf16)
    return high, (v - high.astype(f32)).astype(bf16)


def running(mask, v):
    high, rest = halves(v)
    left = (v - high.astype(f32) - rest.astype(f32)).astype(bf16)
    parts = dot(jnp.where(mask, 1.0, 0.0).astype(bf16), jnp.concatenate([high, rest, left], axis=1))
    return parts[:, :LANES] + parts[:, LANES : 2 * LANES] + parts[:, 2 * LANES :]


def expand(v, spread):
    high, rest = halves(v)
    return dot(jnp.concatenate([high, rest], axis=1), spread)


def fold(v):
    return jnp.sum(v.reshape(v.shape[0] // 8, 8, v.shape[1]), axis=0)


def lane(i):
    return slice(i * LANES, (i + 1) * LANES)


def iota(shape, dim):
    return lax.broadcasted_iota(jnp.int32, shape, dim)


def tri(lower):
    rows, cols = iota((CHUNK, CHUNK), 0), iota((CHUNK, CHUNK), 1)
    return (rows >= cols) if lower else (rows <= cols)


def conv_rows(convp, tile):
    return [jnp.broadcast_to(convp[k : k + 1, lane(tile)], (ROWS, LANES)) for k in range(CONV + 1)]


def conv_pre(shifted, proj, weights, tile, part):
    cols = lane(tile)
    taps = [
        shifted[k * CHUNK + part.start : k * CHUNK + part.stop, cols] for k in range(CONV - 1)
    ] + [proj[part, cols].astype(f32)]
    pre = taps[0] * weights[0] + weights[CONV]
    for k in range(1, CONV):
        pre = pre + taps[k] * weights[k]
    return pre, taps


def pieces():
    return [(start, slice(start, start + ROWS)) for start in range(0, CHUNK, ROWS)]


def pair_stack(v):
    side = iota(v.shape, 1) < HEADDIM
    zero = jnp.zeros_like(v)
    return jnp.concatenate([jnp.where(side, v, zero), jnp.where(side, zero, v)], axis=0)


def conv_state_kernel(
    proj, halo, convp, headp, spread, shifts, x_out, bc_out, u_out, cum_out, cumt_out, dt_out, hst_out,
    pfx_out, send_out, ext, shifted, state, scaled, total,
):
    step = pl.program_id(0)

    @pl.when(step == 0)
    def _():
        ext[0:16, :] = halo[...]
        state[...] = jnp.zeros_like(state)
        total[...] = jnp.zeros_like(total)

    @pl.when(step > 0)
    def _():
        ext[0:16, :] = ext[CHUNK : CHUNK + 16, :]

    ext[16:, :] = proj[:, :XBC]
    shifted[...] = dot(shifts[...], ext[...])
    raw = proj[:, XBC:].astype(f32) + headp[0:1, :]
    steps = jnp.maximum(raw, 0.0) + jnp.log1p(jnp.exp(-jnp.abs(raw)))
    log_decay = steps * (headp[1:2, :] * (-LOG2E))
    cum = running(tri(True), log_decay)
    cum_out[...] = cum
    cumt_out[...] = jnp.transpose(cum)[0:32, :]
    dt_out[...] = steps
    last = cum[CHUNK - 1 : CHUNK, :]
    decayed = jnp.broadcast_to(jnp.exp2(last), (8, LANES))
    wide = expand(jnp.concatenate([steps, jnp.exp2(last - cum), decayed], axis=0), spread[...])
    steps_wide, tail_wide = wide[:CHUNK], wide[CHUNK : 2 * CHUNK]
    decay = wide[2 * CHUNK : 2 * CHUNK + 1]
    for tile in range(TILES):
        cols = lane(tile)
        weights = conv_rows(convp, tile)
        for _, part in pieces():
            pre, _ = conv_pre(shifted, proj, weights, tile, part)
            value = (pre * sigmoid(pre)).astype(bf16)
            if tile < PAIRS:
                x_out[part, cols] = value
                u = (value.astype(f32) * steps_wide[part, cols]).astype(bf16)
                u_out[part, cols] = u
                scaled[part, cols] = (u.astype(f32) * tail_wide[part, cols]).astype(bf16)
            else:
                bc_out[part, lane(tile - PAIRS)] = value
    new_state = state[...] * decay + dot_tn(bc_out[:, :STATE], scaled[...])
    state[...] = new_state
    hst_out[0] = new_state
    new_total = total[...] + jnp.broadcast_to(last, (8, LANES))
    total[...] = new_total
    pfx_out[0] = new_total

    @pl.when(step == pl.num_programs(0) - 1)
    def _():
        send_out[:STATE, :] = new_state.astype(bf16)
        row = iota((EXTRA, LANES), 0)
        wide = jnp.broadcast_to(new_total[0:1, :], (EXTRA, LANES))
        high, rest = halves(wide)
        left = (wide - high.astype(f32) - rest.astype(f32)).astype(bf16)
        parts = jnp.where(
            row == 0,
            high.astype(f32),
            jnp.where(row == 1, rest.astype(f32), jnp.where(row == 2, left.astype(f32), 0.0)),
        )
        send_out[STATE:, :] = dot(parts.astype(bf16), spread[:LANES, :]).astype(bf16)


def within_kernel(u, bc, cum, cumt, y_out, weights):
    scores = jnp.where(tri(True), dot_nt(bc[:, STATE:], bc[:, :STATE]), 0.0)
    for _, part in pieces():
        rows_cum = cum[part, :]
        rows_scores = scores[part]
        for head in range(HEADS):
            gap = rows_cum[:, head : head + 1] - cumt[head : head + 1, :]
            weights[part, lane(head)] = (jnp.exp2(jnp.minimum(gap, 0.0)) * rows_scores).astype(bf16)
    for pair in range(PAIRS):
        both = slice(2 * pair * LANES, 2 * (pair + 1) * LANES)
        y_out[:, lane(pair)] = dot(weights[:, both], pair_stack(u[:, lane(pair)]))


def arrived(gathered, logs, rank, groups, later):
    sums = [
        jnp.sum(logs[g].astype(f32), axis=0, keepdims=True) for g in range(groups)
    ]
    entered = jnp.zeros((STATE, INNER), f32)
    for g in range(groups):
        between = jnp.zeros((1, INNER), f32)
        for s in range(groups):
            if (s < g) if later else (s > g):
                inside = (s > rank) if later else (s < rank)
                between = between + jnp.where(inside, sums[s], 0.0)
        counts = (g > rank) if later else (g < rank)
        weight = jnp.where(counts, jnp.exp2(between), 0.0)
        entered = entered + gathered[g].astype(f32) * weight
    return entered


def gate_kernel(
    groups, rank, y_in, x, bc, cum, hst_a, hst_b, gathered, logs, gate, tok, cot, wout, spread, rows,
    block_out, hidden_out, y_out, dy_out, dgate_out, dcc_out, ust_out, glocal_out, ng_out, h0_out,
    prefix, h0, gsum, hg_all, mixed_all, dy_scaled,
):
    step = pl.program_id(0)

    @pl.when(step == 0)
    def _():
        value = arrived(gathered, logs, rank[0], groups, False)
        h0[...] = value
        h0_out[...] = value
        prefix[...] = jnp.zeros_like(prefix)
        gsum[...] = jnp.zeros_like(gsum)
        ng_out[...] = jnp.zeros_like(ng_out)

    hg_all[...] = dot_nt(cot[...], wout[...])
    gain, skip = rows[0:1, :], rows[1:2, :]
    for sub in range(2):
        whole = slice(sub * CHUNK, (sub + 1) * CHUNK)
        cum_sub = cum[whole, :]
        wide = expand(jnp.exp2(jnp.concatenate([cum_sub, prefix[...]], axis=0)), spread[...])
        grown, start = wide[:CHUNK], wide[CHUNK : CHUNK + 1]
        before = jnp.where(step > 0, hst_a[0], 0.0) if sub == 0 else hst_b[0]
        state_low = (h0[...] * start + before).astype(bf16)
        read = bc[whole, STATE:]
        carried = dot(read, state_low)
        for first, piece in pieces():
            part = slice(sub * CHUNK + first, sub * CHUNK + first + ROWS)
            squares = jnp.zeros((ROWS, LANES), f32)
            cross = jnp.zeros((ROWS, LANES), f32)
            for tile in range(PAIRS):
                cols = lane(tile)
                y = y_in[part, cols] + carried[piece, cols] * grown[piece, cols]
                y_out[part, cols] = y
                mixed = (y + skip[:, cols] * x[part, cols].astype(f32)).astype(bf16)
                mixed_all[piece, cols] = mixed
                gate_val = gate[part, cols].astype(f32)
                gated = mixed.astype(f32) * (gate_val * sigmoid(gate_val))
                squares = squares + gated * gated
                cross = cross + gated * (hg_all[part, cols] * gain[:, cols])
            mean = jnp.sum(squares, axis=1, keepdims=True) * (1.0 / INNER)
            scale = lax.rsqrt(mean + norm_eps)
            cross_mean = jnp.sum(cross, axis=1, keepdims=True) * (1.0 / INNER)
            cross_mean = cross_mean * scale * scale * scale
            scale = jnp.broadcast_to(scale, (ROWS, LANES))
            cross_mean = jnp.broadcast_to(cross_mean, (ROWS, LANES))
            for tile in range(PAIRS):
                cols = lane(tile)
                gate_val = gate[part, cols].astype(f32)
                sig = sigmoid(gate_val)
                silu = gate_val * sig
                mixed = mixed_all[piece, cols].astype(f32)
                gated = mixed * silu
                normal = gated * scale
                hidden_out[part, cols] = (normal * gain[:, cols]).astype(bf16)
                grad = hg_all[part, cols]
                ng_out[:, cols] += fold(grad * normal)
                dgated = grad * gain[:, cols] * scale - gated * cross_mean
                dgate_out[part, cols] = (dgated * mixed * (sig + silu * (1.0 - sig))).astype(bf16)
                dy = (dgated * silu).astype(bf16)
                dy_out[part, cols] = dy
                dy_scaled[piece, cols] = (dy.astype(f32) * grown[piece, cols]).astype(bf16)
        update = dot_tn(read, dy_scaled[...])
        ust_out[sub] = update
        gsum[...] += update * start
        dcc_out[whole, :] = dot_nt(dy_scaled[...], state_low)
        prefix[...] += jnp.broadcast_to(cum_sub[CHUNK - 1 :, :], (8, LANES))
    block_out[...] = tok[...].astype(f32) + dot(hidden_out[...], wout[...])
    glocal_out[...] = gsum[...].astype(bf16)


def within_back_kernel(u, dy, bc, cum, cumt, dxs_out, dbc_out, weights, products, low):
    upper = tri(False)
    scores = jnp.where(upper, dot_nt(bc[:, :STATE], bc[:, STATE:]), 0.0)
    for pair in range(PAIRS):
        both = slice(2 * pair * LANES, 2 * (pair + 1) * LANES)
        products[:, both] = dot_nt(u[:, lane(pair)], pair_stack(dy[:, lane(pair)]))
    for _, part in pieces():
        rows_cum = cum[part, :]
        rows_scores = scores[part]
        total = jnp.zeros((ROWS, LANES), f32)
        for head in range(HEADS):
            gap = cumt[head : head + 1, :] - rows_cum[:, head : head + 1]
            decay = jnp.exp2(jnp.minimum(gap, 0.0))
            weights[part, lane(head)] = (decay * rows_scores).astype(bf16)
            total = total + decay * products[part, lane(head)]
        low[part, :] = jnp.where(upper[part], total, 0.0).astype(bf16)
    for pair in range(PAIRS):
        both = slice(2 * pair * LANES, 2 * (pair + 1) * LANES)
        dxs_out[:, lane(pair)] = dot(weights[:, both], pair_stack(dy[:, lane(pair)]))
    dbc_out[:, :STATE] = dot(low[...], bc[:, STATE:])
    dbc_out[:, STATE:] = dot_tn(low[...], bc[:, :STATE])


def back_kernel(
    groups, rank, dxs, dy, x, u, y, bc, dbc, dcc, cum, dt, hst, pfx, h0, gathered, logs, ust, proj,
    before, halo, convp, headp, spread, collect, rows, shifts, ahead,
    pg_out, first_out, tail_out, wg_out, hg_out, skip_out,
    gstate, ext, shifted, dpres, dlow, scaled, prod,
):
    step = pl.program_id(0)
    chunk = pl.num_programs(0) - 1 - step

    @pl.when(step == 0)
    def _():
        gstate[...] = arrived(gathered, logs, rank[0], groups, True)
        dlow[CHUNK:, :] = jnp.zeros((16, XBC), bf16)
        wg_out[...] = jnp.zeros_like(wg_out)
        hg_out[...] = jnp.zeros_like(hg_out)
        skip_out[...] = jnp.zeros_like(skip_out)

    @pl.when(step > 0)
    def _():
        dlow[CHUNK:, :] = dlow[0:16, :]

    @pl.when(chunk == 0)
    def _():
        ext[0:16, :] = halo[...]

    @pl.when(chunk > 0)
    def _():
        ext[0:16, :] = before[:, :XBC]

    ext[16:, :] = proj[:, :XBC]
    shifted[...] = dot(shifts[...], ext[...])
    grad_state = gstate[...]
    grad_low = grad_state.astype(bf16)
    last = cum[CHUNK - 1 : CHUNK, :]
    decayed = jnp.broadcast_to(jnp.exp2(last), (8, LANES))
    wide = expand(
        jnp.concatenate([jnp.exp2(last - cum[...]), dt[...], decayed, jnp.exp2(pfx[0])], axis=0),
        spread[...],
    )
    tail_wide, steps_wide = wide[:CHUNK], wide[CHUNK : 2 * CHUNK]
    decay = wide[2 * CHUNK : 2 * CHUNK + 1]
    end = wide[2 * CHUNK + 8 : 2 * CHUNK + 9]
    reach = dot(bc[:, :STATE], grad_low)

    def conv_back(tile, grad_of):
        cols = lane(tile)
        weights = conv_rows(convp, tile)
        sums = [jnp.zeros((8, LANES), f32) for _ in range(CONV + 1)]
        for _, part in pieces():
            grad = grad_of(part)
            pre, taps = conv_pre(shifted, proj, weights, tile, part)
            sig = sigmoid(pre)
            dpre = grad * (sig + pre * sig * (1.0 - sig))
            dpres[part, cols] = dpre
            dlow[part, cols] = dpre.astype(bf16)
            sums = [total + fold(dpre * tap) for total, tap in zip(sums, taps)] + [
                sums[CONV] + fold(dpre)
            ]

        for k in range(CONV + 1):
            wg_out[8 * k : 8 * k + 8, cols] += sums[k]

    for tile in range(PAIRS):
        cols = lane(tile)
        rest_cols = slice(INNER + tile * LANES, INNER + (tile + 1) * LANES)
        skip_row = jnp.broadcast_to(rows[1:2, cols], (ROWS, LANES))
        skips = []

        def grad_of(part, cols=cols, rest_cols=rest_cols, skip_row=skip_row, skips=skips):
            below = slice(CHUNK + part.start, CHUNK + part.stop)
            dxs_full = dxs[part, cols] + tail_wide[part, cols] * reach[part, cols]
            uf = u[part, cols].astype(f32)
            dyf = dy[part, cols].astype(f32)
            scaled[part, cols] = (uf * tail_wide[part, cols]).astype(bf16)
            q = uf * dxs_full
            prod[part, cols], prod[part, rest_cols] = halves(q)
            prod[below, cols], prod[below, rest_cols] = halves(dyf * y[part, cols] - q)
            skips.append(fold(dyf * x[part, cols].astype(f32)))
            return skip_row * dyf + steps_wide[part, cols] * dxs_full

        conv_back(tile, grad_of)
        skip_out[:, cols] += sum(skips[1:], skips[0])
    dwrite = dot_nt(scaled[...], grad_low)
    conv_back(PAIRS, lambda part: dbc[part, :STATE] + dwrite[part])
    conv_back(PAIRS + 1, lambda part: dbc[part, STATE:] + dcc[part, :])
    first_out[...] = dpres[0:8, :]
    shifted[...] = dot(ahead[...], dlow[...])
    for tile in range(TILES):
        cols = lane(tile)
        weights = conv_rows(convp, tile)
        for _, part in pieces():
            source = dpres[part, cols] * weights[CONV - 1]
            for k in range(CONV - 1):
                block = (CONV - 2 - k) * CHUNK
                source = source + shifted[block + part.start : block + part.stop, cols] * weights[k]
            pg_out[part, cols] = source.astype(bf16)
            dpres[part, cols] = source

    @pl.when(step == 0)
    def _():
        tail_out[...] = dpres[CHUNK - 8 :, :]


    meet = fold(grad_state * (hst[0] + h0[...] * end))
    meet = jnp.concatenate([meet, jnp.zeros_like(meet)], axis=0)
    high, rest = halves(meet)
    prod[2 * CHUNK :, :INNER] = high
    prod[2 * CHUNK :, INNER:] = rest
    heads = dot(prod[...], collect[...])
    q_heads, gap_heads = heads[:CHUNK], heads[CHUNK : 2 * CHUNK]
    meet_heads = jnp.sum(heads[2 * CHUNK :], axis=0, keepdims=True)
    dlog = running(tri(False), gap_heads) + meet_heads
    sig = sigmoid(proj[:, XBC:].astype(f32) + headp[0:1, :])
    steps = dt[...]
    ratio = jnp.where(steps > 1e-30, sig / jnp.maximum(steps, 1e-30), 1.0)
    raw_grad = q_heads * ratio - dlog * headp[1:2, :] * sig
    pg_out[:, XBC:] = raw_grad.astype(bf16)
    hg_out[0:8, :] += fold(raw_grad)
    hg_out[8:16, :] += fold(dlog * steps * headp[1:2, :]) * (-1.0)
    gstate[...] = grad_state * decay + ust[0]


def swap(v, axis, bit):
    size = lax.axis_size(axis)
    return lax.ppermute(v, axis, [(i, i ^ (1 << bit)) for i in range(size)])


def mesh_bits():
    found = []
    for axis in ("dp", "seq"):
        for bit in reversed(range(lax.axis_size(axis).bit_length() - 1)):
            found.append((axis, bit))
    return found


def mine(axis, bit):
    return (lax.axis_index(axis) >> bit) & 1


def merge_pair(v, other, place, axis, bit):
    second = mine(axis, bit) == 1
    return jnp.stack([jnp.where(second, other, v), jnp.where(second, v, other)], axis=place)


def gather_step(v, place, axis, bit):
    return merge_pair(v, swap(v, axis, bit), place, axis, bit)


def gather_pairs(v, bits, lead=0):
    for place, (axis, bit) in enumerate(bits):
        v = gather_step(v, lead + place, axis, bit)
    return v


def flat(v):
    return v.reshape(-1, v.shape[-1])


def blocks(v, bits):
    return v.reshape((2,) * len(bits) + (v.shape[0] >> len(bits), v.shape[1]))


def split_pair(v, place, axis, bit):
    own = mine(axis, bit)
    keep = lax.dynamic_index_in_dim(v, own, place, keepdims=False)
    give = lax.dynamic_index_in_dim(v, 1 - own, place, keepdims=False)
    return keep, give


def add_low(keep, got):
    return (keep.astype(f32) + got.astype(f32)).astype(keep.dtype)


def scatter_step(v, place, axis, bit):
    keep, give = split_pair(v, place, axis, bit)
    return add_low(keep, swap(give, axis, bit))


def scatter_pairs(v, bits, lead=0):
    for place in reversed(range(len(bits))):
        v = scatter_step(v, lead + place, *bits[place])
    return v


def sum_pairs(v, bits):
    for axis, bit in bits:
        v = v + swap(v, axis, bit)
    return v


def full(shape):
    return pl.BlockSpec(shape, lambda c: (0,) * len(shape))


def by_chunk(width, rows=CHUNK):
    return pl.BlockSpec((rows, width), lambda c: (c, 0))


def shape(dims, dtype):
    return jax.ShapeDtypeStruct(dims, dtype)


def params():
    return pltpu.CompilerParams(dimension_semantics=("arbitrary",), vmem_limit_bytes=VMEM)


def cost(flops, moved):
    return pl.CostEstimate(flops=flops, bytes_accessed=moved, transcendentals=0)


def spread_map():
    heads = np.arange(LANES)[:, None]
    cols = np.arange(INNER)[None, :] // HEADDIM
    once = (heads == cols).astype(ml_dtypes.bfloat16)
    return np.concatenate([once, once], axis=0)


def shift_map(first):
    rows = np.arange((CONV - 1) * CHUNK)
    picked = rows % CHUNK + rows // CHUNK + first
    return (picked[:, None] == np.arange(CHUNK + 16)[None, :]).astype(ml_dtypes.bfloat16)


def unpack_channels(channels):
    pieces = []
    offset = 0
    for piece_len in (D, INNER, XBC * CONV, XBC, HEADS, HEADS, HEADS):
        pieces.append(channels[offset : offset + piece_len])
        offset = offset + piece_len
    pre_gain, norm_gain, conv_flat, conv_bias, step_bias, rate_log, skip_gain = pieces
    return (
        pre_gain,
        norm_gain,
        conv_flat.reshape(XBC, CONV),
        conv_bias,
        step_bias,
        rate_log,
        skip_gain,
    )


def pre_norm(tok_vals, pre_gain):
    return (
        tok_vals * lax.rsqrt(jnp.mean(tok_vals * tok_vals, -1, keepdims=True) + norm_eps) * pre_gain
    )


def adamw_step(weight, moment, second, gradient, step_rate, decay_rate):
    moment_next = beta_one * moment + (1.0 - beta_one) * gradient
    second_next = beta_two * second + (1.0 - beta_two) * gradient * gradient
    first_fix = 1.0 - beta_one**STEP
    second_fix = 1.0 - beta_two**STEP
    update = moment_next / first_fix / (jnp.sqrt(second_next / second_fix) + adam_eps)
    return (weight - step_rate * (update + decay_rate * weight), moment_next, second_next)


def local(
    tokens,
    cotangent,
    in_weight,
    in_moment,
    in_second,
    out_weight,
    out_moment,
    out_second,
    channels,
    channel_moment,
    channel_second,
):
    groups = lax.axis_size("seq")
    bits = mesh_bits()
    seq_bits = [(axis, bit) for axis, bit in bits if axis == "seq"]
    seq_rank = lax.axis_index("seq")
    rank = seq_rank.astype(jnp.int32).reshape(1)
    tok_low = tokens[0]
    cot_low = cotangent[0]
    count = tok_low.shape[0]
    chunks = count // CHUNK

    def quarter(weight):
        size = weight.shape[0] // groups
        return lax.dynamic_slice_in_dim(weight, seq_rank * size, size, 0).astype(bf16)

    in_part = quarter(in_weight)
    side_part = jnp.pad(in_part[:, INNER:], ((0, 0), (0, SIDE + INNER - PROJ)))
    out_rows = out_weight.shape[0] // groups
    in_rows = in_weight.shape[0] // groups
    beside = jnp.concatenate(
        [quarter(out_weight), in_part[:, :D], in_part[:, D:INNER]], axis=0
    )
    barrier = lax.optimization_barrier
    cross = len(bits) - 3
    (x_axis, x_bit), (y_axis, y_bit), (core_axis, core_bit) = bits[cross:]
    early = cross // 2
    side = gather_pairs(side_part, bits[:early])
    beside = gather_pairs(beside, bits[:early])
    side, tok_low = barrier((side, tok_low))
    side = gather_pairs(side, bits[early:cross], early)
    side, beside = barrier((side, beside))
    half = SIDE // 256 * 128
    left, right = side[..., :half], side[..., half:]
    got_l, got_r = swap(left, x_axis, x_bit), swap(right, y_axis, y_bit)
    beside = gather_pairs(beside, bits[early:cross], early)
    left = merge_pair(left, got_l, cross, x_axis, x_bit)
    right = merge_pair(right, got_r, cross, y_axis, y_bit)
    got_l, got_r = swap(left, y_axis, y_bit), swap(right, x_axis, x_bit)
    got_l, got_r, beside = barrier((got_l, got_r, beside))
    left = merge_pair(left, got_l, cross + 1, y_axis, y_bit)
    right = merge_pair(right, got_r, cross, x_axis, x_bit)
    got_l, got_r = swap(left, core_axis, core_bit), swap(right, core_axis, core_bit)
    beside_l, beside_r = beside[..., : D // 2], beside[..., D // 2 :]
    got_b = swap(beside_l, x_axis, x_bit), swap(beside_r, y_axis, y_bit)
    left = merge_pair(left, got_l, cross + 2, core_axis, core_bit)
    right = merge_pair(right, got_r, cross + 2, core_axis, core_bit)
    full_side = jnp.concatenate([flat(left), flat(right)], axis=1)

    pre_gain, norm_gain, conv_weight, conv_bias, step_bias, rate_log, skip_gain = unpack_channels(
        channels
    )
    forward = [(s, s + 1) for s in range(groups - 1)]
    backward = [(s + 1, s) for s in range(groups - 1)]
    tok_halo = lax.ppermute(tokens[0, count - 16 :], "seq", forward)
    halo_norm = pre_norm(tok_halo.astype(f32), pre_gain).astype(bf16)
    tok_vals = tok_low.astype(f32)
    normed_low = pre_norm(tok_vals, pre_gain).astype(bf16)

    convp = jnp.concatenate(
        [conv_weight.T, conv_bias[None, :], jnp.zeros((3, XBC), f32)], axis=0
    )
    pad_heads = lambda v: jnp.pad(v, (0, LANES - HEADS))[None, :]
    headp = jnp.concatenate(
        [pad_heads(step_bias), pad_heads(jnp.exp(rate_log)), jnp.zeros((6, LANES), f32)], axis=0
    )
    rows = jnp.concatenate(
        [norm_gain[None, :], jnp.repeat(skip_gain, HEADDIM)[None, :], jnp.zeros((6, INNER), f32)],
        axis=0,
    )
    spread = spread_map()
    collect = np.concatenate([spread[:LANES].T, spread[:LANES].T], axis=0)

    proj = dot(normed_low, full_side).astype(bf16)
    halo = dot(halo_norm, full_side[:, :XBC]).astype(bf16)
    proj, halo, got_b = barrier((proj, halo, got_b))
    beside_l = merge_pair(beside_l, got_b[0], cross, x_axis, x_bit)
    beside_r = merge_pair(beside_r, got_b[1], cross, y_axis, y_bit)
    got_b = swap(beside_l, y_axis, y_bit), swap(beside_r, x_axis, x_bit)

    x, bc, u, cum, cumt, dt, hst, pfx, send = pl.pallas_call(
        conv_state_kernel,
        grid=(chunks,),
        in_specs=[
            by_chunk(SIDE), full((16, XBC)), full((8, XBC)), full((8, LANES)),
            full((2 * LANES, INNER)), full(((CONV - 1) * CHUNK, CHUNK + 16)),
        ],
        out_specs=[
            by_chunk(INNER), by_chunk(2 * STATE), by_chunk(INNER), by_chunk(LANES),
            pl.BlockSpec((32, CHUNK), lambda c: (0, c)), by_chunk(LANES),
            pl.BlockSpec((1, STATE, INNER), lambda c: (c, 0, 0)),
            pl.BlockSpec((1, 8, LANES), lambda c: (c, 0, 0)),
            full((STATE + EXTRA, INNER)),
        ],
        out_shape=[
            shape((count, INNER), bf16), shape((count, 2 * STATE), bf16),
            shape((count, INNER), bf16), shape((count, LANES), f32), shape((32, count), f32),
            shape((count, LANES), f32), shape((chunks, STATE, INNER), f32),
            shape((chunks, 8, LANES), f32), shape((STATE + EXTRA, INNER), bf16),
        ],
        scratch_shapes=[
            pltpu.VMEM((CHUNK + 16, XBC), bf16), pltpu.VMEM(((CONV - 1) * CHUNK, XBC), f32),
            pltpu.VMEM((STATE, INNER), f32), pltpu.VMEM((CHUNK, INNER), bf16),
            pltpu.VMEM((8, LANES), f32),
        ],
        compiler_params=params(),
        cost_estimate=cost(24 * 10**9, 24 * 2**20),
        name="conv_state",
    )(proj, halo, convp, headp, spread, shift_map(13))

    states = lax.all_gather(send, "seq", axis=0, tiled=False)
    x, bc, u, cum, cumt, dt, hst, pfx, got_b = barrier(
        (x, bc, u, cum, cumt, dt, hst, pfx, got_b)
    )
    beside_l = merge_pair(beside_l, got_b[0], cross + 1, y_axis, y_bit)
    beside_r = merge_pair(beside_r, got_b[1], cross, x_axis, x_bit)
    beside = jnp.concatenate([beside_l, beside_r], axis=-1)
    got_b = swap(beside, core_axis, core_bit)

    y_within = pl.pallas_call(
        within_kernel,
        grid=(chunks,),
        in_specs=[
            by_chunk(INNER), by_chunk(2 * STATE), by_chunk(LANES),
            pl.BlockSpec((32, CHUNK), lambda c: (0, c)),
        ],
        out_specs=by_chunk(INNER),
        out_shape=shape((count, INNER), f32),
        scratch_shapes=[pltpu.VMEM((CHUNK, HEADS * LANES), bf16)],
        compiler_params=params(),
        cost_estimate=cost(11 * 10**9, 16 * 2**20),
        name="within",
    )(u, bc, cum, cumt)
    y_within, got_b = barrier((y_within, got_b))
    beside = merge_pair(beside, got_b, cross + 2, core_axis, core_bit)
    full_out = flat(beside[..., :out_rows, :])
    full_gate = jnp.concatenate(
        [
            flat(beside[..., out_rows : out_rows + in_rows, :]),
            flat(beside[..., out_rows + in_rows :, :]),
        ],
        axis=1,
    )
    gate = dot(normed_low, full_gate).astype(bf16)

    gathered_spec = full((groups, STATE, INNER))
    logs_spec = pl.BlockSpec((groups, EXTRA, INNER), lambda c: (0, STATE // EXTRA, 0))
    smem = pl.BlockSpec(memory_space=pltpu.SMEM)

    def gate_call(*refs):
        gate_kernel(groups, *refs)

    def by_two(width):
        return by_chunk(width, 2 * CHUNK)

    block, hidden, y, dy, dgate, dcc, ust, glocal, ng, h0 = pl.pallas_call(
        gate_call,
        grid=(chunks // 2,),
        in_specs=[
            smem, by_two(INNER), by_two(INNER), by_two(2 * STATE), by_two(LANES),
            pl.BlockSpec((1, STATE, INNER), lambda c: (jnp.maximum(2 * c - 1, 0), 0, 0)),
            pl.BlockSpec((1, STATE, INNER), lambda c: (2 * c, 0, 0)),
            gathered_spec, logs_spec, by_two(INNER), by_two(D), by_two(D),
            full((INNER, D)), full((2 * LANES, INNER)), full((8, INNER)),
        ],
        out_specs=[
            by_two(D), by_two(INNER), by_two(INNER), by_two(INNER), by_two(INNER),
            by_two(LANES), pl.BlockSpec((2, STATE, INNER), lambda c: (c, 0, 0)),
            full((STATE, INNER)), full((8, INNER)), full((STATE, INNER)),
        ],
        out_shape=[
            shape((count, D), f32), shape((count, INNER), bf16), shape((count, INNER), f32),
            shape((count, INNER), bf16), shape((count, INNER), bf16), shape((count, LANES), f32),
            shape((chunks, STATE, INNER), f32), shape((STATE, INNER), bf16), shape((8, INNER), f32),
            shape((STATE, INNER), f32),
        ],
        scratch_shapes=[
            pltpu.VMEM((8, LANES), f32), pltpu.VMEM((STATE, INNER), f32),
            pltpu.VMEM((STATE, INNER), f32), pltpu.VMEM((2 * CHUNK, INNER), f32), pltpu.VMEM((CHUNK, INNER), bf16),
            pltpu.VMEM((CHUNK, INNER), bf16),
        ],
        compiler_params=params(),
        cost_estimate=cost(24 * 10**9, 48 * 2**20),
        name="gate_norm",
    )(
        rank, y_within, x, bc, cum, hst, hst, states, states, gate, tok_low, cot_low, full_out, spread, rows,
    )

    grads = lax.all_gather(glocal, "seq", axis=0, tiled=False)

    def product(left, right):
        return lax.dot_general(left, right, TN, preferred_element_type=f32).astype(bf16)

    beside = jnp.concatenate(
        [
            blocks(product(hidden, cot_low), bits),
            blocks(product(normed_low, dgate[:, :D]), bits),
            blocks(product(normed_low, dgate[:, D:]), bits),
        ],
        axis=-2,
    )
    keep_b, give_b = split_pair(beside, cross + 2, core_axis, core_bit)
    got_b = swap(give_b, core_axis, core_bit)
    anywhere = pl.BlockSpec(memory_space=pl.ANY)

    def within_back_call(u, dy, bc, cum, cumt, sent, *rest):
        within_back_kernel(u, dy, bc, cum, cumt, *rest)

    dxs, dbc = pl.pallas_call(
        within_back_call,
        grid=(chunks,),
        in_specs=[
            by_chunk(INNER), by_chunk(INNER), by_chunk(2 * STATE), by_chunk(LANES),
            pl.BlockSpec((32, CHUNK), lambda c: (0, c)), anywhere,
        ],
        out_specs=[by_chunk(INNER), by_chunk(2 * STATE)],
        out_shape=[shape((count, INNER), f32), shape((count, 2 * STATE), f32)],
        scratch_shapes=[
            pltpu.VMEM((CHUNK, HEADS * LANES), bf16), pltpu.VMEM((CHUNK, HEADS * LANES), f32),
            pltpu.VMEM((CHUNK, LANES), bf16),
        ],
        compiler_params=params(),
        cost_estimate=cost(12 * 10**9, 16 * 2**20),
        name="within_back",
    )(u, dy, bc, cum, cumt, give_b)

    got_b, dxs, dbc = barrier((got_b, dxs, dbc))
    keep_b, give_b = split_pair(add_low(keep_b, got_b), cross + 1, y_axis, y_bit)
    got_b = swap(give_b, y_axis, y_bit)

    def back(width, height=CHUNK):
        return pl.BlockSpec((height, width), lambda c: (chunks - 1 - c, 0))

    def back_three(height):
        return pl.BlockSpec((1, height, INNER), lambda c: (chunks - 1 - c, 0, 0))

    def back_call(sent, *refs):
        back_kernel(groups, *refs)

    per = CHUNK // 16
    pg, first, tail, wg, hgr, skip = pl.pallas_call(
        back_call,
        grid=(chunks,),
        in_specs=[
            anywhere, smem, back(INNER), back(INNER), back(INNER), back(INNER), back(INNER), back(2 * STATE),
            back(2 * STATE), back(LANES), back(LANES), back(LANES), back_three(STATE),
            pl.BlockSpec((1, 8, LANES), lambda c: (chunks - 1 - c, 0, 0)),
            full((STATE, INNER)), gathered_spec, logs_spec, back_three(STATE), back(SIDE),
            pl.BlockSpec(
                (16, SIDE), lambda c: (jnp.maximum((chunks - 1 - c) * per - 1, 0), 0)
            ),
            full((16, XBC)), full((8, XBC)), full((8, LANES)), full((2 * LANES, INNER)),
            full((2 * INNER, LANES)), full((8, INNER)),
            full(((CONV - 1) * CHUNK, CHUNK + 16)), full(((CONV - 1) * CHUNK, CHUNK + 16)),
        ],
        out_specs=[
            back(SIDE), full((8, XBC)), full((8, XBC)), full((40, XBC)), full((16, LANES)),
            full((8, INNER)),
        ],
        out_shape=[
            shape((count, SIDE), bf16), shape((8, XBC), f32), shape((8, XBC), f32),
            shape((40, XBC), f32), shape((16, LANES), f32), shape((8, INNER), f32),
        ],
        scratch_shapes=[
            pltpu.VMEM((STATE, INNER), f32), pltpu.VMEM((CHUNK + 16, XBC), bf16),
            pltpu.VMEM(((CONV - 1) * CHUNK, XBC), f32), pltpu.VMEM((CHUNK, XBC), f32),
            pltpu.VMEM((CHUNK + 16, XBC), bf16), pltpu.VMEM((CHUNK, INNER), bf16),
            pltpu.VMEM((2 * CHUNK + 16, 2 * INNER), bf16),
        ],
        compiler_params=params(),
        cost_estimate=cost(47 * 10**9, 48 * 2**20),
        name="mixer_back",
    )(
        give_b, rank, dxs, dy, x, u, y, bc, dbc, dcc, cum, dt, hst, pfx, h0, grads, states, ust, proj, proj,
        halo, convp, headp, spread, collect, rows, shift_map(13), shift_map(1),
    )

    got_b, pg, first, tail, wg, hgr, skip = barrier((got_b, pg, first, tail, wg, hgr, skip))
    keep_b, give_b = split_pair(add_low(keep_b, got_b), cross, x_axis, x_bit)
    got_b = swap(give_b, x_axis, x_bit)
    after = lax.ppermute(first, "seq", backward)
    fixes = [jnp.zeros((5, XBC), f32)]
    for m in range(CONV - 1):
        fix = convp[0] * after[m]
        for k in range(1, m + 1):
            fix = fix + convp[k] * after[m - k]
        fixes.append(fix[None, :])
    tail_low = (tail + jnp.concatenate(fixes, axis=0)).astype(bf16)
    pg = lax.dynamic_update_slice(pg, tail_low, (count - 8, 0))

    left = blocks(product(normed_low, pg[:, :half]), bits)
    right = blocks(product(normed_low, pg[:, half:]), bits)
    keep_l, give_l = split_pair(left, cross + 2, core_axis, core_bit)
    keep_r, give_r = split_pair(right, cross + 2, core_axis, core_bit)
    got_l, got_r = swap(give_l, core_axis, core_bit), swap(give_r, core_axis, core_bit)
    pg, dgate, _, _ = barrier((pg, dgate, give_l, give_r))
    normed_grad = lax.dot_general(dgate, full_gate, NT, preferred_element_type=f32)
    normed_grad = normed_grad + lax.dot_general(pg, full_side, NT, preferred_element_type=f32)
    got_l, got_r, got_b, normed_grad = barrier((got_l, got_r, got_b, normed_grad))
    keep_l, give_l = split_pair(add_low(keep_l, got_l), cross + 1, y_axis, y_bit)
    keep_r, give_r = split_pair(add_low(keep_r, got_r), cross, x_axis, x_bit)
    got_l, got_r = swap(give_l, y_axis, y_bit), swap(give_r, x_axis, x_bit)
    beside = add_low(keep_b, got_b)
    keep_b, give_b = split_pair(beside, cross - 1, *bits[cross - 1])
    got_b = swap(give_b, *bits[cross - 1])
    normed_grad, wg, hgr, skip, ng, _, _, _ = barrier(
        (normed_grad, wg, hgr, skip, ng, give_l, give_r, give_b)
    )
    _, norm_pull = jax.vjp(pre_norm, tok_vals, pre_gain)
    tok_norm_grad, pre_gain_grad = norm_pull(normed_grad)
    token_grad = (cot_low.astype(f32) + tok_norm_grad)[None]
    got_l, got_r, got_b, token_grad, pre_gain_grad = barrier(
        (got_l, got_r, got_b, token_grad, pre_gain_grad)
    )
    wg_sum = jnp.sum(wg.reshape(5, 8, XBC), axis=1)
    chan_grad = jnp.concatenate(
        [
            pre_gain_grad,
            jnp.sum(ng, axis=0),
            wg_sum[:CONV].T.reshape(-1),
            wg_sum[CONV],
            jnp.sum(hgr[:8, :HEADS], axis=0),
            jnp.sum(hgr[8:, :HEADS], axis=0),
            jnp.sum(skip.reshape(8, HEADS, HEADDIM), axis=(0, 2)),
        ]
    )

    keep_l, give_l = split_pair(add_low(keep_l, got_l), cross, x_axis, x_bit)
    keep_r, give_r = split_pair(add_low(keep_r, got_r), cross, y_axis, y_bit)
    got_l, got_r = swap(give_l, x_axis, x_bit), swap(give_r, y_axis, y_bit)
    beside = scatter_pairs(add_low(keep_b, got_b), bits[: cross - 1])
    chan_grad = sum_pairs(chan_grad, bits[cross : cross + 1])
    got_l, got_r, beside, chan_grad = barrier((got_l, got_r, beside, chan_grad))
    side = jnp.concatenate([add_low(keep_l, got_l), add_low(keep_r, got_r)], axis=-1)
    for index, place in enumerate(reversed(range(cross))):
        keep, give = split_pair(side, place, *bits[place])
        give, beside, chan_grad = barrier((give, beside, chan_grad))
        got = swap(give, *bits[place])
        if index < 2:
            beside = gather_step(beside, index, *seq_bits[index])
        chan_grad = sum_pairs(chan_grad, [bits[place]])
        got, beside, chan_grad = barrier((got, beside, chan_grad))
        side = add_low(keep, got)
    side, chan_grad = barrier((side, chan_grad))
    got = swap(side, y_axis, y_bit)
    chan_grad = sum_pairs(chan_grad, seq_bits[:1])
    got, chan_grad = barrier((got, chan_grad))
    side = merge_pair(side, got, 0, y_axis, y_bit)
    side, chan_grad = barrier((side, chan_grad))
    got = swap(side, core_axis, core_bit)
    chan_grad = sum_pairs(chan_grad, seq_bits[1:])
    side = flat(merge_pair(side, got, 1, core_axis, core_bit))

    beside = beside.astype(f32)
    out_grad = flat(beside[..., :out_rows, :])
    in_grad = jnp.concatenate(
        [
            flat(beside[..., out_rows : out_rows + in_rows, :]),
            flat(beside[..., out_rows + in_rows :, :]),
            side[:, : PROJ - INNER].astype(f32),
        ],
        axis=1,
    )
    in_new, in_mom, in_sec = adamw_step(
        in_weight, in_moment, in_second, in_grad, rate_matrix, decay_matrix
    )
    out_new, out_mom, out_sec = adamw_step(
        out_weight, out_moment, out_second, out_grad, rate_matrix, decay_matrix
    )
    chan_new, chan_mom, chan_sec = adamw_step(
        channels, channel_moment, channel_second, chan_grad, rate_channel, 0.0
    )
    return (
        block[None],
        token_grad,
        in_new,
        in_mom,
        in_sec,
        out_new,
        out_mom,
        out_sec,
        chan_new,
        chan_mom,
        chan_sec,
    )


def solution(mesh):
    acts = P("dp", "seq", None)
    rows = P("dp", None)
    specs = (acts, acts) + (rows,) * 6 + (P(),) * 3
    return jax.shard_map(local, mesh=mesh, in_specs=specs, out_specs=specs, check_vma=False)
```

```python
import math

import jax
import jax.numpy as jnp
import ml_dtypes
import numpy as np
from jax import lax
from jax.experimental import pallas as pl
from jax.experimental.pallas import tpu as pltpu
from jax.sharding import PartitionSpec as P

D = 768
HEADS = 24
HEADDIM = 64
STATE = 128
CONV = 4
STEP = 10
INNER = 1536
XBC = 1792
PROJ = 3352
SIDE = 1920
LANES = 128
CHUNK = 128
ROWS = 32
PAIRS = HEADS // 2
TILES = XBC // LANES
EXTRA = 16

norm_eps = 1e-05
beta_one = 0.9
beta_two = 0.999
adam_eps = 1e-08
rate_matrix = 0.1
rate_channel = 0.5
decay_matrix = 0.1
LOG2E = 1.0 / math.log(2.0)
VMEM = 56 * 1024 * 1024

f32 = jnp.float32
bf16 = jnp.bfloat16
NT = (((1,), (1,)), ((), ()))
TN = (((0,), (0,)), ((), ()))


def dot(a, b):
    return jnp.dot(a, b, preferred_element_type=f32)


def dot_nt(a, b):
    return lax.dot_general(a, b, NT, preferred_element_type=f32)


def dot_tn(a, b):
    return lax.dot_general(a, b, TN, preferred_element_type=f32)


def sigmoid(v):
    return 0.5 * jnp.tanh(0.5 * v) + 0.5


def halves(v):
    high = v.astype(bf16)
    return high, (v - high.astype(f32)).astype(bf16)


def running(mask, v):
    high, rest = halves(v)
    left = (v - high.astype(f32) - rest.astype(f32)).astype(bf16)
    parts = dot(jnp.where(mask, 1.0, 0.0).astype(bf16), jnp.concatenate([high, rest, left], axis=1))
    return parts[:, :LANES] + parts[:, LANES : 2 * LANES] + parts[:, 2 * LANES :]


def expand(v, spread):
    high, rest = halves(v)
    return dot(jnp.concatenate([high, rest], axis=1), spread)


def fold(v):
    return jnp.sum(v.reshape(v.shape[0] // 8, 8, v.shape[1]), axis=0)


def lane(i):
    return slice(i * LANES, (i + 1) * LANES)


def iota(shape, dim):
    return lax.broadcasted_iota(jnp.int32, shape, dim)


def tri(lower):
    rows, cols = iota((CHUNK, CHUNK), 0), iota((CHUNK, CHUNK), 1)
    return (rows >= cols) if lower else (rows <= cols)


def conv_rows(convp, tile):
    return [jnp.broadcast_to(convp[k : k + 1, lane(tile)], (ROWS, LANES)) for k in range(CONV + 1)]


def conv_pre(shifted, proj, weights, tile, part):
    cols = lane(tile)
    taps = [
        shifted[k * CHUNK + part.start : k * CHUNK + part.stop, cols] for k in range(CONV - 1)
    ] + [proj[part, cols].astype(f32)]
    pre = taps[0] * weights[0] + weights[CONV]
    for k in range(1, CONV):
        pre = pre + taps[k] * weights[k]
    return pre, taps


def pieces():
    return [(start, slice(start, start + ROWS)) for start in range(0, CHUNK, ROWS)]


def pair_stack(v):
    side = iota(v.shape, 1) < HEADDIM
    zero = jnp.zeros_like(v)
    return jnp.concatenate([jnp.where(side, v, zero), jnp.where(side, zero, v)], axis=0)


def conv_state_kernel(
    proj, halo, convp, headp, spread, shifts, x_out, bc_out, u_out, cum_out, cumt_out, dt_out, hst_out,
    pfx_out, send_out, ext, shifted, state, scaled, total,
):
    step = pl.program_id(0)

    @pl.when(step == 0)
    def _():
        ext[0:16, :] = halo[...]
        state[...] = jnp.zeros_like(state)
        total[...] = jnp.zeros_like(total)

    @pl.when(step > 0)
    def _():
        ext[0:16, :] = ext[CHUNK : CHUNK + 16, :]

    ext[16:, :] = proj[:, :XBC]
    shifted[...] = dot(shifts[...], ext[...])
    raw = proj[:, XBC:].astype(f32) + headp[0:1, :]
    steps = jnp.maximum(raw, 0.0) + jnp.log1p(jnp.exp(-jnp.abs(raw)))
    log_decay = steps * (headp[1:2, :] * (-LOG2E))
    cum = running(tri(True), log_decay)
    cum_out[...] = cum
    cumt_out[...] = jnp.transpose(cum)[0:32, :]
    dt_out[...] = steps
    last = cum[CHUNK - 1 : CHUNK, :]
    decayed = jnp.broadcast_to(jnp.exp2(last), (8, LANES))
    wide = expand(jnp.concatenate([steps, jnp.exp2(last - cum), decayed], axis=0), spread[...])
    steps_wide, tail_wide = wide[:CHUNK], wide[CHUNK : 2 * CHUNK]
    decay = wide[2 * CHUNK : 2 * CHUNK + 1]
    for tile in range(TILES):
        cols = lane(tile)
        weights = conv_rows(convp, tile)
        for _, part in pieces():
            pre, _ = conv_pre(shifted, proj, weights, tile, part)
            value = (pre * sigmoid(pre)).astype(bf16)
            if tile < PAIRS:
                x_out[part, cols] = value
                u = (value.astype(f32) * steps_wide[part, cols]).astype(bf16)
                u_out[part, cols] = u
                scaled[part, cols] = (u.astype(f32) * tail_wide[part, cols]).astype(bf16)
            else:
                bc_out[part, lane(tile - PAIRS)] = value
    new_state = state[...] * decay + dot_tn(bc_out[:, :STATE], scaled[...])
    state[...] = new_state
    hst_out[0] = new_state
    new_total = total[...] + jnp.broadcast_to(last, (8, LANES))
    total[...] = new_total
    pfx_out[0] = new_total

    @pl.when(step == pl.num_programs(0) - 1)
    def _():
        send_out[:STATE, :] = new_state.astype(bf16)
        row = iota((EXTRA, LANES), 0)
        wide = jnp.broadcast_to(new_total[0:1, :], (EXTRA, LANES))
        high, rest = halves(wide)
        left = (wide - high.astype(f32) - rest.astype(f32)).astype(bf16)
        parts = jnp.where(
            row == 0,
            high.astype(f32),
            jnp.where(row == 1, rest.astype(f32), jnp.where(row == 2, left.astype(f32), 0.0)),
        )
        send_out[STATE:, :] = dot(parts.astype(bf16), spread[:LANES, :]).astype(bf16)


def within_kernel(u, bc, cum, cumt, y_out, weights):
    scores = jnp.where(tri(True), dot_nt(bc[:, STATE:], bc[:, :STATE]), 0.0)
    for _, part in pieces():
        rows_cum = cum[part, :]
        rows_scores = scores[part]
        for head in range(HEADS):
            gap = rows_cum[:, head : head + 1] - cumt[head : head + 1, :]
            weights[part, lane(head)] = (jnp.exp2(jnp.minimum(gap, 0.0)) * rows_scores).astype(bf16)
    for pair in range(PAIRS):
        both = slice(2 * pair * LANES, 2 * (pair + 1) * LANES)
        y_out[:, lane(pair)] = dot(weights[:, both], pair_stack(u[:, lane(pair)]))


def arrived(gathered, logs, rank, groups, later):
    sums = [
        jnp.sum(logs[g].astype(f32), axis=0, keepdims=True) for g in range(groups)
    ]
    entered = jnp.zeros((STATE, INNER), f32)
    for g in range(groups):
        between = jnp.zeros((1, INNER), f32)
        for s in range(groups):
            if (s < g) if later else (s > g):
                inside = (s > rank) if later else (s < rank)
                between = between + jnp.where(inside, sums[s], 0.0)
        counts = (g > rank) if later else (g < rank)
        weight = jnp.where(counts, jnp.exp2(between), 0.0)
        entered = entered + gathered[g].astype(f32) * weight
    return entered


def gate_kernel(
    groups, rank, y_in, x, bc, cum, hst_a, hst_b, gathered, logs, gate, tok, cot, wout, spread, rows,
    block_out, hidden_out, y_out, dy_out, dgate_out, dcc_out, ust_out, glocal_out, ng_out, h0_out,
    prefix, h0, gsum, hg_all, mixed_all, dy_scaled,
):
    step = pl.program_id(0)

    @pl.when(step == 0)
    def _():
        value = arrived(gathered, logs, rank[0], groups, False)
        h0[...] = value
        h0_out[...] = value
        prefix[...] = jnp.zeros_like(prefix)
        gsum[...] = jnp.zeros_like(gsum)
        ng_out[...] = jnp.zeros_like(ng_out)

    hg_all[...] = dot_nt(cot[...], wout[...])
    gain, skip = rows[0:1, :], rows[1:2, :]
    for sub in range(2):
        whole = slice(sub * CHUNK, (sub + 1) * CHUNK)
        cum_sub = cum[whole, :]
        wide = expand(jnp.exp2(jnp.concatenate([cum_sub, prefix[...]], axis=0)), spread[...])
        grown, start = wide[:CHUNK], wide[CHUNK : CHUNK + 1]
        before = jnp.where(step > 0, hst_a[0], 0.0) if sub == 0 else hst_b[0]
        state_low = (h0[...] * start + before).astype(bf16)
        read = bc[whole, STATE:]
        carried = dot(read, state_low)
        for first, piece in pieces():
            part = slice(sub * CHUNK + first, sub * CHUNK + first + ROWS)
            squares = jnp.zeros((ROWS, LANES), f32)
            cross = jnp.zeros((ROWS, LANES), f32)
            for tile in range(PAIRS):
                cols = lane(tile)
                y = y_in[part, cols] + carried[piece, cols] * grown[piece, cols]
                y_out[part, cols] = y
                mixed = (y + skip[:, cols] * x[part, cols].astype(f32)).astype(bf16)
                mixed_all[piece, cols] = mixed
                gate_val = gate[part, cols].astype(f32)
                gated = mixed.astype(f32) * (gate_val * sigmoid(gate_val))
                squares = squares + gated * gated
                cross = cross + gated * (hg_all[part, cols] * gain[:, cols])
            mean = jnp.sum(squares, axis=1, keepdims=True) * (1.0 / INNER)
            scale = lax.rsqrt(mean + norm_eps)
            cross_mean = jnp.sum(cross, axis=1, keepdims=True) * (1.0 / INNER)
            cross_mean = cross_mean * scale * scale * scale
            scale = jnp.broadcast_to(scale, (ROWS, LANES))
            cross_mean = jnp.broadcast_to(cross_mean, (ROWS, LANES))
            for tile in range(PAIRS):
                cols = lane(tile)
                gate_val = gate[part, cols].astype(f32)
                sig = sigmoid(gate_val)
                silu = gate_val * sig
                mixed = mixed_all[piece, cols].astype(f32)
                gated = mixed * silu
                normal = gated * scale
                hidden_out[part, cols] = (normal * gain[:, cols]).astype(bf16)
                grad = hg_all[part, cols]
                ng_out[:, cols] += fold(grad * normal)
                dgated = grad * gain[:, cols] * scale - gated * cross_mean
                dgate_out[part, cols] = (dgated * mixed * (sig + silu * (1.0 - sig))).astype(bf16)
                dy = (dgated * silu).astype(bf16)
                dy_out[part, cols] = dy
                dy_scaled[piece, cols] = (dy.astype(f32) * grown[piece, cols]).astype(bf16)
        update = dot_tn(read, dy_scaled[...])
        ust_out[sub] = update
        gsum[...] += update * start
        dcc_out[whole, :] = dot_nt(dy_scaled[...], state_low)
        prefix[...] += jnp.broadcast_to(cum_sub[CHUNK - 1 :, :], (8, LANES))
    block_out[...] = tok[...].astype(f32) + dot(hidden_out[...], wout[...])
    glocal_out[...] = gsum[...].astype(bf16)


def within_back_kernel(u, dy, bc, cum, cumt, dxs_out, dbc_out, weights, products, low):
    upper = tri(False)
    scores = jnp.where(upper, dot_nt(bc[:, :STATE], bc[:, STATE:]), 0.0)
    for pair in range(PAIRS):
        both = slice(2 * pair * LANES, 2 * (pair + 1) * LANES)
        products[:, both] = dot_nt(u[:, lane(pair)], pair_stack(dy[:, lane(pair)]))
    for _, part in pieces():
        rows_cum = cum[part, :]
        rows_scores = scores[part]
        total = jnp.zeros((ROWS, LANES), f32)
        for head in range(HEADS):
            gap = cumt[head : head + 1, :] - rows_cum[:, head : head + 1]
            decay = jnp.exp2(jnp.minimum(gap, 0.0))
            weights[part, lane(head)] = (decay * rows_scores).astype(bf16)
            total = total + decay * products[part, lane(head)]
        low[part, :] = jnp.where(upper[part], total, 0.0).astype(bf16)
    for pair in range(PAIRS):
        both = slice(2 * pair * LANES, 2 * (pair + 1) * LANES)
        dxs_out[:, lane(pair)] = dot(weights[:, both], pair_stack(dy[:, lane(pair)]))
    dbc_out[:, :STATE] = dot(low[...], bc[:, STATE:])
    dbc_out[:, STATE:] = dot_tn(low[...], bc[:, :STATE])


def back_kernel(
    groups, rank, dxs, dy, x, u, y, bc, dbc, dcc, cum, dt, hst, pfx, h0, gathered, logs, ust, proj,
    before, halo, convp, headp, spread, collect, rows, shifts, ahead,
    pg_out, first_out, tail_out, wg_out, hg_out, skip_out,
    gstate, ext, shifted, dpres, dlow, scaled, prod,
):
    step = pl.program_id(0)
    chunk = pl.num_programs(0) - 1 - step

    @pl.when(step == 0)
    def _():
        gstate[...] = arrived(gathered, logs, rank[0], groups, True)
        dlow[CHUNK:, :] = jnp.zeros((16, XBC), bf16)
        wg_out[...] = jnp.zeros_like(wg_out)
        hg_out[...] = jnp.zeros_like(hg_out)
        skip_out[...] = jnp.zeros_like(skip_out)

    @pl.when(step > 0)
    def _():
        dlow[CHUNK:, :] = dlow[0:16, :]

    @pl.when(chunk == 0)
    def _():
        ext[0:16, :] = halo[...]

    @pl.when(chunk > 0)
    def _():
        ext[0:16, :] = before[:, :XBC]

    ext[16:, :] = proj[:, :XBC]
    shifted[...] = dot(shifts[...], ext[...])
    grad_state = gstate[...]
    grad_low = grad_state.astype(bf16)
    last = cum[CHUNK - 1 : CHUNK, :]
    decayed = jnp.broadcast_to(jnp.exp2(last), (8, LANES))
    wide = expand(
        jnp.concatenate([jnp.exp2(last - cum[...]), dt[...], decayed, jnp.exp2(pfx[0])], axis=0),
        spread[...],
    )
    tail_wide, steps_wide = wide[:CHUNK], wide[CHUNK : 2 * CHUNK]
    decay = wide[2 * CHUNK : 2 * CHUNK + 1]
    end = wide[2 * CHUNK + 8 : 2 * CHUNK + 9]
    reach = dot(bc[:, :STATE], grad_low)

    def conv_back(tile, grad_of):
        cols = lane(tile)
        weights = conv_rows(convp, tile)
        sums = [jnp.zeros((8, LANES), f32) for _ in range(CONV + 1)]
        for _, part in pieces():
            grad = grad_of(part)
            pre, taps = conv_pre(shifted, proj, weights, tile, part)
            sig = sigmoid(pre)
            dpre = grad * (sig + pre * sig * (1.0 - sig))
            dpres[part, cols] = dpre
            dlow[part, cols] = dpre.astype(bf16)
            sums = [total + fold(dpre * tap) for total, tap in zip(sums, taps)] + [
                sums[CONV] + fold(dpre)
            ]

        for k in range(CONV + 1):
            wg_out[8 * k : 8 * k + 8, cols] += sums[k]

    for tile in range(PAIRS):
        cols = lane(tile)
        rest_cols = slice(INNER + tile * LANES, INNER + (tile + 1) * LANES)
        skip_row = jnp.broadcast_to(rows[1:2, cols], (ROWS, LANES))
        skips = []

        def grad_of(part, cols=cols, rest_cols=rest_cols, skip_row=skip_row, skips=skips):
            below = slice(CHUNK + part.start, CHUNK + part.stop)
            dxs_full = dxs[part, cols] + tail_wide[part, cols] * reach[part, cols]
            uf = u[part, cols].astype(f32)
            dyf = dy[part, cols].astype(f32)
            scaled[part, cols] = (uf * tail_wide[part, cols]).astype(bf16)
            q = uf * dxs_full
            prod[part, cols], prod[part, rest_cols] = halves(q)
            prod[below, cols], prod[below, rest_cols] = halves(dyf * y[part, cols] - q)
            skips.append(fold(dyf * x[part, cols].astype(f32)))
            return skip_row * dyf + steps_wide[part, cols] * dxs_full

        conv_back(tile, grad_of)
        skip_out[:, cols] += sum(skips[1:], skips[0])
    dwrite = dot_nt(scaled[...], grad_low)
    conv_back(PAIRS, lambda part: dbc[part, :STATE] + dwrite[part])
    conv_back(PAIRS + 1, lambda part: dbc[part, STATE:] + dcc[part, :])
    first_out[...] = dpres[0:8, :]
    shifted[...] = dot(ahead[...], dlow[...])
    for tile in range(TILES):
        cols = lane(tile)
        weights = conv_rows(convp, tile)
        for _, part in pieces():
            source = dpres[part, cols] * weights[CONV - 1]
            for k in range(CONV - 1):
                block = (CONV - 2 - k) * CHUNK
                source = source + shifted[block + part.start : block + part.stop, cols] * weights[k]
            pg_out[part, cols] = source.astype(bf16)
            dpres[part, cols] = source

    @pl.when(step == 0)
    def _():
        tail_out[...] = dpres[CHUNK - 8 :, :]


    meet = fold(grad_state * (hst[0] + h0[...] * end))
    meet = jnp.concatenate([meet, jnp.zeros_like(meet)], axis=0)
    high, rest = halves(meet)
    prod[2 * CHUNK :, :INNER] = high
    prod[2 * CHUNK :, INNER:] = rest
    heads = dot(prod[...], collect[...])
    q_heads, gap_heads = heads[:CHUNK], heads[CHUNK : 2 * CHUNK]
    meet_heads = jnp.sum(heads[2 * CHUNK :], axis=0, keepdims=True)
    dlog = running(tri(False), gap_heads) + meet_heads
    sig = sigmoid(proj[:, XBC:].astype(f32) + headp[0:1, :])
    steps = dt[...]
    ratio = jnp.where(steps > 1e-30, sig / jnp.maximum(steps, 1e-30), 1.0)
    raw_grad = q_heads * ratio - dlog * headp[1:2, :] * sig
    pg_out[:, XBC:] = raw_grad.astype(bf16)
    hg_out[0:8, :] += fold(raw_grad)
    hg_out[8:16, :] += fold(dlog * steps * headp[1:2, :]) * (-1.0)
    gstate[...] = grad_state * decay + ust[0]


def swap(v, axis, bit):
    size = lax.axis_size(axis)
    return lax.ppermute(v, axis, [(i, i ^ (1 << bit)) for i in range(size)])


def mesh_bits():
    found = []
    for axis in ("dp", "seq"):
        for bit in reversed(range(lax.axis_size(axis).bit_length() - 1)):
            found.append((axis, bit))
    return found


def mine(axis, bit):
    return (lax.axis_index(axis) >> bit) & 1


def merge_pair(v, other, place, axis, bit):
    second = mine(axis, bit) == 1
    return jnp.stack([jnp.where(second, other, v), jnp.where(second, v, other)], axis=place)


def gather_step(v, place, axis, bit):
    return merge_pair(v, swap(v, axis, bit), place, axis, bit)


def gather_pairs(v, bits, lead=0):
    for place, (axis, bit) in enumerate(bits):
        v = gather_step(v, lead + place, axis, bit)
    return v


def flat(v):
    return v.reshape(-1, v.shape[-1])


def blocks(v, bits):
    return v.reshape((2,) * len(bits) + (v.shape[0] >> len(bits), v.shape[1]))


def split_pair(v, place, axis, bit):
    own = mine(axis, bit)
    keep = lax.dynamic_index_in_dim(v, own, place, keepdims=False)
    give = lax.dynamic_index_in_dim(v, 1 - own, place, keepdims=False)
    return keep, give


def add_low(keep, got):
    return (keep.astype(f32) + got.astype(f32)).astype(keep.dtype)


def scatter_step(v, place, axis, bit):
    keep, give = split_pair(v, place, axis, bit)
    return add_low(keep, swap(give, axis, bit))


def scatter_pairs(v, bits, lead=0):
    for place in reversed(range(len(bits))):
        v = scatter_step(v, lead + place, *bits[place])
    return v


def sum_pairs(v, bits):
    for axis, bit in bits:
        v = v + swap(v, axis, bit)
    return v


def full(shape):
    return pl.BlockSpec(shape, lambda c: (0,) * len(shape))


def by_chunk(width, rows=CHUNK):
    return pl.BlockSpec((rows, width), lambda c: (c, 0))


def shape(dims, dtype):
    return jax.ShapeDtypeStruct(dims, dtype)


def params():
    return pltpu.CompilerParams(dimension_semantics=("arbitrary",), vmem_limit_bytes=VMEM)


def cost(flops, moved):
    return pl.CostEstimate(flops=flops, bytes_accessed=moved, transcendentals=0)


def spread_map():
    heads = np.arange(LANES)[:, None]
    cols = np.arange(INNER)[None, :] // HEADDIM
    once = (heads == cols).astype(ml_dtypes.bfloat16)
    return np.concatenate([once, once], axis=0)


def shift_map(first):
    rows = np.arange((CONV - 1) * CHUNK)
    picked = rows % CHUNK + rows // CHUNK + first
    return (picked[:, None] == np.arange(CHUNK + 16)[None, :]).astype(ml_dtypes.bfloat16)


def unpack_channels(channels):
    pieces = []
    offset = 0
    for piece_len in (D, INNER, XBC * CONV, XBC, HEADS, HEADS, HEADS):
        pieces.append(channels[offset : offset + piece_len])
        offset = offset + piece_len
    pre_gain, norm_gain, conv_flat, conv_bias, step_bias, rate_log, skip_gain = pieces
    return (
        pre_gain,
        norm_gain,
        conv_flat.reshape(XBC, CONV),
        conv_bias,
        step_bias,
        rate_log,
        skip_gain,
    )


def pre_norm(tok_vals, pre_gain):
    return (
        tok_vals * lax.rsqrt(jnp.mean(tok_vals * tok_vals, -1, keepdims=True) + norm_eps) * pre_gain
    )


def adamw_step(weight, moment, second, gradient, step_rate, decay_rate):
    moment_next = beta_one * moment + (1.0 - beta_one) * gradient
    second_next = beta_two * second + (1.0 - beta_two) * gradient * gradient
    first_fix = 1.0 - beta_one**STEP
    second_fix = 1.0 - beta_two**STEP
    update = moment_next / first_fix / (jnp.sqrt(second_next / second_fix) + adam_eps)
    return (weight - step_rate * (update + decay_rate * weight), moment_next, second_next)


def local(
    tokens,
    cotangent,
    in_weight,
    in_moment,
    in_second,
    out_weight,
    out_moment,
    out_second,
    channels,
    channel_moment,
    channel_second,
):
    groups = lax.axis_size("seq")
    bits = mesh_bits()
    seq_bits = [(axis, bit) for axis, bit in bits if axis == "seq"]
    seq_rank = lax.axis_index("seq")
    rank = seq_rank.astype(jnp.int32).reshape(1)
    tok_low = tokens[0]
    cot_low = cotangent[0]
    count = tok_low.shape[0]
    chunks = count // CHUNK

    def quarter(weight):
        size = weight.shape[0] // groups
        return lax.dynamic_slice_in_dim(weight, seq_rank * size, size, 0).astype(bf16)

    in_part = quarter(in_weight)
    side_part = jnp.pad(in_part[:, INNER:], ((0, 0), (0, SIDE + INNER - PROJ)))
    out_rows = out_weight.shape[0] // groups
    in_rows = in_weight.shape[0] // groups
    beside = jnp.concatenate(
        [quarter(out_weight), in_part[:, :D], in_part[:, D:INNER]], axis=0
    )
    barrier = lax.optimization_barrier
    cross = len(bits) - 3
    (x_axis, x_bit), (y_axis, y_bit), (core_axis, core_bit) = bits[cross:]
    early = cross // 2
    side = gather_pairs(side_part, bits[:early])
    beside = gather_pairs(beside, bits[:early])
    side, tok_low = barrier((side, tok_low))
    side = gather_pairs(side, bits[early:cross], early)
    side, beside = barrier((side, beside))
    half = SIDE // 256 * 128
    left, right = side[..., :half], side[..., half:]
    got_l, got_r = swap(left, x_axis, x_bit), swap(right, y_axis, y_bit)
    beside = gather_pairs(beside, bits[early:cross], early)
    left = merge_pair(left, got_l, cross, x_axis, x_bit)
    right = merge_pair(right, got_r, cross, y_axis, y_bit)
    got_l, got_r = swap(left, y_axis, y_bit), swap(right, x_axis, x_bit)
    got_l, got_r, beside = barrier((got_l, got_r, beside))
    left = merge_pair(left, got_l, cross + 1, y_axis, y_bit)
    right = merge_pair(right, got_r, cross, x_axis, x_bit)
    got_l, got_r = swap(left, core_axis, core_bit), swap(right, core_axis, core_bit)
    beside_l, beside_r = beside[..., : D // 2], beside[..., D // 2 :]
    got_b = swap(beside_l, x_axis, x_bit), swap(beside_r, y_axis, y_bit)
    left = merge_pair(left, got_l, cross + 2, core_axis, core_bit)
    right = merge_pair(right, got_r, cross + 2, core_axis, core_bit)
    full_side = jnp.concatenate([flat(left), flat(right)], axis=1)

    pre_gain, norm_gain, conv_weight, conv_bias, step_bias, rate_log, skip_gain = unpack_channels(
        channels
    )
    forward = [(s, s + 1) for s in range(groups - 1)]
    backward = [(s + 1, s) for s in range(groups - 1)]
    tok_halo = lax.ppermute(tokens[0, count - 16 :], "seq", forward)
    halo_norm = pre_norm(tok_halo.astype(f32), pre_gain).astype(bf16)
    tok_vals = tok_low.astype(f32)
    normed_low = pre_norm(tok_vals, pre_gain).astype(bf16)

    convp = jnp.concatenate(
        [conv_weight.T, conv_bias[None, :], jnp.zeros((3, XBC), f32)], axis=0
    )
    pad_heads = lambda v: jnp.pad(v, (0, LANES - HEADS))[None, :]
    headp = jnp.concatenate(
        [pad_heads(step_bias), pad_heads(jnp.exp(rate_log)), jnp.zeros((6, LANES), f32)], axis=0
    )
    rows = jnp.concatenate(
        [norm_gain[None, :], jnp.repeat(skip_gain, HEADDIM)[None, :], jnp.zeros((6, INNER), f32)],
        axis=0,
    )
    spread = spread_map()
    collect = np.concatenate([spread[:LANES].T, spread[:LANES].T], axis=0)

    proj = dot(normed_low, full_side).astype(bf16)
    halo = dot(halo_norm, full_side[:, :XBC]).astype(bf16)
    proj, halo, got_b = barrier((proj, halo, got_b))
    beside_l = merge_pair(beside_l, got_b[0], cross, x_axis, x_bit)
    beside_r = merge_pair(beside_r, got_b[1], cross, y_axis, y_bit)
    got_b = swap(beside_l, y_axis, y_bit), swap(beside_r, x_axis, x_bit)

    x, bc, u, cum, cumt, dt, hst, pfx, send = pl.pallas_call(
        conv_state_kernel,
        grid=(chunks,),
        in_specs=[
            by_chunk(SIDE), full((16, XBC)), full((8, XBC)), full((8, LANES)),
            full((2 * LANES, INNER)), full(((CONV - 1) * CHUNK, CHUNK + 16)),
        ],
        out_specs=[
            by_chunk(INNER), by_chunk(2 * STATE), by_chunk(INNER), by_chunk(LANES),
            pl.BlockSpec((32, CHUNK), lambda c: (0, c)), by_chunk(LANES),
            pl.BlockSpec((1, STATE, INNER), lambda c: (c, 0, 0)),
            pl.BlockSpec((1, 8, LANES), lambda c: (c, 0, 0)),
            full((STATE + EXTRA, INNER)),
        ],
        out_shape=[
            shape((count, INNER), bf16), shape((count, 2 * STATE), bf16),
            shape((count, INNER), bf16), shape((count, LANES), f32), shape((32, count), f32),
            shape((count, LANES), f32), shape((chunks, STATE, INNER), f32),
            shape((chunks, 8, LANES), f32), shape((STATE + EXTRA, INNER), bf16),
        ],
        scratch_shapes=[
            pltpu.VMEM((CHUNK + 16, XBC), bf16), pltpu.VMEM(((CONV - 1) * CHUNK, XBC), f32),
            pltpu.VMEM((STATE, INNER), f32), pltpu.VMEM((CHUNK, INNER), bf16),
            pltpu.VMEM((8, LANES), f32),
        ],
        compiler_params=params(),
        cost_estimate=cost(24 * 10**9, 24 * 2**20),
        name="conv_state",
    )(proj, halo, convp, headp, spread, shift_map(13))

    states = lax.all_gather(send, "seq", axis=0, tiled=False)
    x, bc, u, cum, cumt, dt, hst, pfx, got_b = barrier(
        (x, bc, u, cum, cumt, dt, hst, pfx, got_b)
    )
    beside_l = merge_pair(beside_l, got_b[0], cross + 1, y_axis, y_bit)
    beside_r = merge_pair(beside_r, got_b[1], cross, x_axis, x_bit)
    beside = jnp.concatenate([beside_l, beside_r], axis=-1)
    got_b = swap(beside, core_axis, core_bit)

    y_within = pl.pallas_call(
        within_kernel,
        grid=(chunks,),
        in_specs=[
            by_chunk(INNER), by_chunk(2 * STATE), by_chunk(LANES),
            pl.BlockSpec((32, CHUNK), lambda c: (0, c)),
        ],
        out_specs=by_chunk(INNER),
        out_shape=shape((count, INNER), f32),
        scratch_shapes=[pltpu.VMEM((CHUNK, HEADS * LANES), bf16)],
        compiler_params=params(),
        cost_estimate=cost(11 * 10**9, 16 * 2**20),
        name="within",
    )(u, bc, cum, cumt)
    y_within, got_b = barrier((y_within, got_b))
    beside = merge_pair(beside, got_b, cross + 2, core_axis, core_bit)
    full_out = flat(beside[..., :out_rows, :])
    full_gate = jnp.concatenate(
        [
            flat(beside[..., out_rows : out_rows + in_rows, :]),
            flat(beside[..., out_rows + in_rows :, :]),
        ],
        axis=1,
    )
    gate = dot(normed_low, full_gate).astype(bf16)

    gathered_spec = full((groups, STATE, INNER))
    logs_spec = pl.BlockSpec((groups, EXTRA, INNER), lambda c: (0, STATE // EXTRA, 0))
    smem = pl.BlockSpec(memory_space=pltpu.SMEM)

    def gate_call(*refs):
        gate_kernel(groups, *refs)

    def by_two(width):
        return by_chunk(width, 2 * CHUNK)

    block, hidden, y, dy, dgate, dcc, ust, glocal, ng, h0 = pl.pallas_call(
        gate_call,
        grid=(chunks // 2,),
        in_specs=[
            smem, by_two(INNER), by_two(INNER), by_two(2 * STATE), by_two(LANES),
            pl.BlockSpec((1, STATE, INNER), lambda c: (jnp.maximum(2 * c - 1, 0), 0, 0)),
            pl.BlockSpec((1, STATE, INNER), lambda c: (2 * c, 0, 0)),
            gathered_spec, logs_spec, by_two(INNER), by_two(D), by_two(D),
            full((INNER, D)), full((2 * LANES, INNER)), full((8, INNER)),
        ],
        out_specs=[
            by_two(D), by_two(INNER), by_two(INNER), by_two(INNER), by_two(INNER),
            by_two(LANES), pl.BlockSpec((2, STATE, INNER), lambda c: (c, 0, 0)),
            full((STATE, INNER)), full((8, INNER)), full((STATE, INNER)),
        ],
        out_shape=[
            shape((count, D), f32), shape((count, INNER), bf16), shape((count, INNER), f32),
            shape((count, INNER), bf16), shape((count, INNER), bf16), shape((count, LANES), f32),
            shape((chunks, STATE, INNER), f32), shape((STATE, INNER), bf16), shape((8, INNER), f32),
            shape((STATE, INNER), f32),
        ],
        scratch_shapes=[
            pltpu.VMEM((8, LANES), f32), pltpu.VMEM((STATE, INNER), f32),
            pltpu.VMEM((STATE, INNER), f32), pltpu.VMEM((2 * CHUNK, INNER), f32), pltpu.VMEM((CHUNK, INNER), bf16),
            pltpu.VMEM((CHUNK, INNER), bf16),
        ],
        compiler_params=params(),
        cost_estimate=cost(24 * 10**9, 48 * 2**20),
        name="gate_norm",
    )(
        rank, y_within, x, bc, cum, hst, hst, states, states, gate, tok_low, cot_low, full_out, spread, rows,
    )

    grads = lax.all_gather(glocal, "seq", axis=0, tiled=False)

    def product(left, right):
        return lax.dot_general(left, right, TN, preferred_element_type=f32).astype(bf16)

    gate_blocks = blocks(product(normed_low, dgate), bits)
    beside = jnp.concatenate(
        [blocks(product(hidden, cot_low), bits), gate_blocks[..., :D], gate_blocks[..., D:]],
        axis=-2,
    )
    keep_b, give_b = split_pair(beside, cross + 2, core_axis, core_bit)
    got_b = swap(give_b, core_axis, core_bit)
    anywhere = pl.BlockSpec(memory_space=pl.ANY)

    def within_back_call(u, dy, bc, cum, cumt, sent, *rest):
        within_back_kernel(u, dy, bc, cum, cumt, *rest)

    dxs, dbc = pl.pallas_call(
        within_back_call,
        grid=(chunks,),
        in_specs=[
            by_chunk(INNER), by_chunk(INNER), by_chunk(2 * STATE), by_chunk(LANES),
            pl.BlockSpec((32, CHUNK), lambda c: (0, c)), anywhere,
        ],
        out_specs=[by_chunk(INNER), by_chunk(2 * STATE)],
        out_shape=[shape((count, INNER), f32), shape((count, 2 * STATE), f32)],
        scratch_shapes=[
            pltpu.VMEM((CHUNK, HEADS * LANES), bf16), pltpu.VMEM((CHUNK, HEADS * LANES), f32),
            pltpu.VMEM((CHUNK, LANES), bf16),
        ],
        compiler_params=params(),
        cost_estimate=cost(12 * 10**9, 16 * 2**20),
        name="within_back",
    )(u, dy, bc, cum, cumt, give_b)

    got_b, dxs, dbc = barrier((got_b, dxs, dbc))
    beside = add_low(keep_b, got_b)
    keep_b, give_b = split_pair(beside[..., : D // 2], cross + 1, y_axis, y_bit)
    keep_c, give_c = split_pair(beside[..., D // 2 :], cross, x_axis, x_bit)
    got_b, got_c = swap(give_b, y_axis, y_bit), swap(give_c, x_axis, x_bit)

    def back(width, height=CHUNK):
        return pl.BlockSpec((height, width), lambda c: (chunks - 1 - c, 0))

    def back_three(height):
        return pl.BlockSpec((1, height, INNER), lambda c: (chunks - 1 - c, 0, 0))

    def back_call(sent_b, sent_c, *refs):
        back_kernel(groups, *refs)

    per = CHUNK // 16
    pg, first, tail, wg, hgr, skip = pl.pallas_call(
        back_call,
        grid=(chunks,),
        in_specs=[
            anywhere, anywhere, smem, back(INNER), back(INNER), back(INNER), back(INNER), back(INNER), back(2 * STATE),
            back(2 * STATE), back(LANES), back(LANES), back(LANES), back_three(STATE),
            pl.BlockSpec((1, 8, LANES), lambda c: (chunks - 1 - c, 0, 0)),
            full((STATE, INNER)), gathered_spec, logs_spec, back_three(STATE), back(SIDE),
            pl.BlockSpec(
                (16, SIDE), lambda c: (jnp.maximum((chunks - 1 - c) * per - 1, 0), 0)
            ),
            full((16, XBC)), full((8, XBC)), full((8, LANES)), full((2 * LANES, INNER)),
            full((2 * INNER, LANES)), full((8, INNER)),
            full(((CONV - 1) * CHUNK, CHUNK + 16)), full(((CONV - 1) * CHUNK, CHUNK + 16)),
        ],
        out_specs=[
            back(SIDE), full((8, XBC)), full((8, XBC)), full((40, XBC)), full((16, LANES)),
            full((8, INNER)),
        ],
        out_shape=[
            shape((count, SIDE), bf16), shape((8, XBC), f32), shape((8, XBC), f32),
            shape((40, XBC), f32), shape((16, LANES), f32), shape((8, INNER), f32),
        ],
        scratch_shapes=[
            pltpu.VMEM((STATE, INNER), f32), pltpu.VMEM((CHUNK + 16, XBC), bf16),
            pltpu.VMEM(((CONV - 1) * CHUNK, XBC), f32), pltpu.VMEM((CHUNK, XBC), f32),
            pltpu.VMEM((CHUNK + 16, XBC), bf16), pltpu.VMEM((CHUNK, INNER), bf16),
            pltpu.VMEM((2 * CHUNK + 16, 2 * INNER), bf16),
        ],
        compiler_params=params(),
        cost_estimate=cost(47 * 10**9, 48 * 2**20),
        name="mixer_back",
    )(
        give_b, give_c, rank, dxs, dy, x, u, y, bc, dbc, dcc, cum, dt, hst, pfx, h0, grads, states, ust, proj, proj,
        halo, convp, headp, spread, collect, rows, shift_map(13), shift_map(1),
    )

    got_b, got_c, pg, first, tail, wg, hgr, skip = barrier(
        (got_b, got_c, pg, first, tail, wg, hgr, skip)
    )
    keep_b, give_b = split_pair(add_low(keep_b, got_b), cross, x_axis, x_bit)
    keep_c, give_c = split_pair(add_low(keep_c, got_c), cross, y_axis, y_bit)
    got_b, got_c = swap(give_b, x_axis, x_bit), swap(give_c, y_axis, y_bit)
    after = lax.ppermute(first, "seq", backward)
    fixes = [jnp.zeros((5, XBC), f32)]
    for m in range(CONV - 1):
        fix = convp[0] * after[m]
        for k in range(1, m + 1):
            fix = fix + convp[k] * after[m - k]
        fixes.append(fix[None, :])
    tail_low = (tail + jnp.concatenate(fixes, axis=0)).astype(bf16)
    pg = lax.dynamic_update_slice(pg, tail_low, (count - 8, 0))

    left = blocks(product(normed_low, pg[:, :half]), bits)
    right = blocks(product(normed_low, pg[:, half:]), bits)
    keep_l, give_l = split_pair(left, cross + 2, core_axis, core_bit)
    keep_r, give_r = split_pair(right, cross + 2, core_axis, core_bit)
    got_l, got_r = swap(give_l, core_axis, core_bit), swap(give_r, core_axis, core_bit)
    pg, dgate, _, _ = barrier((pg, dgate, give_l, give_r))
    normed_grad = lax.dot_general(dgate, full_gate, NT, preferred_element_type=f32)
    normed_grad = normed_grad + lax.dot_general(pg, full_side, NT, preferred_element_type=f32)
    got_l, got_r, got_b, got_c, normed_grad = barrier((got_l, got_r, got_b, got_c, normed_grad))
    keep_l, give_l = split_pair(add_low(keep_l, got_l), cross + 1, y_axis, y_bit)
    keep_r, give_r = split_pair(add_low(keep_r, got_r), cross, x_axis, x_bit)
    got_l, got_r = swap(give_l, y_axis, y_bit), swap(give_r, x_axis, x_bit)
    beside = jnp.concatenate([add_low(keep_b, got_b), add_low(keep_c, got_c)], axis=-1)
    keep_b, give_b = split_pair(beside, cross - 1, *bits[cross - 1])
    got_b = swap(give_b, *bits[cross - 1])
    normed_grad, wg, hgr, skip, ng, _, _, _ = barrier(
        (normed_grad, wg, hgr, skip, ng, give_l, give_r, give_b)
    )
    _, norm_pull = jax.vjp(pre_norm, tok_vals, pre_gain)
    tok_norm_grad, pre_gain_grad = norm_pull(normed_grad)
    token_grad = (cot_low.astype(f32) + tok_norm_grad)[None]
    got_l, got_r, got_b, token_grad, pre_gain_grad = barrier(
        (got_l, got_r, got_b, token_grad, pre_gain_grad)
    )
    wg_sum = jnp.sum(wg.reshape(5, 8, XBC), axis=1)
    chan_grad = jnp.concatenate(
        [
            pre_gain_grad,
            jnp.sum(ng, axis=0),
            wg_sum[:CONV].T.reshape(-1),
            wg_sum[CONV],
            jnp.sum(hgr[:8, :HEADS], axis=0),
            jnp.sum(hgr[8:, :HEADS], axis=0),
            jnp.sum(skip.reshape(8, HEADS, HEADDIM), axis=(0, 2)),
        ]
    )

    keep_l, give_l = split_pair(add_low(keep_l, got_l), cross, x_axis, x_bit)
    keep_r, give_r = split_pair(add_low(keep_r, got_r), cross, y_axis, y_bit)
    got_l, got_r = swap(give_l, x_axis, x_bit), swap(give_r, y_axis, y_bit)
    beside = scatter_pairs(add_low(keep_b, got_b), bits[: cross - 1])
    chan_grad = sum_pairs(chan_grad, bits[cross : cross + 1])
    got_l, got_r, beside, chan_grad = barrier((got_l, got_r, beside, chan_grad))
    side = jnp.concatenate([add_low(keep_l, got_l), add_low(keep_r, got_r)], axis=-1)
    for index, place in enumerate(reversed(range(cross))):
        keep, give = split_pair(side, place, *bits[place])
        give, beside, chan_grad = barrier((give, beside, chan_grad))
        got = swap(give, *bits[place])
        if index < 2:
            beside = gather_step(beside, index, *seq_bits[index])
        chan_grad = sum_pairs(chan_grad, [bits[place]])
        got, beside, chan_grad = barrier((got, beside, chan_grad))
        side = add_low(keep, got)
    side, chan_grad = barrier((side, chan_grad))
    got = swap(side, y_axis, y_bit)
    chan_grad = sum_pairs(chan_grad, seq_bits[:1])
    got, chan_grad = barrier((got, chan_grad))
    side = merge_pair(side, got, 0, y_axis, y_bit)
    side, chan_grad = barrier((side, chan_grad))
    got = swap(side, core_axis, core_bit)
    chan_grad = sum_pairs(chan_grad, seq_bits[1:])
    side = flat(merge_pair(side, got, 1, core_axis, core_bit))

    beside = beside.astype(f32)
    out_grad = flat(beside[..., :out_rows, :])
    in_grad = jnp.concatenate(
        [
            flat(beside[..., out_rows : out_rows + in_rows, :]),
            flat(beside[..., out_rows + in_rows :, :]),
            side[:, : PROJ - INNER].astype(f32),
        ],
        axis=1,
    )
    in_new, in_mom, in_sec = adamw_step(
        in_weight, in_moment, in_second, in_grad, rate_matrix, decay_matrix
    )
    out_new, out_mom, out_sec = adamw_step(
        out_weight, out_moment, out_second, out_grad, rate_matrix, decay_matrix
    )
    chan_new, chan_mom, chan_sec = adamw_step(
        channels, channel_moment, channel_second, chan_grad, rate_channel, 0.0
    )
    return (
        block[None],
        token_grad,
        in_new,
        in_mom,
        in_sec,
        out_new,
        out_mom,
        out_sec,
        chan_new,
        chan_mom,
        chan_sec,
    )


def solution(mesh):
    acts = P("dp", "seq", None)
    rows = P("dp", None)
    specs = (acts, acts) + (rows,) * 6 + (P(),) * 3
    return jax.shard_map(local, mesh=mesh, in_specs=specs, out_specs=specs, check_vma=False)
```
